128 devices in a mesh: shard: 16 (over x_hi, y, core), context: 2 (over x_lo), tensor: 4 (over z).
Axes of the slice: x: 4 (x_hi: 2, x_lo: 2; x = x_hi * 2 + x_lo), y: 4, z: 4, core: 2. Of those that a mesh axis runs over, the one named last changes fastest.
Arguments:
- hidden_in: bfloat16 [16, 1792, 1536], P('shard', ('context', 'tensor')), may hold values from -1.1953125 to 1.1953125
- cotangent: bfloat16 [16, 1792, 1536], P('shard', ('context', 'tensor')), may hold values from -9 to 9
- prefix: int32 [16], P('shard'), may hold values from 1 to 1344, as said below
- positions: int32 [16, 1792], P('shard', 'context'), may hold values from 0 to 3582, as said below
- norm_gains: float32 [2, 1536], replicated, may hold values from 0.38 to 2.5
- gains_first: float32 [2, 1536], replicated, may hold values from -0.0002695215 to 0.0002695215
- gains_second: float32 [2, 1536], replicated, may hold values from 6.253602e-09 to 1.8760806e-08
- input_weight: float32 [1536, 2560], P(('shard', 'context'), 'tensor'), may hold values from -0.22963966 to 0.22963966
- input_first: float32 [1536, 2560], P(('shard', 'context'), 'tensor'), may hold values from -8.9840505e-05 to 8.9840505e-05
- input_second: float32 [1536, 2560], P(('shard', 'context'), 'tensor'), may hold values from 1.2507204e-09 to 1.6676273e-08
- output_weight: float32 [1536, 1536], P('tensor', ('shard', 'context')), may hold values from -0.75 to 0.75
- output_first: float32 [1536, 1536], P('tensor', ('shard', 'context')), may hold values from -8.9840505e-05 to 8.9840505e-05
- output_second: float32 [1536, 1536], P('tensor', ('shard', 'context')), may hold values from 4.1690681e-10 to 1.2507204e-09
- expand_weight: float32 [2, 1536, 3840], P(None, ('shard', 'context'), 'tensor'), may hold values from -0.22963966 to 0.22963966
- expand_first: float32 [2, 1536, 3840], P(None, ('shard', 'context'), 'tensor'), may hold values from -8.9840505e-05 to 8.9840505e-05
- expand_second: float32 [2, 1536, 3840], P(None, ('shard', 'context'), 'tensor'), may hold values from 1.2507204e-09 to 1.6676273e-08
- shrink_weight: float32 [3840, 1536], P('tensor', ('shard', 'context')), may hold values from -0.09375 to 0.09375
- shrink_first: float32 [3840, 1536], P('tensor', ('shard', 'context')), may hold values from -8.9840505e-05 to 8.9840505e-05
- shrink_second: float32 [3840, 1536], P('tensor', ('shard', 'context')), may hold values from 1.2507204e-09 to 1.6676273e-08
Outputs:
- block_output: bfloat16 [16, 1792, 1536], P('shard', ('context', 'tensor'))
- input_gradient: float32 [16, 1792, 1536], P('shard', ('context', 'tensor'))
- gradient_norm: float32 [], replicated
- gains_momentum: float32 [2, 1536], replicated
- gains_variance: float32 [2, 1536], replicated
- gains_updated: float32 [2, 1536], replicated
- input_momentum: float32 [1536, 2560], P(('shard', 'context'), 'tensor')
- input_variance: float32 [1536, 2560], P(('shard', 'context'), 'tensor')
- input_updated: float32 [1536, 2560], P(('shard', 'context'), 'tensor')
- output_momentum: float32 [1536, 1536], P('tensor', ('shard', 'context'))
- output_variance: float32 [1536, 1536], P('tensor', ('shard', 'context'))
- output_updated: float32 [1536, 1536], P('tensor', ('shard', 'context'))
- expand_momentum: float32 [2, 1536, 3840], P(None, ('shard', 'context'), 'tensor')
- expand_variance: float32 [2, 1536, 3840], P(None, ('shard', 'context'), 'tensor')
- expand_updated: float32 [2, 1536, 3840], P(None, ('shard', 'context'), 'tensor')
- shrink_momentum: float32 [3840, 1536], P('tensor', ('shard', 'context'))
- shrink_variance: float32 [3840, 1536], P('tensor', ('shard', 'context'))
- shrink_updated: float32 [3840, 1536], P('tensor', ('shard', 'context'))
The draws below stay inside these ranges and needn't reach their ends.
Inputs may be any that keep to these rules, and one draw needn't show every extreme that they name: The first sequence's prefix is exactly 1344. Within a sequence the positions start at 0 and rise by 1 or 2 from one token to the next; in the first sequence they rise by 2 throughout.
All inputs are finite; a program needn't handle non-finite values.
Results may differ from the reference program's by a relative error of at most 0.04.
Values may be sent and summed in bfloat16 or wider, within the bound.
A program may use at most 192 MiB of HBM per device.

```python
import math
import jax
import jax.numpy as jnp
from jax import lax

D = 1536
HD = 64
KV = 8
GROUP = 3
FF = 3840
QKV = 2560
HQ = 1536
PARAMS = 23986176
LEN = 1792
SEQS = 16
STEP = 10


def linear_ramp(count, low_end, high_end):
    return jnp.linspace(low_end, high_end, count, dtype=jnp.float32)


def draw_cotangent(key, part):
    key = jax.random.fold_in(key, 2)
    random_part = jnp.clip(jax.random.normal(key, (SEQS, LEN, D), jnp.float32), -5.0, 5.0)
    rising = linear_ramp(D, 0.6, 1.8)
    return (random_part * rising).astype(jnp.bfloat16)


def draw_prefix(key, part):
    key = jax.random.fold_in(key, 7)
    ceiling = LEN * 3 // 4
    lengths = jax.random.randint(key, (SEQS,), 1, ceiling + 1)
    return lengths.at[0].set(ceiling).astype(jnp.int32)


def draw_positions(key, part):
    key = jax.random.fold_in(key, 8)
    stride = jax.random.randint(key, (SEQS, LEN), 1, 3)
    stride = stride.at[0].set(2)
    return (jnp.cumsum(stride, axis=1) - stride).astype(jnp.int32)


def draw_norm_gains(key, part):
    key = jax.random.fold_in(key, 1)
    random_part = 1.0 + 0.05 * jnp.clip(jax.random.normal(key, (2, D), jnp.float32), -3.0, 3.0)
    rising = linear_ramp(D, 0.6, 1.8)
    return random_part * rising


def draw_input_weight(key, part):
    key = jax.random.fold_in(key, 3)
    random_part = jnp.clip(jax.random.normal(key, (D, QKV), jnp.float32), -5.0, 5.0)
    rising = linear_ramp(KV, 0.6, 1.8)
    columns = jnp.arange(QKV, dtype=jnp.int32)
    slot_index = columns // HD % (GROUP + 2)
    head_index = columns // ((GROUP + 2) * HD)
    scaling = jnp.where(slot_index == GROUP + 1, rising[head_index], 1.0)
    return random_part * scaling * D ** (-0.5)


def draw_expand_weight(key, part):
    key = jax.random.fold_in(key, 4)
    random_part = jnp.clip(jax.random.normal(key, (2, D, FF), jnp.float32), -5.0, 5.0)
    rising = linear_ramp(FF, 0.6, 1.8)
    scaling = jnp.stack([jnp.ones((FF,), jnp.float32), rising])[:, None, :]
    return random_part * scaling * D ** (-0.5)


def block_scale(rng, dims, shards, low, top_value):
    factor_of, own = 1.0, jax.random.fold_in(rng, 6)
    for axis_at, parts in shards:
        draws = jnp.exp(jax.random.uniform(jax.random.fold_in(own, axis_at), (parts,), jnp.float32, low / len(shards), top_value / len(shards)))
        factor_of = factor_of * jnp.repeat(draws, dims[axis_at] // parts).reshape([-1 if axis == axis_at else 1 for axis in range(len(dims))])
    return factor_of


def bell_draw(stream_key, shape, scale, most, split=(), kind=jnp.bfloat16):
    entries = scale * jax.random.normal(stream_key, shape, jnp.float32)
    if split:
        entries = entries * block_scale(stream_key, shape, split, -0.22, 0.18)
    return jnp.clip(entries, -most, most).astype(kind)


def setup_inputs(seed: int = 0) -> dict:
    seeds = jax.random.split(jax.random.key(seed), 20)
    return {
        "hidden_in": bell_draw(seeds[0], (SEQS, LEN, D), 0.2, 1.1953125, ((0, 16), (1, 8))),
        "cotangent": draw_cotangent(jax.random.fold_in(seeds[19], 71), 0),
        "prefix": draw_prefix(jax.random.fold_in(seeds[19], 71), 0),
        "positions": draw_positions(jax.random.fold_in(seeds[19], 71), 0),
        "norm_gains": draw_norm_gains(jax.random.fold_in(seeds[19], 71), 0),
        "gains_first": bell_draw(seeds[5], (2, D), (0.33 * PARAMS ** -0.5), 0.0002695215, (), jnp.float32),
        "gains_second": jnp.clip(jnp.exp(jax.random.uniform(seeds[6], (2, D), jnp.float32, math.log(6.253602080619203e-09), math.log(1.8760806241857608e-08))), 6.253602080619203e-09, 1.8760806241857608e-08),
        "input_weight": draw_input_weight(jax.random.fold_in(seeds[19], 71), 0),
        "input_first": bell_draw(seeds[8], (D, QKV), (0.11 * PARAMS ** -0.5), 8.984050509752706e-05, ((0, 32), (1, 4)), jnp.float32),
        "input_second": jnp.clip(jnp.exp(math.log(1.6676272807103487e-08) - 2.5902672 * jax.random.uniform(seeds[9], (D, QKV), jnp.float32) ** block_scale(seeds[9], (D, QKV), ((0, 32), (1, 4)), -0.2, 0.2)), 1.2507204161238406e-09, 1.6676272807103487e-08),
        "output_weight": bell_draw(seeds[10], (HQ, D), HD ** -0.5, 0.75, ((0, 4), (1, 32)), jnp.float32),
        "output_first": bell_draw(seeds[11], (HQ, D), (0.11 * PARAMS ** -0.5), 8.984050509752706e-05, ((0, 4), (1, 32)), jnp.float32),
        "output_second": jnp.clip(jnp.exp(math.log(1.2507204161238406e-09) - 1.0986123 * jax.random.uniform(seeds[12], (HQ, D), jnp.float32) ** block_scale(seeds[12], (HQ, D), ((0, 4), (1, 32)), -0.2, 0.2)), 4.1690681462647206e-10, 1.2507204161238406e-09),
        "expand_weight": draw_expand_weight(jax.random.fold_in(seeds[19], 71), 0),
        "expand_first": bell_draw(seeds[14], (2, D, FF), (0.11 * PARAMS ** -0.5), 8.984050509752706e-05, ((1, 32), (2, 4)), jnp.float32),
        "expand_second": jnp.clip(jnp.exp(math.log(1.6676272807103487e-08) - 2.5902672 * jax.random.uniform(seeds[15], (2, D, FF), jnp.float32) ** block_scale(seeds[15], (2, D, FF), ((1, 32), (2, 4)), -0.2, 0.2)), 1.2507204161238406e-09, 1.6676272807103487e-08),
        "shrink_weight": bell_draw(seeds[16], (FF, D), FF ** -0.5, 0.09375, ((0, 4), (1, 32)), jnp.float32),
        "shrink_first": bell_draw(seeds[17], (FF, D), (0.11 * PARAMS ** -0.5), 8.984050509752706e-05, ((0, 4), (1, 32)), jnp.float32),
        "shrink_second": jnp.clip(jnp.exp(math.log(1.6676272807103487e-08) - 2.5902672 * jax.random.uniform(seeds[18], (FF, D), jnp.float32) ** block_scale(seeds[18], (FF, D), ((0, 4), (1, 32)), -0.2, 0.2)), 1.2507204161238406e-09, 1.6676272807103487e-08),
    }


EPS = 1e-05
RESID = 1.4 / math.sqrt(52.0)
ROPE_BASE = 10000.0
MAX_NORM = 1.0
RATE = 0.1
GAIN_RATE = 1.0
BETA_ONE = 0.9
BETA_TWO = 0.95
ADAM_EPS = 1e-08
DECAY = 0.1
NEG = -1e+30
PRECISE = lax.Precision.HIGHEST

@jax.custom_vjp
def low(v):
    return lax.optimization_barrier(v.astype(jnp.bfloat16)).astype(jnp.float32)

@jax.custom_vjp
def low_back(v):
    return v

def low_keep(v):
    return (low(v), None)

def low_pass(kept, grad):
    return (grad,)

def back_keep(v):
    return (v, None)

def back_low(kept, grad):
    return (low(grad),)
low.defvjp(low_keep, low_pass)
low_back.defvjp(back_keep, back_low)

def angles(places):
    half_width = HD // 2
    frequency = ROPE_BASE ** (-2.0 * jnp.arange(half_width, dtype=jnp.float32) / HD)
    phase_turn = places.astype(jnp.float32)[..., None] * frequency
    return (jnp.cos(phase_turn), jnp.sin(phase_turn))

def rotate(values, cos_part, sin_part):
    half_width = values.shape[-1] // 2
    lower_half = values[..., :half_width]
    upper_half = values[..., half_width:]
    return jnp.concatenate([lower_half * cos_part - upper_half * sin_part, upper_half * cos_part + lower_half * sin_part], axis=-1)

def visible(query_count, key_count, row_start, prefix_len):
    row_index = row_start + jnp.arange(query_count, dtype=jnp.int32)[:, None]
    col_index = jnp.arange(key_count, dtype=jnp.int32)[None, :]
    return (col_index <= row_index) | (col_index < prefix_len)

def rms_norm(values, gains):
    return values * lax.rsqrt(lax.optimization_barrier(jnp.mean(values * values, axis=-1, keepdims=True)) + EPS) * gains

def layer(inputs, norm_gains, input_weight, output_weight, expand_weight, shrink_weight, places, prefix_len):
    length = inputs.shape[0]
    first_input = low(rms_norm(inputs, norm_gains[0]))
    packed_projection = low_back(jnp.dot(first_input, low(input_weight), precision=PRECISE))
    packed_parts = packed_projection.reshape(length, KV, GROUP + 2, HD)
    cos_part, sin_part = angles(places)
    queries = low(rotate(packed_parts[:, :, :GROUP], cos_part[:, None, None], sin_part[:, None, None]))
    key_rows = low(rotate(packed_parts[:, :, GROUP], cos_part[:, None], sin_part[:, None]))
    value_rows = low(packed_parts[:, :, GROUP + 1])
    scores = low_back(jnp.einsum('qgjd,kgd->gjqk', queries, key_rows, precision=PRECISE) * HD ** (-0.5))
    scores = jnp.where(visible(length, length, 0, prefix_len), scores, NEG)
    row_max = lax.optimization_barrier(jnp.max(scores, axis=-1, keepdims=True))
    shifted = jnp.exp(scores - row_max)
    probs_low = low(shifted / lax.optimization_barrier(jnp.sum(shifted, axis=-1, keepdims=True)))
    attended = jnp.einsum('gjqk,kgd->qgjd', probs_low, value_rows, precision=PRECISE).reshape(length, KV * GROUP * HD)
    attended = low_back(low(attended))
    projected = low_back(jnp.dot(attended, low(output_weight), precision=PRECISE))
    residual = inputs + RESID * projected
    second_input = low(rms_norm(residual, norm_gains[1]))
    gate_value = low_back(jnp.dot(second_input, low(expand_weight[0]), precision=PRECISE))
    up_value = low_back(jnp.dot(second_input, low(expand_weight[1]), precision=PRECISE))
    gated_hidden = low(jax.nn.silu(gate_value) * up_value)
    shrunk = low_back(jnp.dot(gated_hidden, low(shrink_weight), precision=PRECISE))
    return residual + RESID * shrunk

def adamw(weight, gradient, momentum, variance, step_rate, decay_rate):
    momentum_new = BETA_ONE * momentum + (1.0 - BETA_ONE) * gradient
    variance_new = BETA_TWO * variance + (1.0 - BETA_TWO) * gradient * gradient
    momentum_hat = momentum_new / (1.0 - BETA_ONE ** STEP)
    variance_hat = variance_new / (1.0 - BETA_TWO ** STEP)
    updated = weight - step_rate * (momentum_hat / (jnp.sqrt(variance_hat) + ADAM_EPS) + decay_rate * weight)
    return (momentum_new, variance_new, updated)

def reference(hidden_in, cotangent, prefix, positions, norm_gains, gains_first, gains_second, input_weight, input_first, input_second, output_weight, output_first, output_second, expand_weight, expand_first, expand_second, shrink_weight, shrink_first, shrink_second):
    params = (norm_gains, input_weight, output_weight, expand_weight, shrink_weight)

    def accumulate(totals, slices):
        inputs, cot_rows, prefix_len, places = slices

        def single(inputs_f, gains_f, in_f, out_f, expand_f, shrink_f):
            return layer(inputs_f, gains_f, in_f, out_f, expand_f, shrink_f, places, prefix_len)
        result, pullback = jax.vjp(single, inputs.astype(jnp.float32), params[0], params[1], params[2], params[3], params[4])
        gradients = pullback(cot_rows.astype(jnp.float32))
        totals = tuple((total + gradient for total, gradient in zip(totals, gradients[1:])))
        return (totals, (result.astype(jnp.bfloat16), gradients[0]))
    zeros = tuple((jnp.zeros_like(param) for param in params))
    totals, (block_output, input_gradient) = lax.scan(accumulate, zeros, (hidden_in, cotangent, prefix, positions))
    squares = jnp.sum(totals[0] * totals[0])
    for gradient in totals[1:]:
        squares = squares + jnp.sum(gradient * gradient)
    gradient_norm = jnp.sqrt(squares)
    factor = jnp.minimum(1.0, MAX_NORM / (gradient_norm + 1e-06))
    gains_new = adamw(norm_gains, factor * totals[0], gains_first, gains_second, GAIN_RATE, 0.0)
    input_new = adamw(input_weight, factor * totals[1], input_first, input_second, RATE, DECAY)
    output_new = adamw(output_weight, factor * totals[2], output_first, output_second, RATE, DECAY)
    expand_new = adamw(expand_weight, factor * totals[3], expand_first, expand_second, RATE, DECAY)
    shrink_new = adamw(shrink_weight, factor * totals[4], shrink_first, shrink_second, RATE, DECAY)
    return (block_output, input_gradient, gradient_norm, gains_new[0], gains_new[1], gains_new[2], input_new[0], input_new[1], input_new[2], output_new[0], output_new[1], output_new[2], expand_new[0], expand_new[1], expand_new[2], shrink_new[0], shrink_new[1], shrink_new[2])
```

```python
import functools
import math

import jax
import jax.numpy as jnp
from jax import lax
from jax.experimental import pallas as pl
from jax.experimental.pallas import tpu as pltpu
from jax.sharding import PartitionSpec as P

HD = 64
GROUP = 3
STEP = 10
HEADS = 2
BLOCKS = 7
VMEM_MOST = 60 * 2**20
MESH = pl.DeviceIdType.MESH


EPS = 1e-05
RESID = 1.4 / math.sqrt(52.0)
ROPE_BASE = 10000.0
MAX_NORM = 1.0
RATE = 0.1
GAIN_RATE = 1.0
BETA_ONE = 0.9
BETA_TWO = 0.95
ADAM_EPS = 1e-08
DECAY = 0.1
NEG = -1e30


def angles(places):
    half_width = HD // 2
    frequency = ROPE_BASE ** (-2.0 * jnp.arange(half_width, dtype=jnp.float32) / HD)
    phase_turn = places.astype(jnp.float32)[None, :] * frequency[:, None]
    return (jnp.cos(phase_turn), jnp.sin(phase_turn))


def rms_parts(values):
    scaling = lax.rsqrt(jnp.mean(values * values, axis=-1, keepdims=True) + EPS)
    return (values * scaling, scaling)


def rms_back(gradient, normed, scaling):
    return scaling * (gradient - normed * jnp.mean(gradient * normed, axis=-1, keepdims=True))


def adamw(weight, gradient, momentum, variance, step_rate, decay_rate):
    momentum_new = BETA_ONE * momentum + (1.0 - BETA_ONE) * gradient
    variance_new = BETA_TWO * variance + (1.0 - BETA_TWO) * gradient * gradient
    momentum_hat = momentum_new / (1.0 - BETA_ONE**STEP)
    variance_hat = variance_new / (1.0 - BETA_TWO**STEP)
    updated = weight - step_rate * (
        momentum_hat / (jnp.sqrt(variance_hat) + ADAM_EPS) + decay_rate * weight
    )
    return (momentum_new, variance_new, updated)


def nn(a, b):
    return lax.dot_general(a, b, (((1,), (0,)), ((), ())), preferred_element_type=jnp.float32)


def nt(a, b):
    return lax.dot_general(a, b, (((1,), (1,)), ((), ())), preferred_element_type=jnp.float32)


def place():
    shard = lax.axis_index("shard")
    return (
        shard // 8,
        lax.rem(shard // 2, 4),
        lax.rem(shard, 2),
        lax.axis_index("context"),
        lax.axis_index("tensor"),
    )


def device(xh, y, core, xl, z):
    return {"shard": (xh * 4 + y) * 2 + core, "context": xl, "tensor": z}


def greet(peers):
    barrier = pltpu.get_barrier_semaphore()
    for peer in peers:
        pl.semaphore_signal(barrier, inc=1, device_id=peer, device_id_type=MESH)
    pl.semaphore_wait(barrier, len(peers))


def remote(src, dst, send_sem, recv_sem, peer):
    return pltpu.make_async_remote_copy(
        src_ref=src,
        dst_ref=dst,
        send_sem=send_sem,
        recv_sem=recv_sem,
        device_id=peer,
        device_id_type=MESH,
    )


def turn(block, cos_part, sin_part):
    lower_half, upper_half = block[: HD // 2], block[HD // 2 :]
    return jnp.concatenate(
        [
            lower_half * cos_part - upper_half * sin_part,
            upper_half * cos_part + lower_half * sin_part,
        ],
        axis=0,
    )


def turn_back(block, cos_part, sin_part):
    return turn(block, cos_part, -sin_part)


def lay_keys(held, kv_rows):
    for g in range(HEADS):
        both = jnp.concatenate(
            [held[0, g * 128 : (g + 1) * 128, :], held[1, g * 128 : (g + 1) * 128, :]], axis=1
        )
        kv_rows[g] = jnp.transpose(both.astype(jnp.float32)).astype(jnp.bfloat16)


def by_span(context, b, run):
    near = (context == 0) | (b <= 3)

    @pl.when(near)
    def _():
        run(1408)

    @pl.when(jnp.logical_not(near))
    def _():
        run(1792)


def attend_kernel(
    packed, cos_ref, sin_ref, limit, turned, kv_all, attended, log_total, kv_rows, send_sem, recv_sem
):
    xh, y, core, xl, z = place()
    peer = device(xh, y, core, 1 - xl, z)
    greet([peer])
    cos_part, sin_part = cos_ref[...], sin_ref[...]
    for g in range(HEADS):
        base = g * 5 * HD
        kv_all[xl, g * 128 : g * 128 + HD] = turn(
            packed[base + 3 * HD : base + 4 * HD], cos_part, sin_part
        ).astype(jnp.bfloat16)
        kv_all[xl, g * 128 + HD : (g + 1) * 128] = packed[base + 4 * HD : base + 5 * HD].astype(
            jnp.bfloat16
        )
    copy = remote(kv_all.at[xl], kv_all.at[xl], send_sem, recv_sem, peer)
    copy.start()
    for g in range(HEADS):
        base = g * 5 * HD
        for h in range(GROUP):
            turned[(g * GROUP + h) * HD : (g * GROUP + h + 1) * HD] = (
                turn(packed[base + h * HD : base + (h + 1) * HD], cos_part, sin_part)
                * HD ** (-0.5)
            ).astype(jnp.bfloat16)
    copy.wait()
    lay_keys(kv_all, kv_rows)

    def block(t, carry):
        b, g = t // HEADS, lax.rem(t, HEADS)
        columns = pl.ds(pl.multiple_of(b * 128, 128), 128)

        def run(span):
            head_rows = [
                pl.ds(pl.multiple_of((g * GROUP + h) * HD, HD), HD) for h in range(GROUP)
            ]
            queries = jnp.concatenate([turned[r, columns] for r in head_rows], axis=1)
            queries = jnp.concatenate([queries, jnp.zeros_like(queries)], axis=0)
            scores = nn(kv_rows[g, :span], queries)
            key_index = lax.broadcasted_iota(jnp.int32, (span, 384), 0)
            scores = jnp.where(key_index < limit[b], scores, NEG)
            row_max = jnp.max(scores, axis=0, keepdims=True)
            shifted = jnp.exp(scores - row_max)
            exp_total = jnp.sum(shifted, axis=0, keepdims=True)
            value_rows = pl.ds(pl.multiple_of(g * 128 + HD, HD), HD)
            values = jnp.concatenate([kv_all[0, value_rows], kv_all[1, value_rows]], axis=1)
            total = nn(values[:, :span], shifted.astype(jnp.bfloat16)) * (1.0 / exp_total)
            for h in range(GROUP):
                attended[head_rows[h], columns] = total[:, h * 128 : (h + 1) * 128].astype(
                    jnp.bfloat16
                )
            log_total[t] = row_max + jnp.log(exp_total)

        by_span(xl, b, run)
        return carry

    lax.fori_loop(0, HEADS * BLOCKS, block, 0)


def attend_forward(packed, cos_part, sin_part, limit):
    return pl.pallas_call(
        attend_kernel,
        out_shape=(
            jax.ShapeDtypeStruct((384, 896), jnp.bfloat16),
            jax.ShapeDtypeStruct((2, 256, 896), jnp.bfloat16),
            jax.ShapeDtypeStruct((384, 896), jnp.bfloat16),
            jax.ShapeDtypeStruct((HEADS * BLOCKS, 1, 384), jnp.float32),
        ),
        scratch_shapes=[
            pltpu.VMEM((HEADS, 1792, 128), jnp.bfloat16),
            pltpu.SemaphoreType.DMA,
            pltpu.SemaphoreType.DMA,
        ],
        compiler_params=pltpu.CompilerParams(
            collective_id=1, has_side_effects=True, vmem_limit_bytes=VMEM_MOST
        ),
    )(packed, cos_part, sin_part, limit)


def attend_back_kernel(
    turned,
    kv_all,
    attended,
    log_total,
    grad_attended,
    cos_ref,
    sin_ref,
    limit,
    grad_packed,
    kv_rows,
    sums,
    outgoing,
    incoming,
    send_sem,
    recv_sem,
):
    xh, y, core, xl, z = place()
    peer = device(xh, y, core, 1 - xl, z)
    greet([peer])
    cos_part, sin_part = cos_ref[...], sin_ref[...]
    lay_keys(kv_all, kv_rows)
    sums[...] = jnp.zeros_like(sums)

    def block(t, carry):
        b, g = t // HEADS, lax.rem(t, HEADS)
        columns = pl.ds(pl.multiple_of(b * 128, 128), 128)

        def run(span):
            head_rows = [
                pl.ds(pl.multiple_of((g * GROUP + h) * HD, HD), HD) for h in range(GROUP)
            ]
            queries = jnp.concatenate([turned[r, columns] for r in head_rows], axis=1)
            gradient = jnp.concatenate([grad_attended[r, columns] for r in head_rows], axis=1)
            held = jnp.concatenate([attended[r, columns] for r in head_rows], axis=1)
            inner = jnp.sum(
                gradient.astype(jnp.float32) * held.astype(jnp.float32), axis=0, keepdims=True
            )
            nothing = jnp.zeros_like(queries)
            both = jnp.concatenate(
                [
                    jnp.concatenate([queries, nothing], axis=1),
                    jnp.concatenate([nothing, gradient], axis=1),
                ],
                axis=0,
            )
            products = nn(kv_rows[g, :span], both)
            key_index = lax.broadcasted_iota(jnp.int32, (span, 384), 0)
            probs = jnp.exp(
                jnp.where(key_index < limit[b], products[:, :384], NEG) - log_total[t]
            )
            grad_scores = (probs * (products[:, 384:] - inner)).astype(jnp.bfloat16)
            sums[g, :span] += nt(
                jnp.concatenate([grad_scores, probs.astype(jnp.bfloat16)], axis=1), both
            )
            key_lines = pl.ds(pl.multiple_of(g * 128, HD), HD)
            keys = jnp.concatenate([kv_all[0, key_lines], kv_all[1, key_lines]], axis=1)
            total = nn(keys[:, :span], grad_scores) * HD ** (-0.5)
            cos_here, sin_here = cos_ref[:, columns], sin_ref[:, columns]
            for h in range(GROUP):
                lines = pl.ds(pl.multiple_of((g * 5 + h) * HD, HD), HD)
                grad_packed[lines, columns] = turn_back(
                    total[:, h * 128 : (h + 1) * 128], cos_here, sin_here
                ).astype(jnp.bfloat16)

        by_span(xl, b, run)
        return carry

    lax.fori_loop(0, HEADS * BLOCKS, block, 0)
    for g in range(HEADS):
        theirs = sums[g, pl.ds(pl.multiple_of((1 - xl) * 896, 128), 896)]
        outgoing[g * 128 : (g + 1) * 128] = jnp.transpose(theirs).astype(jnp.bfloat16)
    copy = remote(outgoing, incoming, send_sem, recv_sem, peer)
    copy.start()
    copy.wait()
    for g in range(HEADS):
        mine = jnp.transpose(sums[g, pl.ds(pl.multiple_of(xl * 896, 128), 896)])
        mine = mine + incoming[g * 128 : (g + 1) * 128].astype(jnp.float32)
        base = g * 5 * HD
        grad_packed[base + 3 * HD : base + 4 * HD] = turn_back(
            mine[:HD], cos_part, sin_part
        ).astype(jnp.bfloat16)
        grad_packed[base + 4 * HD : base + 5 * HD] = mine[HD:].astype(jnp.bfloat16)


def attend_backward(turned, kv_all, attended, log_total, grad_attended, cos_part, sin_part, limit):
    return pl.pallas_call(
        attend_back_kernel,
        out_shape=jax.ShapeDtypeStruct((640, 896), jnp.bfloat16),
        scratch_shapes=[
            pltpu.VMEM((HEADS, 1792, 128), jnp.bfloat16),
            pltpu.VMEM((HEADS, 1792, 128), jnp.float32),
            pltpu.VMEM((256, 896), jnp.bfloat16),
            pltpu.VMEM((256, 896), jnp.bfloat16),
            pltpu.SemaphoreType.DMA,
            pltpu.SemaphoreType.DMA,
        ],
        compiler_params=pltpu.CompilerParams(
            collective_id=2, has_side_effects=True, vmem_limit_bytes=VMEM_MOST
        ),
    )(turned, kv_all, attended, log_total, grad_attended, cos_part, sin_part, limit)


def ring_peers():
    xh, y, core, xl, z = place()
    return (
        z,
        lax.rem(z + 1, 4),
        lax.rem(z + 2, 4),
        lax.rem(z + 3, 4),
        device(xh, y, core, xl, lax.rem(z + 1, 4)),
        device(xh, y, core, xl, lax.rem(z + 3, 4)),
    )


def halves(ref, index):
    rows = ref.shape[1] // 2
    return ref.at[index, pl.ds(0, rows)], ref.at[index, pl.ds(rows, rows)]


def ring_gather_begin(own, held, send_sem, recv_sem):
    z, zp, z2, zm, up, down = ring_peers()
    rows = own.shape[0] // 2
    first, second = own.at[pl.ds(0, rows)], own.at[pl.ds(rows, rows)]
    first_to, second_to = halves(held, z)
    copies = [
        remote(first, first_to, send_sem.at[0], recv_sem.at[0], up),
        remote(second, second_to, send_sem.at[1], recv_sem.at[1], down),
        remote(second, second_to, send_sem.at[2], recv_sem.at[2], up),
        remote(first, first_to, send_sem.at[3], recv_sem.at[3], down),
    ]
    for copy in copies:
        copy.start()
    return copies


def ring_gather_forward(held, copies, send_sem, recv_sem):
    z, zp, z2, zm, up, down = ring_peers()
    copies[0].wait_recv()
    below = halves(held, zm)[0]
    on_up = remote(below, below, send_sem.at[4], recv_sem.at[4], up)
    on_up.start()
    copies[1].wait_recv()
    above = halves(held, zp)[1]
    on_down = remote(above, above, send_sem.at[5], recv_sem.at[5], down)
    on_down.start()
    return copies + [on_up, on_down]


def ring_gather_end(copies):
    for copy in copies:
        copy.wait_send()
    for copy in copies[2:]:
        copy.wait_recv()


def ring_gather_kernel(own, held, send_sem, recv_sem, own_sem):
    z, zp, z2, zm, up, down = ring_peers()
    greet([up, down])
    copies = ring_gather_begin(own, held, send_sem, recv_sem)
    keep = pltpu.make_async_copy(own, held.at[z], own_sem)
    keep.start()
    copies = ring_gather_forward(held, copies, send_sem, recv_sem)
    keep.wait()
    ring_gather_end(copies)


def ring_gather(rows, identity):
    count, width = rows.shape
    held = pl.pallas_call(
        ring_gather_kernel,
        out_shape=jax.ShapeDtypeStruct((4, count, width), rows.dtype),
        in_specs=[pl.BlockSpec(memory_space=pl.ANY)],
        out_specs=pl.BlockSpec(memory_space=pl.ANY),
        scratch_shapes=[
            pltpu.SemaphoreType.DMA((6,)),
            pltpu.SemaphoreType.DMA((6,)),
            pltpu.SemaphoreType.DMA,
        ],
        compiler_params=pltpu.CompilerParams(
            collective_id=identity, has_side_effects=True, vmem_limit_bytes=VMEM_MOST
        ),
    )(rows)
    return held.reshape(4 * count, width)


def in_rows(count, step, run):
    def body(i, carry):
        run(pl.ds(pl.multiple_of(i * step, step), step))
        return carry

    lax.fori_loop(0, count // step, body, 0)


def ring_scatter_begin(parts, came, send_sem, recv_sem):
    z, zp, z2, zm, up, down = ring_peers()
    copies = [
        remote(halves(parts, z2)[1], came.at[0], send_sem.at[0], recv_sem.at[0], up),
        remote(halves(parts, z2)[0], came.at[1], send_sem.at[1], recv_sem.at[1], down),
        remote(halves(parts, zp)[0], came.at[2], send_sem.at[2], recv_sem.at[2], up),
        remote(halves(parts, zm)[1], came.at[3], send_sem.at[3], recv_sem.at[3], down),
    ]
    for copy in copies:
        copy.start()
    return copies


def ring_scatter_forward(parts, came, sums, copies, send_sem, recv_sem):
    z, zp, z2, zm, up, down = ring_peers()
    count = came.shape[1]
    copies[0].wait_recv()

    def add_up(rows):
        sums[0, rows] = (
            came[0, rows].astype(jnp.float32)
            + parts[zp, pl.ds(pl.multiple_of(rows.start + count, 16), 16)].astype(jnp.float32)
        ).astype(jnp.bfloat16)

    in_rows(count, 16, add_up)
    on_up = remote(sums.at[0], came.at[4], send_sem.at[4], recv_sem.at[4], up)
    on_up.start()
    copies[1].wait_recv()

    def add_down(rows):
        sums[1, rows] = (
            came[1, rows].astype(jnp.float32) + parts[zm, rows].astype(jnp.float32)
        ).astype(jnp.bfloat16)

    in_rows(count, 16, add_down)
    on_down = remote(sums.at[1], came.at[5], send_sem.at[5], recv_sem.at[5], down)
    on_down.start()
    return copies + [on_up, on_down]


def ring_scatter_end(parts, came, total, copies):
    z, zp, z2, zm, up, down = ring_peers()
    count = came.shape[1]
    for copy in copies[2:]:
        copy.wait_recv()
    for copy in copies:
        copy.wait_send()

    def add(rows):
        later = pl.ds(pl.multiple_of(rows.start + count, 16), 16)
        total[rows] = (
            parts[z, rows].astype(jnp.float32)
            + came[2, rows].astype(jnp.float32)
            + came[5, rows].astype(jnp.float32)
        )
        total[later] = (
            parts[z, later].astype(jnp.float32)
            + came[3, rows].astype(jnp.float32)
            + came[4, rows].astype(jnp.float32)
        )

    in_rows(count, 16, add)


def ring_scatter_kernel(parts, total, came, sums, send_sem, recv_sem):
    z, zp, z2, zm, up, down = ring_peers()
    greet([up, down])
    copies = ring_scatter_begin(parts, came, send_sem, recv_sem)
    copies = ring_scatter_forward(parts, came, sums, copies, send_sem, recv_sem)
    ring_scatter_end(parts, came, total, copies)


def ring_scatter(parts, identity):
    rows, width = parts.shape
    count = rows // 4
    return pl.pallas_call(
        ring_scatter_kernel,
        out_shape=jax.ShapeDtypeStruct((count, width), jnp.float32),
        scratch_shapes=[
            pltpu.VMEM((6, count // 2, width), jnp.bfloat16),
            pltpu.VMEM((2, count // 2, width), jnp.bfloat16),
            pltpu.SemaphoreType.DMA((6,)),
            pltpu.SemaphoreType.DMA((6,)),
        ],
        compiler_params=pltpu.CompilerParams(
            collective_id=identity, has_side_effects=True, vmem_limit_bytes=VMEM_MOST
        ),
    )(parts.reshape(4, count, width))


def plane():
    xh, y, core, xl, z = place()
    ys = [lax.rem(y + d, 4) for d in (1, 3, 2)]
    step = xh * 2 + xl
    xs = [lax.rem(step + d, 4) for d in (1, 3, 2)]
    xs = [(x // 2, lax.rem(x, 2)) for x in xs]
    y_peers = [device(xh, other, core, xl, z) for other in ys]
    x_peers = [device(h, y, core, l, z) for h, l in xs]
    return ys, xs, y_peers, x_peers, device(xh, y, 1 - core, xl, z)


class PlaneGather:
    def __init__(self, own, held, y_first, send_sem, recv_sem):
        self.own, self.held, self.y_first = own, held, y_first
        self.send_sem, self.recv_sem, self.used = send_sem, recv_sem, 0
        self.copies, self.first, self.second, self.third = [], [], [], []

    def send(self, src, dst, peer):
        copy = remote(src, dst, self.send_sem.at[self.used], self.recv_sem.at[self.used], peer)
        self.used += 1
        copy.start()
        self.copies.append(copy)
        return copy

    def begin(self):
        xh, y, core, xl, z = place()
        ys, xs, y_peers, x_peers, other = plane()
        target = self.held.at[xh, y, core, xl]
        peers = y_peers if self.y_first else x_peers
        self.first = [self.send(self.own, target, peer) for peer in peers]

    def line(self, where):
        xh, y, core, xl, z = place()
        if self.y_first:
            return self.held.at[where[0], :, core, where[1]]
        return self.held.at[:, where, core, :]

    def spread(self):
        xh, y, core, xl, z = place()
        ys, xs, y_peers, x_peers, other = plane()
        for copy in self.first:
            copy.wait_recv()
        mine = self.line((xh, xl) if self.y_first else y)
        peers = x_peers if self.y_first else y_peers
        self.second = [self.send(mine, mine, peer) for peer in peers]
        self.third = [self.send(mine, mine, other)]

    def share(self):
        ys, xs, y_peers, x_peers, other = plane()
        wheres = xs if self.y_first else ys
        for copy, where in zip(self.second, (wheres[1], wheres[0], wheres[2])):
            copy.wait_recv()
            line = self.line(where)
            self.third.append(self.send(line, line, other))

    def end(self):
        for copy in self.third:
            copy.wait_recv()
        for copy in self.copies:
            copy.wait_send()


def start_kernel(
    first, shrunk, w_in, w_gate, w_up, w_out, w_shrink, *refs
):
    owns = (w_in, w_gate, w_up, w_out, w_shrink)
    (first_all, shrunk_all), helds = refs[:2], refs[2:7]
    ring_send, ring_recv, plane_send, plane_recv, own_sem = refs[7:]
    xh, y, core, xl, z = place()
    z, zp, z2, zm, up, down = ring_peers()
    ys, xs, y_peers, x_peers, other = plane()
    greet([up, down, other] + y_peers + x_peers)
    gathers = [
        PlaneGather(own, held, i in (1, 2), plane_send.at[i], plane_recv.at[i])
        for i, (own, held) in enumerate(zip(owns, helds))
    ]
    keeps = [
        pltpu.make_async_copy(own, held.at[xh, y, core, xl], own_sem.at[i])
        for i, (own, held) in enumerate(zip(owns, helds))
    ]
    keeps.append(pltpu.make_async_copy(first, first_all.at[z], own_sem.at[5]))
    keeps.append(pltpu.make_async_copy(shrunk, shrunk_all.at[z], own_sem.at[6]))
    for gather in gathers:
        gather.begin()
    copies = ring_gather_begin(first, first_all, ring_send.at[0], ring_recv.at[0])
    for keep in keeps:
        keep.start()
    for keep in keeps:
        keep.wait()
    for gather in gathers:
        gather.spread()
    copies = ring_gather_forward(first_all, copies, ring_send.at[0], ring_recv.at[0])
    later = ring_gather_begin(shrunk, shrunk_all, ring_send.at[1], ring_recv.at[1])
    for gather in gathers:
        gather.share()
    later = ring_gather_forward(shrunk_all, later, ring_send.at[1], ring_recv.at[1])
    for gather in gathers:
        gather.end()
    ring_gather_end(copies)
    ring_gather_end(later)


def start(first, shrunk, weights):
    any_place = pl.BlockSpec(memory_space=pl.ANY)
    rows, width = first.shape
    outs = pl.pallas_call(
        start_kernel,
        out_shape=(jax.ShapeDtypeStruct((4, rows, width), jnp.bfloat16),) * 2
        + tuple(jax.ShapeDtypeStruct((2, 4, 2, 2) + w.shape, jnp.bfloat16) for w in weights),
        in_specs=[any_place] * 7,
        out_specs=(any_place,) * 7,
        scratch_shapes=[
            pltpu.SemaphoreType.DMA((2, 6)),
            pltpu.SemaphoreType.DMA((2, 6)),
            pltpu.SemaphoreType.DMA((5, 10)),
            pltpu.SemaphoreType.DMA((5, 10)),
            pltpu.SemaphoreType.DMA((7,)),
        ],
        compiler_params=pltpu.CompilerParams(
            collective_id=0, has_side_effects=True, vmem_limit_bytes=VMEM_MOST
        ),
    )(first, shrunk, *weights)
    return (
        outs[0].reshape(4 * rows, width),
        outs[1].reshape(4 * rows, width),
    ) + tuple(held.reshape(1536, -1) for held in outs[2:])


class PlaneScatter:
    def __init__(self, parts, came, halved, across, lined, last, x_first, send_sem, recv_sem):
        self.parts, self.came, self.halved = parts, came, halved
        self.across, self.lined, self.last, self.x_first = across, lined, last, x_first
        self.send_sem, self.recv_sem, self.used, self.copies = send_sem, recv_sem, 0, []

    def send(self, src, dst, peer):
        copy = remote(src, dst, self.send_sem.at[self.used], self.recv_sem.at[self.used], peer)
        self.used += 1
        copy.start()
        self.copies.append(copy)
        return copy

    def begin(self):
        xh, y, core, xl, z = place()
        ys, xs, y_peers, x_peers, other = plane()
        self.wheres = (xs[::-1] + [(xh, xl)]) if self.x_first else (ys[::-1] + [y])
        self.first = []
        for where in self.wheres:
            if self.x_first:
                src = self.parts.at[where[0], :, 1 - core, where[1]]
                dst = self.came.at[where[0], :, where[1]]
            else:
                src, dst = self.parts.at[:, where, 1 - core, :], self.came.at[:, where, :]
            self.first.append(self.send(src, dst, other))

    def fold(self):
        xh, y, core, xl, z = place()
        ys, xs, y_peers, x_peers, other = plane()
        peers = x_peers[::-1] if self.x_first else y_peers[::-1]
        self.second = []
        for k, (where, copy) in enumerate(zip(self.wheres, self.first)):
            copy.wait_recv()

            def add(i, carry, where=where, k=k):
                def rows(r):
                    if self.x_first:
                        h, l, v = where[0], where[1], i
                    else:
                        h, l, v = i // 2, lax.rem(i, 2), where
                    total = self.parts[h, v, core, l, r].astype(jnp.float32) + self.came[
                        h, v, l, r
                    ].astype(jnp.float32)
                    self.halved[k, i, r] = total.astype(jnp.bfloat16)

                in_rows(48, 16, rows)
                return carry

            lax.fori_loop(0, 4, add, 0)
            if k < 3:
                self.second.append(self.send(self.halved.at[k], self.across.at[k], peers[k]))

    def line(self):
        xh, y, core, xl, z = place()
        ys, xs, y_peers, x_peers, other = plane()
        for copy in self.second:
            copy.wait_recv()

        def add(i, carry):
            def rows(r):
                total = self.halved[3, i, r].astype(jnp.float32)
                for k in range(3):
                    total = total + self.across[k, i, r].astype(jnp.float32)
                self.lined[i, r] = total.astype(jnp.bfloat16)

            in_rows(48, 16, rows)
            return carry

        lax.fori_loop(0, 4, add, 0)
        if self.x_first:
            self.mine, targets, peers = y, ys, y_peers
        else:
            self.mine, targets, peers = xh * 2 + xl, [h * 2 + l for h, l in xs], x_peers
        self.third = [
            self.send(self.lined.at[target], self.last.at[k], peer)
            for k, (target, peer) in enumerate(zip(targets, peers))
        ]

    def end(self, total_ref):
        for copy in self.third:
            copy.wait_recv()

        def rows(r):
            total = self.lined[self.mine, r].astype(jnp.float32)
            for k in range(3):
                total = total + self.last[k, r].astype(jnp.float32)
            total_ref[r] = total

        in_rows(48, 16, rows)
        for copy in self.copies:
            copy.wait_send()


def scatter_scratch(width):
    return [
        pltpu.VMEM((2, 4, 2, 48, width), jnp.bfloat16),
        pltpu.VMEM((4, 4, 48, width), jnp.bfloat16),
        pltpu.VMEM((3, 4, 48, width), jnp.bfloat16),
        pltpu.VMEM((4, 48, width), jnp.bfloat16),
        pltpu.VMEM((3, 48, width), jnp.bfloat16),
    ]


def plane_scatter_kernel(turns, *refs):
    n = len(turns)
    parts, totals, scratch = refs[:n], refs[n : 2 * n], refs[2 * n :]
    send_sem, recv_sem = scratch[-2:]
    ys, xs, y_peers, x_peers, other = plane()
    greet([other] + y_peers + x_peers)
    scatters = [
        PlaneScatter(
            parts[i], *scratch[5 * i : 5 * i + 5], turns[i], send_sem.at[i], recv_sem.at[i]
        )
        for i in range(n)
    ]
    for scatter in scatters:
        scatter.begin()
    for scatter in scatters:
        scatter.fold()
    for scatter in scatters:
        scatter.line()
    for scatter, total in zip(scatters, totals):
        scatter.end(total)


def plane_scatter(gradients, turns, identity):
    shaped = [g.reshape(2, 4, 2, 2, 48, g.shape[-1]) for g in gradients]
    scratch = []
    for g in gradients:
        scratch += scatter_scratch(g.shape[-1])
    n = len(gradients)
    return pl.pallas_call(
        functools.partial(plane_scatter_kernel, turns),
        out_shape=tuple(jax.ShapeDtypeStruct((48, g.shape[-1]), jnp.float32) for g in gradients),
        scratch_shapes=scratch
        + [pltpu.SemaphoreType.DMA((n, 10)), pltpu.SemaphoreType.DMA((n, 10))],
        compiler_params=pltpu.CompilerParams(
            collective_id=identity, has_side_effects=True, vmem_limit_bytes=VMEM_MOST
        ),
    )(*shaped)


def sum_kernel(own, total, held, send_sem, recv_sem):
    xh, y, core, xl, z = place()
    ys, xs, y_peers, x_peers, other = plane()
    z_peers = [device(xh, y, core, xl, lax.rem(z + d, 4)) for d in (1, 3, 2)]
    greet([other] + z_peers + x_peers + y_peers)
    total[...] = own[...]
    groups = ((z_peers, z, 4), (x_peers, xh * 2 + xl, 4), (y_peers, y, 4), ([other], core, 2))
    for axis, (group, here, count) in enumerate(groups):
        held[axis, here] = total[...]
        copies = [
            remote(
                held.at[axis, here],
                held.at[axis, here],
                send_sem.at[axis * 3 + k],
                recv_sem.at[axis * 3 + k],
                peer,
            )
            for k, peer in enumerate(group)
        ]
        for copy in copies:
            copy.start()
        for copy in copies:
            copy.wait()
        order = held[axis, 0]
        for k in range(1, count):
            order = order + held[axis, k]
        total[...] = order


def sum_everywhere(own, identity):
    return pl.pallas_call(
        sum_kernel,
        out_shape=jax.ShapeDtypeStruct(own.shape, jnp.float32),
        scratch_shapes=[
            pltpu.VMEM((4, 4) + own.shape, jnp.float32),
            pltpu.SemaphoreType.DMA((12,)),
            pltpu.SemaphoreType.DMA((12,)),
        ],
        compiler_params=pltpu.CompilerParams(
            collective_id=identity, has_side_effects=True, vmem_limit_bytes=VMEM_MOST
        ),
    )(own)


def product(a, b, a_dim, b_dim):
    return lax.dot_general(
        a, b, (((a_dim,), (b_dim,)), ((), ())), preferred_element_type=jnp.float32
    )


def shards(
    hidden_in,
    cotangent,
    prefix,
    positions,
    norm_gains,
    gains_first,
    gains_second,
    input_weight,
    input_first,
    input_second,
    output_weight,
    output_first,
    output_second,
    expand_weight,
    expand_first,
    expand_second,
    shrink_weight,
    shrink_first,
    shrink_second,
):
    low = jnp.bfloat16
    x_rows = hidden_in[0].astype(jnp.float32)
    grad_out = cotangent[0].astype(jnp.float32)
    normed_one, scale_one = rms_parts(x_rows)
    first_own = (normed_one * norm_gains[0]).astype(low)
    shrunk_own = (RESID * grad_out).astype(low)
    first_all, shrunk_gradient, w_in, w_gate, w_up, w_out, w_shrink = start(
        first_own,
        shrunk_own,
        (
            input_weight.astype(low),
            expand_weight[0].astype(low),
            expand_weight[1].astype(low),
            output_weight.T.astype(low),
            shrink_weight.T.astype(low),
        ),
    )
    cos_part, sin_part = angles(positions[0])
    row_index = lax.axis_index("context") * 896 + jnp.arange(896, dtype=jnp.int32)
    limit = jnp.maximum(row_index + 1, prefix[0]).reshape(BLOCKS, 1, 128)
    limit = jnp.concatenate([limit] * GROUP, axis=2)
    packed = product(w_in, first_all, 0, 1)
    turned, kv_all, attended, log_total = attend_forward(packed, cos_part, sin_part, limit)
    projected = ring_scatter(product(attended, w_out, 0, 1).astype(low), 3)
    residual = x_rows + RESID * projected
    normed_two, scale_two = rms_parts(residual)
    second_all = ring_gather((normed_two * norm_gains[1]).astype(low), 4)
    gate_value = product(second_all, w_gate, 1, 0)
    up_value = product(second_all, w_up, 1, 0)
    sigmoid_gate = jax.nn.sigmoid(gate_value)
    gate_active = gate_value * sigmoid_gate
    gated_hidden = (gate_active * up_value).astype(low)
    grad_activated = product(shrunk_gradient, w_shrink, 1, 0)
    gate_gradient = (
        grad_activated * up_value * sigmoid_gate * (1.0 + gate_value * (1.0 - sigmoid_gate))
    ).astype(low)
    up_gradient = (grad_activated * gate_active).astype(low)
    second_terms = product(gate_gradient, w_gate, 1, 1) + product(up_gradient, w_up, 1, 1)
    grad_second = ring_scatter(second_terms.astype(low), 5)
    gain_two = jnp.sum(grad_second * normed_two, axis=0)
    grad_residual = grad_out + rms_back(grad_second * norm_gains[1], normed_two, scale_two)
    projected_gradient = ring_gather((RESID * grad_residual).astype(low), 6)
    grad_attended = product(w_out, projected_gradient, 0, 1).astype(low)
    grad_packed = attend_backward(
        turned, kv_all, attended, log_total, grad_attended, cos_part, sin_part, limit
    )
    grad_first = ring_scatter(product(grad_packed, w_in, 0, 1).astype(low), 7)
    gain_one = jnp.sum(grad_first * normed_one, axis=0)
    input_gradient = grad_residual + rms_back(grad_first * norm_gains[0], normed_one, scale_one)
    shrunk = ring_scatter(product(gated_hidden, w_shrink, 1, 1).astype(low), 8)
    block_output = (residual + RESID * shrunk).astype(low)
    grad_gate, grad_up, grad_output, grad_shrink, grad_input = plane_scatter(
        (
            product(second_all, gate_gradient, 0, 0).astype(low),
            product(second_all, up_gradient, 0, 0).astype(low),
            product(projected_gradient, attended, 0, 1).astype(low),
            product(shrunk_gradient, gated_hidden, 0, 0).astype(low),
            product(first_all, grad_packed, 0, 1).astype(low),
        ),
        (True, True, False, False, False),
        9,
    )
    grad_expand = jnp.stack([grad_gate, grad_up])
    grad_output, grad_shrink = grad_output.T, grad_shrink.T
    reduced = (grad_input, grad_output, grad_expand, grad_shrink)
    local_squares = sum(jnp.sum(g * g) for g in reduced)
    gains_local = jnp.stack([gain_one, gain_two]).reshape(24, 128)
    message = jnp.concatenate([gains_local, jnp.full((8, 128), local_squares)], axis=0)
    message = sum_everywhere(message, 10)
    grad_gains = message[:24].reshape(2, 1536)
    squares = message[24, 0] + jnp.sum(grad_gains * grad_gains)
    gradient_norm = jnp.sqrt(squares)
    factor = jnp.minimum(1.0, MAX_NORM / (gradient_norm + 1e-06))
    gains_new = adamw(norm_gains, factor * grad_gains, gains_first, gains_second, GAIN_RATE, 0.0)
    input_new = adamw(input_weight, factor * reduced[0], input_first, input_second, RATE, DECAY)
    output_new = adamw(output_weight, factor * reduced[1], output_first, output_second, RATE, DECAY)
    expand_new = adamw(expand_weight, factor * reduced[2], expand_first, expand_second, RATE, DECAY)
    shrink_new = adamw(shrink_weight, factor * reduced[3], shrink_first, shrink_second, RATE, DECAY)
    return (
        block_output[None],
        input_gradient[None],
        gradient_norm,
        *gains_new,
        *input_new,
        *output_new,
        *expand_new,
        *shrink_new,
    )


def solution(mesh):
    return jax.shard_map(
        shards,
        mesh=mesh,
        in_specs=(
            P("shard", ("context", "tensor"), None),
            P("shard", ("context", "tensor"), None),
            P("shard"),
            P("shard", "context"),
            P(),
            P(),
            P(),
            P(("shard", "context"), "tensor"),
            P(("shard", "context"), "tensor"),
            P(("shard", "context"), "tensor"),
            P("tensor", ("shard", "context")),
            P("tensor", ("shard", "context")),
            P("tensor", ("shard", "context")),
            P(None, ("shard", "context"), "tensor"),
            P(None, ("shard", "context"), "tensor"),
            P(None, ("shard", "context"), "tensor"),
            P("tensor", ("shard", "context")),
            P("tensor", ("shard", "context")),
            P("tensor", ("shard", "context")),
        ),
        out_specs=(
            P("shard", ("context", "tensor"), None),
            P("shard", ("context", "tensor"), None),
            P(),
            P(),
            P(),
            P(),
            P(("shard", "context"), "tensor"),
            P(("shard", "context"), "tensor"),
            P(("shard", "context"), "tensor"),
            P("tensor", ("shard", "context")),
            P("tensor", ("shard", "context")),
            P("tensor", ("shard", "context")),
            P(None, ("shard", "context"), "tensor"),
            P(None, ("shard", "context"), "tensor"),
            P(None, ("shard", "context"), "tensor"),
            P("tensor", ("shard", "context")),
            P("tensor", ("shard", "context")),
            P("tensor", ("shard", "context")),
        ),
        check_vma=False,
    )
```

```python
import functools
import math

import jax
import jax.numpy as jnp
from jax import lax
from jax.experimental import pallas as pl
from jax.experimental.pallas import tpu as pltpu
from jax.sharding import PartitionSpec as P

HD = 64
GROUP = 3
STEP = 10
HEADS = 2
BLOCKS = 7
VMEM_MOST = 60 * 2**20
MESH = pl.DeviceIdType.MESH


EPS = 1e-05
RESID = 1.4 / math.sqrt(52.0)
ROPE_BASE = 10000.0
MAX_NORM = 1.0
RATE = 0.1
GAIN_RATE = 1.0
BETA_ONE = 0.9
BETA_TWO = 0.95
ADAM_EPS = 1e-08
DECAY = 0.1
NEG = -1e30


def angles(places):
    half_width = HD // 2
    frequency = ROPE_BASE ** (-2.0 * jnp.arange(half_width, dtype=jnp.float32) / HD)
    phase_turn = places.astype(jnp.float32)[None, :] * frequency[:, None]
    return (jnp.cos(phase_turn), jnp.sin(phase_turn))


def rms_parts(values):
    scaling = lax.rsqrt(jnp.mean(values * values, axis=-1, keepdims=True) + EPS)
    return (values * scaling, scaling)


def rms_back(gradient, normed, scaling):
    return scaling * (gradient - normed * jnp.mean(gradient * normed, axis=-1, keepdims=True))


def adamw(weight, gradient, momentum, variance, step_rate, decay_rate):
    momentum_new = BETA_ONE * momentum + (1.0 - BETA_ONE) * gradient
    variance_new = BETA_TWO * variance + (1.0 - BETA_TWO) * gradient * gradient
    momentum_hat = momentum_new / (1.0 - BETA_ONE**STEP)
    variance_hat = variance_new / (1.0 - BETA_TWO**STEP)
    updated = weight - step_rate * (
        momentum_hat / (jnp.sqrt(variance_hat) + ADAM_EPS) + decay_rate * weight
    )
    return (momentum_new, variance_new, updated)


def nn(a, b):
    return lax.dot_general(a, b, (((1,), (0,)), ((), ())), preferred_element_type=jnp.float32)


def nt(a, b):
    return lax.dot_general(a, b, (((1,), (1,)), ((), ())), preferred_element_type=jnp.float32)


def place():
    shard = lax.axis_index("shard")
    return (
        shard // 8,
        lax.rem(shard // 2, 4),
        lax.rem(shard, 2),
        lax.axis_index("context"),
        lax.axis_index("tensor"),
    )


def device(xh, y, core, xl, z):
    return {"shard": (xh * 4 + y) * 2 + core, "context": xl, "tensor": z}


def greet(peers):
    barrier = pltpu.get_barrier_semaphore()
    for peer in peers:
        pl.semaphore_signal(barrier, inc=1, device_id=peer, device_id_type=MESH)
    pl.semaphore_wait(barrier, len(peers))


def remote(src, dst, send_sem, recv_sem, peer):
    return pltpu.make_async_remote_copy(
        src_ref=src,
        dst_ref=dst,
        send_sem=send_sem,
        recv_sem=recv_sem,
        device_id=peer,
        device_id_type=MESH,
    )


def turn(block, cos_part, sin_part):
    lower_half, upper_half = block[: HD // 2], block[HD // 2 :]
    return jnp.concatenate(
        [
            lower_half * cos_part - upper_half * sin_part,
            upper_half * cos_part + lower_half * sin_part,
        ],
        axis=0,
    )


def turn_back(block, cos_part, sin_part):
    return turn(block, cos_part, -sin_part)


def by_span(context, b, run):
    near = (context == 0) | (b <= 3)

    @pl.when(near)
    def _():
        run(1408)

    @pl.when(jnp.logical_not(near))
    def _():
        run(1792)


def attend_back_kernel(
    turned,
    kv_rows,
    kv_lines,
    attended,
    log_total,
    grad_attended,
    cos_ref,
    sin_ref,
    limit,
    grad_packed,
    sums,
    outgoing,
    incoming,
    send_sem,
    recv_sem,
):
    xh, y, core, xl, z = place()
    peer = device(xh, y, core, 1 - xl, z)
    greet([peer])
    cos_part, sin_part = cos_ref[...], sin_ref[...]
    sums[...] = jnp.zeros_like(sums)

    def block(t, carry):
        b, g = t // HEADS, lax.rem(t, HEADS)
        columns = pl.ds(pl.multiple_of(b * 128, 128), 128)

        def run(span):
            head_rows = [
                pl.ds(pl.multiple_of((g * GROUP + h) * HD, HD), HD) for h in range(GROUP)
            ]
            queries = jnp.concatenate([turned[r, columns] for r in head_rows], axis=1)
            gradient = jnp.concatenate([grad_attended[r, columns] for r in head_rows], axis=1)
            held = jnp.concatenate([attended[r, columns] for r in head_rows], axis=1)
            inner = jnp.sum(
                gradient.astype(jnp.float32) * held.astype(jnp.float32), axis=0, keepdims=True
            )
            nothing = jnp.zeros_like(queries)
            both = jnp.concatenate(
                [
                    jnp.concatenate([queries, nothing], axis=1),
                    jnp.concatenate([nothing, gradient], axis=1),
                ],
                axis=0,
            )
            products = nn(kv_rows[g, :span], both)
            key_index = lax.broadcasted_iota(jnp.int32, (span, 384), 0)
            probs = jnp.exp(
                jnp.where(key_index < limit[b], products[:, :384], NEG) - log_total[t]
            )
            grad_scores = (probs * (products[:, 384:] - inner)).astype(jnp.bfloat16)
            sums[g, :span] += nt(
                jnp.concatenate([grad_scores, probs.astype(jnp.bfloat16)], axis=1), both
            )
            total = nn(kv_lines[g, :HD, :span], grad_scores) * HD ** (-0.5)
            cos_here, sin_here = cos_ref[:, columns], sin_ref[:, columns]
            for h in range(GROUP):
                lines = pl.ds(pl.multiple_of((g * 5 + h) * HD, HD), HD)
                grad_packed[lines, columns] = turn_back(
                    total[:, h * 128 : (h + 1) * 128], cos_here, sin_here
                ).astype(jnp.bfloat16)

        by_span(xl, b, run)
        return carry

    lax.fori_loop(0, HEADS * BLOCKS, block, 0)
    for g in range(HEADS):
        theirs = sums[g, pl.ds(pl.multiple_of((1 - xl) * 896, 128), 896)]
        outgoing[g * 128 : (g + 1) * 128] = jnp.transpose(theirs).astype(jnp.bfloat16)
    copy = remote(outgoing, incoming, send_sem, recv_sem, peer)
    copy.start()
    copy.wait()
    for g in range(HEADS):
        mine = jnp.transpose(sums[g, pl.ds(pl.multiple_of(xl * 896, 128), 896)])
        mine = mine + incoming[g * 128 : (g + 1) * 128].astype(jnp.float32)
        base = g * 5 * HD
        grad_packed[base + 3 * HD : base + 4 * HD] = turn_back(
            mine[:HD], cos_part, sin_part
        ).astype(jnp.bfloat16)
        grad_packed[base + 4 * HD : base + 5 * HD] = mine[HD:].astype(jnp.bfloat16)


def attend_backward(
    turned, kv_rows, kv_lines, attended, log_total, grad_attended, cos_part, sin_part, limit
):
    return pl.pallas_call(
        attend_back_kernel,
        out_shape=jax.ShapeDtypeStruct((640, 896), jnp.bfloat16),
        scratch_shapes=[
            pltpu.VMEM((HEADS, 1792, 128), jnp.float32),
            pltpu.VMEM((256, 896), jnp.bfloat16),
            pltpu.VMEM((256, 896), jnp.bfloat16),
            pltpu.SemaphoreType.DMA,
            pltpu.SemaphoreType.DMA,
        ],
        compiler_params=pltpu.CompilerParams(
            collective_id=2, has_side_effects=True, vmem_limit_bytes=VMEM_MOST
        ),
    )(turned, kv_rows, kv_lines, attended, log_total, grad_attended, cos_part, sin_part, limit)


def ring_peers():
    xh, y, core, xl, z = place()
    return (
        z,
        lax.rem(z + 1, 4),
        lax.rem(z + 2, 4),
        lax.rem(z + 3, 4),
        device(xh, y, core, xl, lax.rem(z + 1, 4)),
        device(xh, y, core, xl, lax.rem(z + 3, 4)),
    )


def halves(ref, index):
    rows = ref.shape[1] // 2
    return ref.at[index, pl.ds(0, rows)], ref.at[index, pl.ds(rows, rows)]


def ring_gather_begin(own, held, send_sem, recv_sem):
    z, zp, z2, zm, up, down = ring_peers()
    rows = own.shape[0] // 2
    first, second = own.at[pl.ds(0, rows)], own.at[pl.ds(rows, rows)]
    first_to, second_to = halves(held, z)
    copies = [
        remote(first, first_to, send_sem.at[0], recv_sem.at[0], up),
        remote(second, second_to, send_sem.at[1], recv_sem.at[1], down),
        remote(second, second_to, send_sem.at[2], recv_sem.at[2], up),
        remote(first, first_to, send_sem.at[3], recv_sem.at[3], down),
    ]
    for copy in copies:
        copy.start()
    return copies


def ring_gather_forward(held, copies, send_sem, recv_sem):
    z, zp, z2, zm, up, down = ring_peers()
    copies[0].wait_recv()
    below = halves(held, zm)[0]
    on_up = remote(below, below, send_sem.at[4], recv_sem.at[4], up)
    on_up.start()
    copies[1].wait_recv()
    above = halves(held, zp)[1]
    on_down = remote(above, above, send_sem.at[5], recv_sem.at[5], down)
    on_down.start()
    return copies + [on_up, on_down]


def ring_gather_end(copies):
    for copy in copies:
        copy.wait_send()
    for copy in copies[2:]:
        copy.wait_recv()


def ring_gather_kernel(own, held, send_sem, recv_sem, own_sem):
    z, zp, z2, zm, up, down = ring_peers()
    greet([up, down])
    copies = ring_gather_begin(own, held, send_sem, recv_sem)
    keep = pltpu.make_async_copy(own, held.at[z], own_sem)
    keep.start()
    copies = ring_gather_forward(held, copies, send_sem, recv_sem)
    keep.wait()
    ring_gather_end(copies)


def ring_gather(rows, identity):
    count, width = rows.shape
    held = pl.pallas_call(
        ring_gather_kernel,
        out_shape=jax.ShapeDtypeStruct((4, count, width), rows.dtype),
        in_specs=[pl.BlockSpec(memory_space=pl.ANY)],
        out_specs=pl.BlockSpec(memory_space=pl.ANY),
        scratch_shapes=[
            pltpu.SemaphoreType.DMA((6,)),
            pltpu.SemaphoreType.DMA((6,)),
            pltpu.SemaphoreType.DMA,
        ],
        compiler_params=pltpu.CompilerParams(
            collective_id=identity, has_side_effects=True, vmem_limit_bytes=VMEM_MOST
        ),
    )(rows)
    return held.reshape(4 * count, width)


def in_rows(count, step, run):
    def body(i, carry):
        run(pl.ds(pl.multiple_of(i * step, step), step))
        return carry

    lax.fori_loop(0, count // step, body, 0)


def ring_scatter_begin(parts, came, send_sem, recv_sem):
    z, zp, z2, zm, up, down = ring_peers()
    copies = [
        remote(halves(parts, z2)[1], came.at[0], send_sem.at[0], recv_sem.at[0], up),
        remote(halves(parts, z2)[0], came.at[1], send_sem.at[1], recv_sem.at[1], down),
        remote(halves(parts, zp)[0], came.at[2], send_sem.at[2], recv_sem.at[2], up),
        remote(halves(parts, zm)[1], came.at[3], send_sem.at[3], recv_sem.at[3], down),
    ]
    for copy in copies:
        copy.start()
    return copies


def ring_scatter_forward(parts, came, sums, copies, send_sem, recv_sem):
    z, zp, z2, zm, up, down = ring_peers()
    count = came.shape[1]
    copies[0].wait_recv()

    def add_up(rows):
        sums[0, rows] = (
            came[0, rows].astype(jnp.float32)
            + parts[zp, pl.ds(pl.multiple_of(rows.start + count, 16), 16)].astype(jnp.float32)
        ).astype(jnp.bfloat16)

    in_rows(count, 16, add_up)
    on_up = remote(sums.at[0], came.at[4], send_sem.at[4], recv_sem.at[4], up)
    on_up.start()
    copies[1].wait_recv()

    def add_down(rows):
        sums[1, rows] = (
            came[1, rows].astype(jnp.float32) + parts[zm, rows].astype(jnp.float32)
        ).astype(jnp.bfloat16)

    in_rows(count, 16, add_down)
    on_down = remote(sums.at[1], came.at[5], send_sem.at[5], recv_sem.at[5], down)
    on_down.start()
    return copies + [on_up, on_down]


def ring_scatter_end(parts, came, total, copies):
    z, zp, z2, zm, up, down = ring_peers()
    count = came.shape[1]
    for copy in copies[2:]:
        copy.wait_recv()
    for copy in copies:
        copy.wait_send()

    def add(rows):
        later = pl.ds(pl.multiple_of(rows.start + count, 16), 16)
        total[rows] = (
            parts[z, rows].astype(jnp.float32)
            + came[2, rows].astype(jnp.float32)
            + came[5, rows].astype(jnp.float32)
        )
        total[later] = (
            parts[z, later].astype(jnp.float32)
            + came[3, rows].astype(jnp.float32)
            + came[4, rows].astype(jnp.float32)
        )

    in_rows(count, 16, add)


def ring_scatter_kernel(parts, total, came, sums, send_sem, recv_sem):
    z, zp, z2, zm, up, down = ring_peers()
    greet([up, down])
    copies = ring_scatter_begin(parts, came, send_sem, recv_sem)
    copies = ring_scatter_forward(parts, came, sums, copies, send_sem, recv_sem)
    ring_scatter_end(parts, came, total, copies)


def ring_scatter(parts, identity):
    rows, width = parts.shape
    count = rows // 4
    return pl.pallas_call(
        ring_scatter_kernel,
        out_shape=jax.ShapeDtypeStruct((count, width), jnp.float32),
        scratch_shapes=[
            pltpu.VMEM((6, count // 2, width), jnp.bfloat16),
            pltpu.VMEM((2, count // 2, width), jnp.bfloat16),
            pltpu.SemaphoreType.DMA((6,)),
            pltpu.SemaphoreType.DMA((6,)),
        ],
        compiler_params=pltpu.CompilerParams(
            collective_id=identity, has_side_effects=True, vmem_limit_bytes=VMEM_MOST
        ),
    )(parts.reshape(4, count, width))


def plane():
    xh, y, core, xl, z = place()
    ys = [lax.rem(y + d, 4) for d in (1, 3, 2)]
    step = xh * 2 + xl
    xs = [lax.rem(step + d, 4) for d in (1, 3, 2)]
    xs = [(x // 2, lax.rem(x, 2)) for x in xs]
    y_peers = [device(xh, other, core, xl, z) for other in ys]
    x_peers = [device(h, y, core, l, z) for h, l in xs]
    return ys, xs, y_peers, x_peers, device(xh, y, 1 - core, xl, z)


class PlaneGather:
    def __init__(self, own, held, y_first, send_sem, recv_sem):
        self.own, self.held, self.y_first = own, held, y_first
        self.send_sem, self.recv_sem, self.used = send_sem, recv_sem, 0
        self.copies, self.first, self.second, self.third = [], [], [], []

    def send(self, src, dst, peer):
        copy = remote(src, dst, self.send_sem.at[self.used], self.recv_sem.at[self.used], peer)
        self.used += 1
        copy.start()
        self.copies.append(copy)
        return copy

    def begin(self):
        xh, y, core, xl, z = place()
        ys, xs, y_peers, x_peers, other = plane()
        target = self.held.at[xh, y, core, xl]
        peers = y_peers if self.y_first else x_peers
        self.first = [self.send(self.own, target, peer) for peer in peers]

    def line(self, where):
        xh, y, core, xl, z = place()
        if self.y_first:
            return self.held.at[where[0], :, core, where[1]]
        return self.held.at[:, where, core, :]

    def spread(self):
        xh, y, core, xl, z = place()
        ys, xs, y_peers, x_peers, other = plane()
        for copy in self.first:
            copy.wait_recv()
        mine = self.line((xh, xl) if self.y_first else y)
        peers = x_peers if self.y_first else y_peers
        self.second = [self.send(mine, mine, peer) for peer in peers]
        self.third = [self.send(mine, mine, other)]

    def share(self):
        ys, xs, y_peers, x_peers, other = plane()
        wheres = xs if self.y_first else ys
        for copy, where in zip(self.second, (wheres[1], wheres[0], wheres[2])):
            copy.wait_recv()
            line = self.line(where)
            self.third.append(self.send(line, line, other))

    def end(self):
        for copy in self.third:
            copy.wait_recv()
        for copy in self.copies:
            copy.wait_send()


class PlaneScatter:
    def __init__(self, parts, came, halved, across, lined, last, x_first, send_sem, recv_sem):
        self.parts, self.came, self.halved = parts, came, halved
        self.across, self.lined, self.last, self.x_first = across, lined, last, x_first
        self.send_sem, self.recv_sem, self.used, self.copies = send_sem, recv_sem, 0, []

    def send(self, src, dst, peer):
        copy = remote(src, dst, self.send_sem.at[self.used], self.recv_sem.at[self.used], peer)
        self.used += 1
        copy.start()
        self.copies.append(copy)
        return copy

    def begin(self):
        xh, y, core, xl, z = place()
        ys, xs, y_peers, x_peers, other = plane()
        self.wheres = (xs[::-1] + [(xh, xl)]) if self.x_first else (ys[::-1] + [y])
        self.first = []
        for where in self.wheres:
            if self.x_first:
                src = self.parts.at[where[0], :, 1 - core, where[1]]
                dst = self.came.at[where[0], :, where[1]]
            else:
                src, dst = self.parts.at[:, where, 1 - core, :], self.came.at[:, where, :]
            self.first.append(self.send(src, dst, other))

    def fold(self):
        xh, y, core, xl, z = place()
        ys, xs, y_peers, x_peers, other = plane()
        peers = x_peers[::-1] if self.x_first else y_peers[::-1]
        self.second = []
        for k, (where, copy) in enumerate(zip(self.wheres, self.first)):
            copy.wait_recv()

            def add(i, carry, where=where, k=k):
                def rows(r):
                    if self.x_first:
                        h, l, v = where[0], where[1], i
                    else:
                        h, l, v = i // 2, lax.rem(i, 2), where
                    total = self.parts[h, v, core, l, r].astype(jnp.float32) + self.came[
                        h, v, l, r
                    ].astype(jnp.float32)
                    self.halved[k, i, r] = total.astype(jnp.bfloat16)

                in_rows(48, 16, rows)
                return carry

            lax.fori_loop(0, 4, add, 0)
            if k < 3:
                self.second.append(self.send(self.halved.at[k], self.across.at[k], peers[k]))

    def line(self):
        xh, y, core, xl, z = place()
        ys, xs, y_peers, x_peers, other = plane()
        for copy in self.second:
            copy.wait_recv()

        def add(i, carry):
            def rows(r):
                total = self.halved[3, i, r].astype(jnp.float32)
                for k in range(3):
                    total = total + self.across[k, i, r].astype(jnp.float32)
                self.lined[i, r] = total.astype(jnp.bfloat16)

            in_rows(48, 16, rows)
            return carry

        lax.fori_loop(0, 4, add, 0)
        if self.x_first:
            self.mine, targets, peers = y, ys, y_peers
        else:
            self.mine, targets, peers = xh * 2 + xl, [h * 2 + l for h, l in xs], x_peers
        self.third = [
            self.send(self.lined.at[target], self.last.at[k], peer)
            for k, (target, peer) in enumerate(zip(targets, peers))
        ]

    def end(self, total_ref):
        for copy in self.third:
            copy.wait_recv()

        def rows(r):
            total = self.lined[self.mine, r].astype(jnp.float32)
            for k in range(3):
                total = total + self.last[k, r].astype(jnp.float32)
            total_ref[r] = total

        in_rows(48, 16, rows)
        for copy in self.copies:
            copy.wait_send()


def scatter_scratch(width):
    return [
        pltpu.VMEM((2, 4, 2, 48, width), jnp.bfloat16),
        pltpu.VMEM((4, 4, 48, width), jnp.bfloat16),
        pltpu.VMEM((3, 4, 48, width), jnp.bfloat16),
        pltpu.VMEM((4, 48, width), jnp.bfloat16),
        pltpu.VMEM((3, 48, width), jnp.bfloat16),
    ]


def plane_scatter_kernel(turns, *refs):
    n = len(turns)
    parts, totals, scratch = refs[:n], refs[n : 2 * n], refs[2 * n :]
    send_sem, recv_sem = scratch[-2:]
    ys, xs, y_peers, x_peers, other = plane()
    greet([other] + y_peers + x_peers)
    scatters = [
        PlaneScatter(
            parts[i], *scratch[5 * i : 5 * i + 5], turns[i], send_sem.at[i], recv_sem.at[i]
        )
        for i in range(n)
    ]
    for scatter in scatters:
        scatter.begin()
    for scatter in scatters:
        scatter.fold()
    for scatter in scatters:
        scatter.line()
    for scatter, total in zip(scatters, totals):
        scatter.end(total)


def plane_scatter(gradients, turns, identity):
    shaped = [g.reshape(2, 4, 2, 2, 48, g.shape[-1]) for g in gradients]
    scratch = []
    for g in gradients:
        scratch += scatter_scratch(g.shape[-1])
    n = len(gradients)
    return pl.pallas_call(
        functools.partial(plane_scatter_kernel, turns),
        out_shape=tuple(jax.ShapeDtypeStruct((48, g.shape[-1]), jnp.float32) for g in gradients),
        scratch_shapes=scratch
        + [pltpu.SemaphoreType.DMA((n, 10)), pltpu.SemaphoreType.DMA((n, 10))],
        compiler_params=pltpu.CompilerParams(
            collective_id=identity, has_side_effects=True, vmem_limit_bytes=VMEM_MOST
        ),
    )(*shaped)


def sum_kernel(own, total, held, send_sem, recv_sem):
    xh, y, core, xl, z = place()
    ys, xs, y_peers, x_peers, other = plane()
    z_peers = [device(xh, y, core, xl, lax.rem(z + d, 4)) for d in (1, 3, 2)]
    greet([other] + z_peers + x_peers + y_peers)
    total[...] = own[...]
    groups = ((z_peers, z, 4), (x_peers, xh * 2 + xl, 4), (y_peers, y, 4), ([other], core, 2))
    for axis, (group, here, count) in enumerate(groups):
        held[axis, here] = total[...]
        copies = [
            remote(
                held.at[axis, here],
                held.at[axis, here],
                send_sem.at[axis * 3 + k],
                recv_sem.at[axis * 3 + k],
                peer,
            )
            for k, peer in enumerate(group)
        ]
        for copy in copies:
            copy.start()
        for copy in copies:
            copy.wait()
        order = held[axis, 0]
        for k in range(1, count):
            order = order + held[axis, k]
        total[...] = order


def sum_everywhere(own, identity):
    return pl.pallas_call(
        sum_kernel,
        out_shape=jax.ShapeDtypeStruct(own.shape, jnp.float32),
        scratch_shapes=[
            pltpu.VMEM((4, 4) + own.shape, jnp.float32),
            pltpu.SemaphoreType.DMA((12,)),
            pltpu.SemaphoreType.DMA((12,)),
        ],
        compiler_params=pltpu.CompilerParams(
            collective_id=identity, has_side_effects=True, vmem_limit_bytes=VMEM_MOST
        ),
    )(own)


def swap_halves(block):
    lane = lax.broadcasted_iota(jnp.int32, block.shape, 1)
    return jnp.where(
        lane < HD // 2, pltpu.roll(block, 128 - HD // 2, 1), pltpu.roll(block, HD // 2, 1)
    )


def front_kernel(*refs):
    (first, shrunk, w_in, w_gate, w_up, w_out, w_shrink) = refs[:7]
    (cos_ref, sin_ref, key_cos, key_sin, limit) = refs[7:12]
    (first_all, shrunk_all, in_all, gate_all, up_all, out_all, shrink_all) = refs[12:19]
    (turned, kv_rows, kv_lines, attended, log_total, total) = refs[19:25]
    (packed, held_rows, parts, came, sums) = refs[25:30]
    (ring_send, ring_recv, plane_send, plane_recv) = refs[30:34]
    (kv_send, kv_recv, own_sem, out_sem) = refs[34:]
    xh, y, core, xl, z = place()
    z, zp, z2, zm, up, down = ring_peers()
    ys, xs, y_peers, x_peers, other = plane()
    beside = device(xh, y, core, 1 - xl, z)
    greet([up, down, other] + y_peers + x_peers)
    owns = (w_in, w_out, w_gate, w_up, w_shrink)
    helds = (in_all, out_all, gate_all, up_all, shrink_all)
    gathers = [
        PlaneGather(own, held, i in (2, 3), plane_send.at[i], plane_recv.at[i])
        for i, (own, held) in enumerate(zip(owns, helds))
    ]
    for gather in gathers[:2]:
        gather.begin()
    ring = ring_gather_begin(first, first_all, ring_send.at[0], ring_recv.at[0])
    keeps = [
        pltpu.make_async_copy(own, held.at[xh, y, core, xl], own_sem.at[i])
        for i, (own, held) in enumerate(zip(owns, helds))
    ]
    keeps.append(pltpu.make_async_copy(first, first_all.at[z], own_sem.at[5]))
    keeps.append(pltpu.make_async_copy(shrunk, shrunk_all.at[z], own_sem.at[6]))
    for keep in keeps:
        keep.start()
    for keep in keeps:
        keep.wait()
    for gather in gathers[:2]:
        gather.spread()
    ring = ring_gather_forward(first_all, ring, ring_send.at[0], ring_recv.at[0])
    gathers[0].share()
    gathers[1].share()
    gathers[0].end()
    for gather in gathers[2:]:
        gather.begin()

    def project(c, rows):
        out = nn(first_all[c], in_all[...].reshape(1536, 640))
        packed[rows] = out
        for g in range(HEADS):
            block = out[:, g * 320 + 192 : g * 320 + 320]
            mine = pl.ds(pl.multiple_of(xl * 896 + c * 224, 16), 224)
            kv_rows[g, mine] = (
                block * key_cos[rows] + swap_halves(block) * key_sin[rows]
            ).astype(jnp.bfloat16)

    kv_copies = []
    for i, c in enumerate((z, zm, zp, z2)):
        if i == 1:
            ring[2].wait_recv()
        if i == 2:
            ring[3].wait_recv()
        if i == 3:
            ring[4].wait_recv()
            ring[5].wait_recv()
        project(c, pl.ds(pl.multiple_of(c * 224, 16), 224))
        mine = kv_rows.at[:, pl.ds(pl.multiple_of(xl * 896 + c * 224, 16), 224)]
        kv_copies.append(remote(mine, mine, kv_send.at[i], kv_recv.at[i], beside))
        kv_copies[-1].start()
    later = ring_gather_begin(shrunk, shrunk_all, ring_send.at[1], ring_recv.at[1])

    def turn_block(b, carry):
        columns = pl.ds(pl.multiple_of(b * 128, 128), 128)
        lines = jnp.transpose(packed[columns])
        cos_here, sin_here = cos_ref[:, columns], sin_ref[:, columns]
        for g in range(HEADS):
            for h in range(GROUP):
                at = (g * 5 + h) * HD
                turned[(g * GROUP + h) * HD : (g * GROUP + h + 1) * HD, columns] = (
                    turn(lines[at : at + HD], cos_here, sin_here) * HD ** (-0.5)
                ).astype(jnp.bfloat16)
        return carry

    lax.fori_loop(0, BLOCKS, turn_block, 0)
    for copy in kv_copies:
        copy.wait_recv()
    for gather in gathers[2:]:
        gather.spread()
    for g in range(HEADS):
        kv_lines[g] = jnp.transpose(kv_rows[g].astype(jnp.float32)).astype(jnp.bfloat16)

    def block(t, carry):
        b, g = t // HEADS, lax.rem(t, HEADS)
        columns = pl.ds(pl.multiple_of(b * 128, 128), 128)

        def run(span):
            head_rows = [
                pl.ds(pl.multiple_of((g * GROUP + h) * HD, HD), HD) for h in range(GROUP)
            ]
            queries = jnp.concatenate([turned[r, columns] for r in head_rows], axis=1)
            queries = jnp.concatenate([queries, jnp.zeros_like(queries)], axis=0)
            scores = nn(kv_rows[g, :span], queries)
            key_index = lax.broadcasted_iota(jnp.int32, (span, 384), 0)
            scores = jnp.where(key_index < limit[b], scores, NEG)
            row_max = jnp.max(scores, axis=0, keepdims=True)
            shifted = jnp.exp(scores - row_max)
            exp_total = jnp.sum(shifted, axis=0, keepdims=True)
            out = nn(kv_lines[g, HD:, :span], shifted.astype(jnp.bfloat16)) * (1.0 / exp_total)
            for h in range(GROUP):
                attended[head_rows[h], columns] = out[:, h * 128 : (h + 1) * 128].astype(
                    jnp.bfloat16
                )
            log_total[t] = row_max + jnp.log(exp_total)

        by_span(xl, b, run)
        return carry

    lax.fori_loop(0, 6, block, 0)
    later = ring_gather_forward(shrunk_all, later, ring_send.at[1], ring_recv.at[1])
    lax.fori_loop(6, HEADS * BLOCKS, block, 0)
    gathers[1].end()
    fetch = pltpu.make_async_copy(out_all, held_rows, out_sem)
    fetch.start()
    tokens = jnp.transpose(attended[...].astype(jnp.float32)).astype(jnp.bfloat16)
    packed_low = tokens.reshape(4, 224, 384)
    fetch.wait()
    for c in range(4):
        parts[c] = nt(packed_low[c], held_rows[...].reshape(1536, 384)).astype(jnp.bfloat16)
    scatter = ring_scatter_begin(parts, came, ring_send.at[2], ring_recv.at[2])
    scatter = ring_scatter_forward(
        parts, came, sums, scatter, ring_send.at[2], ring_recv.at[2]
    )
    for gather in gathers[2:]:
        gather.share()
    for gather in gathers[2:]:
        gather.end()
    ring_gather_end(later)
    for copy in kv_copies + ring:
        copy.wait_send()
    ring_scatter_end(parts, came, total, scatter)


def front(first, shrunk, weights, tables):
    any_place = pl.BlockSpec(memory_space=pl.ANY)
    whole = pl.BlockSpec(memory_space=pltpu.VMEM)
    rows, width = first.shape
    gathered = [
        jax.ShapeDtypeStruct((2, 4, 2, 2) + w.shape, jnp.bfloat16) for w in weights
    ]
    outs = pl.pallas_call(
        front_kernel,
        out_shape=(
            jax.ShapeDtypeStruct((4, rows, width), jnp.bfloat16),
            jax.ShapeDtypeStruct((4, rows, width), jnp.bfloat16),
            *gathered,
            jax.ShapeDtypeStruct((384, 896), jnp.bfloat16),
            jax.ShapeDtypeStruct((HEADS, 1792, 128), jnp.bfloat16),
            jax.ShapeDtypeStruct((HEADS, 128, 1792), jnp.bfloat16),
            jax.ShapeDtypeStruct((384, 896), jnp.bfloat16),
            jax.ShapeDtypeStruct((HEADS * BLOCKS, 1, 384), jnp.float32),
            jax.ShapeDtypeStruct((rows, width), jnp.float32),
        ),
        in_specs=[whole] * 12,
        out_specs=(whole, any_place, whole) + (any_place,) * 4 + (whole,) * 6,
        scratch_shapes=[
            pltpu.VMEM((896, 640), jnp.float32),
            pltpu.VMEM((2, 4, 2, 2, 48, 384), jnp.bfloat16),
            pltpu.VMEM((4, rows, width), jnp.bfloat16),
            pltpu.VMEM((6, rows // 2, width), jnp.bfloat16),
            pltpu.VMEM((2, rows // 2, width), jnp.bfloat16),
            pltpu.SemaphoreType.DMA((3, 6)),
            pltpu.SemaphoreType.DMA((3, 6)),
            pltpu.SemaphoreType.DMA((5, 10)),
            pltpu.SemaphoreType.DMA((5, 10)),
            pltpu.SemaphoreType.DMA((4,)),
            pltpu.SemaphoreType.DMA((4,)),
            pltpu.SemaphoreType.DMA((7,)),
            pltpu.SemaphoreType.DMA,
        ],
        compiler_params=pltpu.CompilerParams(
            collective_id=0, has_side_effects=True, vmem_limit_bytes=VMEM_MOST
        ),
    )(first, shrunk, *weights, *tables)
    return (
        outs[0].reshape(4 * rows, width),
        outs[1].reshape(4 * rows, width),
        *(held.reshape(1536, -1) for held in outs[2:7]),
        *outs[7:],
    )


def product(a, b, a_dim, b_dim):
    return lax.dot_general(
        a, b, (((a_dim,), (b_dim,)), ((), ())), preferred_element_type=jnp.float32
    )


def shards(
    hidden_in,
    cotangent,
    prefix,
    positions,
    norm_gains,
    gains_first,
    gains_second,
    input_weight,
    input_first,
    input_second,
    output_weight,
    output_first,
    output_second,
    expand_weight,
    expand_first,
    expand_second,
    shrink_weight,
    shrink_first,
    shrink_second,
):
    low = jnp.bfloat16
    x_rows = hidden_in[0].astype(jnp.float32)
    grad_out = cotangent[0].astype(jnp.float32)
    normed_one, scale_one = rms_parts(x_rows)
    first_own = (normed_one * norm_gains[0]).astype(low)
    shrunk_own = (RESID * grad_out).astype(low)
    cos_part, sin_part = angles(positions[0])
    row_index = lax.axis_index("context") * 896 + jnp.arange(896, dtype=jnp.int32)
    limit = jnp.maximum(row_index + 1, prefix[0]).reshape(BLOCKS, 1, 128)
    limit = jnp.concatenate([limit] * GROUP, axis=2)
    still = jnp.ones((896, HD), jnp.float32)
    key_cos = jnp.concatenate([cos_part.T, cos_part.T, still], axis=1)
    key_sin = jnp.concatenate([-sin_part.T, sin_part.T, 0.0 * still], axis=1)
    (
        first_all,
        shrunk_gradient,
        w_in,
        w_gate,
        w_up,
        w_out,
        w_shrink,
        turned,
        kv_rows,
        kv_lines,
        attended,
        log_total,
        projected,
    ) = front(
        first_own,
        shrunk_own,
        (
            input_weight.astype(low),
            expand_weight[0].astype(low),
            expand_weight[1].astype(low),
            output_weight.T.astype(low),
            shrink_weight.T.astype(low),
        ),
        (cos_part, sin_part, key_cos, key_sin, limit),
    )
    residual = x_rows + RESID * projected
    normed_two, scale_two = rms_parts(residual)
    second_all = ring_gather((normed_two * norm_gains[1]).astype(low), 4)
    gate_value = product(second_all, w_gate, 1, 0)
    up_value = product(second_all, w_up, 1, 0)
    sigmoid_gate = jax.nn.sigmoid(gate_value)
    gate_active = gate_value * sigmoid_gate
    gated_hidden = (gate_active * up_value).astype(low)
    grad_activated = product(shrunk_gradient, w_shrink, 1, 0)
    gate_gradient = (
        grad_activated * up_value * sigmoid_gate * (1.0 + gate_value * (1.0 - sigmoid_gate))
    ).astype(low)
    up_gradient = (grad_activated * gate_active).astype(low)
    second_terms = product(gate_gradient, w_gate, 1, 1) + product(up_gradient, w_up, 1, 1)
    grad_second = ring_scatter(second_terms.astype(low), 5)
    gain_two = jnp.sum(grad_second * normed_two, axis=0)
    grad_residual = grad_out + rms_back(grad_second * norm_gains[1], normed_two, scale_two)
    projected_gradient = ring_gather((RESID * grad_residual).astype(low), 6)
    grad_attended = product(w_out, projected_gradient, 0, 1).astype(low)
    grad_packed = attend_backward(
        turned, kv_rows, kv_lines, attended, log_total, grad_attended, cos_part, sin_part, limit
    )
    grad_first = ring_scatter(product(grad_packed, w_in, 0, 1).astype(low), 7)
    gain_one = jnp.sum(grad_first * normed_one, axis=0)
    input_gradient = grad_residual + rms_back(grad_first * norm_gains[0], normed_one, scale_one)
    shrunk = ring_scatter(product(gated_hidden, w_shrink, 1, 1).astype(low), 8)
    block_output = (residual + RESID * shrunk).astype(low)
    grad_gate, grad_up, grad_output, grad_shrink, grad_input = plane_scatter(
        (
            product(second_all, gate_gradient, 0, 0).astype(low),
            product(second_all, up_gradient, 0, 0).astype(low),
            product(projected_gradient, attended, 0, 1).astype(low),
            product(shrunk_gradient, gated_hidden, 0, 0).astype(low),
            product(first_all, grad_packed, 0, 1).astype(low),
        ),
        (True, True, False, False, False),
        9,
    )
    grad_expand = jnp.stack([grad_gate, grad_up])
    grad_output, grad_shrink = grad_output.T, grad_shrink.T
    reduced = (grad_input, grad_output, grad_expand, grad_shrink)
    local_squares = sum(jnp.sum(g * g) for g in reduced)
    gains_local = jnp.stack([gain_one, gain_two]).reshape(24, 128)
    message = jnp.concatenate([gains_local, jnp.full((8, 128), local_squares)], axis=0)
    message = sum_everywhere(message, 10)
    grad_gains = message[:24].reshape(2, 1536)
    squares = message[24, 0] + jnp.sum(grad_gains * grad_gains)
    gradient_norm = jnp.sqrt(squares)
    factor = jnp.minimum(1.0, MAX_NORM / (gradient_norm + 1e-06))
    gains_new = adamw(norm_gains, factor * grad_gains, gains_first, gains_second, GAIN_RATE, 0.0)
    input_new = adamw(input_weight, factor * reduced[0], input_first, input_second, RATE, DECAY)
    output_new = adamw(output_weight, factor * reduced[1], output_first, output_second, RATE, DECAY)
    expand_new = adamw(expand_weight, factor * reduced[2], expand_first, expand_second, RATE, DECAY)
    shrink_new = adamw(shrink_weight, factor * reduced[3], shrink_first, shrink_second, RATE, DECAY)
    return (
        block_output[None],
        input_gradient[None],
        gradient_norm,
        *gains_new,
        *input_new,
        *output_new,
        *expand_new,
        *shrink_new,
    )


def solution(mesh):
    return jax.shard_map(
        shards,
        mesh=mesh,
        in_specs=(
            P("shard", ("context", "tensor"), None),
            P("shard", ("context", "tensor"), None),
            P("shard"),
            P("shard", "context"),
            P(),
            P(),
            P(),
            P(("shard", "context"), "tensor"),
            P(("shard", "context"), "tensor"),
            P(("shard", "context"), "tensor"),
            P("tensor", ("shard", "context")),
            P("tensor", ("shard", "context")),
            P("tensor", ("shard", "context")),
            P(None, ("shard", "context"), "tensor"),
            P(None, ("shard", "context"), "tensor"),
            P(None, ("shard", "context"), "tensor"),
            P("tensor", ("shard", "context")),
            P("tensor", ("shard", "context")),
            P("tensor", ("shard", "context")),
        ),
        out_specs=(
            P("shard", ("context", "tensor"), None),
            P("shard", ("context", "tensor"), None),
            P(),
            P(),
            P(),
            P(),
            P(("shard", "context"), "tensor"),
            P(("shard", "context"), "tensor"),
            P(("shard", "context"), "tensor"),
            P("tensor", ("shard", "context")),
            P("tensor", ("shard", "context")),
            P("tensor", ("shard", "context")),
            P(None, ("shard", "context"), "tensor"),
            P(None, ("shard", "context"), "tensor"),
            P(None, ("shard", "context"), "tensor"),
            P("tensor", ("shard", "context")),
            P("tensor", ("shard", "context")),
            P("tensor", ("shard", "context")),
        ),
        check_vma=False,
    )
```

```python
import functools
import math

import jax
import jax.numpy as jnp
from jax import lax
from jax.experimental import pallas as pl
from jax.experimental.pallas import tpu as pltpu
from jax.sharding import PartitionSpec as P

HD = 64
GROUP = 3
STEP = 10
HEADS = 2
BLOCKS = 7
VMEM_MOST = 60 * 2**20
MESH = pl.DeviceIdType.MESH


EPS = 1e-05
RESID = 1.4 / math.sqrt(52.0)
ROPE_BASE = 10000.0
MAX_NORM = 1.0
RATE = 0.1
GAIN_RATE = 1.0
BETA_ONE = 0.9
BETA_TWO = 0.95
ADAM_EPS = 1e-08
DECAY = 0.1
NEG = -1e30


def angles(places):
    half_width = HD // 2
    frequency = ROPE_BASE ** (-2.0 * jnp.arange(half_width, dtype=jnp.float32) / HD)
    phase_turn = places.astype(jnp.float32)[None, :] * frequency[:, None]
    return (jnp.cos(phase_turn), jnp.sin(phase_turn))


def rms_parts(values):
    scaling = lax.rsqrt(jnp.mean(values * values, axis=-1, keepdims=True) + EPS)
    return (values * scaling, scaling)


def rms_back(gradient, normed, scaling):
    return scaling * (gradient - normed * jnp.mean(gradient * normed, axis=-1, keepdims=True))


def adamw(weight, gradient, momentum, variance, step_rate, decay_rate):
    momentum_new = BETA_ONE * momentum + (1.0 - BETA_ONE) * gradient
    variance_new = BETA_TWO * variance + (1.0 - BETA_TWO) * gradient * gradient
    momentum_hat = momentum_new / (1.0 - BETA_ONE**STEP)
    variance_hat = variance_new / (1.0 - BETA_TWO**STEP)
    updated = weight - step_rate * (
        momentum_hat / (jnp.sqrt(variance_hat) + ADAM_EPS) + decay_rate * weight
    )
    return (momentum_new, variance_new, updated)


def nn(a, b):
    return lax.dot_general(a, b, (((1,), (0,)), ((), ())), preferred_element_type=jnp.float32)


def nt(a, b):
    return lax.dot_general(a, b, (((1,), (1,)), ((), ())), preferred_element_type=jnp.float32)


def place():
    shard = lax.axis_index("shard")
    return (
        shard // 8,
        lax.rem(shard // 2, 4),
        lax.rem(shard, 2),
        lax.axis_index("context"),
        lax.axis_index("tensor"),
    )


def device(xh, y, core, xl, z):
    return {"shard": (xh * 4 + y) * 2 + core, "context": xl, "tensor": z}


def greet(peers):
    barrier = pltpu.get_barrier_semaphore()
    for peer in peers:
        pl.semaphore_signal(barrier, inc=1, device_id=peer, device_id_type=MESH)
    pl.semaphore_wait(barrier, len(peers))


def remote(src, dst, send_sem, recv_sem, peer):
    return pltpu.make_async_remote_copy(
        src_ref=src,
        dst_ref=dst,
        send_sem=send_sem,
        recv_sem=recv_sem,
        device_id=peer,
        device_id_type=MESH,
    )


def turn(block, cos_part, sin_part):
    lower_half, upper_half = block[: HD // 2], block[HD // 2 :]
    return jnp.concatenate(
        [
            lower_half * cos_part - upper_half * sin_part,
            upper_half * cos_part + lower_half * sin_part,
        ],
        axis=0,
    )


def turn_back(block, cos_part, sin_part):
    return turn(block, cos_part, -sin_part)


def by_span(context, b, run):
    near = (context == 0) | (b <= 3)

    @pl.when(near)
    def _():
        run(1408)

    @pl.when(jnp.logical_not(near))
    def _():
        run(1792)


def attend_back_kernel(
    turned,
    kv_rows,
    kv_lines,
    attended,
    log_total,
    grad_attended,
    cos_ref,
    sin_ref,
    limit,
    grad_packed,
    sums,
    outgoing,
    incoming,
    send_sem,
    recv_sem,
):
    xh, y, core, xl, z = place()
    peer = device(xh, y, core, 1 - xl, z)
    greet([peer])
    cos_part, sin_part = cos_ref[...], sin_ref[...]
    sums[...] = jnp.zeros_like(sums)

    def block(t, carry):
        b, g = t // HEADS, lax.rem(t, HEADS)
        columns = pl.ds(pl.multiple_of(b * 128, 128), 128)

        def run(span):
            head_rows = [
                pl.ds(pl.multiple_of((g * GROUP + h) * HD, HD), HD) for h in range(GROUP)
            ]
            queries = jnp.concatenate([turned[r, columns] for r in head_rows], axis=1)
            gradient = jnp.concatenate([grad_attended[r, columns] for r in head_rows], axis=1)
            held = jnp.concatenate([attended[r, columns] for r in head_rows], axis=1)
            inner = jnp.sum(
                gradient.astype(jnp.float32) * held.astype(jnp.float32), axis=0, keepdims=True
            )
            nothing = jnp.zeros_like(queries)
            both = jnp.concatenate(
                [
                    jnp.concatenate([queries, nothing], axis=1),
                    jnp.concatenate([nothing, gradient], axis=1),
                ],
                axis=0,
            )
            products = nn(kv_rows[g, :span], both)
            key_index = lax.broadcasted_iota(jnp.int32, (span, 384), 0)
            probs = jnp.exp(
                jnp.where(key_index < limit[b], products[:, :384], NEG) - log_total[t]
            )
            grad_scores = (probs * (products[:, 384:] - inner)).astype(jnp.bfloat16)
            sums[g, :span] += nt(
                jnp.concatenate([grad_scores, probs.astype(jnp.bfloat16)], axis=1), both
            )
            total = nn(kv_lines[g, :HD, :span], grad_scores) * HD ** (-0.5)
            cos_here, sin_here = cos_ref[:, columns], sin_ref[:, columns]
            for h in range(GROUP):
                lines = pl.ds(pl.multiple_of((g * 5 + h) * HD, HD), HD)
                grad_packed[lines, columns] = turn_back(
                    total[:, h * 128 : (h + 1) * 128], cos_here, sin_here
                ).astype(jnp.bfloat16)

        by_span(xl, b, run)
        return carry

    lax.fori_loop(0, HEADS * BLOCKS, block, 0)
    for g in range(HEADS):
        theirs = sums[g, pl.ds(pl.multiple_of((1 - xl) * 896, 128), 896)]
        outgoing[g * 128 : (g + 1) * 128] = jnp.transpose(theirs).astype(jnp.bfloat16)
    copy = remote(outgoing, incoming, send_sem, recv_sem, peer)
    copy.start()
    copy.wait()
    for g in range(HEADS):
        mine = jnp.transpose(sums[g, pl.ds(pl.multiple_of(xl * 896, 128), 896)])
        mine = mine + incoming[g * 128 : (g + 1) * 128].astype(jnp.float32)
        base = g * 5 * HD
        grad_packed[base + 3 * HD : base + 4 * HD] = turn_back(
            mine[:HD], cos_part, sin_part
        ).astype(jnp.bfloat16)
        grad_packed[base + 4 * HD : base + 5 * HD] = mine[HD:].astype(jnp.bfloat16)


def attend_backward(
    turned, kv_rows, kv_lines, attended, log_total, grad_attended, cos_part, sin_part, limit
):
    return pl.pallas_call(
        attend_back_kernel,
        out_shape=jax.ShapeDtypeStruct((640, 896), jnp.bfloat16),
        scratch_shapes=[
            pltpu.VMEM((HEADS, 1792, 128), jnp.float32),
            pltpu.VMEM((256, 896), jnp.bfloat16),
            pltpu.VMEM((256, 896), jnp.bfloat16),
            pltpu.SemaphoreType.DMA,
            pltpu.SemaphoreType.DMA,
        ],
        compiler_params=pltpu.CompilerParams(
            collective_id=2, has_side_effects=True, vmem_limit_bytes=VMEM_MOST
        ),
    )(turned, kv_rows, kv_lines, attended, log_total, grad_attended, cos_part, sin_part, limit)


def ring_peers():
    xh, y, core, xl, z = place()
    return (
        z,
        lax.rem(z + 1, 4),
        lax.rem(z + 2, 4),
        lax.rem(z + 3, 4),
        device(xh, y, core, xl, lax.rem(z + 1, 4)),
        device(xh, y, core, xl, lax.rem(z + 3, 4)),
    )


def halves(ref, index):
    rows = ref.shape[1] // 2
    return ref.at[index, pl.ds(0, rows)], ref.at[index, pl.ds(rows, rows)]


def ring_gather_begin(own, held, send_sem, recv_sem):
    z, zp, z2, zm, up, down = ring_peers()
    rows = own.shape[0] // 2
    first, second = own.at[pl.ds(0, rows)], own.at[pl.ds(rows, rows)]
    first_to, second_to = halves(held, z)
    copies = [
        remote(first, first_to, send_sem.at[0], recv_sem.at[0], up),
        remote(second, second_to, send_sem.at[1], recv_sem.at[1], down),
        remote(second, second_to, send_sem.at[2], recv_sem.at[2], up),
        remote(first, first_to, send_sem.at[3], recv_sem.at[3], down),
    ]
    for copy in copies:
        copy.start()
    return copies


def ring_gather_forward(held, copies, send_sem, recv_sem):
    z, zp, z2, zm, up, down = ring_peers()
    copies[0].wait_recv()
    below = halves(held, zm)[0]
    on_up = remote(below, below, send_sem.at[4], recv_sem.at[4], up)
    on_up.start()
    copies[1].wait_recv()
    above = halves(held, zp)[1]
    on_down = remote(above, above, send_sem.at[5], recv_sem.at[5], down)
    on_down.start()
    return copies + [on_up, on_down]


def ring_gather_end(copies):
    for copy in copies:
        copy.wait_send()
    for copy in copies[2:]:
        copy.wait_recv()


def ring_gather_kernel(own, held, send_sem, recv_sem, own_sem):
    z, zp, z2, zm, up, down = ring_peers()
    greet([up, down])
    copies = ring_gather_begin(own, held, send_sem, recv_sem)
    keep = pltpu.make_async_copy(own, held.at[z], own_sem)
    keep.start()
    copies = ring_gather_forward(held, copies, send_sem, recv_sem)
    keep.wait()
    ring_gather_end(copies)


def ring_gather(rows, identity):
    count, width = rows.shape
    held = pl.pallas_call(
        ring_gather_kernel,
        out_shape=jax.ShapeDtypeStruct((4, count, width), rows.dtype),
        in_specs=[pl.BlockSpec(memory_space=pl.ANY)],
        out_specs=pl.BlockSpec(memory_space=pl.ANY),
        scratch_shapes=[
            pltpu.SemaphoreType.DMA((6,)),
            pltpu.SemaphoreType.DMA((6,)),
            pltpu.SemaphoreType.DMA,
        ],
        compiler_params=pltpu.CompilerParams(
            collective_id=identity, has_side_effects=True, vmem_limit_bytes=VMEM_MOST
        ),
    )(rows)
    return held.reshape(4 * count, width)


def in_rows(count, step, run):
    def body(i, carry):
        run(pl.ds(pl.multiple_of(i * step, step), step))
        return carry

    lax.fori_loop(0, count // step, body, 0)


def ring_scatter_near(parts, came, send_sem, recv_sem):
    z, zp, z2, zm, up, down = ring_peers()
    copies = [
        remote(halves(parts, zp)[0], came.at[2], send_sem.at[2], recv_sem.at[2], up),
        remote(halves(parts, zm)[1], came.at[3], send_sem.at[3], recv_sem.at[3], down),
    ]
    for copy in copies:
        copy.start()
    return copies


def ring_scatter_far(parts, came, send_sem, recv_sem):
    z, zp, z2, zm, up, down = ring_peers()
    copies = [
        remote(halves(parts, z2)[1], came.at[0], send_sem.at[0], recv_sem.at[0], up),
        remote(halves(parts, z2)[0], came.at[1], send_sem.at[1], recv_sem.at[1], down),
    ]
    for copy in copies:
        copy.start()
    return copies


def ring_scatter_begin(parts, came, send_sem, recv_sem):
    far = ring_scatter_far(parts, came, send_sem, recv_sem)
    return far + ring_scatter_near(parts, came, send_sem, recv_sem)


def ring_scatter_forward(parts, came, sums, copies, send_sem, recv_sem):
    z, zp, z2, zm, up, down = ring_peers()
    count = came.shape[1]
    copies[0].wait_recv()

    def add_up(rows):
        sums[0, rows] = (
            came[0, rows].astype(jnp.float32)
            + parts[zp, pl.ds(pl.multiple_of(rows.start + count, 16), 16)].astype(jnp.float32)
        ).astype(jnp.bfloat16)

    in_rows(count, 16, add_up)
    on_up = remote(sums.at[0], came.at[4], send_sem.at[4], recv_sem.at[4], up)
    on_up.start()
    copies[1].wait_recv()

    def add_down(rows):
        sums[1, rows] = (
            came[1, rows].astype(jnp.float32) + parts[zm, rows].astype(jnp.float32)
        ).astype(jnp.bfloat16)

    in_rows(count, 16, add_down)
    on_down = remote(sums.at[1], came.at[5], send_sem.at[5], recv_sem.at[5], down)
    on_down.start()
    return copies + [on_up, on_down]


def ring_scatter_end(parts, came, total, copies):
    z, zp, z2, zm, up, down = ring_peers()
    count = came.shape[1]
    for copy in copies[2:]:
        copy.wait_recv()
    for copy in copies:
        copy.wait_send()

    def add(rows):
        later = pl.ds(pl.multiple_of(rows.start + count, 16), 16)
        total[rows] = (
            parts[z, rows].astype(jnp.float32)
            + came[2, rows].astype(jnp.float32)
            + came[5, rows].astype(jnp.float32)
        )
        total[later] = (
            parts[z, later].astype(jnp.float32)
            + came[3, rows].astype(jnp.float32)
            + came[4, rows].astype(jnp.float32)
        )

    in_rows(count, 16, add)


def ring_scatter_kernel(parts, total, came, sums, send_sem, recv_sem):
    z, zp, z2, zm, up, down = ring_peers()
    greet([up, down])
    copies = ring_scatter_begin(parts, came, send_sem, recv_sem)
    copies = ring_scatter_forward(parts, came, sums, copies, send_sem, recv_sem)
    ring_scatter_end(parts, came, total, copies)


def ring_scatter(parts, identity):
    rows, width = parts.shape
    count = rows // 4
    return pl.pallas_call(
        ring_scatter_kernel,
        out_shape=jax.ShapeDtypeStruct((count, width), jnp.float32),
        scratch_shapes=[
            pltpu.VMEM((6, count // 2, width), jnp.bfloat16),
            pltpu.VMEM((2, count // 2, width), jnp.bfloat16),
            pltpu.SemaphoreType.DMA((6,)),
            pltpu.SemaphoreType.DMA((6,)),
        ],
        compiler_params=pltpu.CompilerParams(
            collective_id=identity, has_side_effects=True, vmem_limit_bytes=VMEM_MOST
        ),
    )(parts.reshape(4, count, width))


def plane():
    xh, y, core, xl, z = place()
    ys = [lax.rem(y + d, 4) for d in (1, 3, 2)]
    step = xh * 2 + xl
    xs = [lax.rem(step + d, 4) for d in (1, 3, 2)]
    xs = [(x // 2, lax.rem(x, 2)) for x in xs]
    y_peers = [device(xh, other, core, xl, z) for other in ys]
    x_peers = [device(h, y, core, l, z) for h, l in xs]
    return ys, xs, y_peers, x_peers, device(xh, y, 1 - core, xl, z)


class PlaneGather:
    def __init__(self, own, held, y_first, send_sem, recv_sem):
        self.own, self.held, self.y_first = own, held, y_first
        self.send_sem, self.recv_sem, self.used = send_sem, recv_sem, 0
        self.copies, self.first, self.second, self.third = [], [], [], []

    def send(self, src, dst, peer):
        copy = remote(src, dst, self.send_sem.at[self.used], self.recv_sem.at[self.used], peer)
        self.used += 1
        copy.start()
        self.copies.append(copy)
        return copy

    def begin(self):
        xh, y, core, xl, z = place()
        ys, xs, y_peers, x_peers, other = plane()
        target = self.held.at[xh, y, core, xl]
        peers = y_peers if self.y_first else x_peers
        self.first = [self.send(self.own, target, peer) for peer in peers]

    def line(self, where):
        xh, y, core, xl, z = place()
        if self.y_first:
            return self.held.at[where[0], :, core, where[1]]
        return self.held.at[:, where, core, :]

    def spread(self):
        xh, y, core, xl, z = place()
        ys, xs, y_peers, x_peers, other = plane()
        for copy in self.first:
            copy.wait_recv()
        mine = self.line((xh, xl) if self.y_first else y)
        peers = x_peers if self.y_first else y_peers
        self.second = [self.send(mine, mine, peer) for peer in peers]
        self.third = [self.send(mine, mine, other)]

    def share(self):
        ys, xs, y_peers, x_peers, other = plane()
        wheres = xs if self.y_first else ys
        for copy, where in zip(self.second, (wheres[1], wheres[0], wheres[2])):
            copy.wait_recv()
            line = self.line(where)
            self.third.append(self.send(line, line, other))

    def end(self):
        for copy in self.third:
            copy.wait_recv()
        for copy in self.copies:
            copy.wait_send()


class PlaneScatter:
    def __init__(self, parts, came, halved, across, lined, last, x_first, send_sem, recv_sem):
        self.parts, self.came, self.halved = parts, came, halved
        self.across, self.lined, self.last, self.x_first = across, lined, last, x_first
        self.send_sem, self.recv_sem, self.used, self.copies = send_sem, recv_sem, 0, []

    def send(self, src, dst, peer):
        copy = remote(src, dst, self.send_sem.at[self.used], self.recv_sem.at[self.used], peer)
        self.used += 1
        copy.start()
        self.copies.append(copy)
        return copy

    def begin(self):
        xh, y, core, xl, z = place()
        ys, xs, y_peers, x_peers, other = plane()
        self.wheres = (xs[::-1] + [(xh, xl)]) if self.x_first else (ys[::-1] + [y])
        self.first = []
        for where in self.wheres:
            if self.x_first:
                src = self.parts.at[where[0], :, 1 - core, where[1]]
                dst = self.came.at[where[0], :, where[1]]
            else:
                src, dst = self.parts.at[:, where, 1 - core, :], self.came.at[:, where, :]
            self.first.append(self.send(src, dst, other))

    def fold(self):
        xh, y, core, xl, z = place()
        ys, xs, y_peers, x_peers, other = plane()
        peers = x_peers[::-1] if self.x_first else y_peers[::-1]
        self.second = []
        for k, (where, copy) in enumerate(zip(self.wheres, self.first)):
            copy.wait_recv()

            def add(i, carry, where=where, k=k):
                def rows(r):
                    if self.x_first:
                        h, l, v = where[0], where[1], i
                    else:
                        h, l, v = i // 2, lax.rem(i, 2), where
                    total = self.parts[h, v, core, l, r].astype(jnp.float32) + self.came[
                        h, v, l, r
                    ].astype(jnp.float32)
                    self.halved[k, i, r] = total.astype(jnp.bfloat16)

                in_rows(48, 16, rows)
                return carry

            lax.fori_loop(0, 4, add, 0)
            if k < 3:
                self.second.append(self.send(self.halved.at[k], self.across.at[k], peers[k]))

    def line(self):
        xh, y, core, xl, z = place()
        ys, xs, y_peers, x_peers, other = plane()
        for copy in self.second:
            copy.wait_recv()

        def add(i, carry):
            def rows(r):
                total = self.halved[3, i, r].astype(jnp.float32)
                for k in range(3):
                    total = total + self.across[k, i, r].astype(jnp.float32)
                self.lined[i, r] = total.astype(jnp.bfloat16)

            in_rows(48, 16, rows)
            return carry

        lax.fori_loop(0, 4, add, 0)
        if self.x_first:
            self.mine, targets, peers = y, ys, y_peers
        else:
            self.mine, targets, peers = xh * 2 + xl, [h * 2 + l for h, l in xs], x_peers
        self.third = [
            self.send(self.lined.at[target], self.last.at[k], peer)
            for k, (target, peer) in enumerate(zip(targets, peers))
        ]

    def end(self, total_ref):
        for copy in self.third:
            copy.wait_recv()

        def rows(r):
            total = self.lined[self.mine, r].astype(jnp.float32)
            for k in range(3):
                total = total + self.last[k, r].astype(jnp.float32)
            total_ref[r] = total

        in_rows(48, 16, rows)
        for copy in self.copies:
            copy.wait_send()


def scatter_scratch(width):
    return [
        pltpu.VMEM((2, 4, 2, 48, width), jnp.bfloat16),
        pltpu.VMEM((4, 4, 48, width), jnp.bfloat16),
        pltpu.VMEM((3, 4, 48, width), jnp.bfloat16),
        pltpu.VMEM((4, 48, width), jnp.bfloat16),
        pltpu.VMEM((3, 48, width), jnp.bfloat16),
    ]


def plane_scatter_kernel(turns, *refs):
    n = len(turns)
    parts, totals, scratch = refs[:n], refs[n : 2 * n], refs[2 * n :]
    send_sem, recv_sem = scratch[-2:]
    ys, xs, y_peers, x_peers, other = plane()
    greet([other] + y_peers + x_peers)
    scatters = [
        PlaneScatter(
            parts[i], *scratch[5 * i : 5 * i + 5], turns[i], send_sem.at[i], recv_sem.at[i]
        )
        for i in range(n)
    ]
    for scatter in scatters:
        scatter.begin()
    for scatter in scatters:
        scatter.fold()
    for scatter in scatters:
        scatter.line()
    for scatter, total in zip(scatters, totals):
        scatter.end(total)


def plane_scatter(gradients, turns, identity):
    shaped = [g.reshape(2, 4, 2, 2, 48, g.shape[-1]) for g in gradients]
    scratch = []
    for g in gradients:
        scratch += scatter_scratch(g.shape[-1])
    n = len(gradients)
    return pl.pallas_call(
        functools.partial(plane_scatter_kernel, turns),
        out_shape=tuple(jax.ShapeDtypeStruct((48, g.shape[-1]), jnp.float32) for g in gradients),
        scratch_shapes=scratch
        + [pltpu.SemaphoreType.DMA((n, 10)), pltpu.SemaphoreType.DMA((n, 10))],
        compiler_params=pltpu.CompilerParams(
            collective_id=identity, has_side_effects=True, vmem_limit_bytes=VMEM_MOST
        ),
    )(*shaped)


def sum_kernel(own, total, held, send_sem, recv_sem):
    xh, y, core, xl, z = place()
    ys, xs, y_peers, x_peers, other = plane()
    z_peers = [device(xh, y, core, xl, lax.rem(z + d, 4)) for d in (1, 3, 2)]
    greet([other] + z_peers + x_peers + y_peers)
    total[...] = own[...]
    groups = ((z_peers, z, 4), (x_peers, xh * 2 + xl, 4), (y_peers, y, 4), ([other], core, 2))
    for axis, (group, here, count) in enumerate(groups):
        held[axis, here] = total[...]
        copies = [
            remote(
                held.at[axis, here],
                held.at[axis, here],
                send_sem.at[axis * 3 + k],
                recv_sem.at[axis * 3 + k],
                peer,
            )
            for k, peer in enumerate(group)
        ]
        for copy in copies:
            copy.start()
        for copy in copies:
            copy.wait()
        order = held[axis, 0]
        for k in range(1, count):
            order = order + held[axis, k]
        total[...] = order


def sum_everywhere(own, identity):
    return pl.pallas_call(
        sum_kernel,
        out_shape=jax.ShapeDtypeStruct(own.shape, jnp.float32),
        scratch_shapes=[
            pltpu.VMEM((4, 4) + own.shape, jnp.float32),
            pltpu.SemaphoreType.DMA((12,)),
            pltpu.SemaphoreType.DMA((12,)),
        ],
        compiler_params=pltpu.CompilerParams(
            collective_id=identity, has_side_effects=True, vmem_limit_bytes=VMEM_MOST
        ),
    )(own)


def swap_halves(block):
    lane = lax.broadcasted_iota(jnp.int32, block.shape, 1)
    return jnp.where(
        lane < HD // 2, pltpu.roll(block, 128 - HD // 2, 1), pltpu.roll(block, HD // 2, 1)
    )


def front_kernel(*refs):
    (first, shrunk, w_in, w_gate, w_up, w_out, w_shrink) = refs[:7]
    (cos_ref, sin_ref, key_cos, key_sin, limit) = refs[7:12]
    (first_all, shrunk_all, in_all, gate_all, up_all, out_all, shrink_all) = refs[12:19]
    (turned, kv_rows, kv_lines, attended, log_total, total) = refs[19:25]
    (packed, held_rows, parts, came, sums) = refs[25:30]
    (ring_send, ring_recv, plane_send, plane_recv) = refs[30:34]
    (kv_send, kv_recv, own_sem, out_sem) = refs[34:]
    xh, y, core, xl, z = place()
    z, zp, z2, zm, up, down = ring_peers()
    ys, xs, y_peers, x_peers, other = plane()
    beside = device(xh, y, core, 1 - xl, z)
    greet([up, down, other] + y_peers + x_peers)
    owns = (w_in, w_out, w_gate, w_up, w_shrink)
    helds = (in_all, out_all, gate_all, up_all, shrink_all)
    gathers = [
        PlaneGather(own, held, i in (2, 3), plane_send.at[i], plane_recv.at[i])
        for i, (own, held) in enumerate(zip(owns, helds))
    ]
    for gather in gathers[:2]:
        gather.begin()
    ring = ring_gather_begin(first, first_all, ring_send.at[0], ring_recv.at[0])
    keeps = [
        pltpu.make_async_copy(own, held.at[xh, y, core, xl], own_sem.at[i])
        for i, (own, held) in enumerate(zip(owns, helds))
    ]
    keeps.append(pltpu.make_async_copy(first, first_all.at[z], own_sem.at[5]))
    keeps.append(pltpu.make_async_copy(shrunk, shrunk_all.at[z], own_sem.at[6]))
    for keep in keeps:
        keep.start()
    for keep in keeps:
        keep.wait()
    for gather in gathers[:2]:
        gather.spread()
    ring = ring_gather_forward(first_all, ring, ring_send.at[0], ring_recv.at[0])
    gathers[0].share()
    gathers[1].share()
    gathers[0].end()
    for gather in gathers[2:]:
        gather.begin()

    def project(c, rows):
        out = nn(first_all[c], in_all[...].reshape(1536, 640))
        packed[rows] = out
        for g in range(HEADS):
            block = out[:, g * 320 + 192 : g * 320 + 320]
            mine = pl.ds(pl.multiple_of(xl * 896 + c * 224, 16), 224)
            kv_rows[g, mine] = (
                block * key_cos[rows] + swap_halves(block) * key_sin[rows]
            ).astype(jnp.bfloat16)

    kv_copies = []
    for i, c in enumerate((z, zm, zp, z2)):
        if i == 1:
            ring[2].wait_recv()
        if i == 2:
            ring[3].wait_recv()
        if i == 3:
            ring[4].wait_recv()
            ring[5].wait_recv()
        project(c, pl.ds(pl.multiple_of(c * 224, 16), 224))
        mine = kv_rows.at[:, pl.ds(pl.multiple_of(xl * 896 + c * 224, 16), 224)]
        kv_copies.append(remote(mine, mine, kv_send.at[i], kv_recv.at[i], beside))
        kv_copies[-1].start()
    later = ring_gather_begin(shrunk, shrunk_all, ring_send.at[1], ring_recv.at[1])

    def turn_block(b, carry):
        columns = pl.ds(pl.multiple_of(b * 128, 128), 128)
        lines = jnp.transpose(packed[columns])
        cos_here, sin_here = cos_ref[:, columns], sin_ref[:, columns]
        for g in range(HEADS):
            for h in range(GROUP):
                at = (g * 5 + h) * HD
                turned[(g * GROUP + h) * HD : (g * GROUP + h + 1) * HD, columns] = (
                    turn(lines[at : at + HD], cos_here, sin_here) * HD ** (-0.5)
                ).astype(jnp.bfloat16)
        return carry

    lax.fori_loop(0, BLOCKS, turn_block, 0)
    for copy in kv_copies:
        copy.wait_recv()
    for gather in gathers[2:]:
        gather.spread()
    for g in range(HEADS):
        kv_lines[g] = jnp.transpose(kv_rows[g].astype(jnp.float32)).astype(jnp.bfloat16)

    def block(t, carry):
        b, g = t // HEADS, lax.rem(t, HEADS)
        columns = pl.ds(pl.multiple_of(b * 128, 128), 128)

        def run(span):
            head_rows = [
                pl.ds(pl.multiple_of((g * GROUP + h) * HD, HD), HD) for h in range(GROUP)
            ]
            queries = jnp.concatenate([turned[r, columns] for r in head_rows], axis=1)
            queries = jnp.concatenate([queries, jnp.zeros_like(queries)], axis=0)
            scores = nn(kv_rows[g, :span], queries)
            key_index = lax.broadcasted_iota(jnp.int32, (span, 384), 0)
            scores = jnp.where(key_index < limit[b], scores, NEG)
            row_max = jnp.max(scores, axis=0, keepdims=True)
            shifted = jnp.exp(scores - row_max)
            exp_total = jnp.sum(shifted, axis=0, keepdims=True)
            out = nn(kv_lines[g, HD:, :span], shifted.astype(jnp.bfloat16)) * (1.0 / exp_total)
            for h in range(GROUP):
                attended[head_rows[h], columns] = out[:, h * 128 : (h + 1) * 128].astype(
                    jnp.bfloat16
                )
            log_total[t] = row_max + jnp.log(exp_total)

        by_span(xl, b, run)
        return carry

    lax.fori_loop(0, 6, block, 0)
    later = ring_gather_forward(shrunk_all, later, ring_send.at[1], ring_recv.at[1])
    lax.fori_loop(6, HEADS * BLOCKS, block, 0)
    gathers[1].end()
    fetch = pltpu.make_async_copy(out_all, held_rows, out_sem)
    fetch.start()
    tokens = jnp.transpose(attended[...].astype(jnp.float32)).astype(jnp.bfloat16)
    packed_low = tokens.reshape(4, 224, 384)
    fetch.wait()
    for c in range(4):
        parts[c] = nt(packed_low[c], held_rows[...].reshape(1536, 384)).astype(jnp.bfloat16)
    scatter = ring_scatter_begin(parts, came, ring_send.at[2], ring_recv.at[2])
    scatter = ring_scatter_forward(
        parts, came, sums, scatter, ring_send.at[2], ring_recv.at[2]
    )
    for gather in gathers[2:]:
        gather.share()
    for gather in gathers[2:]:
        gather.end()
    ring_gather_end(later)
    for copy in kv_copies + ring:
        copy.wait_send()
    ring_scatter_end(parts, came, total, scatter)


def front(first, shrunk, weights, tables):
    any_place = pl.BlockSpec(memory_space=pl.ANY)
    whole = pl.BlockSpec(memory_space=pltpu.VMEM)
    rows, width = first.shape
    gathered = [
        jax.ShapeDtypeStruct((2, 4, 2, 2) + w.shape, jnp.bfloat16) for w in weights
    ]
    outs = pl.pallas_call(
        front_kernel,
        out_shape=(
            jax.ShapeDtypeStruct((4, rows, width), jnp.bfloat16),
            jax.ShapeDtypeStruct((4, rows, width), jnp.bfloat16),
            *gathered,
            jax.ShapeDtypeStruct((384, 896), jnp.bfloat16),
            jax.ShapeDtypeStruct((HEADS, 1792, 128), jnp.bfloat16),
            jax.ShapeDtypeStruct((HEADS, 128, 1792), jnp.bfloat16),
            jax.ShapeDtypeStruct((384, 896), jnp.bfloat16),
            jax.ShapeDtypeStruct((HEADS * BLOCKS, 1, 384), jnp.float32),
            jax.ShapeDtypeStruct((rows, width), jnp.float32),
        ),
        in_specs=[whole] * 12,
        out_specs=(whole, any_place, whole) + (any_place,) * 4 + (whole,) * 6,
        scratch_shapes=[
            pltpu.VMEM((896, 640), jnp.float32),
            pltpu.VMEM((2, 4, 2, 2, 48, 384), jnp.bfloat16),
            pltpu.VMEM((4, rows, width), jnp.bfloat16),
            pltpu.VMEM((6, rows // 2, width), jnp.bfloat16),
            pltpu.VMEM((2, rows // 2, width), jnp.bfloat16),
            pltpu.SemaphoreType.DMA((3, 6)),
            pltpu.SemaphoreType.DMA((3, 6)),
            pltpu.SemaphoreType.DMA((5, 10)),
            pltpu.SemaphoreType.DMA((5, 10)),
            pltpu.SemaphoreType.DMA((4,)),
            pltpu.SemaphoreType.DMA((4,)),
            pltpu.SemaphoreType.DMA((7,)),
            pltpu.SemaphoreType.DMA,
        ],
        compiler_params=pltpu.CompilerParams(
            collective_id=0, has_side_effects=True, vmem_limit_bytes=VMEM_MOST
        ),
    )(first, shrunk, *weights, *tables)
    return (
        outs[0].reshape(4 * rows, width),
        outs[1],
        *(held.reshape(1536, -1) for held in outs[2:7]),
        *outs[7:],
    )


def tn(a, b):
    return lax.dot_general(a, b, (((0,), (0,)), ((), ())), preferred_element_type=jnp.float32)


def middle_kernel(*refs):
    (hidden, cotangent, projected, gain) = refs[:4]
    (shrunk_from, gate_from, up_from, shrink_from) = refs[4:8]
    (residual, grad_residual, turned_back, gain_two) = refs[8:12]
    (grad_gate, grad_up, grad_shrink, out_parts) = refs[12:16]
    (shrunk_all, w_gate, w_up, w_shrink) = refs[16:20]
    (second_all, activated_back, gated, gate_back, up_back) = refs[20:25]
    (parts, came, sums, total) = refs[25:29]
    (ring_send, ring_recv, load_sem) = refs[29:]
    z, zp, z2, zm, up, down = ring_peers()
    greet([up, down])
    loads = [
        pltpu.make_async_copy(src, dst, load_sem.at[i])
        for i, (src, dst) in enumerate(
            (
                (shrink_from, w_shrink),
                (shrunk_from, shrunk_all),
                (gate_from, w_gate),
                (up_from, w_up),
            )
        )
    ]
    for load in loads:
        load.start()
    rows = hidden[...].astype(jnp.float32) + RESID * projected[...]
    residual[...] = rows
    scaling = lax.rsqrt(jnp.mean(rows * rows, axis=-1, keepdims=True) + EPS)
    second_all[z] = (rows * scaling * gain[...]).astype(jnp.bfloat16)
    ring = ring_gather_begin(second_all.at[z], second_all, ring_send.at[0], ring_recv.at[0])
    loads[0].wait()
    loads[1].wait()
    for c in range(4):
        activated_back[c] = nn(shrunk_all[c], w_shrink[...])
    loads[2].wait()
    loads[3].wait()

    def feed(c):
        gate_value = nn(second_all[c], w_gate[...])
        up_value = nn(second_all[c], w_up[...])
        sigmoid_gate = 1.0 / (1.0 + jnp.exp(-gate_value))
        gate_active = gate_value * sigmoid_gate
        gated[c] = (gate_active * up_value).astype(jnp.bfloat16)
        gradient = activated_back[c]
        gate_back[c] = (
            gradient * up_value * sigmoid_gate * (1.0 + gate_value * (1.0 - sigmoid_gate))
        ).astype(jnp.bfloat16)
        up_back[c] = (gradient * gate_active).astype(jnp.bfloat16)
        parts[c] = (nt(gate_back[c], w_gate[...]) + nt(up_back[c], w_up[...])).astype(
            jnp.bfloat16
        )

    feed(z)
    ring = ring_gather_forward(second_all, ring, ring_send.at[0], ring_recv.at[0])
    ring[2].wait_recv()
    feed(zm)
    ring[3].wait_recv()
    feed(zp)
    near = ring_scatter_near(parts, came, ring_send.at[1], ring_recv.at[1])
    ring[4].wait_recv()
    ring[5].wait_recv()
    feed(z2)
    far = ring_scatter_far(parts, came, ring_send.at[1], ring_recv.at[1])
    second_rows = second_all[...].reshape(896, 1536)
    grad_gate[...] = tn(second_rows, gate_back[...].reshape(896, 960)).astype(jnp.bfloat16)
    scatter = ring_scatter_forward(
        parts, came, sums, far + near, ring_send.at[1], ring_recv.at[1]
    )
    grad_up[...] = tn(second_rows, up_back[...].reshape(896, 960)).astype(jnp.bfloat16)
    grad_shrink[...] = tn(
        shrunk_all[...].reshape(896, 1536), gated[...].reshape(896, 960)
    ).astype(jnp.bfloat16)
    for c in range(4):
        out_parts[c] = nt(gated[c], w_shrink[...]).astype(jnp.bfloat16)
    for copy in ring:
        copy.wait_send()
    ring_scatter_end(parts, came, total, scatter)
    rows = residual[...]
    scaling = lax.rsqrt(jnp.mean(rows * rows, axis=-1, keepdims=True) + EPS)
    normed = rows * scaling
    gradient = total[...]
    gain_two[...] = jnp.sum(gradient * normed, axis=0, keepdims=True)
    gradient = gradient * gain[...]
    back = cotangent[...].astype(jnp.float32) + scaling * (
        gradient - normed * jnp.mean(gradient * normed, axis=-1, keepdims=True)
    )
    grad_residual[...] = back
    turned_back[...] = (RESID * back).astype(jnp.bfloat16)


def middle(hidden, cotangent, projected, gain, shrunk_all, w_gate, w_up, w_shrink):
    any_place = pl.BlockSpec(memory_space=pl.ANY)
    whole = pl.BlockSpec(memory_space=pltpu.VMEM)
    rows, width = hidden.shape
    low, full = jnp.bfloat16, jnp.float32
    return pl.pallas_call(
        middle_kernel,
        out_shape=(
            jax.ShapeDtypeStruct((rows, width), full),
            jax.ShapeDtypeStruct((rows, width), full),
            jax.ShapeDtypeStruct((rows, width), low),
            jax.ShapeDtypeStruct((1, width), full),
            jax.ShapeDtypeStruct((1536, 960), low),
            jax.ShapeDtypeStruct((1536, 960), low),
            jax.ShapeDtypeStruct((1536, 960), low),
            jax.ShapeDtypeStruct((4, rows, width), low),
        ),
        in_specs=[whole] * 4 + [any_place] * 4,
        out_specs=(whole,) * 8,
        scratch_shapes=[
            pltpu.VMEM((4, rows, width), low),
            pltpu.VMEM((1536, 960), low),
            pltpu.VMEM((1536, 960), low),
            pltpu.VMEM((1536, 960), low),
            pltpu.VMEM((4, rows, width), low),
            pltpu.VMEM((4, rows, 960), full),
            pltpu.VMEM((4, rows, 960), low),
            pltpu.VMEM((4, rows, 960), low),
            pltpu.VMEM((4, rows, 960), low),
            pltpu.VMEM((4, rows, width), low),
            pltpu.VMEM((6, rows // 2, width), low),
            pltpu.VMEM((2, rows // 2, width), low),
            pltpu.VMEM((rows, width), full),
            pltpu.SemaphoreType.DMA((2, 6)),
            pltpu.SemaphoreType.DMA((2, 6)),
            pltpu.SemaphoreType.DMA((4,)),
        ],
        compiler_params=pltpu.CompilerParams(
            collective_id=4, has_side_effects=True, vmem_limit_bytes=VMEM_MOST
        ),
    )(hidden, cotangent, projected, gain, shrunk_all, w_gate, w_up, w_shrink)


def product(a, b, a_dim, b_dim):
    return lax.dot_general(
        a, b, (((a_dim,), (b_dim,)), ((), ())), preferred_element_type=jnp.float32
    )


def shards(
    hidden_in,
    cotangent,
    prefix,
    positions,
    norm_gains,
    gains_first,
    gains_second,
    input_weight,
    input_first,
    input_second,
    output_weight,
    output_first,
    output_second,
    expand_weight,
    expand_first,
    expand_second,
    shrink_weight,
    shrink_first,
    shrink_second,
):
    low = jnp.bfloat16
    x_rows = hidden_in[0].astype(jnp.float32)
    normed_one, scale_one = rms_parts(x_rows)
    first_own = (normed_one * norm_gains[0]).astype(low)
    shrunk_own = (RESID * cotangent[0].astype(jnp.float32)).astype(low)
    cos_part, sin_part = angles(positions[0])
    row_index = lax.axis_index("context") * 896 + jnp.arange(896, dtype=jnp.int32)
    limit = jnp.maximum(row_index + 1, prefix[0]).reshape(BLOCKS, 1, 128)
    limit = jnp.concatenate([limit] * GROUP, axis=2)
    still = jnp.ones((896, HD), jnp.float32)
    key_cos = jnp.concatenate([cos_part.T, cos_part.T, still], axis=1)
    key_sin = jnp.concatenate([-sin_part.T, sin_part.T, 0.0 * still], axis=1)
    (
        first_all,
        shrunk_all,
        w_in,
        w_gate,
        w_up,
        w_out,
        w_shrink,
        turned,
        kv_rows,
        kv_lines,
        attended,
        log_total,
        projected,
    ) = front(
        first_own,
        shrunk_own,
        (
            input_weight.astype(low),
            expand_weight[0].astype(low),
            expand_weight[1].astype(low),
            output_weight.T.astype(low),
            shrink_weight.T.astype(low),
        ),
        (cos_part, sin_part, key_cos, key_sin, limit),
    )
    (
        residual,
        grad_residual,
        projected_gradient,
        gain_two,
        grad_gate,
        grad_up,
        grad_shrink,
        out_parts,
    ) = middle(
        hidden_in[0],
        cotangent[0],
        projected,
        norm_gains[1:],
        shrunk_all,
        w_gate,
        w_up,
        w_shrink,
    )
    projected_gradient = ring_gather(projected_gradient, 6)
    grad_attended = product(w_out, projected_gradient, 0, 1).astype(low)
    grad_packed = attend_backward(
        turned, kv_rows, kv_lines, attended, log_total, grad_attended, cos_part, sin_part, limit
    )
    grad_first = ring_scatter(product(grad_packed, w_in, 0, 1).astype(low), 7)
    gain_one = jnp.sum(grad_first * normed_one, axis=0)
    input_gradient = grad_residual + rms_back(grad_first * norm_gains[0], normed_one, scale_one)
    shrunk = ring_scatter(out_parts.reshape(896, 1536), 8)
    block_output = (residual + RESID * shrunk).astype(low)
    grad_gate, grad_up, grad_output, grad_shrink, grad_input = plane_scatter(
        (
            grad_gate,
            grad_up,
            product(projected_gradient, attended, 0, 1).astype(low),
            grad_shrink,
            product(first_all, grad_packed, 0, 1).astype(low),
        ),
        (True, True, False, False, False),
        9,
    )
    grad_expand = jnp.stack([grad_gate, grad_up])
    grad_output, grad_shrink = grad_output.T, grad_shrink.T
    reduced = (grad_input, grad_output, grad_expand, grad_shrink)
    local_squares = sum(jnp.sum(g * g) for g in reduced)
    gains_local = jnp.stack([gain_one, gain_two[0]]).reshape(24, 128)
    message = jnp.concatenate([gains_local, jnp.full((8, 128), local_squares)], axis=0)
    message = sum_everywhere(message, 10)
    grad_gains = message[:24].reshape(2, 1536)
    squares = message[24, 0] + jnp.sum(grad_gains * grad_gains)
    gradient_norm = jnp.sqrt(squares)
    factor = jnp.minimum(1.0, MAX_NORM / (gradient_norm + 1e-06))
    gains_new = adamw(norm_gains, factor * grad_gains, gains_first, gains_second, GAIN_RATE, 0.0)
    input_new = adamw(input_weight, factor * reduced[0], input_first, input_second, RATE, DECAY)
    output_new = adamw(output_weight, factor * reduced[1], output_first, output_second, RATE, DECAY)
    expand_new = adamw(expand_weight, factor * reduced[2], expand_first, expand_second, RATE, DECAY)
    shrink_new = adamw(shrink_weight, factor * reduced[3], shrink_first, shrink_second, RATE, DECAY)
    return (
        block_output[None],
        input_gradient[None],
        gradient_norm,
        *gains_new,
        *input_new,
        *output_new,
        *expand_new,
        *shrink_new,
    )


def solution(mesh):
    return jax.shard_map(
        shards,
        mesh=mesh,
        in_specs=(
            P("shard", ("context", "tensor"), None),
            P("shard", ("context", "tensor"), None),
            P("shard"),
            P("shard", "context"),
            P(),
            P(),
            P(),
            P(("shard", "context"), "tensor"),
            P(("shard", "context"), "tensor"),
            P(("shard", "context"), "tensor"),
            P("tensor", ("shard", "context")),
            P("tensor", ("shard", "context")),
            P("tensor", ("shard", "context")),
            P(None, ("shard", "context"), "tensor"),
            P(None, ("shard", "context"), "tensor"),
            P(None, ("shard", "context"), "tensor"),
            P("tensor", ("shard", "context")),
            P("tensor", ("shard", "context")),
            P("tensor", ("shard", "context")),
        ),
        out_specs=(
            P("shard", ("context", "tensor"), None),
            P("shard", ("context", "tensor"), None),
            P(),
            P(),
            P(),
            P(),
            P(("shard", "context"), "tensor"),
            P(("shard", "context"), "tensor"),
            P(("shard", "context"), "tensor"),
            P("tensor", ("shard", "context")),
            P("tensor", ("shard", "context")),
            P("tensor", ("shard", "context")),
            P(None, ("shard", "context"), "tensor"),
            P(None, ("shard", "context"), "tensor"),
            P(None, ("shard", "context"), "tensor"),
            P("tensor", ("shard", "context")),
            P("tensor", ("shard", "context")),
            P("tensor", ("shard", "context")),
        ),
        check_vma=False,
    )
```

```python
import functools
import math

import jax
import jax.numpy as jnp
from jax import lax
from jax.experimental import pallas as pl
from jax.experimental.pallas import tpu as pltpu
from jax.sharding import PartitionSpec as P

HD = 64
GROUP = 3
STEP = 10
HEADS = 2
BLOCKS = 7
VMEM_MOST = 60 * 2**20
MESH = pl.DeviceIdType.MESH


EPS = 1e-05
RESID = 1.4 / math.sqrt(52.0)
ROPE_BASE = 10000.0
MAX_NORM = 1.0
RATE = 0.1
GAIN_RATE = 1.0
BETA_ONE = 0.9
BETA_TWO = 0.95
ADAM_EPS = 1e-08
DECAY = 0.1
NEG = -1e30


def angles(places):
    half_width = HD // 2
    frequency = ROPE_BASE ** (-2.0 * jnp.arange(half_width, dtype=jnp.float32) / HD)
    phase_turn = places.astype(jnp.float32)[None, :] * frequency[:, None]
    return (jnp.cos(phase_turn), jnp.sin(phase_turn))


def rms_parts(values):
    scaling = lax.rsqrt(jnp.mean(values * values, axis=-1, keepdims=True) + EPS)
    return (values * scaling, scaling)


def rms_back(gradient, normed, scaling):
    return scaling * (gradient - normed * jnp.mean(gradient * normed, axis=-1, keepdims=True))


def adamw(weight, gradient, momentum, variance, step_rate, decay_rate):
    momentum_new = BETA_ONE * momentum + (1.0 - BETA_ONE) * gradient
    variance_new = BETA_TWO * variance + (1.0 - BETA_TWO) * gradient * gradient
    momentum_hat = momentum_new / (1.0 - BETA_ONE**STEP)
    variance_hat = variance_new / (1.0 - BETA_TWO**STEP)
    updated = weight - step_rate * (
        momentum_hat / (jnp.sqrt(variance_hat) + ADAM_EPS) + decay_rate * weight
    )
    return (momentum_new, variance_new, updated)


def nn(a, b):
    return lax.dot_general(a, b, (((1,), (0,)), ((), ())), preferred_element_type=jnp.float32)


def nt(a, b):
    return lax.dot_general(a, b, (((1,), (1,)), ((), ())), preferred_element_type=jnp.float32)


def place():
    shard = lax.axis_index("shard")
    return (
        shard // 8,
        lax.rem(shard // 2, 4),
        lax.rem(shard, 2),
        lax.axis_index("context"),
        lax.axis_index("tensor"),
    )


def device(xh, y, core, xl, z):
    return {"shard": (xh * 4 + y) * 2 + core, "context": xl, "tensor": z}


def greet(peers):
    barrier = pltpu.get_barrier_semaphore()
    for peer in peers:
        pl.semaphore_signal(barrier, inc=1, device_id=peer, device_id_type=MESH)
    pl.semaphore_wait(barrier, len(peers))


def remote(src, dst, send_sem, recv_sem, peer):
    return pltpu.make_async_remote_copy(
        src_ref=src,
        dst_ref=dst,
        send_sem=send_sem,
        recv_sem=recv_sem,
        device_id=peer,
        device_id_type=MESH,
    )


def turn(block, cos_part, sin_part):
    lower_half, upper_half = block[: HD // 2], block[HD // 2 :]
    return jnp.concatenate(
        [
            lower_half * cos_part - upper_half * sin_part,
            upper_half * cos_part + lower_half * sin_part,
        ],
        axis=0,
    )


def turn_back(block, cos_part, sin_part):
    return turn(block, cos_part, -sin_part)


def by_span(context, b, run):
    near = (context == 0) | (b <= 3)

    @pl.when(near)
    def _():
        run(1408)

    @pl.when(jnp.logical_not(near))
    def _():
        run(1792)


def ring_peers():
    xh, y, core, xl, z = place()
    return (
        z,
        lax.rem(z + 1, 4),
        lax.rem(z + 2, 4),
        lax.rem(z + 3, 4),
        device(xh, y, core, xl, lax.rem(z + 1, 4)),
        device(xh, y, core, xl, lax.rem(z + 3, 4)),
    )


def halves(ref, index):
    rows = ref.shape[1] // 2
    return ref.at[index, pl.ds(0, rows)], ref.at[index, pl.ds(rows, rows)]


def ring_gather_begin(own, held, send_sem, recv_sem):
    z, zp, z2, zm, up, down = ring_peers()
    rows = own.shape[0] // 2
    first, second = own.at[pl.ds(0, rows)], own.at[pl.ds(rows, rows)]
    first_to, second_to = halves(held, z)
    copies = [
        remote(first, first_to, send_sem.at[0], recv_sem.at[0], up),
        remote(second, second_to, send_sem.at[1], recv_sem.at[1], down),
        remote(second, second_to, send_sem.at[2], recv_sem.at[2], up),
        remote(first, first_to, send_sem.at[3], recv_sem.at[3], down),
    ]
    for copy in copies:
        copy.start()
    return copies


def ring_gather_forward(held, copies, send_sem, recv_sem):
    z, zp, z2, zm, up, down = ring_peers()
    copies[0].wait_recv()
    below = halves(held, zm)[0]
    on_up = remote(below, below, send_sem.at[4], recv_sem.at[4], up)
    on_up.start()
    copies[1].wait_recv()
    above = halves(held, zp)[1]
    on_down = remote(above, above, send_sem.at[5], recv_sem.at[5], down)
    on_down.start()
    return copies + [on_up, on_down]


def ring_gather_end(copies):
    for copy in copies:
        copy.wait_send()
    for copy in copies[2:]:
        copy.wait_recv()


def in_rows(count, step, run):
    def body(i, carry):
        run(pl.ds(pl.multiple_of(i * step, step), step))
        return carry

    lax.fori_loop(0, count // step, body, 0)


def ring_scatter_near(parts, came, send_sem, recv_sem):
    z, zp, z2, zm, up, down = ring_peers()
    copies = [
        remote(halves(parts, zp)[0], came.at[2], send_sem.at[2], recv_sem.at[2], up),
        remote(halves(parts, zm)[1], came.at[3], send_sem.at[3], recv_sem.at[3], down),
    ]
    for copy in copies:
        copy.start()
    return copies


def ring_scatter_far(parts, came, send_sem, recv_sem):
    z, zp, z2, zm, up, down = ring_peers()
    copies = [
        remote(halves(parts, z2)[1], came.at[0], send_sem.at[0], recv_sem.at[0], up),
        remote(halves(parts, z2)[0], came.at[1], send_sem.at[1], recv_sem.at[1], down),
    ]
    for copy in copies:
        copy.start()
    return copies


def ring_scatter_begin(parts, came, send_sem, recv_sem):
    far = ring_scatter_far(parts, came, send_sem, recv_sem)
    return far + ring_scatter_near(parts, came, send_sem, recv_sem)


def ring_scatter_forward(parts, came, sums, copies, send_sem, recv_sem):
    z, zp, z2, zm, up, down = ring_peers()
    count = came.shape[1]
    copies[0].wait_recv()

    def add_up(rows):
        sums[0, rows] = (
            came[0, rows].astype(jnp.float32)
            + parts[zp, pl.ds(pl.multiple_of(rows.start + count, 16), 16)].astype(jnp.float32)
        ).astype(jnp.bfloat16)

    in_rows(count, 16, add_up)
    on_up = remote(sums.at[0], came.at[4], send_sem.at[4], recv_sem.at[4], up)
    on_up.start()
    copies[1].wait_recv()

    def add_down(rows):
        sums[1, rows] = (
            came[1, rows].astype(jnp.float32) + parts[zm, rows].astype(jnp.float32)
        ).astype(jnp.bfloat16)

    in_rows(count, 16, add_down)
    on_down = remote(sums.at[1], came.at[5], send_sem.at[5], recv_sem.at[5], down)
    on_down.start()
    return copies + [on_up, on_down]


def ring_scatter_end(parts, came, total, copies):
    z, zp, z2, zm, up, down = ring_peers()
    count = came.shape[1]
    for copy in copies[2:]:
        copy.wait_recv()
    for copy in copies:
        copy.wait_send()

    def add(rows):
        later = pl.ds(pl.multiple_of(rows.start + count, 16), 16)
        total[rows] = (
            parts[z, rows].astype(jnp.float32)
            + came[2, rows].astype(jnp.float32)
            + came[5, rows].astype(jnp.float32)
        )
        total[later] = (
            parts[z, later].astype(jnp.float32)
            + came[3, rows].astype(jnp.float32)
            + came[4, rows].astype(jnp.float32)
        )

    in_rows(count, 16, add)


def plane():
    xh, y, core, xl, z = place()
    ys = [lax.rem(y + d, 4) for d in (1, 3, 2)]
    step = xh * 2 + xl
    xs = [lax.rem(step + d, 4) for d in (1, 3, 2)]
    xs = [(x // 2, lax.rem(x, 2)) for x in xs]
    y_peers = [device(xh, other, core, xl, z) for other in ys]
    x_peers = [device(h, y, core, l, z) for h, l in xs]
    return ys, xs, y_peers, x_peers, device(xh, y, 1 - core, xl, z)


class PlaneGather:
    def __init__(self, own, held, y_first, send_sem, recv_sem):
        self.own, self.held, self.y_first = own, held, y_first
        self.send_sem, self.recv_sem, self.used = send_sem, recv_sem, 0
        self.copies, self.first, self.second, self.third = [], [], [], []

    def send(self, src, dst, peer):
        copy = remote(src, dst, self.send_sem.at[self.used], self.recv_sem.at[self.used], peer)
        self.used += 1
        copy.start()
        self.copies.append(copy)
        return copy

    def begin(self):
        xh, y, core, xl, z = place()
        ys, xs, y_peers, x_peers, other = plane()
        target = self.held.at[xh, y, core, xl]
        peers = y_peers if self.y_first else x_peers
        self.first = [self.send(self.own, target, peer) for peer in peers]

    def line(self, where):
        xh, y, core, xl, z = place()
        if self.y_first:
            return self.held.at[where[0], :, core, where[1]]
        return self.held.at[:, where, core, :]

    def spread(self):
        xh, y, core, xl, z = place()
        ys, xs, y_peers, x_peers, other = plane()
        for copy in self.first:
            copy.wait_recv()
        mine = self.line((xh, xl) if self.y_first else y)
        peers = x_peers if self.y_first else y_peers
        self.second = [self.send(mine, mine, peer) for peer in peers]
        self.third = [self.send(mine, mine, other)]

    def share(self):
        ys, xs, y_peers, x_peers, other = plane()
        wheres = xs if self.y_first else ys
        for copy, where in zip(self.second, (wheres[1], wheres[0], wheres[2])):
            copy.wait_recv()
            line = self.line(where)
            self.third.append(self.send(line, line, other))

    def end(self):
        for copy in self.third:
            copy.wait_recv()
        for copy in self.copies:
            copy.wait_send()


def sum_kernel(own, total, held, send_sem, recv_sem):
    xh, y, core, xl, z = place()
    ys, xs, y_peers, x_peers, other = plane()
    z_peers = [device(xh, y, core, xl, lax.rem(z + d, 4)) for d in (1, 3, 2)]
    greet([other] + z_peers + x_peers + y_peers)
    total[...] = own[...]
    groups = ((z_peers, z, 4), (x_peers, xh * 2 + xl, 4), (y_peers, y, 4), ([other], core, 2))
    for axis, (group, here, count) in enumerate(groups):
        held[axis, here] = total[...]
        copies = [
            remote(
                held.at[axis, here],
                held.at[axis, here],
                send_sem.at[axis * 3 + k],
                recv_sem.at[axis * 3 + k],
                peer,
            )
            for k, peer in enumerate(group)
        ]
        for copy in copies:
            copy.start()
        for copy in copies:
            copy.wait()
        order = held[axis, 0]
        for k in range(1, count):
            order = order + held[axis, k]
        total[...] = order


def sum_everywhere(own, identity):
    return pl.pallas_call(
        sum_kernel,
        out_shape=jax.ShapeDtypeStruct(own.shape, jnp.float32),
        scratch_shapes=[
            pltpu.VMEM((4, 4) + own.shape, jnp.float32),
            pltpu.SemaphoreType.DMA((12,)),
            pltpu.SemaphoreType.DMA((12,)),
        ],
        compiler_params=pltpu.CompilerParams(
            collective_id=identity, has_side_effects=True, vmem_limit_bytes=VMEM_MOST
        ),
    )(own)


def swap_halves(block):
    lane = lax.broadcasted_iota(jnp.int32, block.shape, 1)
    return jnp.where(
        lane < HD // 2, pltpu.roll(block, 128 - HD // 2, 1), pltpu.roll(block, HD // 2, 1)
    )


def front_kernel(*refs):
    (first, shrunk, w_in, w_gate, w_up, w_out, w_shrink) = refs[:7]
    (cos_ref, sin_ref, key_cos, key_sin, limit) = refs[7:12]
    (first_all, shrunk_all, in_all, gate_all, up_all, out_all, shrink_all) = refs[12:19]
    (turned, kv_rows, kv_lines, attended, tokens, log_total, total) = refs[19:26]
    (packed, held_rows, parts, came, sums) = refs[26:31]
    (ring_send, ring_recv, plane_send, plane_recv) = refs[31:35]
    (kv_send, kv_recv, own_sem, out_sem) = refs[35:]
    xh, y, core, xl, z = place()
    z, zp, z2, zm, up, down = ring_peers()
    ys, xs, y_peers, x_peers, other = plane()
    beside = device(xh, y, core, 1 - xl, z)
    greet([up, down, other] + y_peers + x_peers)
    owns = (w_in, w_out, w_gate, w_up, w_shrink)
    helds = (in_all, out_all, gate_all, up_all, shrink_all)
    gathers = [
        PlaneGather(own, held, i in (2, 3), plane_send.at[i], plane_recv.at[i])
        for i, (own, held) in enumerate(zip(owns, helds))
    ]
    for gather in gathers[:2]:
        gather.begin()
    ring = ring_gather_begin(first, first_all, ring_send.at[0], ring_recv.at[0])
    keeps = [
        pltpu.make_async_copy(own, held.at[xh, y, core, xl], own_sem.at[i])
        for i, (own, held) in enumerate(zip(owns, helds))
    ]
    keeps.append(pltpu.make_async_copy(first, first_all.at[z], own_sem.at[5]))
    keeps.append(pltpu.make_async_copy(shrunk, shrunk_all.at[z], own_sem.at[6]))
    for keep in keeps:
        keep.start()
    for keep in keeps:
        keep.wait()
    for gather in gathers[:2]:
        gather.spread()
    ring = ring_gather_forward(first_all, ring, ring_send.at[0], ring_recv.at[0])
    gathers[0].share()
    gathers[1].share()
    gathers[0].end()
    for gather in gathers[2:]:
        gather.begin()

    def project(c, rows):
        out = nn(first_all[c], in_all[...].reshape(1536, 640))
        packed[rows] = out
        for g in range(HEADS):
            block = out[:, g * 320 + 192 : g * 320 + 320]
            mine = pl.ds(pl.multiple_of(xl * 896 + c * 224, 16), 224)
            kv_rows[g, mine] = (
                block * key_cos[rows] + swap_halves(block) * key_sin[rows]
            ).astype(jnp.bfloat16)

    kv_copies = []
    for i, c in enumerate((z, zm, zp, z2)):
        if i == 1:
            ring[2].wait_recv()
        if i == 2:
            ring[3].wait_recv()
        if i == 3:
            ring[4].wait_recv()
            ring[5].wait_recv()
        project(c, pl.ds(pl.multiple_of(c * 224, 16), 224))
        mine = kv_rows.at[:, pl.ds(pl.multiple_of(xl * 896 + c * 224, 16), 224)]
        kv_copies.append(remote(mine, mine, kv_send.at[i], kv_recv.at[i], beside))
        kv_copies[-1].start()
    later = ring_gather_begin(shrunk, shrunk_all, ring_send.at[1], ring_recv.at[1])

    def turn_block(b, carry):
        columns = pl.ds(pl.multiple_of(b * 128, 128), 128)
        lines = jnp.transpose(packed[columns])
        cos_here, sin_here = cos_ref[:, columns], sin_ref[:, columns]
        for g in range(HEADS):
            for h in range(GROUP):
                at = (g * 5 + h) * HD
                turned[(g * GROUP + h) * HD : (g * GROUP + h + 1) * HD, columns] = (
                    turn(lines[at : at + HD], cos_here, sin_here) * HD ** (-0.5)
                ).astype(jnp.bfloat16)
        return carry

    lax.fori_loop(0, BLOCKS, turn_block, 0)
    for copy in kv_copies:
        copy.wait_recv()
    for gather in gathers[2:]:
        gather.spread()
    for g in range(HEADS):
        kv_lines[g] = jnp.transpose(kv_rows[g].astype(jnp.float32)).astype(jnp.bfloat16)

    def block(t, carry):
        b, g = t // HEADS, lax.rem(t, HEADS)
        columns = pl.ds(pl.multiple_of(b * 128, 128), 128)

        def run(span):
            head_rows = [
                pl.ds(pl.multiple_of((g * GROUP + h) * HD, HD), HD) for h in range(GROUP)
            ]
            queries = jnp.concatenate([turned[r, columns] for r in head_rows], axis=1)
            queries = jnp.concatenate([queries, jnp.zeros_like(queries)], axis=0)
            scores = nn(kv_rows[g, :span], queries)
            key_index = lax.broadcasted_iota(jnp.int32, (span, 384), 0)
            scores = jnp.where(key_index < limit[b], scores, NEG)
            row_max = jnp.max(scores, axis=0, keepdims=True)
            shifted = jnp.exp(scores - row_max)
            exp_total = jnp.sum(shifted, axis=0, keepdims=True)
            out = nn(kv_lines[g, HD:, :span], shifted.astype(jnp.bfloat16)) * (1.0 / exp_total)
            for h in range(GROUP):
                attended[head_rows[h], columns] = out[:, h * 128 : (h + 1) * 128].astype(
                    jnp.bfloat16
                )
            log_total[t] = row_max + jnp.log(exp_total)

        by_span(xl, b, run)
        return carry

    lax.fori_loop(0, 6, block, 0)
    later = ring_gather_forward(shrunk_all, later, ring_send.at[1], ring_recv.at[1])
    lax.fori_loop(6, HEADS * BLOCKS, block, 0)
    gathers[1].end()
    fetch = pltpu.make_async_copy(out_all, held_rows, out_sem)
    fetch.start()
    tokens[...] = jnp.transpose(attended[...].astype(jnp.float32)).astype(jnp.bfloat16)
    fetch.wait()
    for c in range(4):
        parts[c] = nt(tokens[c * 224 : (c + 1) * 224], held_rows[...].reshape(1536, 384)).astype(jnp.bfloat16)
    scatter = ring_scatter_begin(parts, came, ring_send.at[2], ring_recv.at[2])
    scatter = ring_scatter_forward(
        parts, came, sums, scatter, ring_send.at[2], ring_recv.at[2]
    )
    for gather in gathers[2:]:
        gather.share()
    for gather in gathers[2:]:
        gather.end()
    ring_gather_end(later)
    for copy in kv_copies + ring:
        copy.wait_send()
    ring_scatter_end(parts, came, total, scatter)


def front(first, shrunk, weights, tables):
    any_place = pl.BlockSpec(memory_space=pl.ANY)
    whole = pl.BlockSpec(memory_space=pltpu.VMEM)
    rows, width = first.shape
    gathered = [
        jax.ShapeDtypeStruct((2, 4, 2, 2) + w.shape, jnp.bfloat16) for w in weights
    ]
    outs = pl.pallas_call(
        front_kernel,
        out_shape=(
            jax.ShapeDtypeStruct((4, rows, width), jnp.bfloat16),
            jax.ShapeDtypeStruct((4, rows, width), jnp.bfloat16),
            *gathered,
            jax.ShapeDtypeStruct((384, 896), jnp.bfloat16),
            jax.ShapeDtypeStruct((HEADS, 1792, 128), jnp.bfloat16),
            jax.ShapeDtypeStruct((HEADS, 128, 1792), jnp.bfloat16),
            jax.ShapeDtypeStruct((384, 896), jnp.bfloat16),
            jax.ShapeDtypeStruct((896, 384), jnp.bfloat16),
            jax.ShapeDtypeStruct((HEADS * BLOCKS, 1, 384), jnp.float32),
            jax.ShapeDtypeStruct((rows, width), jnp.float32),
        ),
        in_specs=[whole] * 12,
        out_specs=(whole, any_place, whole) + (any_place,) * 4 + (whole,) * 7,
        scratch_shapes=[
            pltpu.VMEM((896, 640), jnp.float32),
            pltpu.VMEM((2, 4, 2, 2, 48, 384), jnp.bfloat16),
            pltpu.VMEM((4, rows, width), jnp.bfloat16),
            pltpu.VMEM((6, rows // 2, width), jnp.bfloat16),
            pltpu.VMEM((2, rows // 2, width), jnp.bfloat16),
            pltpu.SemaphoreType.DMA((3, 6)),
            pltpu.SemaphoreType.DMA((3, 6)),
            pltpu.SemaphoreType.DMA((5, 10)),
            pltpu.SemaphoreType.DMA((5, 10)),
            pltpu.SemaphoreType.DMA((4,)),
            pltpu.SemaphoreType.DMA((4,)),
            pltpu.SemaphoreType.DMA((7,)),
            pltpu.SemaphoreType.DMA,
        ],
        compiler_params=pltpu.CompilerParams(
            collective_id=0, has_side_effects=True, vmem_limit_bytes=VMEM_MOST
        ),
    )(first, shrunk, *weights, *tables)
    return (
        outs[0],
        outs[1],
        *(held.reshape(1536, -1) for held in outs[2:7]),
        *outs[7:],
    )


def tn(a, b):
    return lax.dot_general(a, b, (((0,), (0,)), ((), ())), preferred_element_type=jnp.float32)


def middle_kernel(*refs):
    (hidden, cotangent, projected, gain) = refs[:4]
    (shrunk_from, gate_from, up_from, shrink_from) = refs[4:8]
    (residual, grad_residual, turned_back, gain_two) = refs[8:12]
    (grad_gate, grad_up, grad_shrink, out_parts) = refs[12:16]
    (shrunk_all, w_gate, w_up, w_shrink) = refs[16:20]
    (second_all, activated_back, gated, gate_back, up_back) = refs[20:25]
    (parts, came, sums, total) = refs[25:29]
    (ring_send, ring_recv, load_sem) = refs[29:]
    z, zp, z2, zm, up, down = ring_peers()
    greet([up, down])
    loads = [
        pltpu.make_async_copy(src, dst, load_sem.at[i])
        for i, (src, dst) in enumerate(
            (
                (shrink_from, w_shrink),
                (shrunk_from, shrunk_all),
                (gate_from, w_gate),
                (up_from, w_up),
            )
        )
    ]
    for load in loads:
        load.start()
    rows = hidden[...].astype(jnp.float32) + RESID * projected[...]
    residual[...] = rows
    scaling = lax.rsqrt(jnp.mean(rows * rows, axis=-1, keepdims=True) + EPS)
    second_all[z] = (rows * scaling * gain[...]).astype(jnp.bfloat16)
    ring = ring_gather_begin(second_all.at[z], second_all, ring_send.at[0], ring_recv.at[0])
    loads[0].wait()
    loads[1].wait()
    for c in range(4):
        activated_back[c] = nn(shrunk_all[c], w_shrink[...])
    loads[2].wait()
    loads[3].wait()

    def feed(c):
        gate_value = nn(second_all[c], w_gate[...])
        up_value = nn(second_all[c], w_up[...])
        sigmoid_gate = 1.0 / (1.0 + jnp.exp(-gate_value))
        gate_active = gate_value * sigmoid_gate
        gated[c] = (gate_active * up_value).astype(jnp.bfloat16)
        gradient = activated_back[c]
        gate_back[c] = (
            gradient * up_value * sigmoid_gate * (1.0 + gate_value * (1.0 - sigmoid_gate))
        ).astype(jnp.bfloat16)
        up_back[c] = (gradient * gate_active).astype(jnp.bfloat16)
        parts[c] = (nt(gate_back[c], w_gate[...]) + nt(up_back[c], w_up[...])).astype(
            jnp.bfloat16
        )

    feed(z)
    ring = ring_gather_forward(second_all, ring, ring_send.at[0], ring_recv.at[0])
    ring[2].wait_recv()
    feed(zm)
    ring[3].wait_recv()
    feed(zp)
    near = ring_scatter_near(parts, came, ring_send.at[1], ring_recv.at[1])
    ring[4].wait_recv()
    ring[5].wait_recv()
    feed(z2)
    far = ring_scatter_far(parts, came, ring_send.at[1], ring_recv.at[1])
    second_rows = second_all[...].reshape(896, 1536)
    grad_gate[...] = tn(second_rows, gate_back[...].reshape(896, 960)).astype(jnp.bfloat16)
    scatter = ring_scatter_forward(
        parts, came, sums, far + near, ring_send.at[1], ring_recv.at[1]
    )
    grad_up[...] = tn(second_rows, up_back[...].reshape(896, 960)).astype(jnp.bfloat16)
    grad_shrink[...] = tn(
        shrunk_all[...].reshape(896, 1536), gated[...].reshape(896, 960)
    ).astype(jnp.bfloat16)
    for c in range(4):
        out_parts[c] = nt(gated[c], w_shrink[...]).astype(jnp.bfloat16)
    for copy in ring:
        copy.wait_send()
    ring_scatter_end(parts, came, total, scatter)
    rows = residual[...]
    scaling = lax.rsqrt(jnp.mean(rows * rows, axis=-1, keepdims=True) + EPS)
    normed = rows * scaling
    gradient = total[...]
    gain_two[...] = jnp.sum(gradient * normed, axis=0, keepdims=True)
    gradient = gradient * gain[...]
    back = cotangent[...].astype(jnp.float32) + scaling * (
        gradient - normed * jnp.mean(gradient * normed, axis=-1, keepdims=True)
    )
    grad_residual[...] = back
    turned_back[...] = (RESID * back).astype(jnp.bfloat16)


def middle(hidden, cotangent, projected, gain, shrunk_all, w_gate, w_up, w_shrink):
    any_place = pl.BlockSpec(memory_space=pl.ANY)
    whole = pl.BlockSpec(memory_space=pltpu.VMEM)
    rows, width = hidden.shape
    low, full = jnp.bfloat16, jnp.float32
    return pl.pallas_call(
        middle_kernel,
        out_shape=(
            jax.ShapeDtypeStruct((rows, width), full),
            jax.ShapeDtypeStruct((rows, width), full),
            jax.ShapeDtypeStruct((rows, width), low),
            jax.ShapeDtypeStruct((1, width), full),
            jax.ShapeDtypeStruct((1536, 960), low),
            jax.ShapeDtypeStruct((1536, 960), low),
            jax.ShapeDtypeStruct((1536, 960), low),
            jax.ShapeDtypeStruct((4, rows, width), low),
        ),
        in_specs=[whole] * 4 + [any_place] * 4,
        out_specs=(whole,) * 8,
        scratch_shapes=[
            pltpu.VMEM((4, rows, width), low),
            pltpu.VMEM((1536, 960), low),
            pltpu.VMEM((1536, 960), low),
            pltpu.VMEM((1536, 960), low),
            pltpu.VMEM((4, rows, width), low),
            pltpu.VMEM((4, rows, 960), full),
            pltpu.VMEM((4, rows, 960), low),
            pltpu.VMEM((4, rows, 960), low),
            pltpu.VMEM((4, rows, 960), low),
            pltpu.VMEM((4, rows, width), low),
            pltpu.VMEM((6, rows // 2, width), low),
            pltpu.VMEM((2, rows // 2, width), low),
            pltpu.VMEM((rows, width), full),
            pltpu.SemaphoreType.DMA((2, 6)),
            pltpu.SemaphoreType.DMA((2, 6)),
            pltpu.SemaphoreType.DMA((4,)),
        ],
        compiler_params=pltpu.CompilerParams(
            collective_id=4, has_side_effects=True, vmem_limit_bytes=VMEM_MOST
        ),
    )(hidden, cotangent, projected, gain, shrunk_all, w_gate, w_up, w_shrink)


class Scatter:
    def __init__(self, parts, came, across, lined, last, x_first, send_sem, recv_sem):
        self.parts, self.came, self.across = parts, came, across
        self.lined, self.last, self.x_first = lined, last, x_first
        self.send_sem, self.recv_sem, self.used, self.copies = send_sem, recv_sem, 0, []
        xh, y, core, xl, z = place()
        ys, xs, y_peers, x_peers, self.other = plane()
        if x_first:
            self.lines, self.peers = xs[::-1] + [(xh, xl)], x_peers[::-1]
            self.mine, self.targets, self.target_peers = y, ys, y_peers
        else:
            self.lines, self.peers = ys[::-1] + [y], y_peers[::-1]
            self.mine, self.targets, self.target_peers = (xh, xl), xs, x_peers

    def send(self, src, dst, peer):
        copy = remote(src, dst, self.send_sem.at[self.used], self.recv_sem.at[self.used], peer)
        self.used += 1
        copy.start()
        self.copies.append(copy)
        return copy

    def in_line(self, line):
        return (line[0], slice(None), line[1]) if self.x_first else (slice(None), line)

    def begin(self):
        core = place()[2]
        self.first = []
        for line in self.lines:
            if self.x_first:
                src = self.parts.at[line[0], :, 1 - core, line[1]]
            else:
                src = self.parts.at[:, line, 1 - core]
            self.first.append(self.send(src, self.came.at[self.in_line(line)], self.other))

    def stage(self, held, sem):
        copy = pltpu.make_async_copy(self.parts.at[:, :, place()[2]], held, sem)
        copy.start()
        return copy

    def at(self, line, i):
        return (line[0], i, line[1]) if self.x_first else (i // 2, line, lax.rem(i, 2))

    def spot(self, i):
        if self.x_first:
            return (i,)
        return (i[0], i[1]) if isinstance(i, tuple) else (i // 2, lax.rem(i, 2))

    def fold(self, held=None):
        core = place()[2]
        self.second = []
        for k, (line, copy) in enumerate(zip(self.lines, self.first)):
            copy.wait_recv()

            def add(i, carry, line=line):
                at = self.at(line, i)
                if held is None:
                    own = self.parts[at[0], at[1], core, at[2]]
                else:
                    own = held[at]
                self.came[at] = (
                    own.astype(jnp.float32) + self.came[at].astype(jnp.float32)
                ).astype(jnp.bfloat16)
                return carry

            lax.fori_loop(0, 4, add, 0)
            if k < 3:
                self.second.append(
                    self.send(
                        self.came.at[self.in_line(line)], self.across.at[k], self.peers[k]
                    )
                )

    def line(self):
        for copy in self.second:
            copy.wait_recv()

        def add(i, carry):
            spot = self.spot(i)
            total = self.came[self.at(self.lines[3], i)].astype(jnp.float32)
            for k in range(3):
                total = total + self.across[(k,) + spot].astype(jnp.float32)
            self.lined[spot] = total.astype(jnp.bfloat16)
            return carry

        lax.fori_loop(0, 4, add, 0)
        self.third = [
            self.send(self.lined.at[self.spot(target)], self.last.at[k], peer)
            for k, (target, peer) in enumerate(zip(self.targets, self.target_peers))
        ]

    def end(self, total_ref):
        for copy in self.third:
            copy.wait_recv()
        total = self.lined[self.spot(self.mine)].astype(jnp.float32)
        for k in range(3):
            total = total + self.last[k].astype(jnp.float32)
        total_ref[...] = total
        for copy in self.copies:
            copy.wait_send()


def scatter_room(width, x_first):
    line = (4,) if x_first else (2, 2)
    return [
        pltpu.VMEM((2, 4, 2, 48, width), jnp.bfloat16),
        pltpu.VMEM((3,) + line + (48, width), jnp.bfloat16),
        pltpu.VMEM(line + (48, width), jnp.bfloat16),
        pltpu.VMEM((3, 48, width), jnp.bfloat16),
    ]


def back_kernel(*refs):
    (own, out_from, in_from, first_from, out_terms) = refs[:5]
    gradients = refs[5:8]
    (turned, kv_rows, kv_lines, attended, tokens, log_total) = refs[8:14]
    (cos_ref, sin_ref, key_cos, key_sin, limit) = refs[14:19]
    (shrunk_total, first_total) = refs[19:21]
    totals = refs[21:26]
    (proj_all, w_out, w_in, grad_tokens, grad_lines, grad_queries, grad_packed) = refs[26:33]
    (sums, outgoing, incoming, parts, came_one, came_two, ring_sums) = refs[33:40]
    stages, out_parts, in_parts = refs[40:42], refs[42], refs[43]
    rooms = refs[44:64]
    (ring_send, ring_recv, plane_send, plane_recv, kv_send, kv_recv, load_sem) = refs[64:]
    xh, y, core, xl, z = place()
    z, zp, z2, zm, up, down = ring_peers()
    ys, xs, y_peers, x_peers, other = plane()
    beside = device(xh, y, core, 1 - xl, z)
    greet([up, down, other] + y_peers + x_peers)
    ring = ring_gather_begin(own, proj_all, ring_send.at[0], ring_recv.at[0])
    every = [
        Scatter(
            terms,
            *rooms[4 * i : 4 * i + 4],
            SCATTER_TURNS[i],
            plane_send.at[i],
            plane_recv.at[i],
        )
        for i, terms in enumerate(tuple(gradients) + (out_parts, in_parts))
    ]
    feed, out_scatter, in_scatter = every[:3], every[3], every[4]
    for scatter in feed:
        scatter.begin()

    def load(src, dst, i):
        copy = pltpu.make_async_copy(src, dst, load_sem.at[i])
        copy.start()
        return copy

    load_out = load(out_from, w_out, 0)
    keep = load(own, proj_all.at[z], 1)
    staged = [feed[i].stage(stages[i], load_sem.at[2 + i]) for i in range(2)]
    load_terms = load(out_terms, parts, 5)
    load_in = load(in_from, w_in, 6)
    sums[...] = jnp.zeros_like(sums)

    def give(c):
        rows = pl.ds(pl.multiple_of(c * 224, 16), 224)
        grad_tokens[rows] = nn(proj_all[c], w_out[...]).astype(jnp.bfloat16)

    def which(i):
        shifted = i - 3 + (3 - z) // 3
        return lax.rem(2 * z + shifted + (shifted + 7) // 7 + 7, 7)

    def lay(b):
        columns = pl.ds(pl.multiple_of(b * 128, 128), 128)
        grad_lines[:, columns] = jnp.transpose(
            grad_tokens[columns].astype(jnp.float32)
        ).astype(jnp.bfloat16)

    def block(b, g):
        columns = pl.ds(pl.multiple_of(b * 128, 128), 128)

        def run(span):
            head_rows = [
                pl.ds(pl.multiple_of((g * GROUP + h) * HD, HD), HD) for h in range(GROUP)
            ]
            queries = jnp.concatenate([turned[r, columns] for r in head_rows], axis=1)
            gradient = jnp.concatenate([grad_lines[r, columns] for r in head_rows], axis=1)
            held = jnp.concatenate([attended[r, columns] for r in head_rows], axis=1)
            inner = jnp.sum(
                gradient.astype(jnp.float32) * held.astype(jnp.float32), axis=0, keepdims=True
            )
            nothing = jnp.zeros_like(queries)
            both = jnp.concatenate(
                [
                    jnp.concatenate([queries, nothing], axis=1),
                    jnp.concatenate([nothing, gradient], axis=1),
                ],
                axis=0,
            )
            products = nn(kv_rows[g, :span], both)
            key_index = lax.broadcasted_iota(jnp.int32, (span, 384), 0)
            probs = jnp.exp(
                jnp.where(key_index < limit[b], products[:, :384], NEG)
                - log_total[b * HEADS + g]
            )
            grad_scores = (probs * (products[:, 384:] - inner)).astype(jnp.bfloat16)
            sums[g, :span] += nt(
                jnp.concatenate([grad_scores, probs.astype(jnp.bfloat16)], axis=1), both
            )
            total = nn(kv_lines[g, :HD, :span], grad_scores) * HD ** (-0.5)
            cos_here, sin_here = cos_ref[:, columns], sin_ref[:, columns]
            back = [
                turn_back(total[:, h * 128 : (h + 1) * 128], cos_here, sin_here)
                for h in range(GROUP)
            ]
            grad_queries[g, columns] = jnp.transpose(jnp.concatenate(back, axis=0)).astype(
                jnp.bfloat16
            )

        by_span(xl, b, run)

    def both_heads(t, carry):
        block(which(lax.div(t, 2)), lax.rem(t, 2))
        return carry

    keep.wait()
    load_out.wait()
    give(z)
    lay(2 * z)

    def own_block(g, carry):
        block(2 * z, g)
        return carry

    lax.fori_loop(0, 2, own_block, 0)
    ring = ring_gather_forward(proj_all, ring, ring_send.at[0], ring_recv.at[0])
    staged[0].wait()
    feed[0].fold(stages[0])
    staged[0] = feed[2].stage(stages[0], load_sem.at[4])
    staged[1].wait()
    feed[1].fold(stages[1])
    staged[0].wait()
    feed[2].fold(stages[0])
    ring[2].wait_recv()
    give(zm)
    ring[3].wait_recv()
    give(zp)
    for i in range(1, 4):
        lay(which(i))
    lax.fori_loop(2, 8, both_heads, 0)
    ring[4].wait_recv()
    ring[5].wait_recv()
    give(z2)
    for i in range(4, 7):
        lay(which(i))
    for copy in ring:
        copy.wait_send()
    out_parts[...] = (
        tn(proj_all[...].reshape(896, 1536), tokens[...])
        .astype(jnp.bfloat16)
        .reshape(2, 4, 2, 2, 48, 384)
    )
    out_scatter.begin()
    load_first = load(first_from, proj_all, 7)
    load_terms.wait()
    shrunk = ring_scatter_begin(parts, came_one, ring_send.at[1], ring_recv.at[1])

    def exchange(g):
        theirs = sums[g, pl.ds(pl.multiple_of((1 - xl) * 896, 128), 896)]
        outgoing[g] = theirs.astype(jnp.bfloat16)
        copy = remote(outgoing.at[g], incoming.at[g], kv_send.at[g], kv_recv.at[g], beside)
        copy.start()
        return copy

    def far_block(g):
        def body(i, carry):
            block(which(i), g)
            return carry

        lax.fori_loop(4, 7, body, 0)

    far_block(0)
    kv_copies = [exchange(0)]
    shrunk = ring_scatter_forward(
        parts, came_one, ring_sums, shrunk, ring_send.at[1], ring_recv.at[1]
    )
    out_scatter.fold()
    far_block(1)
    kv_copies.append(exchange(1))
    for scatter in feed:
        scatter.line()
    out_scatter.line()
    load_in.wait()
    load_first.wait()
    ring_scatter_end(parts, came_one, shrunk_total, shrunk)
    for g in range(HEADS):
        kv_copies[g].wait()
        mine = sums[g, pl.ds(pl.multiple_of(xl * 896, 128), 896)] + incoming[g].astype(
            jnp.float32
        )
        mine = mine * key_cos[...] - swap_halves(mine) * key_sin[...]
        grad_packed[:, g * 320 : g * 320 + 192] = grad_queries[g]
        grad_packed[:, g * 320 + 192 : g * 320 + 320] = mine.astype(jnp.bfloat16)

    def spread(c):
        rows = pl.ds(pl.multiple_of(c * 224, 16), 224)
        parts[c] = nt(grad_packed[rows], w_in[...]).astype(jnp.bfloat16)

    spread(z2)
    far = ring_scatter_far(parts, came_two, ring_send.at[2], ring_recv.at[2])
    spread(zp)
    spread(zm)
    near = ring_scatter_near(parts, came_two, ring_send.at[2], ring_recv.at[2])
    in_parts[...] = (
        tn(proj_all[...].reshape(896, 1536), grad_packed[...])
        .astype(jnp.bfloat16)
        .reshape(2, 4, 2, 2, 48, 640)
    )
    in_scatter.begin()
    spread(z)
    in_scatter.fold()
    ring = ring_scatter_forward(
        parts, came_two, ring_sums, far + near, ring_send.at[2], ring_recv.at[2]
    )
    for i in range(4):
        every[i].end(totals[i])
    in_scatter.line()
    ring_scatter_end(parts, came_two, first_total, ring)
    in_scatter.end(totals[4])


SCATTER_TURNS = (True, True, False, False, False)


def back(own, w_out, w_in, first_all, out_terms, gradients, saved, tables):
    any_place = pl.BlockSpec(memory_space=pl.ANY)
    whole = pl.BlockSpec(memory_space=pltpu.VMEM)
    rows, width = own.shape
    low, full = jnp.bfloat16, jnp.float32
    widths = [g.shape[-1] for g in gradients] + [384, 640]
    rooms = []
    for w, turn_first in zip(widths, SCATTER_TURNS):
        rooms += scatter_room(w, turn_first)
    return pl.pallas_call(
        back_kernel,
        out_shape=(jax.ShapeDtypeStruct((rows, width), full),) * 2
        + tuple(jax.ShapeDtypeStruct((48, w), full) for w in widths),
        in_specs=[whole] + [any_place] * 7 + [whole] * 11,
        out_specs=(whole,) * 7,
        scratch_shapes=[
            pltpu.VMEM((4, rows, width), low),
            pltpu.VMEM((1536, 384), low),
            pltpu.VMEM((1536, 640), low),
            pltpu.VMEM((896, 384), low),
            pltpu.VMEM((384, 896), low),
            pltpu.VMEM((HEADS, 896, 192), low),
            pltpu.VMEM((896, 640), low),
            pltpu.VMEM((HEADS, 1792, 128), full),
            pltpu.VMEM((HEADS, 896, 128), low),
            pltpu.VMEM((HEADS, 896, 128), low),
            pltpu.VMEM((4, rows, width), low),
            pltpu.VMEM((6, rows // 2, width), low),
            pltpu.VMEM((6, rows // 2, width), low),
            pltpu.VMEM((2, rows // 2, width), low),
            pltpu.VMEM((2, 4, 2, 48, 960), low),
            pltpu.VMEM((2, 4, 2, 48, 960), low),
            pltpu.VMEM((2, 4, 2, 2, 48, 384), low),
            pltpu.VMEM((2, 4, 2, 2, 48, 640), low),
            *rooms,
            pltpu.SemaphoreType.DMA((3, 6)),
            pltpu.SemaphoreType.DMA((3, 6)),
            pltpu.SemaphoreType.DMA((5, 10)),
            pltpu.SemaphoreType.DMA((5, 10)),
            pltpu.SemaphoreType.DMA((2,)),
            pltpu.SemaphoreType.DMA((2,)),
            pltpu.SemaphoreType.DMA((8,)),
        ],
        compiler_params=pltpu.CompilerParams(
            collective_id=2, has_side_effects=True, vmem_limit_bytes=BACK_VMEM
        ),
    )(
        own,
        w_out,
        w_in,
        first_all,
        out_terms,
        *(g.reshape(2, 4, 2, 2, 48, g.shape[-1]) for g in gradients),
        *saved,
        *tables,
    )


BACK_VMEM = 63 * 2**20


def product(a, b, a_dim, b_dim):
    return lax.dot_general(
        a, b, (((a_dim,), (b_dim,)), ((), ())), preferred_element_type=jnp.float32
    )


def shards(
    hidden_in,
    cotangent,
    prefix,
    positions,
    norm_gains,
    gains_first,
    gains_second,
    input_weight,
    input_first,
    input_second,
    output_weight,
    output_first,
    output_second,
    expand_weight,
    expand_first,
    expand_second,
    shrink_weight,
    shrink_first,
    shrink_second,
):
    low = jnp.bfloat16
    x_rows = hidden_in[0].astype(jnp.float32)
    normed_one, scale_one = rms_parts(x_rows)
    first_own = (normed_one * norm_gains[0]).astype(low)
    shrunk_own = (RESID * cotangent[0].astype(jnp.float32)).astype(low)
    cos_part, sin_part = angles(positions[0])
    row_index = lax.axis_index("context") * 896 + jnp.arange(896, dtype=jnp.int32)
    limit = jnp.maximum(row_index + 1, prefix[0]).reshape(BLOCKS, 1, 128)
    limit = jnp.concatenate([limit] * GROUP, axis=2)
    still = jnp.ones((896, HD), jnp.float32)
    key_cos = jnp.concatenate([cos_part.T, cos_part.T, still], axis=1)
    key_sin = jnp.concatenate([-sin_part.T, sin_part.T, 0.0 * still], axis=1)
    tables = (cos_part, sin_part, key_cos, key_sin, limit)
    (
        first_all,
        shrunk_all,
        w_in,
        w_gate,
        w_up,
        w_out,
        w_shrink,
        turned,
        kv_rows,
        kv_lines,
        attended,
        tokens,
        log_total,
        projected,
    ) = front(
        first_own,
        shrunk_own,
        (
            input_weight.astype(low),
            expand_weight[0].astype(low),
            expand_weight[1].astype(low),
            output_weight.T.astype(low),
            shrink_weight.T.astype(low),
        ),
        tables,
    )
    (
        residual,
        grad_residual,
        projected_gradient,
        gain_two,
        grad_gate,
        grad_up,
        grad_shrink,
        out_parts,
    ) = middle(
        hidden_in[0],
        cotangent[0],
        projected,
        norm_gains[1:],
        shrunk_all,
        w_gate,
        w_up,
        w_shrink,
    )
    shrunk, grad_first, grad_gate, grad_up, grad_shrink, grad_output, grad_input = back(
        projected_gradient,
        w_out,
        w_in,
        first_all,
        out_parts,
        (grad_gate, grad_up, grad_shrink),
        (turned, kv_rows, kv_lines, attended, tokens, log_total),
        tables,
    )
    gain_one = jnp.sum(grad_first * normed_one, axis=0)
    input_gradient = grad_residual + rms_back(grad_first * norm_gains[0], normed_one, scale_one)
    block_output = (residual + RESID * shrunk).astype(low)
    grad_expand = jnp.stack([grad_gate, grad_up])
    grad_output, grad_shrink = grad_output.T, grad_shrink.T
    reduced = (grad_input, grad_output, grad_expand, grad_shrink)
    local_squares = sum(jnp.sum(g * g) for g in reduced)
    gains_local = jnp.stack([gain_one, gain_two[0]]).reshape(24, 128)
    message = jnp.concatenate([gains_local, jnp.full((8, 128), local_squares)], axis=0)
    message = sum_everywhere(message, 10)
    grad_gains = message[:24].reshape(2, 1536)
    squares = message[24, 0] + jnp.sum(grad_gains * grad_gains)
    gradient_norm = jnp.sqrt(squares)
    factor = jnp.minimum(1.0, MAX_NORM / (gradient_norm + 1e-06))
    gains_new = adamw(norm_gains, factor * grad_gains, gains_first, gains_second, GAIN_RATE, 0.0)
    input_new = adamw(input_weight, factor * reduced[0], input_first, input_second, RATE, DECAY)
    output_new = adamw(output_weight, factor * reduced[1], output_first, output_second, RATE, DECAY)
    expand_new = adamw(expand_weight, factor * reduced[2], expand_first, expand_second, RATE, DECAY)
    shrink_new = adamw(shrink_weight, factor * reduced[3], shrink_first, shrink_second, RATE, DECAY)
    return (
        block_output[None],
        input_gradient[None],
        gradient_norm,
        *gains_new,
        *input_new,
        *output_new,
        *expand_new,
        *shrink_new,
    )


def solution(mesh):
    return jax.shard_map(
        shards,
        mesh=mesh,
        in_specs=(
            P("shard", ("context", "tensor"), None),
            P("shard", ("context", "tensor"), None),
            P("shard"),
            P("shard", "context"),
            P(),
            P(),
            P(),
            P(("shard", "context"), "tensor"),
            P(("shard", "context"), "tensor"),
            P(("shard", "context"), "tensor"),
            P("tensor", ("shard", "context")),
            P("tensor", ("shard", "context")),
            P("tensor", ("shard", "context")),
            P(None, ("shard", "context"), "tensor"),
            P(None, ("shard", "context"), "tensor"),
            P(None, ("shard", "context"), "tensor"),
            P("tensor", ("shard", "context")),
            P("tensor", ("shard", "context")),
            P("tensor", ("shard", "context")),
        ),
        out_specs=(
            P("shard", ("context", "tensor"), None),
            P("shard", ("context", "tensor"), None),
            P(),
            P(),
            P(),
            P(),
            P(("shard", "context"), "tensor"),
            P(("shard", "context"), "tensor"),
            P(("shard", "context"), "tensor"),
            P("tensor", ("shard", "context")),
            P("tensor", ("shard", "context")),
            P("tensor", ("shard", "context")),
            P(None, ("shard", "context"), "tensor"),
            P(None, ("shard", "context"), "tensor"),
            P(None, ("shard", "context"), "tensor"),
            P("tensor", ("shard", "context")),
            P("tensor", ("shard", "context")),
            P("tensor", ("shard", "context")),
        ),
        check_vma=False,
    )
```

```python
import functools
import math

import jax
import jax.numpy as jnp
from jax import lax
from jax.experimental import pallas as pl
from jax.experimental.pallas import tpu as pltpu
from jax.sharding import PartitionSpec as P

HD = 64
GROUP = 3
STEP = 10
HEADS = 2
BLOCKS = 7
VMEM_MOST = 60 * 2**20
MESH = pl.DeviceIdType.MESH


EPS = 1e-05
RESID = 1.4 / math.sqrt(52.0)
ROPE_BASE = 10000.0
MAX_NORM = 1.0
RATE = 0.1
GAIN_RATE = 1.0
BETA_ONE = 0.9
BETA_TWO = 0.95
ADAM_EPS = 1e-08
DECAY = 0.1
NEG = -1e30


def angles(places):
    half_width = HD // 2
    frequency = ROPE_BASE ** (-2.0 * jnp.arange(half_width, dtype=jnp.float32) / HD)
    phase_turn = places.astype(jnp.float32)[None, :] * frequency[:, None]
    return (jnp.cos(phase_turn), jnp.sin(phase_turn))


def adamw(weight, gradient, momentum, variance, step_rate, decay_rate):
    momentum_new = BETA_ONE * momentum + (1.0 - BETA_ONE) * gradient
    variance_new = BETA_TWO * variance + (1.0 - BETA_TWO) * gradient * gradient
    momentum_hat = momentum_new / (1.0 - BETA_ONE**STEP)
    variance_hat = variance_new / (1.0 - BETA_TWO**STEP)
    updated = weight - step_rate * (
        momentum_hat / (jnp.sqrt(variance_hat) + ADAM_EPS) + decay_rate * weight
    )
    return (momentum_new, variance_new, updated)


def nn(a, b):
    return lax.dot_general(a, b, (((1,), (0,)), ((), ())), preferred_element_type=jnp.float32)


def nt(a, b):
    return lax.dot_general(a, b, (((1,), (1,)), ((), ())), preferred_element_type=jnp.float32)


def place():
    shard = lax.axis_index("shard")
    return (
        shard // 8,
        lax.rem(shard // 2, 4),
        lax.rem(shard, 2),
        lax.axis_index("context"),
        lax.axis_index("tensor"),
    )


def device(xh, y, core, xl, z):
    return {"shard": (xh * 4 + y) * 2 + core, "context": xl, "tensor": z}


def hail(peers):
    barrier = pltpu.get_barrier_semaphore()
    for peer in peers:
        pl.semaphore_signal(barrier, inc=1, device_id=peer, device_id_type=MESH)


def meet(peers):
    pl.semaphore_wait(pltpu.get_barrier_semaphore(), len(peers))


def remote(src, dst, send_sem, recv_sem, peer):
    return pltpu.make_async_remote_copy(
        src_ref=src,
        dst_ref=dst,
        send_sem=send_sem,
        recv_sem=recv_sem,
        device_id=peer,
        device_id_type=MESH,
    )


def turn(block, cos_part, sin_part):
    lower_half, upper_half = block[: HD // 2], block[HD // 2 :]
    return jnp.concatenate(
        [
            lower_half * cos_part - upper_half * sin_part,
            upper_half * cos_part + lower_half * sin_part,
        ],
        axis=0,
    )


def turn_back(block, cos_part, sin_part):
    return turn(block, cos_part, -sin_part)


def by_span(context, b, run):
    near = (context == 0) | (b <= 3)

    @pl.when(near)
    def _():
        run(1408)

    @pl.when(jnp.logical_not(near))
    def _():
        run(1792)


def limits(prefix, xl, b):
    lane = lax.broadcasted_iota(jnp.int32, (1, GROUP * 128), 1)
    row = xl * 896 + b * 128 + lax.rem(lane, 128)
    return jnp.maximum(row + 1, prefix[0])


def key_tables(cos_ref, sin_ref, key_cos, key_sin):
    cos_part, sin_part = jnp.transpose(cos_ref[...]), jnp.transpose(sin_ref[...])
    still = jnp.ones((896, HD), jnp.float32)
    key_cos[...] = jnp.concatenate([cos_part, cos_part, still], axis=1)
    key_sin[...] = jnp.concatenate([-sin_part, sin_part, 0.0 * still], axis=1)


def arrival(z, i):
    shifted = i - 3 + (3 - z) // 3
    return lax.rem(2 * z + shifted + (shifted + 7) // 7 + 7, 7)


def ring_peers():
    xh, y, core, xl, z = place()
    return (
        z,
        lax.rem(z + 1, 4),
        lax.rem(z + 2, 4),
        lax.rem(z + 3, 4),
        device(xh, y, core, xl, lax.rem(z + 1, 4)),
        device(xh, y, core, xl, lax.rem(z + 3, 4)),
    )


def halves(ref, index):
    rows = ref.shape[1] // 2
    return ref.at[index, pl.ds(0, rows)], ref.at[index, pl.ds(rows, rows)]


def ring_gather_begin(own, held, send_sem, recv_sem):
    z, zp, z2, zm, up, down = ring_peers()
    rows = own.shape[0] // 2
    first, second = own.at[pl.ds(0, rows)], own.at[pl.ds(rows, rows)]
    first_to, second_to = halves(held, z)
    copies = [
        remote(first, first_to, send_sem.at[0], recv_sem.at[0], up),
        remote(second, second_to, send_sem.at[1], recv_sem.at[1], down),
        remote(second, second_to, send_sem.at[2], recv_sem.at[2], up),
        remote(first, first_to, send_sem.at[3], recv_sem.at[3], down),
    ]
    for copy in copies:
        copy.start()
    return copies


def ring_gather_forward(held, copies, send_sem, recv_sem):
    z, zp, z2, zm, up, down = ring_peers()
    copies[0].wait_recv()
    below = halves(held, zm)[0]
    on_up = remote(below, below, send_sem.at[4], recv_sem.at[4], up)
    on_up.start()
    copies[1].wait_recv()
    above = halves(held, zp)[1]
    on_down = remote(above, above, send_sem.at[5], recv_sem.at[5], down)
    on_down.start()
    return copies + [on_up, on_down]


def ring_gather_end(copies):
    for copy in copies:
        copy.wait_send()
    for copy in copies[2:]:
        copy.wait_recv()


def in_rows(count, step, run):
    def body(i, carry):
        run(pl.ds(pl.multiple_of(i * step, step), step))
        return carry

    lax.fori_loop(0, count // step, body, 0)


def ring_scatter_near(parts, came, send_sem, recv_sem):
    z, zp, z2, zm, up, down = ring_peers()
    copies = [
        remote(halves(parts, zp)[0], came.at[2], send_sem.at[2], recv_sem.at[2], up),
        remote(halves(parts, zm)[1], came.at[3], send_sem.at[3], recv_sem.at[3], down),
    ]
    for copy in copies:
        copy.start()
    return copies


def ring_scatter_far(parts, came, send_sem, recv_sem):
    z, zp, z2, zm, up, down = ring_peers()
    copies = [
        remote(halves(parts, z2)[1], came.at[0], send_sem.at[0], recv_sem.at[0], up),
        remote(halves(parts, z2)[0], came.at[1], send_sem.at[1], recv_sem.at[1], down),
    ]
    for copy in copies:
        copy.start()
    return copies


def ring_scatter_begin(parts, came, send_sem, recv_sem):
    far = ring_scatter_far(parts, came, send_sem, recv_sem)
    return far + ring_scatter_near(parts, came, send_sem, recv_sem)


def ring_scatter_forward(parts, came, sums, copies, send_sem, recv_sem):
    z, zp, z2, zm, up, down = ring_peers()
    count = came.shape[1]
    copies[0].wait_recv()

    def add_up(rows):
        sums[0, rows] = (
            came[0, rows].astype(jnp.float32)
            + parts[zp, pl.ds(pl.multiple_of(rows.start + count, 16), 16)].astype(jnp.float32)
        ).astype(jnp.bfloat16)

    in_rows(count, 16, add_up)
    on_up = remote(sums.at[0], came.at[4], send_sem.at[4], recv_sem.at[4], up)
    on_up.start()
    copies[1].wait_recv()

    def add_down(rows):
        sums[1, rows] = (
            came[1, rows].astype(jnp.float32) + parts[zm, rows].astype(jnp.float32)
        ).astype(jnp.bfloat16)

    in_rows(count, 16, add_down)
    on_down = remote(sums.at[1], came.at[5], send_sem.at[5], recv_sem.at[5], down)
    on_down.start()
    return copies + [on_up, on_down]


def ring_scatter_end(parts, came, total, copies):
    z, zp, z2, zm, up, down = ring_peers()
    count = came.shape[1]
    for copy in copies[2:]:
        copy.wait_recv()
    for copy in copies:
        copy.wait_send()

    def add(rows):
        later = pl.ds(pl.multiple_of(rows.start + count, 16), 16)
        total[rows] = (
            parts[z, rows].astype(jnp.float32)
            + came[2, rows].astype(jnp.float32)
            + came[5, rows].astype(jnp.float32)
        )
        total[later] = (
            parts[z, later].astype(jnp.float32)
            + came[3, rows].astype(jnp.float32)
            + came[4, rows].astype(jnp.float32)
        )

    in_rows(count, 16, add)


def plane():
    xh, y, core, xl, z = place()
    ys = [lax.rem(y + d, 4) for d in (1, 3, 2)]
    step = xh * 2 + xl
    xs = [lax.rem(step + d, 4) for d in (1, 3, 2)]
    xs = [(x // 2, lax.rem(x, 2)) for x in xs]
    y_peers = [device(xh, other, core, xl, z) for other in ys]
    x_peers = [device(h, y, core, l, z) for h, l in xs]
    return ys, xs, y_peers, x_peers, device(xh, y, 1 - core, xl, z)


class PlaneGather:
    def __init__(self, own, held, y_first, send_sem, recv_sem):
        self.own, self.held, self.y_first = own, held, y_first
        self.send_sem, self.recv_sem, self.used = send_sem, recv_sem, 0
        self.copies, self.first, self.second, self.third = [], [], [], []

    def send(self, src, dst, peer):
        copy = remote(src, dst, self.send_sem.at[self.used], self.recv_sem.at[self.used], peer)
        self.used += 1
        copy.start()
        self.copies.append(copy)
        return copy

    def begin(self):
        xh, y, core, xl, z = place()
        ys, xs, y_peers, x_peers, other = plane()
        target = self.held.at[xh, y, core, xl]
        peers = y_peers if self.y_first else x_peers
        self.first = [self.send(self.own, target, peer) for peer in peers]

    def line(self, where):
        xh, y, core, xl, z = place()
        if self.y_first:
            return self.held.at[where[0], :, core, where[1]]
        return self.held.at[:, where, core, :]

    def spread(self):
        xh, y, core, xl, z = place()
        ys, xs, y_peers, x_peers, other = plane()
        for copy in self.first:
            copy.wait_recv()
        mine = self.line((xh, xl) if self.y_first else y)
        peers = x_peers if self.y_first else y_peers
        self.second = [self.send(mine, mine, peer) for peer in peers]
        self.third = [self.send(mine, mine, other)]

    def share(self):
        ys, xs, y_peers, x_peers, other = plane()
        wheres = xs if self.y_first else ys
        for copy, where in zip(self.second, (wheres[1], wheres[0], wheres[2])):
            copy.wait_recv()
            line = self.line(where)
            self.third.append(self.send(line, line, other))

    def end(self):
        for copy in self.third:
            copy.wait_recv()
        for copy in self.copies:
            copy.wait_send()


def swap_halves(block):
    lane = lax.broadcasted_iota(jnp.int32, block.shape, 1)
    return jnp.where(
        lane < HD // 2, pltpu.roll(block, 128 - HD // 2, 1), pltpu.roll(block, HD // 2, 1)
    )


def front_kernel(*refs):
    (hidden, cotangent, gain, m_in, m_expand, m_out, m_shrink) = refs[:7]
    (cos_ref, sin_ref, prefix) = refs[7:10]
    (first_to, shrunk_all, in_to, gate_all, up_all, out_all, shrink_all) = refs[10:17]
    (turned_to, rows_to, lines_to, attended, tokens, log_total, total) = refs[17:24]
    (first_all, shrunk, in_all, w_gate, w_up, w_out, w_shrink) = refs[24:31]
    (turned, kv_rows, kv_lines, key_cos, key_sin) = refs[31:36]
    (packed, held_rows, parts, came, sums) = refs[36:41]
    (ring_send, ring_recv, plane_send, plane_recv) = refs[41:45]
    (kv_send, kv_recv, own_sem, out_sem) = refs[45:]
    xh, y, core, xl, z = place()
    z, zp, z2, zm, up, down = ring_peers()
    ys, xs, y_peers, x_peers, other = plane()
    beside = device(xh, y, core, 1 - xl, z)
    peers = [up, down, other] + y_peers + x_peers
    hail(peers)
    low = jnp.bfloat16
    in_own = in_all.at[xh, y, core, xl]
    in_own[...] = m_in[...].astype(low)
    w_out[...] = m_out[...].astype(low)
    rows = hidden[...].astype(jnp.float32)
    scaling = lax.rsqrt(jnp.mean(rows * rows, axis=-1, keepdims=True) + EPS)
    first_all[z] = (rows * scaling * gain[...]).astype(low)
    meet(peers)
    owns = (in_own, w_out, w_gate, w_up, w_shrink)
    helds = (in_all, out_all, gate_all, up_all, shrink_all)
    gathers = [
        PlaneGather(own, held, i in (2, 3), plane_send.at[i], plane_recv.at[i])
        for i, (own, held) in enumerate(zip(owns, helds))
    ]
    for gather in gathers[:2]:
        gather.begin()
    ring = ring_gather_begin(first_all.at[z], first_all, ring_send.at[0], ring_recv.at[0])
    w_gate[...] = m_expand[0].astype(low)
    w_up[...] = m_expand[1].astype(low)
    w_shrink[...] = m_shrink[...].astype(low)
    shrunk[...] = (RESID * cotangent[...].astype(jnp.float32)).astype(low)
    keeps = [
        pltpu.make_async_copy(own, held.at[xh, y, core, xl], own_sem.at[i])
        for i, (own, held) in enumerate(zip(owns[1:], helds[1:]))
    ]
    keeps.append(pltpu.make_async_copy(shrunk, shrunk_all.at[z], own_sem.at[4]))
    for keep in keeps:
        keep.start()
    for keep in keeps:
        keep.wait()
    for gather in gathers[:2]:
        gather.spread()
    key_tables(cos_ref, sin_ref, key_cos, key_sin)
    ring = ring_gather_forward(first_all, ring, ring_send.at[0], ring_recv.at[0])
    gathers[0].share()
    gathers[1].share()
    gathers[0].end()
    for gather in gathers[2:]:
        gather.begin()

    def project(c, rows):
        out = nn(first_all[c], in_all[...].reshape(1536, 640))
        packed[rows] = out
        for g in range(HEADS):
            block = out[:, g * 320 + 192 : g * 320 + 320]
            mine = pl.ds(pl.multiple_of(xl * 896 + c * 224, 16), 224)
            kv_rows[g, mine] = (
                block * key_cos[rows] + swap_halves(block) * key_sin[rows]
            ).astype(low)

    kv_copies = []
    for i, c in enumerate((z, zm, zp, z2)):
        if i == 1:
            ring[2].wait_recv()
        if i == 2:
            ring[3].wait_recv()
        if i == 3:
            ring[4].wait_recv()
            ring[5].wait_recv()
        project(c, pl.ds(pl.multiple_of(c * 224, 16), 224))
        mine = kv_rows.at[:, pl.ds(pl.multiple_of(xl * 896 + c * 224, 16), 224)]
        kv_copies.append(remote(mine, mine, kv_send.at[i], kv_recv.at[i], beside))
        kv_copies[-1].start()
    later = ring_gather_begin(shrunk, shrunk_all, ring_send.at[1], ring_recv.at[1])
    saves = []

    def save(src, dst):
        saves.append(pltpu.make_async_copy(src, dst, own_sem.at[5 + len(saves)]))
        saves[-1].start()

    save(first_all, first_to)
    save(in_all, in_to)

    def turn_block(b, carry):
        columns = pl.ds(pl.multiple_of(b * 128, 128), 128)
        lines = jnp.transpose(packed[columns])
        cos_here, sin_here = cos_ref[:, columns], sin_ref[:, columns]
        for g in range(HEADS):
            for h in range(GROUP):
                at = (g * 5 + h) * HD
                turned[(g * GROUP + h) * HD : (g * GROUP + h + 1) * HD, columns] = (
                    turn(lines[at : at + HD], cos_here, sin_here) * HD ** (-0.5)
                ).astype(low)
        return carry

    lax.fori_loop(0, BLOCKS, turn_block, 0)
    save(turned, turned_to)
    for copy in kv_copies:
        copy.wait_recv()
    for gather in gathers[2:]:
        gather.spread()
    for g in range(HEADS):
        kv_lines[g] = jnp.transpose(kv_rows[g].astype(jnp.float32)).astype(low)
    save(kv_rows, rows_to)
    save(kv_lines, lines_to)

    def block(b, g):
        columns = pl.ds(pl.multiple_of(b * 128, 128), 128)

        def run(span):
            head_rows = [
                pl.ds(pl.multiple_of((g * GROUP + h) * HD, HD), HD) for h in range(GROUP)
            ]
            queries = jnp.concatenate([turned[r, columns] for r in head_rows], axis=1)
            queries = jnp.concatenate([queries, jnp.zeros_like(queries)], axis=0)
            scores = nn(kv_rows[g, :span], queries)
            key_index = lax.broadcasted_iota(jnp.int32, (span, 384), 0)
            scores = jnp.where(key_index < limits(prefix, xl, b), scores, NEG)
            row_max = jnp.max(scores, axis=0, keepdims=True)
            shifted = jnp.exp(scores - row_max)
            exp_total = jnp.sum(shifted, axis=0, keepdims=True)
            out = nn(kv_lines[g, HD:, :span], shifted.astype(low)) * (1.0 / exp_total)
            for h in range(GROUP):
                attended[head_rows[h], columns] = out[:, h * 128 : (h + 1) * 128].astype(low)
            log_total[b * HEADS + g] = row_max + jnp.log(exp_total)

        by_span(xl, b, run)

    def both_heads(t, carry):
        block(arrival(z, lax.div(t, 2)), lax.rem(t, 2))
        return carry

    def own_block(g, carry):
        block(2 * z, g)
        return carry

    def lay(b):
        columns = pl.ds(pl.multiple_of(b * 128, 128), 128)
        tokens[columns] = jnp.transpose(attended[:, columns].astype(jnp.float32)).astype(low)

    def apply(c):
        mine = pl.ds(pl.multiple_of(c * 224, 16), 224)
        parts[c] = nt(tokens[mine], held_rows[...].reshape(1536, 384)).astype(low)

    lax.fori_loop(8, 14, both_heads, 0)
    later = ring_gather_forward(shrunk_all, later, ring_send.at[1], ring_recv.at[1])
    gathers[1].end()
    fetch = pltpu.make_async_copy(out_all, held_rows, out_sem)
    fetch.start()
    for i in range(4, 7):
        lay(arrival(z, i))
    fetch.wait()
    apply(z2)
    far = ring_scatter_far(parts, came, ring_send.at[2], ring_recv.at[2])
    lax.fori_loop(2, 8, both_heads, 0)
    for i in range(1, 4):
        lay(arrival(z, i))
    apply(zp)
    apply(zm)
    near = ring_scatter_near(parts, came, ring_send.at[2], ring_recv.at[2])
    scatter = ring_scatter_forward(
        parts, came, sums, far + near, ring_send.at[2], ring_recv.at[2]
    )
    lax.fori_loop(0, 2, own_block, 0)
    lay(2 * z)
    apply(z)
    for gather in gathers[2:]:
        gather.share()
    for gather in gathers[2:]:
        gather.end()
    ring_gather_end(later)
    for copy in kv_copies + ring:
        copy.wait_send()
    for copy in saves:
        copy.wait()
    ring_scatter_end(parts, came, total, scatter)


def front(hidden, cotangent, gain, weights, tables, prefix):
    any_place = pl.BlockSpec(memory_space=pl.ANY)
    whole = pl.BlockSpec(memory_space=pltpu.VMEM)
    rows, width = hidden.shape
    low, full = jnp.bfloat16, jnp.float32
    block = (2, 4, 2, 2, 48)
    first_shape, in_shape = (4, rows, width), block + (640,)
    turned_shape, rows_shape, lines_shape = (384, 896), (HEADS, 1792, 128), (HEADS, 128, 1792)
    kept = (first_shape, (4, rows, width), in_shape) + (block + (960,),) * 2
    kept += (block + (384,), block + (960,), turned_shape, rows_shape, lines_shape)
    outs = pl.pallas_call(
        front_kernel,
        out_shape=(
            *(jax.ShapeDtypeStruct(shape, low) for shape in kept),
            jax.ShapeDtypeStruct((384, 896), low),
            jax.ShapeDtypeStruct((896, 384), low),
            jax.ShapeDtypeStruct((HEADS * BLOCKS, 1, 384), full),
            jax.ShapeDtypeStruct((rows, width), full),
        ),
        in_specs=[whole] * 9 + [pl.BlockSpec(memory_space=pltpu.SMEM)],
        out_specs=(any_place,) * 10 + (whole,) * 4,
        scratch_shapes=[
            pltpu.VMEM(first_shape, low),
            pltpu.VMEM((rows, width), low),
            pltpu.VMEM(in_shape, low),
            pltpu.VMEM((48, 960), low),
            pltpu.VMEM((48, 960), low),
            pltpu.VMEM((48, 384), low),
            pltpu.VMEM((48, 960), low),
            pltpu.VMEM(turned_shape, low),
            pltpu.VMEM(rows_shape, low),
            pltpu.VMEM(lines_shape, low),
            pltpu.VMEM((896, 128), full),
            pltpu.VMEM((896, 128), full),
            pltpu.VMEM((896, 640), full),
            pltpu.VMEM(block + (384,), low),
            pltpu.VMEM((4, rows, width), low),
            pltpu.VMEM((6, rows // 2, width), low),
            pltpu.VMEM((2, rows // 2, width), low),
            pltpu.SemaphoreType.DMA((3, 6)),
            pltpu.SemaphoreType.DMA((3, 6)),
            pltpu.SemaphoreType.DMA((5, 10)),
            pltpu.SemaphoreType.DMA((5, 10)),
            pltpu.SemaphoreType.DMA((4,)),
            pltpu.SemaphoreType.DMA((4,)),
            pltpu.SemaphoreType.DMA((10,)),
            pltpu.SemaphoreType.DMA,
        ],
        compiler_params=pltpu.CompilerParams(
            collective_id=0, has_side_effects=True, vmem_limit_bytes=VMEM_MOST
        ),
    )(hidden, cotangent, gain, *weights, *tables, prefix)
    return outs[:2] + tuple(held.reshape(1536, -1) for held in outs[2:7]) + outs[7:]


def tn(a, b):
    return lax.dot_general(a, b, (((0,), (0,)), ((), ())), preferred_element_type=jnp.float32)


def middle_kernel(*refs):
    (hidden, cotangent, projected, gain) = refs[:4]
    (shrunk_from, gate_from, up_from, shrink_from) = refs[4:8]
    (residual, grad_residual, turned_back, gain_two) = refs[8:12]
    (gate_to, up_to, shrink_to, out_to) = refs[12:16]
    (shrunk_all, w_gate, w_up, w_shrink) = refs[16:20]
    (second_all, activated_back, gated, gate_back, up_back) = refs[20:25]
    (parts, came, sums, total) = refs[25:29]
    (grad_gate, grad_up, grad_shrink, out_parts) = refs[29:33]
    (ring_send, ring_recv, load_sem) = refs[33:]
    z, zp, z2, zm, up, down = ring_peers()
    hail([up, down])
    loads = [
        pltpu.make_async_copy(src, dst, load_sem.at[i])
        for i, (src, dst) in enumerate(
            (
                (shrink_from, w_shrink),
                (shrunk_from, shrunk_all),
                (gate_from, w_gate),
                (up_from, w_up),
            )
        )
    ]
    for load in loads:
        load.start()
    rows = hidden[...].astype(jnp.float32) + RESID * projected[...]
    residual[...] = rows
    scaling = lax.rsqrt(jnp.mean(rows * rows, axis=-1, keepdims=True) + EPS)
    second_all[z] = (rows * scaling * gain[...]).astype(jnp.bfloat16)
    meet([up, down])
    ring = ring_gather_begin(second_all.at[z], second_all, ring_send.at[0], ring_recv.at[0])
    loads[0].wait()
    loads[1].wait()
    for c in range(4):
        activated_back[c] = nn(shrunk_all[c], w_shrink[...])
    loads[2].wait()
    loads[3].wait()

    def feed(c):
        gate_value = nn(second_all[c], w_gate[...])
        up_value = nn(second_all[c], w_up[...])
        sigmoid_gate = 1.0 / (1.0 + jnp.exp(-gate_value))
        gate_active = gate_value * sigmoid_gate
        gated[c] = (gate_active * up_value).astype(jnp.bfloat16)
        gradient = activated_back[c]
        gate_back[c] = (
            gradient * up_value * sigmoid_gate * (1.0 + gate_value * (1.0 - sigmoid_gate))
        ).astype(jnp.bfloat16)
        up_back[c] = (gradient * gate_active).astype(jnp.bfloat16)
        parts[c] = (nt(gate_back[c], w_gate[...]) + nt(up_back[c], w_up[...])).astype(
            jnp.bfloat16
        )

    feed(z)
    ring = ring_gather_forward(second_all, ring, ring_send.at[0], ring_recv.at[0])
    ring[2].wait_recv()
    feed(zm)
    ring[3].wait_recv()
    feed(zp)
    near = ring_scatter_near(parts, came, ring_send.at[1], ring_recv.at[1])
    ring[4].wait_recv()
    ring[5].wait_recv()
    feed(z2)
    far = ring_scatter_far(parts, came, ring_send.at[1], ring_recv.at[1])
    second_rows = second_all[...].reshape(896, 1536)
    saves = []

    def save(src, dst):
        saves.append(pltpu.make_async_copy(src, dst, load_sem.at[4 + len(saves)]))
        saves[-1].start()

    grad_gate[...] = tn(second_rows, gate_back[...].reshape(896, 960)).astype(jnp.bfloat16)
    save(grad_gate, gate_to)
    scatter = ring_scatter_forward(
        parts, came, sums, far + near, ring_send.at[1], ring_recv.at[1]
    )
    grad_up[...] = tn(second_rows, up_back[...].reshape(896, 960)).astype(jnp.bfloat16)
    save(grad_up, up_to)
    grad_shrink[...] = tn(
        shrunk_all[...].reshape(896, 1536), gated[...].reshape(896, 960)
    ).astype(jnp.bfloat16)
    save(grad_shrink, shrink_to)
    for c in range(4):
        out_parts[c] = nt(gated[c], w_shrink[...]).astype(jnp.bfloat16)
    save(out_parts, out_to)
    for copy in ring:
        copy.wait_send()
    ring_scatter_end(parts, came, total, scatter)
    rows = residual[...]
    scaling = lax.rsqrt(jnp.mean(rows * rows, axis=-1, keepdims=True) + EPS)
    normed = rows * scaling
    gradient = total[...]
    gain_two[...] = jnp.sum(gradient * normed, axis=0, keepdims=True)
    gradient = gradient * gain[...]
    back = cotangent[...].astype(jnp.float32) + scaling * (
        gradient - normed * jnp.mean(gradient * normed, axis=-1, keepdims=True)
    )
    grad_residual[...] = back
    turned_back[...] = (RESID * back).astype(jnp.bfloat16)
    for copy in saves:
        copy.wait()


def middle(hidden, cotangent, projected, gain, shrunk_all, w_gate, w_up, w_shrink):
    any_place = pl.BlockSpec(memory_space=pl.ANY)
    whole = pl.BlockSpec(memory_space=pltpu.VMEM)
    rows, width = hidden.shape
    low, full = jnp.bfloat16, jnp.float32
    return pl.pallas_call(
        middle_kernel,
        out_shape=(
            jax.ShapeDtypeStruct((rows, width), full),
            jax.ShapeDtypeStruct((rows, width), full),
            jax.ShapeDtypeStruct((rows, width), low),
            jax.ShapeDtypeStruct((1, width), full),
            jax.ShapeDtypeStruct((1536, 960), low),
            jax.ShapeDtypeStruct((1536, 960), low),
            jax.ShapeDtypeStruct((1536, 960), low),
            jax.ShapeDtypeStruct((4, rows, width), low),
        ),
        in_specs=[whole] * 4 + [any_place] * 4,
        out_specs=(whole,) * 4 + (any_place,) * 4,
        scratch_shapes=[
            pltpu.VMEM((4, rows, width), low),
            pltpu.VMEM((1536, 960), low),
            pltpu.VMEM((1536, 960), low),
            pltpu.VMEM((1536, 960), low),
            pltpu.VMEM((4, rows, width), low),
            pltpu.VMEM((4, rows, 960), full),
            pltpu.VMEM((4, rows, 960), low),
            pltpu.VMEM((4, rows, 960), low),
            pltpu.VMEM((4, rows, 960), low),
            pltpu.VMEM((4, rows, width), low),
            pltpu.VMEM((6, rows // 2, width), low),
            pltpu.VMEM((2, rows // 2, width), low),
            pltpu.VMEM((rows, width), full),
            pltpu.VMEM((1536, 960), low),
            pltpu.VMEM((1536, 960), low),
            pltpu.VMEM((1536, 960), low),
            pltpu.VMEM((4, rows, width), low),
            pltpu.SemaphoreType.DMA((2, 6)),
            pltpu.SemaphoreType.DMA((2, 6)),
            pltpu.SemaphoreType.DMA((8,)),
        ],
        compiler_params=pltpu.CompilerParams(
            collective_id=4, has_side_effects=True, vmem_limit_bytes=VMEM_MOST
        ),
    )(hidden, cotangent, projected, gain, shrunk_all, w_gate, w_up, w_shrink)


class Scatter:
    def __init__(self, parts, came, across, lined, last, x_first, send_sem, recv_sem):
        self.parts, self.came, self.across = parts, came, across
        self.lined, self.last, self.x_first = lined, last, x_first
        self.send_sem, self.recv_sem, self.used, self.copies = send_sem, recv_sem, 0, []
        xh, y, core, xl, z = place()
        ys, xs, y_peers, x_peers, self.other = plane()
        if x_first:
            self.lines, self.peers = xs[::-1] + [(xh, xl)], x_peers[::-1]
            self.mine, self.targets, self.target_peers = y, ys, y_peers
        else:
            self.lines, self.peers = ys[::-1] + [y], y_peers[::-1]
            self.mine, self.targets, self.target_peers = (xh, xl), xs, x_peers

    def send(self, src, dst, peer):
        copy = remote(src, dst, self.send_sem.at[self.used], self.recv_sem.at[self.used], peer)
        self.used += 1
        copy.start()
        self.copies.append(copy)
        return copy

    def in_line(self, line):
        return (line[0], slice(None), line[1]) if self.x_first else (slice(None), line)

    def begin(self):
        core = place()[2]
        self.first = []
        for line in self.lines:
            if self.x_first:
                src = self.parts.at[line[0], :, 1 - core, line[1]]
            else:
                src = self.parts.at[:, line, 1 - core]
            self.first.append(self.send(src, self.came.at[self.in_line(line)], self.other))

    def stage(self, held, sem):
        copy = pltpu.make_async_copy(self.parts.at[:, :, place()[2]], held, sem)
        copy.start()
        return copy

    def at(self, line, i):
        return (line[0], i, line[1]) if self.x_first else (i // 2, line, lax.rem(i, 2))

    def spot(self, i):
        if self.x_first:
            return (i,)
        return (i[0], i[1]) if isinstance(i, tuple) else (i // 2, lax.rem(i, 2))

    def fold(self, held=None):
        core = place()[2]
        self.second = []
        for k, (line, copy) in enumerate(zip(self.lines, self.first)):
            copy.wait_recv()

            def add(i, carry, line=line):
                at = self.at(line, i)
                if held is None:
                    own = self.parts[at[0], at[1], core, at[2]]
                else:
                    own = held[at]
                self.came[at] = (
                    own.astype(jnp.float32) + self.came[at].astype(jnp.float32)
                ).astype(jnp.bfloat16)
                return carry

            lax.fori_loop(0, 4, add, 0)
            if k < 3:
                self.second.append(
                    self.send(
                        self.came.at[self.in_line(line)], self.across.at[k], self.peers[k]
                    )
                )

    def line(self):
        for copy in self.second:
            copy.wait_recv()

        def add(i, carry):
            spot = self.spot(i)
            total = self.came[self.at(self.lines[3], i)].astype(jnp.float32)
            for k in range(3):
                total = total + self.across[(k,) + spot].astype(jnp.float32)
            self.lined[spot] = total.astype(jnp.bfloat16)
            return carry

        lax.fori_loop(0, 4, add, 0)
        self.third = [
            self.send(self.lined.at[self.spot(target)], self.last.at[k], peer)
            for k, (target, peer) in enumerate(zip(self.targets, self.target_peers))
        ]

    def end(self, total_ref):
        for copy in self.third:
            copy.wait_recv()
        total = self.lined[self.spot(self.mine)].astype(jnp.float32)
        for k in range(3):
            total = total + self.last[k].astype(jnp.float32)
        total_ref[...] = total
        for copy in self.copies:
            copy.wait_send()


def scatter_room(width, x_first):
    line = (4,) if x_first else (2, 2)
    return [
        pltpu.VMEM((2, 4, 2, 48, width), jnp.bfloat16),
        pltpu.VMEM((3,) + line + (48, width), jnp.bfloat16),
        pltpu.VMEM(line + (48, width), jnp.bfloat16),
        pltpu.VMEM((3, 48, width), jnp.bfloat16),
    ]


def back_kernel(*refs):
    (own, out_from, in_from, first_from, out_terms) = refs[:5]
    gradients = refs[5:8]
    (turned, kv_rows, kv_lines, attended, tokens, log_total) = refs[8:14]
    (cos_ref, sin_ref, prefix) = refs[14:17]
    (shrunk_total, first_total) = refs[17:19]
    totals = refs[19:24]
    (proj_all, w_out, w_in, grad_tokens, grad_lines, grad_queries, grad_packed) = refs[24:31]
    (sums, outgoing, incoming, parts, came_one, came_two, ring_sums) = refs[31:38]
    stages, out_parts, in_parts = refs[38:40], refs[40], refs[41]
    rooms = refs[42:62]
    (key_cos, key_sin) = refs[62:64]
    (ring_send, ring_recv, plane_send, plane_recv, kv_send, kv_recv, load_sem) = refs[64:]
    xh, y, core, xl, z = place()
    z, zp, z2, zm, up, down = ring_peers()
    ys, xs, y_peers, x_peers, other = plane()
    beside = device(xh, y, core, 1 - xl, z)
    peers = [up, down, other] + y_peers + x_peers
    hail(peers)
    sums[...] = jnp.zeros_like(sums)
    key_tables(cos_ref, sin_ref, key_cos, key_sin)
    meet(peers)
    ring = ring_gather_begin(own, proj_all, ring_send.at[0], ring_recv.at[0])
    every = [
        Scatter(
            terms,
            *rooms[4 * i : 4 * i + 4],
            SCATTER_TURNS[i],
            plane_send.at[i],
            plane_recv.at[i],
        )
        for i, terms in enumerate(tuple(gradients) + (out_parts, in_parts))
    ]
    feed, out_scatter, in_scatter = every[:3], every[3], every[4]
    for scatter in feed:
        scatter.begin()

    def load(src, dst, i):
        copy = pltpu.make_async_copy(src, dst, load_sem.at[i])
        copy.start()
        return copy

    load_out = load(out_from, w_out, 0)
    keep = load(own, proj_all.at[z], 1)
    staged = [feed[i].stage(stages[i], load_sem.at[2 + i]) for i in range(2)]
    load_terms = load(out_terms, parts, 5)
    load_in = load(in_from, w_in, 6)

    def give(c):
        rows = pl.ds(pl.multiple_of(c * 224, 16), 224)
        grad_tokens[rows] = nn(proj_all[c], w_out[...]).astype(jnp.bfloat16)

    def lay(b):
        columns = pl.ds(pl.multiple_of(b * 128, 128), 128)
        grad_lines[:, columns] = jnp.transpose(
            grad_tokens[columns].astype(jnp.float32)
        ).astype(jnp.bfloat16)

    def block(b, g):
        columns = pl.ds(pl.multiple_of(b * 128, 128), 128)

        def run(span):
            head_rows = [
                pl.ds(pl.multiple_of((g * GROUP + h) * HD, HD), HD) for h in range(GROUP)
            ]
            queries = jnp.concatenate([turned[r, columns] for r in head_rows], axis=1)
            gradient = jnp.concatenate([grad_lines[r, columns] for r in head_rows], axis=1)
            held = jnp.concatenate([attended[r, columns] for r in head_rows], axis=1)
            inner = jnp.sum(
                gradient.astype(jnp.float32) * held.astype(jnp.float32), axis=0, keepdims=True
            )
            nothing = jnp.zeros_like(queries)
            both = jnp.concatenate(
                [
                    jnp.concatenate([queries, nothing], axis=1),
                    jnp.concatenate([nothing, gradient], axis=1),
                ],
                axis=0,
            )
            products = nn(kv_rows[g, :span], both)
            key_index = lax.broadcasted_iota(jnp.int32, (span, 384), 0)
            probs = jnp.exp(
                jnp.where(key_index < limits(prefix, xl, b), products[:, :384], NEG)
                - log_total[b * HEADS + g]
            )
            grad_scores = (probs * (products[:, 384:] - inner)).astype(jnp.bfloat16)
            sums[g, :span] += nt(
                jnp.concatenate([grad_scores, probs.astype(jnp.bfloat16)], axis=1), both
            )
            total = nn(kv_lines[g, :HD, :span], grad_scores) * HD ** (-0.5)
            cos_here, sin_here = cos_ref[:, columns], sin_ref[:, columns]
            back = [
                turn_back(total[:, h * 128 : (h + 1) * 128], cos_here, sin_here)
                for h in range(GROUP)
            ]
            grad_queries[g, columns] = jnp.transpose(jnp.concatenate(back, axis=0)).astype(
                jnp.bfloat16
            )

        by_span(xl, b, run)

    def both_heads(t, carry):
        block(arrival(z, lax.div(t, 2)), lax.rem(t, 2))
        return carry

    keep.wait()
    load_out.wait()
    give(z)
    lay(2 * z)

    def own_block(g, carry):
        block(2 * z, g)
        return carry

    lax.fori_loop(0, 2, own_block, 0)
    ring = ring_gather_forward(proj_all, ring, ring_send.at[0], ring_recv.at[0])
    staged[0].wait()
    feed[0].fold(stages[0])
    staged[0] = feed[2].stage(stages[0], load_sem.at[4])
    staged[1].wait()
    feed[1].fold(stages[1])
    staged[0].wait()
    feed[2].fold(stages[0])
    ring[2].wait_recv()
    give(zm)
    ring[3].wait_recv()
    give(zp)
    for i in range(1, 4):
        lay(arrival(z, i))
    lax.fori_loop(2, 8, both_heads, 0)
    ring[4].wait_recv()
    ring[5].wait_recv()
    give(z2)
    for i in range(4, 7):
        lay(arrival(z, i))
    for copy in ring:
        copy.wait_send()
    out_parts[...] = (
        tn(proj_all[...].reshape(896, 1536), tokens[...])
        .astype(jnp.bfloat16)
        .reshape(2, 4, 2, 2, 48, 384)
    )
    out_scatter.begin()
    load_first = load(first_from, proj_all, 7)
    load_terms.wait()
    shrunk = ring_scatter_begin(parts, came_one, ring_send.at[1], ring_recv.at[1])

    def exchange(g):
        theirs = sums[g, pl.ds(pl.multiple_of((1 - xl) * 896, 128), 896)]
        outgoing[g] = theirs.astype(jnp.bfloat16)
        copy = remote(outgoing.at[g], incoming.at[g], kv_send.at[g], kv_recv.at[g], beside)
        copy.start()
        return copy

    def far_block(g):
        def body(i, carry):
            block(arrival(z, i), g)
            return carry

        lax.fori_loop(4, 7, body, 0)

    far_block(0)
    kv_copies = [exchange(0)]
    shrunk = ring_scatter_forward(
        parts, came_one, ring_sums, shrunk, ring_send.at[1], ring_recv.at[1]
    )
    out_scatter.fold()
    far_block(1)
    kv_copies.append(exchange(1))
    for scatter in feed:
        scatter.line()
    out_scatter.line()
    load_in.wait()
    load_first.wait()
    ring_scatter_end(parts, came_one, shrunk_total, shrunk)
    for g in range(HEADS):
        kv_copies[g].wait()
        mine = sums[g, pl.ds(pl.multiple_of(xl * 896, 128), 896)] + incoming[g].astype(
            jnp.float32
        )
        mine = mine * key_cos[...] - swap_halves(mine) * key_sin[...]
        grad_packed[:, g * 320 : g * 320 + 192] = grad_queries[g]
        grad_packed[:, g * 320 + 192 : g * 320 + 320] = mine.astype(jnp.bfloat16)

    def spread(c):
        rows = pl.ds(pl.multiple_of(c * 224, 16), 224)
        parts[c] = nt(grad_packed[rows], w_in[...]).astype(jnp.bfloat16)

    spread(z2)
    far = ring_scatter_far(parts, came_two, ring_send.at[2], ring_recv.at[2])
    spread(zp)
    spread(zm)
    near = ring_scatter_near(parts, came_two, ring_send.at[2], ring_recv.at[2])
    in_parts[...] = (
        tn(proj_all[...].reshape(896, 1536), grad_packed[...])
        .astype(jnp.bfloat16)
        .reshape(2, 4, 2, 2, 48, 640)
    )
    in_scatter.begin()
    spread(z)
    in_scatter.fold()
    ring = ring_scatter_forward(
        parts, came_two, ring_sums, far + near, ring_send.at[2], ring_recv.at[2]
    )
    for i in range(4):
        every[i].end(totals[i])
    in_scatter.line()
    ring_scatter_end(parts, came_two, first_total, ring)
    in_scatter.end(totals[4])


SCATTER_TURNS = (True, True, False, False, False)


def back(own, w_out, w_in, first_all, out_terms, gradients, saved, tables, prefix):
    any_place = pl.BlockSpec(memory_space=pl.ANY)
    whole = pl.BlockSpec(memory_space=pltpu.VMEM)
    rows, width = own.shape
    low, full = jnp.bfloat16, jnp.float32
    widths = [g.shape[-1] for g in gradients] + [384, 640]
    rooms = []
    for w, turn_first in zip(widths, SCATTER_TURNS):
        rooms += scatter_room(w, turn_first)
    return pl.pallas_call(
        back_kernel,
        out_shape=(jax.ShapeDtypeStruct((rows, width), full),) * 2
        + tuple(jax.ShapeDtypeStruct((48, w), full) for w in widths),
        in_specs=[whole]
        + [any_place] * 7
        + [whole] * 8
        + [pl.BlockSpec(memory_space=pltpu.SMEM)],
        out_specs=(whole,) * 7,
        scratch_shapes=[
            pltpu.VMEM((4, rows, width), low),
            pltpu.VMEM((1536, 384), low),
            pltpu.VMEM((1536, 640), low),
            pltpu.VMEM((896, 384), low),
            pltpu.VMEM((384, 896), low),
            pltpu.VMEM((HEADS, 896, 192), low),
            pltpu.VMEM((896, 640), low),
            pltpu.VMEM((HEADS, 1792, 128), full),
            pltpu.VMEM((HEADS, 896, 128), low),
            pltpu.VMEM((HEADS, 896, 128), low),
            pltpu.VMEM((4, rows, width), low),
            pltpu.VMEM((6, rows // 2, width), low),
            pltpu.VMEM((6, rows // 2, width), low),
            pltpu.VMEM((2, rows // 2, width), low),
            pltpu.VMEM((2, 4, 2, 48, 960), low),
            pltpu.VMEM((2, 4, 2, 48, 960), low),
            pltpu.VMEM((2, 4, 2, 2, 48, 384), low),
            pltpu.VMEM((2, 4, 2, 2, 48, 640), low),
            *rooms,
            pltpu.VMEM((896, 128), full),
            pltpu.VMEM((896, 128), full),
            pltpu.SemaphoreType.DMA((3, 6)),
            pltpu.SemaphoreType.DMA((3, 6)),
            pltpu.SemaphoreType.DMA((5, 10)),
            pltpu.SemaphoreType.DMA((5, 10)),
            pltpu.SemaphoreType.DMA((2,)),
            pltpu.SemaphoreType.DMA((2,)),
            pltpu.SemaphoreType.DMA((8,)),
        ],
        compiler_params=pltpu.CompilerParams(
            collective_id=2, has_side_effects=True, vmem_limit_bytes=BACK_VMEM
        ),
    )(
        own,
        w_out,
        w_in,
        first_all,
        out_terms,
        *(g.reshape(2, 4, 2, 2, 48, g.shape[-1]) for g in gradients),
        *saved,
        *tables,
        prefix,
    )


BACK_VMEM = 63 * 2**20


def finish_kernel(*refs):
    (grad_first, hidden, grad_residual, gain_two) = refs[:4]
    (gains, gains_first, gains_second) = refs[4:7]
    (grad_gate, grad_up, grad_shrink, grad_output, grad_input) = refs[7:12]
    masters = [refs[12 + 3 * i : 15 + 3 * i] for i in range(4)]
    (input_gradient, norm_ref) = refs[24:26]
    gains_new = refs[26:29]
    news = [refs[29 + 3 * i : 32 + 3 * i] for i in range(4)]
    own, held, sems_out, sems_in = refs[41:]
    xh, y, core, xl, z = place()
    ys, xs, y_peers, x_peers, other = plane()
    groups = (
        (
            [
                device(xh, y, c, xl, lax.rem(z + d, 4))
                for d, c in ((1, core), (3, core), (0, 1 - core), (2, core))
                + ((1, 1 - core), (3, 1 - core), (2, 1 - core))
            ],
            z * 2 + core,
            8,
        ),
        (x_peers, xh * 2 + xl, 4),
        (y_peers, y, 4),
    )
    peers = [peer for group in groups for peer in group[0]]
    hail(peers)
    rows = hidden[...].astype(jnp.float32)
    scaling = lax.rsqrt(jnp.mean(rows * rows, axis=-1, keepdims=True) + EPS)
    normed = rows * scaling
    gradient = grad_first[...]
    gain_one = jnp.sum(gradient * normed, axis=0, keepdims=True)
    squares = jnp.zeros((1, 1), jnp.float32)
    for terms in (grad_gate, grad_up, grad_shrink, grad_output, grad_input):
        held_terms = terms[...]
        squares = squares + jnp.sum(
            jnp.sum(held_terms * held_terms, axis=0, keepdims=True), axis=1, keepdims=True
        )
    for k in range(3):
        own[k : k + 1] = gain_one[:, k * 512 : (k + 1) * 512]
        own[3 + k : 4 + k] = gain_two[:, k * 512 : (k + 1) * 512]
    own[6:8] = jnp.broadcast_to(squares, (2, 512))
    meet(peers)
    used = 0
    for axis, (group, here, count) in enumerate(groups):
        held[axis, here] = own[...]
        spot = held.at[axis, here]
        copies = []
        for peer in group:
            copies.append(remote(spot, spot, sems_out.at[used], sems_in.at[used], peer))
            copies[-1].start()
            used += 1
        if axis == 0:
            gradient = gradient * gains[0:1]
            input_gradient[...] = grad_residual[...] + scaling * (
                gradient - normed * jnp.mean(gradient * normed, axis=-1, keepdims=True)
            )
        for copy in copies:
            copy.wait()
        order = held[axis, 0]
        for k in range(1, count):
            order = order + held[axis, k]
        own[...] = order
    grad_gains = jnp.concatenate(
        [
            jnp.concatenate([own[3 * r + k : 3 * r + k + 1] for k in range(3)], axis=1)
            for r in range(2)
        ],
        axis=0,
    )
    gain_squares = jnp.sum(
        jnp.sum(grad_gains * grad_gains, axis=0, keepdims=True), axis=1, keepdims=True
    )
    gradient_norm = jnp.sqrt(own[6:7, 0:1] + gain_squares)
    norm_ref[...] = gradient_norm
    factor = jnp.minimum(1.0, MAX_NORM / (gradient_norm + 1e-06))

    def put(targets, results):
        for target, result in zip(targets, results):
            target[...] = result

    put(
        gains_new,
        adamw(
            gains[...], factor * grad_gains, gains_first[...], gains_second[...], GAIN_RATE, 0.0
        ),
    )
    for i, terms in ((0, grad_input), (1, grad_output), (3, grad_shrink)):
        weight, first, second = masters[i]
        put(news[i], adamw(weight[...], factor * terms[...], first[...], second[...], RATE, DECAY))
    for k, terms in enumerate((grad_gate, grad_up)):
        weight, first, second = masters[2]
        results = adamw(weight[k], factor * terms[...], first[k], second[k], RATE, DECAY)
        for target, result in zip(news[2], results):
            target[k] = result


def finish(grad_first, hidden, grad_residual, gain_two, gains, gradients, masters):
    rows, width = hidden.shape
    full = jnp.float32
    flat = [array for group in masters for array in group]
    return pl.pallas_call(
        finish_kernel,
        out_shape=(
            jax.ShapeDtypeStruct((rows, width), full),
            jax.ShapeDtypeStruct((1, 1), full),
            *(jax.ShapeDtypeStruct((2, width), full) for _ in range(3)),
            *(jax.ShapeDtypeStruct(array.shape, full) for array in flat),
        ),
        scratch_shapes=[
            pltpu.VMEM((8, 512), full),
            pltpu.VMEM((3, 8, 8, 512), full),
            pltpu.SemaphoreType.DMA((13,)),
            pltpu.SemaphoreType.DMA((13,)),
        ],
        compiler_params=pltpu.CompilerParams(
            collective_id=10, has_side_effects=True, vmem_limit_bytes=VMEM_MOST
        ),
    )(grad_first, hidden, grad_residual, gain_two, *gains, *gradients, *flat)


def shards(
    hidden_in,
    cotangent,
    prefix,
    positions,
    norm_gains,
    gains_first,
    gains_second,
    input_weight,
    input_first,
    input_second,
    output_weight,
    output_first,
    output_second,
    expand_weight,
    expand_first,
    expand_second,
    shrink_weight,
    shrink_first,
    shrink_second,
):
    low = jnp.bfloat16
    hidden, upstream = hidden_in[0], cotangent[0]
    masters = (
        (input_weight, input_first, input_second),
        (output_weight.T, output_first.T, output_second.T),
        (expand_weight, expand_first, expand_second),
        (shrink_weight.T, shrink_first.T, shrink_second.T),
    )
    tables = angles(positions[0])
    (
        first_all,
        shrunk_all,
        w_in,
        w_gate,
        w_up,
        w_out,
        w_shrink,
        turned,
        kv_rows,
        kv_lines,
        attended,
        tokens,
        log_total,
        projected,
    ) = front(
        hidden,
        upstream,
        norm_gains[:1],
        (input_weight, expand_weight, output_weight.T, shrink_weight.T),
        tables,
        prefix,
    )
    (
        residual,
        grad_residual,
        projected_gradient,
        gain_two,
        grad_gate,
        grad_up,
        grad_shrink,
        out_parts,
    ) = middle(
        hidden, upstream, projected, norm_gains[1:], shrunk_all, w_gate, w_up, w_shrink
    )
    shrunk, grad_first, *gradients = back(
        projected_gradient,
        w_out,
        w_in,
        first_all,
        out_parts,
        (grad_gate, grad_up, grad_shrink),
        (turned, kv_rows, kv_lines, attended, tokens, log_total),
        tables,
        prefix,
    )
    block_output = (residual + RESID * shrunk).astype(low)
    outs = finish(
        grad_first,
        hidden,
        grad_residual,
        gain_two,
        (norm_gains, gains_first, gains_second),
        gradients,
        masters,
    )
    input_gradient, gradient_norm = outs[0], outs[1].reshape(())
    gains_new, input_new, output_new, expand_new, shrink_new = (
        outs[2 + 3 * i : 5 + 3 * i] for i in range(5)
    )
    return (
        block_output[None],
        input_gradient[None],
        gradient_norm,
        *gains_new,
        *input_new,
        *(array.T for array in output_new),
        *expand_new,
        *(array.T for array in shrink_new),
    )


def solution(mesh):
    return jax.shard_map(
        shards,
        mesh=mesh,
        in_specs=(
            P("shard", ("context", "tensor"), None),
            P("shard", ("context", "tensor"), None),
            P("shard"),
            P("shard", "context"),
            P(),
            P(),
            P(),
            P(("shard", "context"), "tensor"),
            P(("shard", "context"), "tensor"),
            P(("shard", "context"), "tensor"),
            P("tensor", ("shard", "context")),
            P("tensor", ("shard", "context")),
            P("tensor", ("shard", "context")),
            P(None, ("shard", "context"), "tensor"),
            P(None, ("shard", "context"), "tensor"),
            P(None, ("shard", "context"), "tensor"),
            P("tensor", ("shard", "context")),
            P("tensor", ("shard", "context")),
            P("tensor", ("shard", "context")),
        ),
        out_specs=(
            P("shard", ("context", "tensor"), None),
            P("shard", ("context", "tensor"), None),
            P(),
            P(),
            P(),
            P(),
            P(("shard", "context"), "tensor"),
            P(("shard", "context"), "tensor"),
            P(("shard", "context"), "tensor"),
            P("tensor", ("shard", "context")),
            P("tensor", ("shard", "context")),
            P("tensor", ("shard", "context")),
            P(None, ("shard", "context"), "tensor"),
            P(None, ("shard", "context"), "tensor"),
            P(None, ("shard", "context"), "tensor"),
            P("tensor", ("shard", "context")),
            P("tensor", ("shard", "context")),
            P("tensor", ("shard", "context")),
        ),
        check_vma=False,
    )
```

```python
import functools
import math

import jax
import jax.numpy as jnp
from jax import lax
from jax.experimental import pallas as pl
from jax.experimental.pallas import tpu as pltpu
from jax.sharding import PartitionSpec as P

HD = 64
GROUP = 3
STEP = 10
HEADS = 2
BLOCKS = 7
VMEM_MOST = 60 * 2**20
MESH = pl.DeviceIdType.MESH


EPS = 1e-05
RESID = 1.4 / math.sqrt(52.0)
ROPE_BASE = 10000.0
MAX_NORM = 1.0
RATE = 0.1
GAIN_RATE = 1.0
BETA_ONE = 0.9
BETA_TWO = 0.95
ADAM_EPS = 1e-08
DECAY = 0.1
NEG = -1e30


def angles(places):
    half_width = HD // 2
    frequency = ROPE_BASE ** (-2.0 * jnp.arange(half_width, dtype=jnp.float32) / HD)
    phase_turn = places.astype(jnp.float32)[None, :] * frequency[:, None]
    return (jnp.cos(phase_turn), jnp.sin(phase_turn))


def adamw(weight, gradient, momentum, variance, step_rate, decay_rate):
    momentum_new = BETA_ONE * momentum + (1.0 - BETA_ONE) * gradient
    variance_new = BETA_TWO * variance + (1.0 - BETA_TWO) * gradient * gradient
    momentum_hat = momentum_new / (1.0 - BETA_ONE**STEP)
    variance_hat = variance_new / (1.0 - BETA_TWO**STEP)
    updated = weight - step_rate * (
        momentum_hat / (jnp.sqrt(variance_hat) + ADAM_EPS) + decay_rate * weight
    )
    return (momentum_new, variance_new, updated)


def nn(a, b):
    return lax.dot_general(a, b, (((1,), (0,)), ((), ())), preferred_element_type=jnp.float32)


def nt(a, b):
    return lax.dot_general(a, b, (((1,), (1,)), ((), ())), preferred_element_type=jnp.float32)


def place():
    shard = lax.axis_index("shard")
    return (
        shard // 8,
        lax.rem(shard // 2, 4),
        lax.rem(shard, 2),
        lax.axis_index("context"),
        lax.axis_index("tensor"),
    )


def device(xh, y, core, xl, z):
    return {"shard": (xh * 4 + y) * 2 + core, "context": xl, "tensor": z}


def hail(peers):
    barrier = pltpu.get_barrier_semaphore()
    for peer in peers:
        pl.semaphore_signal(barrier, inc=1, device_id=peer, device_id_type=MESH)


def meet(peers):
    pl.semaphore_wait(pltpu.get_barrier_semaphore(), len(peers))


def remote(src, dst, send_sem, recv_sem, peer):
    return pltpu.make_async_remote_copy(
        src_ref=src,
        dst_ref=dst,
        send_sem=send_sem,
        recv_sem=recv_sem,
        device_id=peer,
        device_id_type=MESH,
    )


def turn(block, cos_part, sin_part):
    lower_half, upper_half = block[: HD // 2], block[HD // 2 :]
    return jnp.concatenate(
        [
            lower_half * cos_part - upper_half * sin_part,
            upper_half * cos_part + lower_half * sin_part,
        ],
        axis=0,
    )


def turn_back(block, cos_part, sin_part):
    return turn(block, cos_part, -sin_part)


def by_span(context, b, run):
    near = (context == 0) | (b <= 3)

    @pl.when(near)
    def _():
        run(1408)

    @pl.when(jnp.logical_not(near))
    def _():
        run(1792)


def limits(prefix, xl, b):
    lane = lax.broadcasted_iota(jnp.int32, (1, GROUP * 128), 1)
    row = xl * 896 + b * 128 + lax.rem(lane, 128)
    return jnp.maximum(row + 1, prefix[0])


def key_tables(cos_ref, sin_ref, key_cos, key_sin):
    cos_part, sin_part = jnp.transpose(cos_ref[...]), jnp.transpose(sin_ref[...])
    still = jnp.ones((896, HD), jnp.float32)
    key_cos[...] = jnp.concatenate([cos_part, cos_part, still], axis=1)
    key_sin[...] = jnp.concatenate([-sin_part, sin_part, 0.0 * still], axis=1)


def arrival(z, i):
    edge = (3 - z) // 3
    if isinstance(i, int) and i < 2:
        shift = i * (2 * edge - 1)
    elif isinstance(i, int) and i > 3:
        shift = i - 2 + edge
    else:
        shift = 3 * i - 8 + edge
    return lax.rem(2 * z + shift + 7, 7)


def arrival_far(z, i):
    return lax.rem(2 * z + i + 5 + (3 - z) // 3, 7)


def ring_peers():
    xh, y, core, xl, z = place()
    return (
        z,
        lax.rem(z + 1, 4),
        lax.rem(z + 2, 4),
        lax.rem(z + 3, 4),
        device(xh, y, core, xl, lax.rem(z + 1, 4)),
        device(xh, y, core, xl, lax.rem(z + 3, 4)),
    )


def halves(ref, index):
    rows = ref.shape[1] // 2
    return ref.at[index, pl.ds(0, rows)], ref.at[index, pl.ds(rows, rows)]


def ring_gather_begin(own, held, send_sem, recv_sem):
    z, zp, z2, zm, up, down = ring_peers()
    rows = own.shape[0] // 2
    first, second = own.at[pl.ds(0, rows)], own.at[pl.ds(rows, rows)]
    first_to, second_to = halves(held, z)
    copies = [
        remote(second, second_to, send_sem.at[0], recv_sem.at[0], up),
        remote(first, first_to, send_sem.at[1], recv_sem.at[1], down),
        remote(first, first_to, send_sem.at[2], recv_sem.at[2], up),
        remote(second, second_to, send_sem.at[3], recv_sem.at[3], down),
    ]
    for copy in copies:
        copy.start()
    return copies


def ring_gather_forward(held, copies, send_sem, recv_sem):
    z, zp, z2, zm, up, down = ring_peers()
    copies[0].wait_recv()
    below = halves(held, zm)[1]
    on_up = remote(below, below, send_sem.at[4], recv_sem.at[4], up)
    on_up.start()
    copies[1].wait_recv()
    above = halves(held, zp)[0]
    on_down = remote(above, above, send_sem.at[5], recv_sem.at[5], down)
    on_down.start()
    return copies + [on_up, on_down]


def ring_gather_end(copies):
    for copy in copies:
        copy.wait_send()
    for copy in copies[2:]:
        copy.wait_recv()


def in_rows(count, step, run):
    def body(i, carry):
        run(pl.ds(pl.multiple_of(i * step, step), step))
        return carry

    lax.fori_loop(0, count // step, body, 0)


def ring_scatter_near(parts, came, send_sem, recv_sem):
    z, zp, z2, zm, up, down = ring_peers()
    copies = [
        remote(halves(parts, zp)[0], came.at[2], send_sem.at[2], recv_sem.at[2], up),
        remote(halves(parts, zm)[1], came.at[3], send_sem.at[3], recv_sem.at[3], down),
    ]
    for copy in copies:
        copy.start()
    return copies


def ring_scatter_far(parts, came, send_sem, recv_sem):
    z, zp, z2, zm, up, down = ring_peers()
    copies = [
        remote(halves(parts, z2)[1], came.at[0], send_sem.at[0], recv_sem.at[0], up),
        remote(halves(parts, z2)[0], came.at[1], send_sem.at[1], recv_sem.at[1], down),
    ]
    for copy in copies:
        copy.start()
    return copies


def ring_scatter_begin(parts, came, send_sem, recv_sem):
    far = ring_scatter_far(parts, came, send_sem, recv_sem)
    return far + ring_scatter_near(parts, came, send_sem, recv_sem)


def ring_scatter_forward(parts, came, sums, copies, send_sem, recv_sem):
    z, zp, z2, zm, up, down = ring_peers()
    count = came.shape[1]
    copies[0].wait_recv()

    def add_up(rows):
        sums[0, rows] = (
            came[0, rows].astype(jnp.float32)
            + parts[zp, pl.ds(pl.multiple_of(rows.start + count, 16), 16)].astype(jnp.float32)
        ).astype(jnp.bfloat16)

    in_rows(count, 16, add_up)
    on_up = remote(sums.at[0], came.at[4], send_sem.at[4], recv_sem.at[4], up)
    on_up.start()
    copies[1].wait_recv()

    def add_down(rows):
        sums[1, rows] = (
            came[1, rows].astype(jnp.float32) + parts[zm, rows].astype(jnp.float32)
        ).astype(jnp.bfloat16)

    in_rows(count, 16, add_down)
    on_down = remote(sums.at[1], came.at[5], send_sem.at[5], recv_sem.at[5], down)
    on_down.start()
    return copies + [on_up, on_down]


def ring_scatter_end(parts, came, total, copies):
    z, zp, z2, zm, up, down = ring_peers()
    count = came.shape[1]
    for copy in copies[2:]:
        copy.wait_recv()
    for copy in copies:
        copy.wait_send()

    def add(rows):
        later = pl.ds(pl.multiple_of(rows.start + count, 16), 16)
        total[rows] = (
            parts[z, rows].astype(jnp.float32)
            + came[2, rows].astype(jnp.float32)
            + came[5, rows].astype(jnp.float32)
        )
        total[later] = (
            parts[z, later].astype(jnp.float32)
            + came[3, rows].astype(jnp.float32)
            + came[4, rows].astype(jnp.float32)
        )

    in_rows(count, 16, add)


def plane():
    xh, y, core, xl, z = place()
    ys = [lax.rem(y + d, 4) for d in (1, 3, 2)]
    step = xh * 2 + xl
    xs = [lax.rem(step + d, 4) for d in (1, 3, 2)]
    xs = [(x // 2, lax.rem(x, 2)) for x in xs]
    y_peers = [device(xh, other, core, xl, z) for other in ys]
    x_peers = [device(h, y, core, l, z) for h, l in xs]
    return ys, xs, y_peers, x_peers, device(xh, y, 1 - core, xl, z)


class PlaneGather:
    def __init__(self, own, held, y_first, shared, send_sem, recv_sem):
        self.own, self.held, self.y_first, self.shared = own, held, y_first, shared
        self.send_sem, self.recv_sem, self.used = send_sem, recv_sem, 0
        self.copies, self.first, self.second, self.third = [], [], [], []

    def send(self, src, dst, peer):
        copy = remote(src, dst, self.send_sem.at[self.used], self.recv_sem.at[self.used], peer)
        self.used += 1
        copy.start()
        self.copies.append(copy)
        return copy

    def begin(self):
        xh, y, core, xl, z = place()
        ys, xs, y_peers, x_peers, other = plane()
        target = self.held.at[xh, y, core, xl]
        peers = y_peers if self.y_first else x_peers
        self.first = [self.send(self.own, target, peer) for peer in peers]

    def line(self, where):
        xh, y, core, xl, z = place()
        if self.y_first:
            return self.held.at[where[0], :, core, where[1]]
        return self.held.at[:, where, core, :]

    def spread(self):
        xh, y, core, xl, z = place()
        ys, xs, y_peers, x_peers, other = plane()
        for copy in self.first:
            copy.wait_recv()
        mine = self.line((xh, xl) if self.y_first else y)
        peers = x_peers if self.y_first else y_peers
        self.second = [self.send(mine, mine, peer) for peer in peers]
        self.third = [self.send(mine, mine, other)] if self.shared else []

    def share(self):
        ys, xs, y_peers, x_peers, other = plane()
        wheres = xs if self.y_first else ys
        for copy, where in zip(self.second, (wheres[1], wheres[0], wheres[2])):
            copy.wait_recv()
            line = self.line(where)
            self.third.append(self.send(line, line, other))

    def end(self):
        for copy in self.third if self.shared else self.second:
            copy.wait_recv()
        for copy in self.copies:
            copy.wait_send()


def swap_halves(block):
    lane = lax.broadcasted_iota(jnp.int32, block.shape, 1)
    return jnp.where(
        lane < HD // 2, pltpu.roll(block, 128 - HD // 2, 1), pltpu.roll(block, HD // 2, 1)
    )


def front_kernel(*refs):
    (hidden, cotangent, gain, m_in, m_expand, m_out, m_shrink) = refs[:7]
    (cos_ref, sin_ref, prefix) = refs[7:10]
    (first_to, shrunk_all, in_to, gate_all, up_all, out_all, shrink_all) = refs[10:17]
    (turned_to, rows_to, lines_to, attended, tokens, log_total, total) = refs[17:24]
    (first_all, shrunk, in_all, w_gate, w_up, w_out, w_shrink) = refs[24:31]
    (turned, kv_rows, kv_lines, key_cos, key_sin) = refs[31:36]
    (packed, held_rows, parts, came, sums) = refs[36:41]
    (ring_send, ring_recv, plane_send, plane_recv) = refs[41:45]
    (kv_send, kv_recv, own_sem, out_sem) = refs[45:]
    xh, y, core, xl, z = place()
    z, zp, z2, zm, up, down = ring_peers()
    ys, xs, y_peers, x_peers, other = plane()
    beside = device(xh, y, core, 1 - xl, z)
    peers = [up, down, other] + y_peers + x_peers
    hail(peers)
    low = jnp.bfloat16
    in_own = in_all.at[xh, y, core, xl]
    in_own[...] = m_in[...].astype(low)
    w_out[...] = m_out[...].astype(low)
    rows = hidden[...].astype(jnp.float32)
    scaling = lax.rsqrt(jnp.mean(rows * rows, axis=-1, keepdims=True) + EPS)
    first_all[z] = (rows * scaling * gain[...]).astype(low)
    meet(peers)
    owns = (in_own, w_out, w_gate, w_up, w_shrink)
    helds = (in_all, out_all, gate_all, up_all, shrink_all)
    gathers = [
        PlaneGather(own, held, i == 4, i < 2, plane_send.at[i], plane_recv.at[i])
        for i, (own, held) in enumerate(zip(owns, helds))
    ]
    for gather in gathers[:2]:
        gather.begin()
    ring = ring_gather_begin(first_all.at[z], first_all, ring_send.at[0], ring_recv.at[0])
    w_gate[...] = m_expand[0].astype(low)
    w_up[...] = m_expand[1].astype(low)
    w_shrink[...] = m_shrink[...].astype(low)
    shrunk[...] = (RESID * cotangent[...].astype(jnp.float32)).astype(low)
    keeps = [
        pltpu.make_async_copy(own, held.at[xh, y, core, xl], own_sem.at[i])
        for i, (own, held) in enumerate(zip(owns[1:], helds[1:]))
    ]
    keeps.append(pltpu.make_async_copy(shrunk, shrunk_all.at[z], own_sem.at[4]))
    for keep in keeps:
        keep.start()
    for keep in keeps:
        keep.wait()
    for gather in gathers[:2]:
        gather.spread()
    for gather in gathers[2:4]:
        gather.begin()
    key_tables(cos_ref, sin_ref, key_cos, key_sin)
    ring = ring_gather_forward(first_all, ring, ring_send.at[0], ring_recv.at[0])
    gathers[0].share()
    gathers[1].share()
    gathers[4].begin()
    for gather in gathers[2:4]:
        gather.spread()
    gathers[0].end()

    def project(c, rows):
        out = nn(first_all[c], in_all[...].reshape(1536, 640))
        packed[rows] = out
        for g in range(HEADS):
            block = out[:, g * 320 + 192 : g * 320 + 320]
            mine = pl.ds(pl.multiple_of(xl * 896 + c * 224, 16), 224)
            kv_rows[g, mine] = (
                block * key_cos[rows] + swap_halves(block) * key_sin[rows]
            ).astype(low)

    kv_copies = []
    for i, c in enumerate((z, zm, zp, z2)):
        if i == 1:
            ring[2].wait_recv()
        if i == 2:
            ring[3].wait_recv()
        if i == 3:
            ring[4].wait_recv()
            ring[5].wait_recv()
        project(c, pl.ds(pl.multiple_of(c * 224, 16), 224))
        mine = kv_rows.at[:, pl.ds(pl.multiple_of(xl * 896 + c * 224, 16), 224)]
        kv_copies.append(remote(mine, mine, kv_send.at[i], kv_recv.at[i], beside))
        kv_copies[-1].start()
    later = ring_gather_begin(shrunk, shrunk_all, ring_send.at[1], ring_recv.at[1])
    saves = []

    def save(src, dst):
        saves.append(pltpu.make_async_copy(src, dst, own_sem.at[5 + len(saves)]))
        saves[-1].start()

    save(first_all, first_to)
    save(in_all, in_to)

    def turn_block(b, carry):
        columns = pl.ds(pl.multiple_of(b * 128, 128), 128)
        lines = jnp.transpose(packed[columns])
        cos_here, sin_here = cos_ref[:, columns], sin_ref[:, columns]
        for g in range(HEADS):
            for h in range(GROUP):
                at = (g * 5 + h) * HD
                turned[(g * GROUP + h) * HD : (g * GROUP + h + 1) * HD, columns] = (
                    turn(lines[at : at + HD], cos_here, sin_here) * HD ** (-0.5)
                ).astype(low)
        return carry

    lax.fori_loop(0, BLOCKS, turn_block, 0)
    save(turned, turned_to)
    for copy in kv_copies:
        copy.wait_recv()
    gathers[4].spread()
    for g in range(HEADS):
        kv_lines[g] = jnp.transpose(kv_rows[g].astype(jnp.float32)).astype(low)
    save(kv_rows, rows_to)
    save(kv_lines, lines_to)

    def block(b, g):
        columns = pl.ds(pl.multiple_of(b * 128, 128), 128)

        def run(span):
            head_rows = [
                pl.ds(pl.multiple_of((g * GROUP + h) * HD, HD), HD) for h in range(GROUP)
            ]
            queries = jnp.concatenate([turned[r, columns] for r in head_rows], axis=1)
            queries = jnp.concatenate([queries, jnp.zeros_like(queries)], axis=0)
            scores = nn(kv_rows[g, :span], queries)
            key_index = lax.broadcasted_iota(jnp.int32, (span, 384), 0)
            scores = jnp.where(key_index < limits(prefix, xl, b), scores, NEG)
            row_max = jnp.max(scores, axis=0, keepdims=True)
            shifted = jnp.exp(scores - row_max)
            exp_total = jnp.sum(shifted, axis=0, keepdims=True)
            out = nn(kv_lines[g, HD:, :span], shifted.astype(low)) * (1.0 / exp_total)
            for h in range(GROUP):
                attended[head_rows[h], columns] = out[:, h * 128 : (h + 1) * 128].astype(low)
            log_total[b * HEADS + g] = row_max + jnp.log(exp_total)

        by_span(xl, b, run)

    def near_heads(t, carry):
        block(arrival(z, lax.div(t, 2)), lax.rem(t, 2))
        return carry

    def far_heads(t, carry):
        block(arrival_far(z, lax.div(t, 2)), lax.rem(t, 2))
        return carry

    def beside_block(g, carry):
        block(arrival(z, 1), g)
        return carry

    def own_block(g, carry):
        block(2 * z, g)
        return carry

    def lay(b):
        columns = pl.ds(pl.multiple_of(b * 128, 128), 128)
        tokens[columns] = jnp.transpose(attended[:, columns].astype(jnp.float32)).astype(low)

    def apply(c):
        mine = pl.ds(pl.multiple_of(c * 224, 16), 224)
        parts[c] = nt(tokens[mine], held_rows[...].reshape(1536, 384)).astype(low)

    lax.fori_loop(8, 14, far_heads, 0)
    later = ring_gather_forward(shrunk_all, later, ring_send.at[1], ring_recv.at[1])
    gathers[1].end()
    fetch = pltpu.make_async_copy(out_all, held_rows, out_sem)
    fetch.start()
    for i in range(4, 7):
        lay(arrival(z, i))
    fetch.wait()
    apply(z2)
    far = ring_scatter_far(parts, came, ring_send.at[2], ring_recv.at[2])
    lax.fori_loop(0, 2, beside_block, 0)
    lax.fori_loop(4, 8, near_heads, 0)
    for i in range(1, 4):
        lay(arrival(z, i))
    apply(zp)
    apply(zm)
    near = ring_scatter_near(parts, came, ring_send.at[2], ring_recv.at[2])
    scatter = ring_scatter_forward(
        parts, came, sums, far + near, ring_send.at[2], ring_recv.at[2]
    )
    lax.fori_loop(0, 2, own_block, 0)
    lay(2 * z)
    apply(z)
    for gather in gathers[2:]:
        gather.end()
    ring_gather_end(later)
    for copy in kv_copies + ring:
        copy.wait_send()
    for copy in saves:
        copy.wait()
    ring_scatter_end(parts, came, total, scatter)


def front(hidden, cotangent, gain, weights, tables, prefix):
    any_place = pl.BlockSpec(memory_space=pl.ANY)
    whole = pl.BlockSpec(memory_space=pltpu.VMEM)
    rows, width = hidden.shape
    low, full = jnp.bfloat16, jnp.float32
    block = (2, 4, 2, 2, 48)
    first_shape, in_shape = (4, rows, width), block + (640,)
    turned_shape, rows_shape, lines_shape = (384, 896), (HEADS, 1792, 128), (HEADS, 128, 1792)
    kept = (first_shape, (4, rows, width), in_shape) + (block + (960,),) * 2
    kept += (block + (384,), block + (960,), turned_shape, rows_shape, lines_shape)
    outs = pl.pallas_call(
        front_kernel,
        out_shape=(
            *(jax.ShapeDtypeStruct(shape, low) for shape in kept),
            jax.ShapeDtypeStruct((384, 896), low),
            jax.ShapeDtypeStruct((896, 384), low),
            jax.ShapeDtypeStruct((HEADS * BLOCKS, 1, 384), full),
            jax.ShapeDtypeStruct((rows, width), full),
        ),
        in_specs=[whole] * 9 + [pl.BlockSpec(memory_space=pltpu.SMEM)],
        out_specs=(any_place,) * 10 + (whole,) * 4,
        scratch_shapes=[
            pltpu.VMEM(first_shape, low),
            pltpu.VMEM((rows, width), low),
            pltpu.VMEM(in_shape, low),
            pltpu.VMEM((48, 960), low),
            pltpu.VMEM((48, 960), low),
            pltpu.VMEM((48, 384), low),
            pltpu.VMEM((48, 960), low),
            pltpu.VMEM(turned_shape, low),
            pltpu.VMEM(rows_shape, low),
            pltpu.VMEM(lines_shape, low),
            pltpu.VMEM((896, 128), full),
            pltpu.VMEM((896, 128), full),
            pltpu.VMEM((896, 640), full),
            pltpu.VMEM(block + (384,), low),
            pltpu.VMEM((4, rows, width), low),
            pltpu.VMEM((6, rows // 2, width), low),
            pltpu.VMEM((2, rows // 2, width), low),
            pltpu.SemaphoreType.DMA((3, 6)),
            pltpu.SemaphoreType.DMA((3, 6)),
            pltpu.SemaphoreType.DMA((5, 10)),
            pltpu.SemaphoreType.DMA((5, 10)),
            pltpu.SemaphoreType.DMA((4,)),
            pltpu.SemaphoreType.DMA((4,)),
            pltpu.SemaphoreType.DMA((10,)),
            pltpu.SemaphoreType.DMA,
        ],
        compiler_params=pltpu.CompilerParams(
            collective_id=0, has_side_effects=True, vmem_limit_bytes=VMEM_MOST
        ),
    )(hidden, cotangent, gain, *weights, *tables, prefix)
    return outs


def tn(a, b):
    return lax.dot_general(a, b, (((0,), (0,)), ((), ())), preferred_element_type=jnp.float32)


def middle_kernel(*refs):
    (hidden, cotangent, projected, gain) = refs[:4]
    (shrunk_from, gate_from, up_from, shrink_from) = refs[4:8]
    (residual, grad_residual, turned_back, gain_two) = refs[8:12]
    (gate_to, up_to, shrink_to, out_to) = refs[12:16]
    (shrunk_all, w_gate, w_up, w_shrink) = refs[16:20]
    (second_all, activated_back, gated, gate_back, up_back) = refs[20:25]
    (parts, came, sums, total) = refs[25:29]
    (grad_gate, grad_up, grad_shrink, out_parts) = refs[29:33]
    (ring_send, ring_recv, load_sem, share_send, share_recv) = refs[33:]
    z, zp, z2, zm, up, down = ring_peers()
    xh, y, core, xl, z = place()

    def flat(weight):
        return weight[...].reshape(1536, 960)

    other = device(xh, y, 1 - core, xl, z)
    hail([up, down, other])
    loads = [
        pltpu.make_async_copy(src, dst, load_sem.at[i])
        for i, (src, dst) in enumerate(
            (
                (shrink_from.at[:, :, core], w_shrink.at[:, :, core]),
                (shrunk_from, shrunk_all),
                (gate_from.at[:, :, core], w_gate.at[:, :, core]),
                (up_from.at[:, :, core], w_up.at[:, :, core]),
            )
        )
    ]
    for load in loads:
        load.start()
    rows = hidden[...].astype(jnp.float32) + RESID * projected[...]
    residual[...] = rows
    scaling = lax.rsqrt(jnp.mean(rows * rows, axis=-1, keepdims=True) + EPS)
    second_all[z] = (rows * scaling * gain[...]).astype(jnp.bfloat16)
    meet([up, down, other])
    ring = ring_gather_begin(second_all.at[z], second_all, ring_send.at[0], ring_recv.at[0])
    shares = [
        remote(
            src.at[:, :, core], dst.at[:, :, core], share_send.at[i], share_recv.at[i], other
        )
        for i, (src, dst) in enumerate(
            ((shrink_from, w_shrink), (gate_from, w_gate), (up_from, w_up))
        )
    ]
    for share in shares:
        share.start()
    loads[0].wait()
    loads[1].wait()
    shares[0].wait_recv()
    for c in range(4):
        activated_back[c] = nn(shrunk_all[c], flat(w_shrink))
    loads[2].wait()
    loads[3].wait()
    shares[1].wait_recv()
    shares[2].wait_recv()

    def feed(c):
        gate_value = nn(second_all[c], flat(w_gate))
        up_value = nn(second_all[c], flat(w_up))
        sigmoid_gate = 1.0 / (1.0 + jnp.exp(-gate_value))
        gate_active = gate_value * sigmoid_gate
        gated[c] = (gate_active * up_value).astype(jnp.bfloat16)
        gradient = activated_back[c]
        gate_back[c] = (
            gradient * up_value * sigmoid_gate * (1.0 + gate_value * (1.0 - sigmoid_gate))
        ).astype(jnp.bfloat16)
        up_back[c] = (gradient * gate_active).astype(jnp.bfloat16)
        parts[c] = (nt(gate_back[c], flat(w_gate)) + nt(up_back[c], flat(w_up))).astype(
            jnp.bfloat16
        )

    feed(z)
    ring = ring_gather_forward(second_all, ring, ring_send.at[0], ring_recv.at[0])
    ring[2].wait_recv()
    feed(zm)
    ring[3].wait_recv()
    feed(zp)
    near = ring_scatter_near(parts, came, ring_send.at[1], ring_recv.at[1])
    ring[4].wait_recv()
    ring[5].wait_recv()
    feed(z2)
    far = ring_scatter_far(parts, came, ring_send.at[1], ring_recv.at[1])
    second_rows = second_all[...].reshape(896, 1536)
    saves = []

    def save(src, dst):
        saves.append(pltpu.make_async_copy(src, dst, load_sem.at[4 + len(saves)]))
        saves[-1].start()

    grad_gate[...] = tn(second_rows, gate_back[...].reshape(896, 960)).astype(jnp.bfloat16)
    save(grad_gate, gate_to)
    scatter = ring_scatter_forward(
        parts, came, sums, far + near, ring_send.at[1], ring_recv.at[1]
    )
    grad_up[...] = tn(second_rows, up_back[...].reshape(896, 960)).astype(jnp.bfloat16)
    save(grad_up, up_to)
    grad_shrink[...] = tn(
        shrunk_all[...].reshape(896, 1536), gated[...].reshape(896, 960)
    ).astype(jnp.bfloat16)
    save(grad_shrink, shrink_to)
    for c in range(4):
        out_parts[c] = nt(gated[c], flat(w_shrink)).astype(jnp.bfloat16)
    save(out_parts, out_to)
    for copy in ring + shares:
        copy.wait_send()
    ring_scatter_end(parts, came, total, scatter)
    rows = residual[...]
    scaling = lax.rsqrt(jnp.mean(rows * rows, axis=-1, keepdims=True) + EPS)
    normed = rows * scaling
    gradient = total[...]
    gain_two[...] = jnp.sum(gradient * normed, axis=0, keepdims=True)
    gradient = gradient * gain[...]
    back = cotangent[...].astype(jnp.float32) + scaling * (
        gradient - normed * jnp.mean(gradient * normed, axis=-1, keepdims=True)
    )
    grad_residual[...] = back
    turned_back[...] = (RESID * back).astype(jnp.bfloat16)
    for copy in saves:
        copy.wait()


def middle(hidden, cotangent, projected, gain, shrunk_all, w_gate, w_up, w_shrink):
    any_place = pl.BlockSpec(memory_space=pl.ANY)
    whole = pl.BlockSpec(memory_space=pltpu.VMEM)
    rows, width = hidden.shape
    low, full = jnp.bfloat16, jnp.float32
    return pl.pallas_call(
        middle_kernel,
        out_shape=(
            jax.ShapeDtypeStruct((rows, width), full),
            jax.ShapeDtypeStruct((rows, width), full),
            jax.ShapeDtypeStruct((rows, width), low),
            jax.ShapeDtypeStruct((1, width), full),
            jax.ShapeDtypeStruct((1536, 960), low),
            jax.ShapeDtypeStruct((1536, 960), low),
            jax.ShapeDtypeStruct((1536, 960), low),
            jax.ShapeDtypeStruct((4, rows, width), low),
        ),
        in_specs=[whole] * 4 + [any_place] * 4,
        out_specs=(whole,) * 4 + (any_place,) * 4,
        scratch_shapes=[
            pltpu.VMEM((4, rows, width), low),
            pltpu.VMEM((2, 4, 2, 2, 48, 960), low),
            pltpu.VMEM((2, 4, 2, 2, 48, 960), low),
            pltpu.VMEM((2, 4, 2, 2, 48, 960), low),
            pltpu.VMEM((4, rows, width), low),
            pltpu.VMEM((4, rows, 960), full),
            pltpu.VMEM((4, rows, 960), low),
            pltpu.VMEM((4, rows, 960), low),
            pltpu.VMEM((4, rows, 960), low),
            pltpu.VMEM((4, rows, width), low),
            pltpu.VMEM((6, rows // 2, width), low),
            pltpu.VMEM((2, rows // 2, width), low),
            pltpu.VMEM((rows, width), full),
            pltpu.VMEM((1536, 960), low),
            pltpu.VMEM((1536, 960), low),
            pltpu.VMEM((1536, 960), low),
            pltpu.VMEM((4, rows, width), low),
            pltpu.SemaphoreType.DMA((2, 6)),
            pltpu.SemaphoreType.DMA((2, 6)),
            pltpu.SemaphoreType.DMA((8,)),
            pltpu.SemaphoreType.DMA((3,)),
            pltpu.SemaphoreType.DMA((3,)),
        ],
        compiler_params=pltpu.CompilerParams(
            collective_id=4, has_side_effects=True, vmem_limit_bytes=VMEM_MOST
        ),
    )(hidden, cotangent, projected, gain, shrunk_all, w_gate, w_up, w_shrink)


class Scatter:
    def __init__(self, parts, came, across, lined, last, x_first, send_sem, recv_sem):
        self.parts, self.came, self.across = parts, came, across
        self.lined, self.last, self.x_first = lined, last, x_first
        self.send_sem, self.recv_sem, self.used, self.copies = send_sem, recv_sem, 0, []
        xh, y, core, xl, z = place()
        ys, xs, y_peers, x_peers, self.other = plane()
        if x_first:
            self.lines, self.peers = xs[::-1] + [(xh, xl)], x_peers[::-1]
            self.mine, self.targets, self.target_peers = y, ys, y_peers
        else:
            self.lines, self.peers = ys[::-1] + [y], y_peers[::-1]
            self.mine, self.targets, self.target_peers = (xh, xl), xs, x_peers

    def send(self, src, dst, peer):
        copy = remote(src, dst, self.send_sem.at[self.used], self.recv_sem.at[self.used], peer)
        self.used += 1
        copy.start()
        self.copies.append(copy)
        return copy

    def in_line(self, line):
        return (line[0], slice(None), line[1]) if self.x_first else (slice(None), line)

    def begin(self):
        core = place()[2]
        self.first = []
        for line in self.lines:
            if self.x_first:
                src = self.parts.at[line[0], :, 1 - core, line[1]]
            else:
                src = self.parts.at[:, line, 1 - core]
            self.first.append(self.send(src, self.came.at[self.in_line(line)], self.other))

    def stage(self, held, sem):
        copy = pltpu.make_async_copy(self.parts.at[:, :, place()[2]], held, sem)
        copy.start()
        return copy

    def at(self, line, i):
        return (line[0], i, line[1]) if self.x_first else (i // 2, line, lax.rem(i, 2))

    def spot(self, i):
        if self.x_first:
            return (i,)
        return (i[0], i[1]) if isinstance(i, tuple) else (i // 2, lax.rem(i, 2))

    def fold(self, held=None):
        core = place()[2]
        self.second = []
        for k, (line, copy) in enumerate(zip(self.lines, self.first)):
            copy.wait_recv()

            def add(i, carry, line=line):
                at = self.at(line, i)
                if held is None:
                    own = self.parts[at[0], at[1], core, at[2]]
                else:
                    own = held[at]
                self.came[at] = (
                    own.astype(jnp.float32) + self.came[at].astype(jnp.float32)
                ).astype(jnp.bfloat16)
                return carry

            lax.fori_loop(0, 4, add, 0)
            if k < 3:
                self.second.append(
                    self.send(
                        self.came.at[self.in_line(line)], self.across.at[k], self.peers[k]
                    )
                )

    def line(self):
        for copy in self.second:
            copy.wait_recv()

        def add(i, carry):
            spot = self.spot(i)
            total = self.came[self.at(self.lines[3], i)].astype(jnp.float32)
            for k in range(3):
                total = total + self.across[(k,) + spot].astype(jnp.float32)
            self.lined[spot] = total.astype(jnp.bfloat16)
            return carry

        lax.fori_loop(0, 4, add, 0)
        self.third = [
            self.send(self.lined.at[self.spot(target)], self.last.at[k], peer)
            for k, (target, peer) in enumerate(zip(self.targets, self.target_peers))
        ]

    def end(self, total_ref):
        for copy in self.third:
            copy.wait_recv()
        total = self.lined[self.spot(self.mine)].astype(jnp.float32)
        for k in range(3):
            total = total + self.last[k].astype(jnp.float32)
        total_ref[...] = total
        for copy in self.copies:
            copy.wait_send()


def scatter_room(width, x_first):
    line = (4,) if x_first else (2, 2)
    return [
        pltpu.VMEM((2, 4, 2, 48, width), jnp.bfloat16),
        pltpu.VMEM((3,) + line + (48, width), jnp.bfloat16),
        pltpu.VMEM(line + (48, width), jnp.bfloat16),
        pltpu.VMEM((3, 48, width), jnp.bfloat16),
    ]


def back_kernel(*refs):
    (own, out_from, in_from, first_from, out_terms) = refs[:5]
    gradients = refs[5:8]
    (turned, kv_rows, kv_lines, attended, tokens, log_total) = refs[8:14]
    (cos_ref, sin_ref, hidden, gain_two, prefix) = refs[14:19]
    (shrunk_total, first_total) = refs[19:21]
    totals = refs[21:26]
    everywhere = refs[26]
    (proj_all, w_out, w_in, grad_tokens, grad_lines, grad_queries, grad_packed) = refs[27:34]
    (sums, outgoing, incoming, parts, came_one, came_two, ring_sums) = refs[34:41]
    stages, out_parts, in_parts = refs[41:43], refs[43], refs[44]
    rooms = refs[45:65]
    (key_cos, key_sin, gathered) = refs[65:68]
    (ring_send, ring_recv, plane_send, plane_recv, kv_send, kv_recv, load_sem) = refs[68:75]
    (sum_send, sum_recv) = refs[75:]
    xh, y, core, xl, z = place()
    z, zp, z2, zm, up, down = ring_peers()
    ys, xs, y_peers, x_peers, other = plane()
    beside = device(xh, y, core, 1 - xl, z)
    column = [
        device(xh, y, c, xl, lax.rem(z + d, 4))
        for d, c in ((1, core), (3, core), (0, 1 - core), (2, core))
        + ((1, 1 - core), (3, 1 - core), (2, 1 - core))
    ]
    peers = column + y_peers + x_peers
    hail(peers)
    sums[...] = jnp.zeros_like(sums)
    key_tables(cos_ref, sin_ref, key_cos, key_sin)
    meet(peers)
    ring = ring_gather_begin(own, proj_all, ring_send.at[0], ring_recv.at[0])
    every = [
        Scatter(
            terms,
            *rooms[4 * i : 4 * i + 4],
            SCATTER_TURNS[i],
            plane_send.at[i],
            plane_recv.at[i],
        )
        for i, terms in enumerate(tuple(gradients) + (out_parts, in_parts))
    ]
    feed, out_scatter, in_scatter = every[:3], every[3], every[4]
    for scatter in feed:
        scatter.begin()

    def load(src, dst, i):
        copy = pltpu.make_async_copy(src, dst, load_sem.at[i])
        copy.start()
        return copy

    load_out = load(out_from, w_out, 0)
    keep = load(own, proj_all.at[z], 1)
    staged = [feed[i].stage(stages[i], load_sem.at[2 + i]) for i in range(2)]
    load_terms = load(out_terms, parts, 5)
    load_in = load(in_from, w_in, 6)

    def give(c, start=0, count=224):
        rows = pl.ds(pl.multiple_of(c * 224 + start, 16), count)
        grad_tokens[rows] = nn(proj_all[c, start : start + count], w_out[...]).astype(
            jnp.bfloat16
        )

    def lay(b):
        columns = pl.ds(pl.multiple_of(b * 128, 128), 128)
        grad_lines[:, columns] = jnp.transpose(
            grad_tokens[columns].astype(jnp.float32)
        ).astype(jnp.bfloat16)

    def block(b, g):
        columns = pl.ds(pl.multiple_of(b * 128, 128), 128)

        def run(span):
            head_rows = [
                pl.ds(pl.multiple_of((g * GROUP + h) * HD, HD), HD) for h in range(GROUP)
            ]
            queries = jnp.concatenate([turned[r, columns] for r in head_rows], axis=1)
            gradient = jnp.concatenate([grad_lines[r, columns] for r in head_rows], axis=1)
            held = jnp.concatenate([attended[r, columns] for r in head_rows], axis=1)
            inner = jnp.sum(
                gradient.astype(jnp.float32) * held.astype(jnp.float32), axis=0, keepdims=True
            )
            nothing = jnp.zeros_like(queries)
            both = jnp.concatenate(
                [
                    jnp.concatenate([queries, nothing], axis=1),
                    jnp.concatenate([nothing, gradient], axis=1),
                ],
                axis=0,
            )
            products = nn(kv_rows[g, :span], both)
            key_index = lax.broadcasted_iota(jnp.int32, (span, 384), 0)
            probs = jnp.exp(
                jnp.where(key_index < limits(prefix, xl, b), products[:, :384], NEG)
                - log_total[b * HEADS + g]
            )
            grad_scores = (probs * (products[:, 384:] - inner)).astype(jnp.bfloat16)
            sums[g, :span] += nt(
                jnp.concatenate([grad_scores, probs.astype(jnp.bfloat16)], axis=1), both
            )
            total = nn(kv_lines[g, :HD, :span], grad_scores) * HD ** (-0.5)
            cos_here, sin_here = cos_ref[:, columns], sin_ref[:, columns]
            back = [
                turn_back(total[:, h * 128 : (h + 1) * 128], cos_here, sin_here)
                for h in range(GROUP)
            ]
            grad_queries[g, columns] = jnp.transpose(jnp.concatenate(back, axis=0)).astype(
                jnp.bfloat16
            )

        by_span(xl, b, run)

    def both_heads(t, carry):
        block(arrival(z, lax.div(t, 2)), lax.rem(t, 2))
        return carry

    keep.wait()
    load_out.wait()
    give(z)
    lay(2 * z)

    def own_block(g, carry):
        block(2 * z, g)
        return carry

    lax.fori_loop(0, 2, own_block, 0)
    ring = ring_gather_forward(proj_all, ring, ring_send.at[0], ring_recv.at[0])
    give(zm, 112, 112)
    give(zp, 0, 112)
    lay(arrival(z, 1))

    def beside_block(g, carry):
        block(arrival(z, 1), g)
        return carry

    staged[0].wait()
    feed[0].fold(stages[0])
    staged[0] = feed[2].stage(stages[0], load_sem.at[4])
    staged[1].wait()
    feed[1].fold(stages[1])
    staged[0].wait()
    feed[2].fold(stages[0])
    lax.fori_loop(0, 2, beside_block, 0)
    ring[2].wait_recv()
    give(zm, 0, 112)
    ring[3].wait_recv()
    give(zp, 112, 112)
    for i in range(2, 4):
        lay(arrival(z, i))
    lax.fori_loop(4, 8, both_heads, 0)
    ring[4].wait_recv()
    ring[5].wait_recv()
    give(z2)
    for i in range(4, 7):
        lay(arrival(z, i))
    for copy in ring:
        copy.wait_send()
    out_parts[...] = (
        tn(proj_all[...].reshape(896, 1536), tokens[...])
        .astype(jnp.bfloat16)
        .reshape(2, 4, 2, 2, 48, 384)
    )
    out_scatter.begin()
    load_first = load(first_from, proj_all, 7)
    load_terms.wait()
    shrunk = ring_scatter_begin(parts, came_one, ring_send.at[1], ring_recv.at[1])

    def exchange(g):
        theirs = sums[g, pl.ds(pl.multiple_of((1 - xl) * 896, 128), 896)]
        outgoing[g] = theirs.astype(jnp.bfloat16)
        copy = remote(outgoing.at[g], incoming.at[g], kv_send.at[g], kv_recv.at[g], beside)
        copy.start()
        return copy

    def far_block(g):
        def body(i, carry):
            block(arrival_far(z, i), g)
            return carry

        lax.fori_loop(4, 7, body, 0)

    far_block(0)
    kv_copies = [exchange(0)]
    shrunk = ring_scatter_forward(
        parts, came_one, ring_sums, shrunk, ring_send.at[1], ring_recv.at[1]
    )
    out_scatter.fold()
    far_block(1)
    kv_copies.append(exchange(1))
    for scatter in feed:
        scatter.line()
    out_scatter.line()
    load_in.wait()
    load_first.wait()
    ring_scatter_end(parts, came_one, shrunk_total, shrunk)
    for g in range(HEADS):
        kv_copies[g].wait()
        mine = sums[g, pl.ds(pl.multiple_of(xl * 896, 128), 896)] + incoming[g].astype(
            jnp.float32
        )
        mine = mine * key_cos[...] - swap_halves(mine) * key_sin[...]
        grad_packed[:, g * 320 : g * 320 + 192] = grad_queries[g]
        grad_packed[:, g * 320 + 192 : g * 320 + 320] = mine.astype(jnp.bfloat16)

    def spread(c):
        rows = pl.ds(pl.multiple_of(c * 224, 16), 224)
        parts[c] = nt(grad_packed[rows], w_in[...]).astype(jnp.bfloat16)

    spread(z2)
    far = ring_scatter_far(parts, came_two, ring_send.at[2], ring_recv.at[2])
    spread(zp)
    spread(zm)
    near = ring_scatter_near(parts, came_two, ring_send.at[2], ring_recv.at[2])
    in_parts[...] = (
        tn(proj_all[...].reshape(896, 1536), grad_packed[...])
        .astype(jnp.bfloat16)
        .reshape(2, 4, 2, 2, 48, 640)
    )
    in_scatter.begin()
    spread(z)
    in_scatter.fold()
    ring = ring_scatter_forward(
        parts, came_two, ring_sums, far + near, ring_send.at[2], ring_recv.at[2]
    )
    for i in range(4):
        every[i].end(totals[i])
    in_scatter.line()
    ring_scatter_end(parts, came_two, first_total, ring)
    rows = hidden[...].astype(jnp.float32)
    scaling = lax.rsqrt(jnp.mean(rows * rows, axis=-1, keepdims=True) + EPS)
    gain_one = jnp.sum(first_total[...] * rows * scaling, axis=0, keepdims=True)
    in_scatter.end(totals[4])
    squares = jnp.zeros((1, 1), jnp.float32)
    for total in totals:
        terms = total[...]
        squares = squares + jnp.sum(
            jnp.sum(terms * terms, axis=0, keepdims=True), axis=1, keepdims=True
        )
    for k in range(3):
        everywhere[k : k + 1] = gain_one[:, k * 512 : (k + 1) * 512]
        everywhere[3 + k : 4 + k] = gain_two[:, k * 512 : (k + 1) * 512]
    everywhere[6:8] = jnp.broadcast_to(squares, (2, 512))
    used = 0
    groups = ((column, z * 2 + core, 8), (x_peers, xh * 2 + xl, 4), (y_peers, y, 4))
    for axis, (group, here, count) in enumerate(groups):
        gathered[axis, here] = everywhere[...]
        spot = gathered.at[axis, here]
        copies = []
        for peer in group:
            copies.append(remote(spot, spot, sum_send.at[used], sum_recv.at[used], peer))
            copies[-1].start()
            used += 1
        for copy in copies:
            copy.wait()
        order = gathered[axis, 0]
        for k in range(1, count):
            order = order + gathered[axis, k]
        everywhere[...] = order


SCATTER_TURNS = (False, False, True, True, False)


def back(
    own, w_out, w_in, first_all, out_terms, gradients, saved, tables, hidden, gain_two, prefix
):
    any_place = pl.BlockSpec(memory_space=pl.ANY)
    whole = pl.BlockSpec(memory_space=pltpu.VMEM)
    rows, width = own.shape
    low, full = jnp.bfloat16, jnp.float32
    widths = [g.shape[-1] for g in gradients] + [384, 640]
    rooms = []
    for w, turn_first in zip(widths, SCATTER_TURNS):
        rooms += scatter_room(w, turn_first)
    return pl.pallas_call(
        back_kernel,
        out_shape=(jax.ShapeDtypeStruct((rows, width), full),) * 2
        + tuple(jax.ShapeDtypeStruct((48, w), full) for w in widths)
        + (jax.ShapeDtypeStruct((8, 512), full),),
        in_specs=[whole]
        + [any_place] * 7
        + [whole] * 10
        + [pl.BlockSpec(memory_space=pltpu.SMEM)],
        out_specs=(whole,) * 8,
        scratch_shapes=[
            pltpu.VMEM((4, rows, width), low),
            pltpu.VMEM((1536, 384), low),
            pltpu.VMEM((1536, 640), low),
            pltpu.VMEM((896, 384), low),
            pltpu.VMEM((384, 896), low),
            pltpu.VMEM((HEADS, 896, 192), low),
            pltpu.VMEM((896, 640), low),
            pltpu.VMEM((HEADS, 1792, 128), full),
            pltpu.VMEM((HEADS, 896, 128), low),
            pltpu.VMEM((HEADS, 896, 128), low),
            pltpu.VMEM((4, rows, width), low),
            pltpu.VMEM((6, rows // 2, width), low),
            pltpu.VMEM((6, rows // 2, width), low),
            pltpu.VMEM((2, rows // 2, width), low),
            pltpu.VMEM((2, 4, 2, 48, 960), low),
            pltpu.VMEM((2, 4, 2, 48, 960), low),
            pltpu.VMEM((2, 4, 2, 2, 48, 384), low),
            pltpu.VMEM((2, 4, 2, 2, 48, 640), low),
            *rooms,
            pltpu.VMEM((896, 128), full),
            pltpu.VMEM((896, 128), full),
            pltpu.VMEM((3, 8, 8, 512), full),
            pltpu.SemaphoreType.DMA((3, 6)),
            pltpu.SemaphoreType.DMA((3, 6)),
            pltpu.SemaphoreType.DMA((5, 10)),
            pltpu.SemaphoreType.DMA((5, 10)),
            pltpu.SemaphoreType.DMA((2,)),
            pltpu.SemaphoreType.DMA((2,)),
            pltpu.SemaphoreType.DMA((8,)),
            pltpu.SemaphoreType.DMA((13,)),
            pltpu.SemaphoreType.DMA((13,)),
        ],
        compiler_params=pltpu.CompilerParams(
            collective_id=2, has_side_effects=True, vmem_limit_bytes=BACK_VMEM
        ),
    )(
        own,
        w_out,
        w_in,
        first_all,
        out_terms,
        *(g.reshape(2, 4, 2, 2, 48, g.shape[-1]) for g in gradients),
        *saved,
        *tables,
        hidden,
        gain_two,
        prefix,
    )


BACK_VMEM = 63 * 2**20


def finish_kernel(*refs):
    (sums, grad_first, hidden, grad_residual, residual, shrunk) = refs[:6]
    (gains, gains_first, gains_second) = refs[6:9]
    (grad_gate, grad_up, grad_shrink, grad_output, grad_input) = refs[9:14]
    masters = [refs[14 + 3 * i : 17 + 3 * i] for i in range(4)]
    (block_output, input_gradient, norm_ref) = refs[26:29]
    gains_new = refs[29:32]
    news = [refs[32 + 3 * i : 35 + 3 * i] for i in range(4)]
    block_output[...] = (residual[...] + RESID * shrunk[...]).astype(jnp.bfloat16)
    rows = hidden[...].astype(jnp.float32)
    scaling = lax.rsqrt(jnp.mean(rows * rows, axis=-1, keepdims=True) + EPS)
    normed = rows * scaling
    gradient = grad_first[...] * gains[0:1]
    input_gradient[...] = grad_residual[...] + scaling * (
        gradient - normed * jnp.mean(gradient * normed, axis=-1, keepdims=True)
    )
    grad_gains = jnp.concatenate(
        [
            jnp.concatenate([sums[3 * r + k : 3 * r + k + 1] for k in range(3)], axis=1)
            for r in range(2)
        ],
        axis=0,
    )
    gain_squares = jnp.sum(
        jnp.sum(grad_gains * grad_gains, axis=0, keepdims=True), axis=1, keepdims=True
    )
    gradient_norm = jnp.sqrt(sums[6:7, 0:1] + gain_squares)
    norm_ref[...] = gradient_norm
    factor = jnp.minimum(1.0, MAX_NORM / (gradient_norm + 1e-06))

    def put(targets, results):
        for target, result in zip(targets, results):
            target[...] = result

    put(
        gains_new,
        adamw(
            gains[...], factor * grad_gains, gains_first[...], gains_second[...], GAIN_RATE, 0.0
        ),
    )
    for i, terms in ((0, grad_input), (1, grad_output), (3, grad_shrink)):
        weight, first, second = masters[i]
        put(news[i], adamw(weight[...], factor * terms[...], first[...], second[...], RATE, DECAY))
    for k, terms in enumerate((grad_gate, grad_up)):
        weight, first, second = masters[2]
        results = adamw(weight[k], factor * terms[...], first[k], second[k], RATE, DECAY)
        for target, result in zip(news[2], results):
            target[k] = result


def finish(sums, rows_in, gains, gradients, masters):
    full = jnp.float32
    flat = [array for group in masters for array in group]

    def cut(array):
        shape = array.shape[:-2] + (array.shape[-2] // 2, array.shape[-1])
        lead = (0,) * (array.ndim - 2)
        return pl.BlockSpec(shape, lambda i: lead + (i, 0))

    def kept(shape):
        return pl.BlockSpec(shape, lambda i: (0, 0))

    width = rows_in[0].shape[1]
    rows = jax.ShapeDtypeStruct(rows_in[0].shape, full)
    return pl.pallas_call(
        finish_kernel,
        grid=(2,),
        out_shape=(
            jax.ShapeDtypeStruct(rows.shape, jnp.bfloat16),
            rows,
            jax.ShapeDtypeStruct((1, 1), full),
            *(jax.ShapeDtypeStruct((2, width), full) for _ in range(3)),
            *(jax.ShapeDtypeStruct(array.shape, full) for array in flat),
        ),
        in_specs=[kept(sums.shape)]
        + [cut(array) for array in rows_in]
        + [kept(array.shape) for array in gains]
        + [cut(array) for array in gradients]
        + [cut(array) for array in flat],
        out_specs=(cut(rows), cut(rows), kept((1, 1)))
        + (kept((2, width)),) * 3
        + tuple(cut(array) for array in flat),
        compiler_params=pltpu.CompilerParams(vmem_limit_bytes=VMEM_MOST),
    )(sums, *rows_in, *gains, *gradients, *flat)


def shards(
    hidden_in,
    cotangent,
    prefix,
    positions,
    norm_gains,
    gains_first,
    gains_second,
    input_weight,
    input_first,
    input_second,
    output_weight,
    output_first,
    output_second,
    expand_weight,
    expand_first,
    expand_second,
    shrink_weight,
    shrink_first,
    shrink_second,
):
    low = jnp.bfloat16
    hidden, upstream = hidden_in[0], cotangent[0]
    masters = (
        (input_weight, input_first, input_second),
        (output_weight.T, output_first.T, output_second.T),
        (expand_weight, expand_first, expand_second),
        (shrink_weight.T, shrink_first.T, shrink_second.T),
    )
    tables = angles(positions[0])
    (
        first_all,
        shrunk_all,
        w_in,
        w_gate,
        w_up,
        w_out,
        w_shrink,
        turned,
        kv_rows,
        kv_lines,
        attended,
        tokens,
        log_total,
        projected,
    ) = front(
        hidden,
        upstream,
        norm_gains[:1],
        (input_weight, expand_weight, output_weight.T, shrink_weight.T),
        tables,
        prefix,
    )
    (
        residual,
        grad_residual,
        projected_gradient,
        gain_two,
        grad_gate,
        grad_up,
        grad_shrink,
        out_parts,
    ) = middle(
        hidden, upstream, projected, norm_gains[1:], shrunk_all, w_gate, w_up, w_shrink
    )
    shrunk, grad_first, *gradients, sums = back(
        projected_gradient,
        w_out.reshape(1536, 384),
        w_in.reshape(1536, 640),
        first_all,
        out_parts,
        (grad_gate, grad_up, grad_shrink),
        (turned, kv_rows, kv_lines, attended, tokens, log_total),
        tables,
        hidden,
        gain_two,
        prefix,
    )
    outs = finish(
        sums,
        (grad_first, hidden, grad_residual, residual, shrunk),
        (norm_gains, gains_first, gains_second),
        gradients,
        masters,
    )
    block_output, input_gradient, gradient_norm = outs[0], outs[1], outs[2].reshape(())
    gains_new, input_new, output_new, expand_new, shrink_new = (
        outs[3 + 3 * i : 6 + 3 * i] for i in range(5)
    )
    return (
        block_output[None],
        input_gradient[None],
        gradient_norm,
        *gains_new,
        *input_new,
        *(array.T for array in output_new),
        *expand_new,
        *(array.T for array in shrink_new),
    )


def solution(mesh):
    return jax.shard_map(
        shards,
        mesh=mesh,
        in_specs=(
            P("shard", ("context", "tensor"), None),
            P("shard", ("context", "tensor"), None),
            P("shard"),
            P("shard", "context"),
            P(),
            P(),
            P(),
            P(("shard", "context"), "tensor"),
            P(("shard", "context"), "tensor"),
            P(("shard", "context"), "tensor"),
            P("tensor", ("shard", "context")),
            P("tensor", ("shard", "context")),
            P("tensor", ("shard", "context")),
            P(None, ("shard", "context"), "tensor"),
            P(None, ("shard", "context"), "tensor"),
            P(None, ("shard", "context"), "tensor"),
            P("tensor", ("shard", "context")),
            P("tensor", ("shard", "context")),
            P("tensor", ("shard", "context")),
        ),
        out_specs=(
            P("shard", ("context", "tensor"), None),
            P("shard", ("context", "tensor"), None),
            P(),
            P(),
            P(),
            P(),
            P(("shard", "context"), "tensor"),
            P(("shard", "context"), "tensor"),
            P(("shard", "context"), "tensor"),
            P("tensor", ("shard", "context")),
            P("tensor", ("shard", "context")),
            P("tensor", ("shard", "context")),
            P(None, ("shard", "context"), "tensor"),
            P(None, ("shard", "context"), "tensor"),
            P(None, ("shard", "context"), "tensor"),
            P("tensor", ("shard", "context")),
            P("tensor", ("shard", "context")),
            P("tensor", ("shard", "context")),
        ),
        check_vma=False,
    )
```

```python
import functools
import math

import jax
import jax.numpy as jnp
from jax import lax
from jax.experimental import pallas as pl
from jax.experimental.pallas import tpu as pltpu
from jax.sharding import PartitionSpec as P

HD = 64
GROUP = 3
STEP = 10
HEADS = 2
BLOCKS = 7
VMEM_MOST = 60 * 2**20
MESH = pl.DeviceIdType.MESH


EPS = 1e-05
RESID = 1.4 / math.sqrt(52.0)
ROPE_BASE = 10000.0
MAX_NORM = 1.0
RATE = 0.1
GAIN_RATE = 1.0
BETA_ONE = 0.9
BETA_TWO = 0.95
ADAM_EPS = 1e-08
DECAY = 0.1
NEG = -1e30


def angles(places):
    half_width = HD // 2
    frequency = ROPE_BASE ** (-2.0 * jnp.arange(half_width, dtype=jnp.float32) / HD)
    phase_turn = places.astype(jnp.float32)[None, :] * frequency[:, None]
    return (jnp.cos(phase_turn), jnp.sin(phase_turn))


def adamw(weight, gradient, momentum, variance, step_rate, decay_rate):
    momentum_new = BETA_ONE * momentum + (1.0 - BETA_ONE) * gradient
    variance_new = BETA_TWO * variance + (1.0 - BETA_TWO) * gradient * gradient
    momentum_hat = momentum_new / (1.0 - BETA_ONE**STEP)
    variance_hat = variance_new / (1.0 - BETA_TWO**STEP)
    updated = weight - step_rate * (
        momentum_hat / (jnp.sqrt(variance_hat) + ADAM_EPS) + decay_rate * weight
    )
    return (momentum_new, variance_new, updated)


def nn(a, b):
    return lax.dot_general(a, b, (((1,), (0,)), ((), ())), preferred_element_type=jnp.float32)


def nt(a, b):
    return lax.dot_general(a, b, (((1,), (1,)), ((), ())), preferred_element_type=jnp.float32)


def place():
    shard = lax.axis_index("shard")
    return (
        shard // 8,
        lax.rem(shard // 2, 4),
        lax.rem(shard, 2),
        lax.axis_index("context"),
        lax.axis_index("tensor"),
    )


def device(xh, y, core, xl, z):
    return {"shard": (xh * 4 + y) * 2 + core, "context": xl, "tensor": z}


def hail(peers):
    barrier = pltpu.get_barrier_semaphore()
    for peer in peers:
        pl.semaphore_signal(barrier, inc=1, device_id=peer, device_id_type=MESH)


def meet(peers):
    pl.semaphore_wait(pltpu.get_barrier_semaphore(), len(peers))


def remote(src, dst, send_sem, recv_sem, peer):
    return pltpu.make_async_remote_copy(
        src_ref=src,
        dst_ref=dst,
        send_sem=send_sem,
        recv_sem=recv_sem,
        device_id=peer,
        device_id_type=MESH,
    )


def turn(block, cos_part, sin_part):
    lower_half, upper_half = block[: HD // 2], block[HD // 2 :]
    return jnp.concatenate(
        [
            lower_half * cos_part - upper_half * sin_part,
            upper_half * cos_part + lower_half * sin_part,
        ],
        axis=0,
    )


def turn_back(block, cos_part, sin_part):
    return turn(block, cos_part, -sin_part)


def by_span(context, b, run):
    near = (context == 0) | (b <= 3)

    @pl.when(near)
    def _():
        run(1408)

    @pl.when(jnp.logical_not(near))
    def _():
        run(1792)


def limits(prefix, xl, b):
    lane = lax.broadcasted_iota(jnp.int32, (1, GROUP * 128), 1)
    row = xl * 896 + b * 128 + lax.rem(lane, 128)
    return jnp.maximum(row + 1, prefix[0])


def key_tables(cos_ref, sin_ref, key_cos, key_sin):
    cos_part, sin_part = jnp.transpose(cos_ref[...]), jnp.transpose(sin_ref[...])
    still = jnp.ones((896, HD), jnp.float32)
    key_cos[...] = jnp.concatenate([cos_part, cos_part, still], axis=1)
    key_sin[...] = jnp.concatenate([-sin_part, sin_part, 0.0 * still], axis=1)


def arrival(z, i):
    edge = (3 - z) // 3
    if isinstance(i, int) and i < 2:
        shift = i * (2 * edge - 1)
    elif isinstance(i, int) and i > 3:
        shift = i - 2 + edge
    else:
        shift = 3 * i - 8 + edge
    return lax.rem(2 * z + shift + 7, 7)


def arrival_far(z, i):
    return lax.rem(2 * z + i + 5 + (3 - z) // 3, 7)


def ring_peers():
    xh, y, core, xl, z = place()
    return (
        z,
        lax.rem(z + 1, 4),
        lax.rem(z + 2, 4),
        lax.rem(z + 3, 4),
        device(xh, y, core, xl, lax.rem(z + 1, 4)),
        device(xh, y, core, xl, lax.rem(z + 3, 4)),
    )


def halves(ref, index):
    rows = ref.shape[1] // 2
    return ref.at[index, pl.ds(0, rows)], ref.at[index, pl.ds(rows, rows)]


def ring_gather_begin(own, held, send_sem, recv_sem):
    z, zp, z2, zm, up, down = ring_peers()
    rows = own.shape[0] // 2
    first, second = own.at[pl.ds(0, rows)], own.at[pl.ds(rows, rows)]
    first_to, second_to = halves(held, z)
    copies = [
        remote(second, second_to, send_sem.at[0], recv_sem.at[0], up),
        remote(first, first_to, send_sem.at[1], recv_sem.at[1], down),
        remote(first, first_to, send_sem.at[2], recv_sem.at[2], up),
        remote(second, second_to, send_sem.at[3], recv_sem.at[3], down),
    ]
    for copy in copies:
        copy.start()
    return copies


def ring_gather_forward(held, copies, send_sem, recv_sem):
    z, zp, z2, zm, up, down = ring_peers()
    copies[0].wait_recv()
    below = halves(held, zm)[1]
    on_up = remote(below, below, send_sem.at[4], recv_sem.at[4], up)
    on_up.start()
    copies[1].wait_recv()
    above = halves(held, zp)[0]
    on_down = remote(above, above, send_sem.at[5], recv_sem.at[5], down)
    on_down.start()
    return copies + [on_up, on_down]


def ring_gather_end(copies):
    for copy in copies:
        copy.wait_send()
    for copy in copies[2:]:
        copy.wait_recv()


def in_rows(count, step, run):
    def body(i, carry):
        run(pl.ds(pl.multiple_of(i * step, step), step))
        return carry

    lax.fori_loop(0, count // step, body, 0)


def ring_scatter_near(parts, came, send_sem, recv_sem):
    z, zp, z2, zm, up, down = ring_peers()
    copies = [
        remote(halves(parts, zp)[0], came.at[2], send_sem.at[2], recv_sem.at[2], up),
        remote(halves(parts, zm)[1], came.at[3], send_sem.at[3], recv_sem.at[3], down),
    ]
    for copy in copies:
        copy.start()
    return copies


def ring_scatter_far(parts, came, send_sem, recv_sem):
    z, zp, z2, zm, up, down = ring_peers()
    copies = [
        remote(halves(parts, z2)[1], came.at[0], send_sem.at[0], recv_sem.at[0], up),
        remote(halves(parts, z2)[0], came.at[1], send_sem.at[1], recv_sem.at[1], down),
    ]
    for copy in copies:
        copy.start()
    return copies


def ring_scatter_begin(parts, came, send_sem, recv_sem):
    far = ring_scatter_far(parts, came, send_sem, recv_sem)
    return far + ring_scatter_near(parts, came, send_sem, recv_sem)


def ring_scatter_forward(parts, came, sums, copies, send_sem, recv_sem):
    z, zp, z2, zm, up, down = ring_peers()
    count = came.shape[1]
    copies[0].wait_recv()

    def add_up(rows):
        sums[0, rows] = (
            came[0, rows].astype(jnp.float32)
            + parts[zp, pl.ds(pl.multiple_of(rows.start + count, 16), 16)].astype(jnp.float32)
        ).astype(jnp.bfloat16)

    in_rows(count, 16, add_up)
    on_up = remote(sums.at[0], came.at[4], send_sem.at[4], recv_sem.at[4], up)
    on_up.start()
    copies[1].wait_recv()

    def add_down(rows):
        sums[1, rows] = (
            came[1, rows].astype(jnp.float32) + parts[zm, rows].astype(jnp.float32)
        ).astype(jnp.bfloat16)

    in_rows(count, 16, add_down)
    on_down = remote(sums.at[1], came.at[5], send_sem.at[5], recv_sem.at[5], down)
    on_down.start()
    return copies + [on_up, on_down]


def ring_scatter_end(parts, came, total, copies):
    z, zp, z2, zm, up, down = ring_peers()
    count = came.shape[1]
    for copy in copies[2:]:
        copy.wait_recv()
    for copy in copies:
        copy.wait_send()

    def add(rows):
        later = pl.ds(pl.multiple_of(rows.start + count, 16), 16)
        total[rows] = (
            parts[z, rows].astype(jnp.float32)
            + came[2, rows].astype(jnp.float32)
            + came[5, rows].astype(jnp.float32)
        )
        total[later] = (
            parts[z, later].astype(jnp.float32)
            + came[3, rows].astype(jnp.float32)
            + came[4, rows].astype(jnp.float32)
        )

    in_rows(count, 16, add)


def plane():
    xh, y, core, xl, z = place()
    ys = [lax.rem(y + d, 4) for d in (1, 3, 2)]
    step = xh * 2 + xl
    xs = [lax.rem(step + d, 4) for d in (1, 3, 2)]
    xs = [(x // 2, lax.rem(x, 2)) for x in xs]
    y_peers = [device(xh, other, core, xl, z) for other in ys]
    x_peers = [device(h, y, core, l, z) for h, l in xs]
    return ys, xs, y_peers, x_peers, device(xh, y, 1 - core, xl, z)


class PlaneGather:
    def __init__(self, own, held, y_first, shared, send_sem, recv_sem):
        self.own, self.held, self.y_first, self.shared = own, held, y_first, shared
        self.send_sem, self.recv_sem, self.used = send_sem, recv_sem, 0
        self.copies, self.first, self.second, self.third = [], [], [], []
        xh, y, core, xl, z = place()
        ys, xs, self.y_peers, self.x_peers, self.other = plane()
        self.core = core
        if y_first:
            self.mine, self.wheres, self.peers = (xh, xl), xs, self.x_peers
        else:
            self.mine, self.wheres, self.peers = y, ys, self.y_peers

    def send(self, src, dst, peer):
        copy = remote(src, dst, self.send_sem.at[self.used], self.recv_sem.at[self.used], peer)
        self.used += 1
        copy.start()
        self.copies.append(copy)
        return copy

    def begin(self):
        xh, y, core, xl, z = place()
        target = self.held.at[xh, y, core, xl]
        peers = self.y_peers if self.y_first else self.x_peers
        self.first = [self.send(self.own, target, peer) for peer in peers]

    def half(self, where, k):
        if self.y_first:
            return self.held.at[where[0], pl.ds(2 * k, 2), self.core, where[1]]
        return self.held.at[k, where, self.core]

    def line(self, where):
        if self.y_first:
            return self.held.at[where[0], :, self.core, where[1]]
        return self.held.at[:, where, self.core]

    def give(self, where):
        line = self.line(where)
        self.third.append(self.send(line, line, self.other))

    def spread(self):
        for copy in self.first:
            copy.wait_recv()
        low_half, high_half = self.half(self.mine, 0), self.half(self.mine, 1)
        ahead, behind = self.peers[:2]
        self.second = [
            self.send(high_half, high_half, ahead),
            self.send(low_half, low_half, behind),
            self.send(low_half, low_half, ahead),
            self.send(high_half, high_half, behind),
        ]
        if self.shared:
            self.give(self.mine)

    def relay(self):
        ahead, behind = self.peers[:2]
        self.second[0].wait_recv()
        part = self.half(self.wheres[1], 1)
        self.second.append(self.send(part, part, ahead))
        self.second[1].wait_recv()
        part = self.half(self.wheres[0], 0)
        self.second.append(self.send(part, part, behind))

    def share(self):
        self.second[2].wait_recv()
        self.give(self.wheres[1])
        self.second[3].wait_recv()
        self.give(self.wheres[0])
        self.second[4].wait_recv()
        self.second[5].wait_recv()
        self.give(self.wheres[2])

    def end(self):
        for copy in self.third if self.shared else self.second[2:]:
            copy.wait_recv()
        for copy in self.copies:
            copy.wait_send()


def swap_halves(block):
    lane = lax.broadcasted_iota(jnp.int32, block.shape, 1)
    return jnp.where(
        lane < HD // 2, pltpu.roll(block, 128 - HD // 2, 1), pltpu.roll(block, HD // 2, 1)
    )


def front_kernel(*refs):
    (hidden, cotangent, gain, m_in, m_expand, m_out, m_shrink) = refs[:7]
    (cos_ref, sin_ref, prefix) = refs[7:10]
    (first_to, shrunk_all, query_to, rest_to) = refs[10:14]
    (gate_all, up_all, out_all, shrink_all) = refs[14:18]
    (turned_to, rows_to, lines_to, attended, tokens, log_total, total) = refs[18:25]
    (first_all, shrunk, in_query, in_rest, w_gate, w_up, w_out, w_shrink) = refs[25:33]
    (turned, kv_rows, kv_lines, key_cos, key_sin) = refs[33:38]
    (packed, held_rows, own_tokens) = refs[38:41]
    (ring_send, ring_recv, plane_send, plane_recv, out_send, out_recv) = refs[41:47]
    (kv_send, kv_recv, token_send, token_recv, own_sem, out_sem) = refs[47:]
    xh, y, core, xl, z = place()
    z, zp, z2, zm, up, down = ring_peers()
    ys, xs, y_peers, x_peers, other = plane()
    beside = device(xh, y, core, 1 - xl, z)
    across = device(xh, y, core, xl, z2)
    peers = [up, down, across, other] + y_peers + x_peers
    hail(peers)
    low = jnp.bfloat16
    query_own, rest_own = in_query.at[xh, y, core, xl], in_rest.at[xh, y, core, xl]
    query_own[...] = m_in[:, :384].astype(low)
    rest_own[...] = m_in[:, 384:].astype(low)
    w_out[z] = m_out[...].astype(low)
    rows = hidden[...].astype(jnp.float32)
    scaling = lax.rsqrt(jnp.mean(rows * rows, axis=-1, keepdims=True) + EPS)
    first_all[z] = (rows * scaling * gain[...]).astype(low)
    meet(peers)
    out_copies = [
        remote(w_out.at[z], w_out.at[z], out_send.at[i], out_recv.at[i], peer)
        for i, peer in enumerate((up, down, across))
    ]
    for copy in out_copies:
        copy.start()
    owns = (query_own, rest_own, w_out, w_gate, w_up, w_shrink)
    helds = (in_query, in_rest, out_all, gate_all, up_all, shrink_all)
    gathers = [
        PlaneGather(own, held, y_first, i < 3, plane_send.at[i], plane_recv.at[i])
        for i, (own, held, y_first) in enumerate(zip(owns, helds, GATHER_TURNS))
    ]
    query_gather, rest_gather, out_gather, *feed_gathers = gathers
    query_gather.begin()
    rest_gather.begin()
    ring = ring_gather_begin(first_all.at[z], first_all, ring_send.at[0], ring_recv.at[0])
    w_gate[...] = m_expand[0].astype(low)
    w_up[...] = m_expand[1].astype(low)
    w_shrink[...] = m_shrink[...].astype(low)
    shrunk[...] = (RESID * cotangent[...].astype(jnp.float32)).astype(low)
    keeps = [
        pltpu.make_async_copy(own, held.at[xh, y, core, xl], own_sem.at[i])
        for i, (own, held) in enumerate(zip(owns[3:], helds[3:]))
    ]
    keeps.append(pltpu.make_async_copy(shrunk, shrunk_all.at[z], own_sem.at[3]))
    for keep in keeps:
        keep.start()
    for copy in out_copies:
        copy.wait_recv()
    out_gather.begin()
    keeps.append(pltpu.make_async_copy(w_out, out_all.at[xh, y, core, xl], own_sem.at[4]))
    keeps[-1].start()
    query_gather.spread()
    rest_gather.spread()
    for keep in keeps:
        keep.wait()
    for gather in feed_gathers:
        gather.begin()
    key_tables(cos_ref, sin_ref, key_cos, key_sin)
    query_gather.relay()
    rest_gather.relay()
    ring = ring_gather_forward(first_all, ring, ring_send.at[0], ring_recv.at[0])
    out_gather.spread()
    query_gather.share()
    rest_gather.share()
    query_gather.end()
    rest_gather.end()

    def project(c, rows):
        out = jnp.concatenate(
            [
                nn(first_all[c], in_query[...].reshape(1536, 384)),
                nn(first_all[c], in_rest[...].reshape(1536, 256)),
            ],
            axis=1,
        )
        packed[rows] = out
        for g in range(HEADS):
            block = out[:, g * 320 + 192 : g * 320 + 320]
            mine = pl.ds(pl.multiple_of(xl * 896 + c * 224, 16), 224)
            kv_rows[g, mine] = (
                block * key_cos[rows] + swap_halves(block) * key_sin[rows]
            ).astype(low)

    kv_copies = []
    for i, c in enumerate((z, zm, zp, z2)):
        if i == 1:
            ring[2].wait_recv()
        if i == 2:
            ring[3].wait_recv()
        if i == 3:
            ring[4].wait_recv()
            ring[5].wait_recv()
        project(c, pl.ds(pl.multiple_of(c * 224, 16), 224))
        mine = kv_rows.at[:, pl.ds(pl.multiple_of(xl * 896 + c * 224, 16), 224)]
        kv_copies.append(remote(mine, mine, kv_send.at[i], kv_recv.at[i], beside))
        kv_copies[-1].start()
    out_gather.relay()
    for gather in feed_gathers:
        gather.spread()
    later = ring_gather_begin(shrunk, shrunk_all, ring_send.at[1], ring_recv.at[1])
    saves = []

    def save(src, dst):
        saves.append(pltpu.make_async_copy(src, dst, own_sem.at[5 + len(saves)]))
        saves[-1].start()

    save(first_all, first_to)
    save(in_query, query_to)
    save(in_rest, rest_to)

    def turn_block(b, carry):
        columns = pl.ds(pl.multiple_of(b * 128, 128), 128)
        lines = jnp.transpose(packed[columns])
        cos_here, sin_here = cos_ref[:, columns], sin_ref[:, columns]
        for g in range(HEADS):
            for h in range(GROUP):
                at = (g * 5 + h) * HD
                turned[(g * GROUP + h) * HD : (g * GROUP + h + 1) * HD, columns] = (
                    turn(lines[at : at + HD], cos_here, sin_here) * HD ** (-0.5)
                ).astype(low)
        return carry

    lax.fori_loop(0, BLOCKS, turn_block, 0)
    save(turned, turned_to)
    for copy in kv_copies:
        copy.wait_recv()
    for g in range(HEADS):
        kv_lines[g] = jnp.transpose(kv_rows[g].astype(jnp.float32)).astype(low)
    save(kv_rows, rows_to)
    save(kv_lines, lines_to)

    def block(b, g):
        columns = pl.ds(pl.multiple_of(b * 128, 128), 128)

        def run(span):
            head_rows = [
                pl.ds(pl.multiple_of((g * GROUP + h) * HD, HD), HD) for h in range(GROUP)
            ]
            queries = jnp.concatenate([turned[r, columns] for r in head_rows], axis=1)
            queries = jnp.concatenate([queries, jnp.zeros_like(queries)], axis=0)
            scores = nn(kv_rows[g, :span], queries)
            key_index = lax.broadcasted_iota(jnp.int32, (span, 384), 0)
            scores = jnp.where(key_index < limits(prefix, xl, b), scores, NEG)
            row_max = jnp.max(scores, axis=0, keepdims=True)
            shifted = jnp.exp(scores - row_max)
            exp_total = jnp.sum(shifted, axis=0, keepdims=True)
            out = nn(kv_lines[g, HD:, :span], shifted.astype(low)) * (1.0 / exp_total)
            for h in range(GROUP):
                attended[head_rows[h], columns] = out[:, h * 128 : (h + 1) * 128].astype(low)
            log_total[b * HEADS + g] = row_max + jnp.log(exp_total)

        by_span(xl, b, run)

    def near_heads(t, carry):
        block(arrival(z, lax.div(t, 2)), lax.rem(t, 2))
        return carry

    def far_heads(t, carry):
        block(arrival_far(z, lax.div(t, 2)), lax.rem(t, 2))
        return carry

    def beside_block(g, carry):
        block(arrival(z, 1), g)
        return carry

    def own_block(g, carry):
        block(2 * z, g)
        return carry

    def lay(b):
        columns = pl.ds(pl.multiple_of(b * 128, 128), 128)
        tokens[columns] = jnp.transpose(attended[:, columns].astype(jnp.float32)).astype(low)

    def post(c, i, peer):
        mine = tokens.at[pl.ds(pl.multiple_of(c * 224, 16), 224)]
        copy = remote(mine, own_tokens.at[z], token_send.at[i], token_recv.at[i], peer)
        copy.start()
        return copy

    lax.fori_loop(8, 14, far_heads, 0)
    for gather in feed_gathers:
        gather.relay()
    later = ring_gather_forward(shrunk_all, later, ring_send.at[1], ring_recv.at[1])
    for i in range(4, 7):
        lay(arrival(z, i))
    token_copies = [post(z2, 0, across)]
    out_gather.share()
    lax.fori_loop(0, 2, beside_block, 0)
    lax.fori_loop(4, 8, near_heads, 0)
    for i in range(1, 4):
        lay(arrival(z, i))
    token_copies += [post(zp, 1, up), post(zm, 2, down)]
    out_gather.end()
    fetch = pltpu.make_async_copy(out_all, held_rows, out_sem)
    fetch.start()
    lax.fori_loop(0, 2, own_block, 0)
    lay(2 * z)
    own_tokens[z] = tokens[pl.ds(pl.multiple_of(z * 224, 16), 224)]
    fetch.wait()
    for copy in token_copies:
        copy.wait_recv()
    projected = jnp.zeros(total.shape, jnp.float32)
    for c in range(4):
        projected = projected + nt(own_tokens[c], held_rows[:, :, :, :, c].reshape(1536, 384))
    total[...] = projected
    for gather in feed_gathers:
        gather.end()
    ring_gather_end(later)
    for copy in kv_copies + ring + token_copies + out_copies:
        copy.wait_send()
    for copy in saves:
        copy.wait()


GATHER_TURNS = (True, False, False, True, True, False)


def front(hidden, cotangent, gain, weights, tables, prefix):
    any_place = pl.BlockSpec(memory_space=pl.ANY)
    whole = pl.BlockSpec(memory_space=pltpu.VMEM)
    rows, width = hidden.shape
    low, full = jnp.bfloat16, jnp.float32
    block = (2, 4, 2, 2, 48)
    first_shape, in_shapes = (4, rows, width), (block + (384,), block + (256,))
    out_shape = block[:4] + (4, 48, 384)
    turned_shape, rows_shape, lines_shape = (384, 896), (HEADS, 1792, 128), (HEADS, 128, 1792)
    kept = (first_shape, (4, rows, width)) + in_shapes + (block + (960,),) * 2
    kept += (out_shape, block + (960,), turned_shape, rows_shape, lines_shape)
    outs = pl.pallas_call(
        front_kernel,
        out_shape=(
            *(jax.ShapeDtypeStruct(shape, low) for shape in kept),
            jax.ShapeDtypeStruct((384, 896), low),
            jax.ShapeDtypeStruct((896, 384), low),
            jax.ShapeDtypeStruct((HEADS * BLOCKS, 1, 384), full),
            jax.ShapeDtypeStruct((rows, width), full),
        ),
        in_specs=[whole] * 9 + [pl.BlockSpec(memory_space=pltpu.SMEM)],
        out_specs=(any_place,) * 11 + (whole,) * 4,
        scratch_shapes=[
            pltpu.VMEM(first_shape, low),
            pltpu.VMEM((rows, width), low),
            pltpu.VMEM(in_shapes[0], low),
            pltpu.VMEM(in_shapes[1], low),
            pltpu.VMEM((48, 960), low),
            pltpu.VMEM((48, 960), low),
            pltpu.VMEM((4, 48, 384), low),
            pltpu.VMEM((48, 960), low),
            pltpu.VMEM(turned_shape, low),
            pltpu.VMEM(rows_shape, low),
            pltpu.VMEM(lines_shape, low),
            pltpu.VMEM((896, 128), full),
            pltpu.VMEM((896, 128), full),
            pltpu.VMEM((896, 640), full),
            pltpu.VMEM(out_shape, low),
            pltpu.VMEM((4, rows, 384), low),
            pltpu.SemaphoreType.DMA((2, 6)),
            pltpu.SemaphoreType.DMA((2, 6)),
            pltpu.SemaphoreType.DMA((6, 13)),
            pltpu.SemaphoreType.DMA((6, 13)),
            pltpu.SemaphoreType.DMA((3,)),
            pltpu.SemaphoreType.DMA((3,)),
            pltpu.SemaphoreType.DMA((4,)),
            pltpu.SemaphoreType.DMA((4,)),
            pltpu.SemaphoreType.DMA((3,)),
            pltpu.SemaphoreType.DMA((3,)),
            pltpu.SemaphoreType.DMA((11,)),
            pltpu.SemaphoreType.DMA,
        ],
        compiler_params=pltpu.CompilerParams(
            collective_id=0, has_side_effects=True, vmem_limit_bytes=VMEM_MOST
        ),
    )(hidden, cotangent, gain, *weights, *tables, prefix)
    return outs


def tn(a, b):
    return lax.dot_general(a, b, (((0,), (0,)), ((), ())), preferred_element_type=jnp.float32)


def middle_kernel(*refs):
    (hidden, cotangent, projected, gain) = refs[:4]
    (shrunk_from, gate_from, up_from, shrink_from) = refs[4:8]
    (residual, grad_residual, turned_back, gain_two) = refs[8:12]
    (gate_to, up_to, shrink_to, out_to) = refs[12:16]
    (shrunk_all, w_gate, w_up, w_shrink) = refs[16:20]
    (second_all, activated_back, gated, gate_back, up_back) = refs[20:25]
    (parts, came, sums, total) = refs[25:29]
    (grad_gate, grad_up, grad_shrink, out_parts) = refs[29:33]
    (ring_send, ring_recv, load_sem, share_send, share_recv) = refs[33:]
    z, zp, z2, zm, up, down = ring_peers()
    xh, y, core, xl, z = place()

    def flat(weight):
        return weight[...].reshape(1536, 960)

    other = device(xh, y, 1 - core, xl, z)
    hail([up, down, other])
    loads = [
        pltpu.make_async_copy(src, dst, load_sem.at[i])
        for i, (src, dst) in enumerate(
            (
                (shrink_from.at[:, :, core], w_shrink.at[:, :, core]),
                (shrunk_from, shrunk_all),
                (gate_from.at[:, :, core], w_gate.at[:, :, core]),
                (up_from.at[:, :, core], w_up.at[:, :, core]),
            )
        )
    ]
    for load in loads:
        load.start()
    rows = hidden[...].astype(jnp.float32) + RESID * projected[...]
    residual[...] = rows
    scaling = lax.rsqrt(jnp.mean(rows * rows, axis=-1, keepdims=True) + EPS)
    second_all[z] = (rows * scaling * gain[...]).astype(jnp.bfloat16)
    meet([up, down, other])
    ring = ring_gather_begin(second_all.at[z], second_all, ring_send.at[0], ring_recv.at[0])
    shares = [
        remote(
            src.at[:, :, core], dst.at[:, :, core], share_send.at[i], share_recv.at[i], other
        )
        for i, (src, dst) in enumerate(
            ((shrink_from, w_shrink), (gate_from, w_gate), (up_from, w_up))
        )
    ]
    for share in shares:
        share.start()
    loads[0].wait()
    loads[1].wait()
    shares[0].wait_recv()
    for c in range(4):
        activated_back[c] = nn(shrunk_all[c], flat(w_shrink))
    loads[2].wait()
    loads[3].wait()
    shares[1].wait_recv()
    shares[2].wait_recv()

    def feed(c):
        gate_value = nn(second_all[c], flat(w_gate))
        up_value = nn(second_all[c], flat(w_up))
        sigmoid_gate = 1.0 / (1.0 + jnp.exp(-gate_value))
        gate_active = gate_value * sigmoid_gate
        gated[c] = (gate_active * up_value).astype(jnp.bfloat16)
        gradient = activated_back[c]
        gate_back[c] = (
            gradient * up_value * sigmoid_gate * (1.0 + gate_value * (1.0 - sigmoid_gate))
        ).astype(jnp.bfloat16)
        up_back[c] = (gradient * gate_active).astype(jnp.bfloat16)
        parts[c] = (nt(gate_back[c], flat(w_gate)) + nt(up_back[c], flat(w_up))).astype(
            jnp.bfloat16
        )

    feed(z)
    ring = ring_gather_forward(second_all, ring, ring_send.at[0], ring_recv.at[0])
    ring[2].wait_recv()
    feed(zm)
    ring[3].wait_recv()
    feed(zp)
    near = ring_scatter_near(parts, came, ring_send.at[1], ring_recv.at[1])
    ring[4].wait_recv()
    ring[5].wait_recv()
    feed(z2)
    far = ring_scatter_far(parts, came, ring_send.at[1], ring_recv.at[1])
    second_rows = second_all[...].reshape(896, 1536)
    saves = []

    def save(src, dst):
        saves.append(pltpu.make_async_copy(src, dst, load_sem.at[4 + len(saves)]))
        saves[-1].start()

    grad_gate[...] = tn(second_rows, gate_back[...].reshape(896, 960)).astype(jnp.bfloat16)
    save(grad_gate, gate_to)
    scatter = ring_scatter_forward(
        parts, came, sums, far + near, ring_send.at[1], ring_recv.at[1]
    )
    grad_up[...] = tn(second_rows, up_back[...].reshape(896, 960)).astype(jnp.bfloat16)
    save(grad_up, up_to)
    grad_shrink[...] = tn(
        shrunk_all[...].reshape(896, 1536), gated[...].reshape(896, 960)
    ).astype(jnp.bfloat16)
    save(grad_shrink, shrink_to)
    for c in range(4):
        out_parts[c] = nt(gated[c], flat(w_shrink)).astype(jnp.bfloat16)
    save(out_parts, out_to)
    for copy in ring + shares:
        copy.wait_send()
    ring_scatter_end(parts, came, total, scatter)
    rows = residual[...]
    scaling = lax.rsqrt(jnp.mean(rows * rows, axis=-1, keepdims=True) + EPS)
    normed = rows * scaling
    gradient = total[...]
    gain_two[...] = jnp.sum(gradient * normed, axis=0, keepdims=True)
    gradient = gradient * gain[...]
    back = cotangent[...].astype(jnp.float32) + scaling * (
        gradient - normed * jnp.mean(gradient * normed, axis=-1, keepdims=True)
    )
    grad_residual[...] = back
    turned_back[...] = (RESID * back).astype(jnp.bfloat16)
    for copy in saves:
        copy.wait()


def middle(hidden, cotangent, projected, gain, shrunk_all, w_gate, w_up, w_shrink):
    any_place = pl.BlockSpec(memory_space=pl.ANY)
    whole = pl.BlockSpec(memory_space=pltpu.VMEM)
    rows, width = hidden.shape
    low, full = jnp.bfloat16, jnp.float32
    return pl.pallas_call(
        middle_kernel,
        out_shape=(
            jax.ShapeDtypeStruct((rows, width), full),
            jax.ShapeDtypeStruct((rows, width), full),
            jax.ShapeDtypeStruct((rows, width), low),
            jax.ShapeDtypeStruct((1, width), full),
            jax.ShapeDtypeStruct((1536, 960), low),
            jax.ShapeDtypeStruct((1536, 960), low),
            jax.ShapeDtypeStruct((1536, 960), low),
            jax.ShapeDtypeStruct((4, rows, width), low),
        ),
        in_specs=[whole] * 4 + [any_place] * 4,
        out_specs=(whole,) * 4 + (any_place,) * 4,
        scratch_shapes=[
            pltpu.VMEM((4, rows, width), low),
            pltpu.VMEM((2, 4, 2, 2, 48, 960), low),
            pltpu.VMEM((2, 4, 2, 2, 48, 960), low),
            pltpu.VMEM((2, 4, 2, 2, 48, 960), low),
            pltpu.VMEM((4, rows, width), low),
            pltpu.VMEM((4, rows, 960), full),
            pltpu.VMEM((4, rows, 960), low),
            pltpu.VMEM((4, rows, 960), low),
            pltpu.VMEM((4, rows, 960), low),
            pltpu.VMEM((4, rows, width), low),
            pltpu.VMEM((6, rows // 2, width), low),
            pltpu.VMEM((2, rows // 2, width), low),
            pltpu.VMEM((rows, width), full),
            pltpu.VMEM((1536, 960), low),
            pltpu.VMEM((1536, 960), low),
            pltpu.VMEM((1536, 960), low),
            pltpu.VMEM((4, rows, width), low),
            pltpu.SemaphoreType.DMA((2, 6)),
            pltpu.SemaphoreType.DMA((2, 6)),
            pltpu.SemaphoreType.DMA((8,)),
            pltpu.SemaphoreType.DMA((3,)),
            pltpu.SemaphoreType.DMA((3,)),
        ],
        compiler_params=pltpu.CompilerParams(
            collective_id=4, has_side_effects=True, vmem_limit_bytes=VMEM_MOST
        ),
    )(hidden, cotangent, projected, gain, shrunk_all, w_gate, w_up, w_shrink)


class Scatter:
    def __init__(self, parts, came, across, lined, last, x_first, send_sem, recv_sem):
        self.parts, self.came, self.across = parts, came, across
        self.lined, self.last, self.x_first = lined, last, x_first
        self.send_sem, self.recv_sem, self.used, self.copies = send_sem, recv_sem, 0, []
        xh, y, core, xl, z = place()
        ys, xs, y_peers, x_peers, self.other = plane()
        if x_first:
            self.lines, self.peers = xs[::-1] + [(xh, xl)], x_peers[::-1]
            self.mine, self.targets, self.target_peers = y, ys, y_peers
        else:
            self.lines, self.peers = ys[::-1] + [y], y_peers[::-1]
            self.mine, self.targets, self.target_peers = (xh, xl), xs, x_peers

    def send(self, src, dst, peer):
        copy = remote(src, dst, self.send_sem.at[self.used], self.recv_sem.at[self.used], peer)
        self.used += 1
        copy.start()
        self.copies.append(copy)
        return copy

    def in_line(self, line):
        return (line[0], slice(None), line[1]) if self.x_first else (slice(None), line)

    def begin(self):
        core = place()[2]
        self.first = []
        for line in self.lines:
            if self.x_first:
                src = self.parts.at[line[0], :, 1 - core, line[1]]
            else:
                src = self.parts.at[:, line, 1 - core]
            self.first.append(self.send(src, self.came.at[self.in_line(line)], self.other))

    def stage(self, held, sem):
        copy = pltpu.make_async_copy(self.parts.at[:, :, place()[2]], held, sem)
        copy.start()
        return copy

    def at(self, line, i):
        return (line[0], i, line[1]) if self.x_first else (i // 2, line, lax.rem(i, 2))

    def spot(self, i):
        if self.x_first:
            return (i,)
        return (i[0], i[1]) if isinstance(i, tuple) else (i // 2, lax.rem(i, 2))

    def fold(self, held=None):
        core = place()[2]
        self.second = []
        for k, (line, copy) in enumerate(zip(self.lines, self.first)):
            copy.wait_recv()

            def add(i, carry, line=line):
                at = self.at(line, i)
                if held is None:
                    own = self.parts[at[0], at[1], core, at[2]]
                else:
                    own = held[at]
                self.came[at] = (
                    own.astype(jnp.float32) + self.came[at].astype(jnp.float32)
                ).astype(jnp.bfloat16)
                return carry

            lax.fori_loop(0, 4, add, 0)
            if k < 3:
                self.second.append(
                    self.send(
                        self.came.at[self.in_line(line)], self.across.at[k], self.peers[k]
                    )
                )

    def line(self):
        for copy in self.second:
            copy.wait_recv()

        def add(i, carry):
            spot = self.spot(i)
            total = self.came[self.at(self.lines[3], i)].astype(jnp.float32)
            for k in range(3):
                total = total + self.across[(k,) + spot].astype(jnp.float32)
            self.lined[spot] = total.astype(jnp.bfloat16)
            return carry

        lax.fori_loop(0, 4, add, 0)
        self.third = [
            self.send(self.lined.at[self.spot(target)], self.last.at[k], peer)
            for k, (target, peer) in enumerate(zip(self.targets, self.target_peers))
        ]

    def end(self, total_ref):
        for copy in self.third:
            copy.wait_recv()
        total = self.lined[self.spot(self.mine)].astype(jnp.float32)
        for k in range(3):
            total = total + self.last[k].astype(jnp.float32)
        total_ref[...] = total
        for copy in self.copies:
            copy.wait_send()


def scatter_room(width, x_first):
    line = (4,) if x_first else (2, 2)
    return [
        pltpu.VMEM((2, 4, 2, 48, width), jnp.bfloat16),
        pltpu.VMEM((3,) + line + (48, width), jnp.bfloat16),
        pltpu.VMEM(line + (48, width), jnp.bfloat16),
        pltpu.VMEM((3, 48, width), jnp.bfloat16),
    ]


def back_kernel(*refs):
    (own, out_from, query_from, rest_from, first_from, out_terms) = refs[:6]
    gradients, refs = refs[6:9], refs[1:]
    (turned, kv_rows, kv_lines, attended, tokens, log_total) = refs[8:14]
    (cos_ref, sin_ref, hidden, gain_two, prefix) = refs[14:19]
    (shrunk_total, first_total) = refs[19:21]
    totals = refs[21:26]
    everywhere = refs[26]
    (proj_all, w_out, w_in, grad_tokens, grad_lines, grad_queries, grad_packed) = refs[27:34]
    (sums, outgoing, incoming, parts, came_one, came_two, ring_sums) = refs[34:41]
    stages, out_parts, in_parts = refs[41:43], refs[43], refs[44]
    rooms = refs[45:65]
    (key_cos, key_sin, gathered) = refs[65:68]
    (ring_send, ring_recv, plane_send, plane_recv, kv_send, kv_recv, load_sem) = refs[68:75]
    (sum_send, sum_recv) = refs[75:]
    xh, y, core, xl, z = place()
    z, zp, z2, zm, up, down = ring_peers()
    ys, xs, y_peers, x_peers, other = plane()
    beside = device(xh, y, core, 1 - xl, z)
    column = [
        device(xh, y, c, xl, lax.rem(z + d, 4))
        for d, c in ((1, core), (3, core), (0, 1 - core), (2, core))
        + ((1, 1 - core), (3, 1 - core), (2, 1 - core))
    ]
    peers = column + y_peers + x_peers
    hail(peers)
    sums[...] = jnp.zeros_like(sums)
    key_tables(cos_ref, sin_ref, key_cos, key_sin)
    meet(peers)
    ring = ring_gather_begin(own, proj_all, ring_send.at[0], ring_recv.at[0])
    every = [
        Scatter(
            terms,
            *rooms[4 * i : 4 * i + 4],
            SCATTER_TURNS[i],
            plane_send.at[i],
            plane_recv.at[i],
        )
        for i, terms in enumerate(tuple(gradients) + (out_parts, in_parts))
    ]
    feed, out_scatter, in_scatter = every[:3], every[3], every[4]
    for scatter in feed:
        scatter.begin()

    def load(src, dst, i):
        copy = pltpu.make_async_copy(src, dst, load_sem.at[i])
        copy.start()
        return copy

    load_out = load(out_from.at[:, :, :, :, z], w_out, 0)
    keep = load(own, proj_all.at[z], 1)
    staged = [feed[i].stage(stages[i], load_sem.at[2 + i]) for i in range(2)]
    load_terms = load(out_terms, parts, 5)
    load_query = load(query_from, w_in.at[:, pl.ds(0, 384)], 6)
    load_rest = load(rest_from, w_in.at[:, pl.ds(384, 256)], 8)

    def give(c, start=0, count=224):
        rows = pl.ds(pl.multiple_of(c * 224 + start, 16), count)
        grad_tokens[rows] = nn(
            proj_all[c, start : start + count], w_out[...].reshape(1536, 384)
        ).astype(jnp.bfloat16)

    def lay(b):
        columns = pl.ds(pl.multiple_of(b * 128, 128), 128)
        grad_lines[:, columns] = jnp.transpose(
            grad_tokens[columns].astype(jnp.float32)
        ).astype(jnp.bfloat16)

    def block(b, g):
        columns = pl.ds(pl.multiple_of(b * 128, 128), 128)

        def run(span):
            head_rows = [
                pl.ds(pl.multiple_of((g * GROUP + h) * HD, HD), HD) for h in range(GROUP)
            ]
            queries = jnp.concatenate([turned[r, columns] for r in head_rows], axis=1)
            gradient = jnp.concatenate([grad_lines[r, columns] for r in head_rows], axis=1)
            held = jnp.concatenate([attended[r, columns] for r in head_rows], axis=1)
            inner = jnp.sum(
                gradient.astype(jnp.float32) * held.astype(jnp.float32), axis=0, keepdims=True
            )
            nothing = jnp.zeros_like(queries)
            both = jnp.concatenate(
                [
                    jnp.concatenate([queries, nothing], axis=1),
                    jnp.concatenate([nothing, gradient], axis=1),
                ],
                axis=0,
            )
            products = nn(kv_rows[g, :span], both)
            key_index = lax.broadcasted_iota(jnp.int32, (span, 384), 0)
            probs = jnp.exp(
                jnp.where(key_index < limits(prefix, xl, b), products[:, :384], NEG)
                - log_total[b * HEADS + g]
            )
            grad_scores = (probs * (products[:, 384:] - inner)).astype(jnp.bfloat16)
            sums[g, :span] += nt(
                jnp.concatenate([grad_scores, probs.astype(jnp.bfloat16)], axis=1), both
            )
            total = nn(kv_lines[g, :HD, :span], grad_scores) * HD ** (-0.5)
            cos_here, sin_here = cos_ref[:, columns], sin_ref[:, columns]
            back = [
                turn_back(total[:, h * 128 : (h + 1) * 128], cos_here, sin_here)
                for h in range(GROUP)
            ]
            grad_queries[g, columns] = jnp.transpose(jnp.concatenate(back, axis=0)).astype(
                jnp.bfloat16
            )

        by_span(xl, b, run)

    def both_heads(t, carry):
        block(arrival(z, lax.div(t, 2)), lax.rem(t, 2))
        return carry

    keep.wait()
    load_out.wait()
    give(z)
    lay(2 * z)

    def own_block(g, carry):
        block(2 * z, g)
        return carry

    lax.fori_loop(0, 2, own_block, 0)
    ring = ring_gather_forward(proj_all, ring, ring_send.at[0], ring_recv.at[0])
    give(zm, 112, 112)
    give(zp, 0, 112)
    lay(arrival(z, 1))

    def beside_block(g, carry):
        block(arrival(z, 1), g)
        return carry

    staged[0].wait()
    feed[0].fold(stages[0])
    staged[0] = feed[2].stage(stages[0], load_sem.at[4])
    staged[1].wait()
    feed[1].fold(stages[1])
    staged[0].wait()
    feed[2].fold(stages[0])
    lax.fori_loop(0, 2, beside_block, 0)
    ring[2].wait_recv()
    give(zm, 0, 112)
    ring[3].wait_recv()
    give(zp, 112, 112)
    for i in range(2, 4):
        lay(arrival(z, i))
    lax.fori_loop(4, 8, both_heads, 0)
    ring[4].wait_recv()
    ring[5].wait_recv()
    give(z2)
    for i in range(4, 7):
        lay(arrival(z, i))
    for copy in ring:
        copy.wait_send()
    out_parts[...] = (
        tn(proj_all[...].reshape(896, 1536), tokens[...])
        .astype(jnp.bfloat16)
        .reshape(2, 4, 2, 2, 48, 384)
    )
    out_scatter.begin()
    load_first = load(first_from, proj_all, 7)
    load_terms.wait()
    shrunk = ring_scatter_begin(parts, came_one, ring_send.at[1], ring_recv.at[1])

    def exchange(g):
        theirs = sums[g, pl.ds(pl.multiple_of((1 - xl) * 896, 128), 896)]
        outgoing[g] = theirs.astype(jnp.bfloat16)
        copy = remote(outgoing.at[g], incoming.at[g], kv_send.at[g], kv_recv.at[g], beside)
        copy.start()
        return copy

    def far_block(g):
        def body(i, carry):
            block(arrival_far(z, i), g)
            return carry

        lax.fori_loop(4, 7, body, 0)

    far_block(0)
    kv_copies = [exchange(0)]
    shrunk = ring_scatter_forward(
        parts, came_one, ring_sums, shrunk, ring_send.at[1], ring_recv.at[1]
    )
    out_scatter.fold()
    far_block(1)
    kv_copies.append(exchange(1))
    for scatter in feed:
        scatter.line()
    out_scatter.line()
    load_query.wait()
    load_rest.wait()
    load_first.wait()
    ring_scatter_end(parts, came_one, shrunk_total, shrunk)
    for g in range(HEADS):
        kv_copies[g].wait()
        mine = sums[g, pl.ds(pl.multiple_of(xl * 896, 128), 896)] + incoming[g].astype(
            jnp.float32
        )
        mine = mine * key_cos[...] - swap_halves(mine) * key_sin[...]
        grad_packed[:, g * 320 : g * 320 + 192] = grad_queries[g]
        grad_packed[:, g * 320 + 192 : g * 320 + 320] = mine.astype(jnp.bfloat16)

    def spread(c):
        rows = pl.ds(pl.multiple_of(c * 224, 16), 224)
        parts[c] = nt(grad_packed[rows], w_in[...]).astype(jnp.bfloat16)

    spread(z2)
    far = ring_scatter_far(parts, came_two, ring_send.at[2], ring_recv.at[2])
    spread(zp)
    spread(zm)
    near = ring_scatter_near(parts, came_two, ring_send.at[2], ring_recv.at[2])
    in_parts[...] = (
        tn(proj_all[...].reshape(896, 1536), grad_packed[...])
        .astype(jnp.bfloat16)
        .reshape(2, 4, 2, 2, 48, 640)
    )
    in_scatter.begin()
    spread(z)
    in_scatter.fold()
    ring = ring_scatter_forward(
        parts, came_two, ring_sums, far + near, ring_send.at[2], ring_recv.at[2]
    )
    for i in range(4):
        every[i].end(totals[i])
    in_scatter.line()
    ring_scatter_end(parts, came_two, first_total, ring)
    rows = hidden[...].astype(jnp.float32)
    scaling = lax.rsqrt(jnp.mean(rows * rows, axis=-1, keepdims=True) + EPS)
    gain_one = jnp.sum(first_total[...] * rows * scaling, axis=0, keepdims=True)
    in_scatter.end(totals[4])
    squares = jnp.zeros((1, 1), jnp.float32)
    for total in totals:
        terms = total[...]
        squares = squares + jnp.sum(
            jnp.sum(terms * terms, axis=0, keepdims=True), axis=1, keepdims=True
        )
    for k in range(3):
        everywhere[k : k + 1] = gain_one[:, k * 512 : (k + 1) * 512]
        everywhere[3 + k : 4 + k] = gain_two[:, k * 512 : (k + 1) * 512]
    everywhere[6:8] = jnp.broadcast_to(squares, (2, 512))
    used = 0
    groups = ((column, z * 2 + core, 8), (x_peers, xh * 2 + xl, 4), (y_peers, y, 4))
    for axis, (group, here, count) in enumerate(groups):
        gathered[axis, here] = everywhere[...]
        spot = gathered.at[axis, here]
        copies = []
        for peer in group:
            copies.append(remote(spot, spot, sum_send.at[used], sum_recv.at[used], peer))
            copies[-1].start()
            used += 1
        for copy in copies:
            copy.wait()
        order = gathered[axis, 0]
        for k in range(1, count):
            order = order + gathered[axis, k]
        everywhere[...] = order


SCATTER_TURNS = (False, False, True, True, False)


def back(
    own, w_out, w_query, w_rest, first_all, out_terms, gradients, saved, tables, hidden, gain_two, prefix
):
    any_place = pl.BlockSpec(memory_space=pl.ANY)
    whole = pl.BlockSpec(memory_space=pltpu.VMEM)
    rows, width = own.shape
    low, full = jnp.bfloat16, jnp.float32
    widths = [g.shape[-1] for g in gradients] + [384, 640]
    rooms = []
    for w, turn_first in zip(widths, SCATTER_TURNS):
        rooms += scatter_room(w, turn_first)
    return pl.pallas_call(
        back_kernel,
        out_shape=(jax.ShapeDtypeStruct((rows, width), full),) * 2
        + tuple(jax.ShapeDtypeStruct((48, w), full) for w in widths)
        + (jax.ShapeDtypeStruct((8, 512), full),),
        in_specs=[whole]
        + [any_place] * 8
        + [whole] * 10
        + [pl.BlockSpec(memory_space=pltpu.SMEM)],
        out_specs=(whole,) * 8,
        scratch_shapes=[
            pltpu.VMEM((4, rows, width), low),
            pltpu.VMEM((2, 4, 2, 2, 48, 384), low),
            pltpu.VMEM((1536, 640), low),
            pltpu.VMEM((896, 384), low),
            pltpu.VMEM((384, 896), low),
            pltpu.VMEM((HEADS, 896, 192), low),
            pltpu.VMEM((896, 640), low),
            pltpu.VMEM((HEADS, 1792, 128), full),
            pltpu.VMEM((HEADS, 896, 128), low),
            pltpu.VMEM((HEADS, 896, 128), low),
            pltpu.VMEM((4, rows, width), low),
            pltpu.VMEM((6, rows // 2, width), low),
            pltpu.VMEM((6, rows // 2, width), low),
            pltpu.VMEM((2, rows // 2, width), low),
            pltpu.VMEM((2, 4, 2, 48, 960), low),
            pltpu.VMEM((2, 4, 2, 48, 960), low),
            pltpu.VMEM((2, 4, 2, 2, 48, 384), low),
            pltpu.VMEM((2, 4, 2, 2, 48, 640), low),
            *rooms,
            pltpu.VMEM((896, 128), full),
            pltpu.VMEM((896, 128), full),
            pltpu.VMEM((3, 8, 8, 512), full),
            pltpu.SemaphoreType.DMA((3, 6)),
            pltpu.SemaphoreType.DMA((3, 6)),
            pltpu.SemaphoreType.DMA((5, 10)),
            pltpu.SemaphoreType.DMA((5, 10)),
            pltpu.SemaphoreType.DMA((2,)),
            pltpu.SemaphoreType.DMA((2,)),
            pltpu.SemaphoreType.DMA((9,)),
            pltpu.SemaphoreType.DMA((13,)),
            pltpu.SemaphoreType.DMA((13,)),
        ],
        compiler_params=pltpu.CompilerParams(
            collective_id=2, has_side_effects=True, vmem_limit_bytes=BACK_VMEM
        ),
    )(
        own,
        w_out,
        w_query,
        w_rest,
        first_all,
        out_terms,
        *(g.reshape(2, 4, 2, 2, 48, g.shape[-1]) for g in gradients),
        *saved,
        *tables,
        hidden,
        gain_two,
        prefix,
    )


BACK_VMEM = 63 * 2**20


def finish_kernel(*refs):
    (sums, grad_first, hidden, grad_residual, residual, shrunk) = refs[:6]
    (gains, gains_first, gains_second) = refs[6:9]
    (grad_gate, grad_up, grad_shrink, grad_output, grad_input) = refs[9:14]
    masters = [refs[14 + 3 * i : 17 + 3 * i] for i in range(4)]
    (block_output, input_gradient, norm_ref) = refs[26:29]
    gains_new = refs[29:32]
    news = [refs[32 + 3 * i : 35 + 3 * i] for i in range(4)]
    block_output[...] = (residual[...] + RESID * shrunk[...]).astype(jnp.bfloat16)
    rows = hidden[...].astype(jnp.float32)
    scaling = lax.rsqrt(jnp.mean(rows * rows, axis=-1, keepdims=True) + EPS)
    normed = rows * scaling
    gradient = grad_first[...] * gains[0:1]
    input_gradient[...] = grad_residual[...] + scaling * (
        gradient - normed * jnp.mean(gradient * normed, axis=-1, keepdims=True)
    )
    grad_gains = jnp.concatenate(
        [
            jnp.concatenate([sums[3 * r + k : 3 * r + k + 1] for k in range(3)], axis=1)
            for r in range(2)
        ],
        axis=0,
    )
    gain_squares = jnp.sum(
        jnp.sum(grad_gains * grad_gains, axis=0, keepdims=True), axis=1, keepdims=True
    )
    gradient_norm = jnp.sqrt(sums[6:7, 0:1] + gain_squares)
    norm_ref[...] = gradient_norm
    factor = jnp.minimum(1.0, MAX_NORM / (gradient_norm + 1e-06))

    def put(targets, results):
        for target, result in zip(targets, results):
            target[...] = result

    put(
        gains_new,
        adamw(
            gains[...], factor * grad_gains, gains_first[...], gains_second[...], GAIN_RATE, 0.0
        ),
    )
    for i, terms in ((0, grad_input), (1, grad_output), (3, grad_shrink)):
        weight, first, second = masters[i]
        put(news[i], adamw(weight[...], factor * terms[...], first[...], second[...], RATE, DECAY))
    for k, terms in enumerate((grad_gate, grad_up)):
        weight, first, second = masters[2]
        results = adamw(weight[k], factor * terms[...], first[k], second[k], RATE, DECAY)
        for target, result in zip(news[2], results):
            target[k] = result


def finish(sums, rows_in, gains, gradients, masters):
    full = jnp.float32
    flat = [array for group in masters for array in group]

    def cut(array):
        shape = array.shape[:-2] + (array.shape[-2] // 2, array.shape[-1])
        lead = (0,) * (array.ndim - 2)
        return pl.BlockSpec(shape, lambda i: lead + (i, 0))

    def kept(shape):
        return pl.BlockSpec(shape, lambda i: (0, 0))

    width = rows_in[0].shape[1]
    rows = jax.ShapeDtypeStruct(rows_in[0].shape, full)
    return pl.pallas_call(
        finish_kernel,
        grid=(2,),
        out_shape=(
            jax.ShapeDtypeStruct(rows.shape, jnp.bfloat16),
            rows,
            jax.ShapeDtypeStruct((1, 1), full),
            *(jax.ShapeDtypeStruct((2, width), full) for _ in range(3)),
            *(jax.ShapeDtypeStruct(array.shape, full) for array in flat),
        ),
        in_specs=[kept(sums.shape)]
        + [cut(array) for array in rows_in]
        + [kept(array.shape) for array in gains]
        + [cut(array) for array in gradients]
        + [cut(array) for array in flat],
        out_specs=(cut(rows), cut(rows), kept((1, 1)))
        + (kept((2, width)),) * 3
        + tuple(cut(array) for array in flat),
        compiler_params=pltpu.CompilerParams(vmem_limit_bytes=VMEM_MOST),
    )(sums, *rows_in, *gains, *gradients, *flat)


def shards(
    hidden_in,
    cotangent,
    prefix,
    positions,
    norm_gains,
    gains_first,
    gains_second,
    input_weight,
    input_first,
    input_second,
    output_weight,
    output_first,
    output_second,
    expand_weight,
    expand_first,
    expand_second,
    shrink_weight,
    shrink_first,
    shrink_second,
):
    low = jnp.bfloat16
    hidden, upstream = hidden_in[0], cotangent[0]
    masters = (
        (input_weight, input_first, input_second),
        (output_weight.T, output_first.T, output_second.T),
        (expand_weight, expand_first, expand_second),
        (shrink_weight.T, shrink_first.T, shrink_second.T),
    )
    tables = angles(positions[0])
    (
        first_all,
        shrunk_all,
        w_query,
        w_rest,
        w_gate,
        w_up,
        w_out,
        w_shrink,
        turned,
        kv_rows,
        kv_lines,
        attended,
        tokens,
        log_total,
        projected,
    ) = front(
        hidden,
        upstream,
        norm_gains[:1],
        (input_weight, expand_weight, output_weight.T, shrink_weight.T),
        tables,
        prefix,
    )
    (
        residual,
        grad_residual,
        projected_gradient,
        gain_two,
        grad_gate,
        grad_up,
        grad_shrink,
        out_parts,
    ) = middle(
        hidden, upstream, projected, norm_gains[1:], shrunk_all, w_gate, w_up, w_shrink
    )
    shrunk, grad_first, *gradients, sums = back(
        projected_gradient,
        w_out,
        w_query.reshape(1536, 384),
        w_rest.reshape(1536, 256),
        first_all,
        out_parts,
        (grad_gate, grad_up, grad_shrink),
        (turned, kv_rows, kv_lines, attended, tokens, log_total),
        tables,
        hidden,
        gain_two,
        prefix,
    )
    outs = finish(
        sums,
        (grad_first, hidden, grad_residual, residual, shrunk),
        (norm_gains, gains_first, gains_second),
        gradients,
        masters,
    )
    block_output, input_gradient, gradient_norm = outs[0], outs[1], outs[2].reshape(())
    gains_new, input_new, output_new, expand_new, shrink_new = (
        outs[3 + 3 * i : 6 + 3 * i] for i in range(5)
    )
    return (
        block_output[None],
        input_gradient[None],
        gradient_norm,
        *gains_new,
        *input_new,
        *(array.T for array in output_new),
        *expand_new,
        *(array.T for array in shrink_new),
    )


def solution(mesh):
    return jax.shard_map(
        shards,
        mesh=mesh,
        in_specs=(
            P("shard", ("context", "tensor"), None),
            P("shard", ("context", "tensor"), None),
            P("shard"),
            P("shard", "context"),
            P(),
            P(),
            P(),
            P(("shard", "context"), "tensor"),
            P(("shard", "context"), "tensor"),
            P(("shard", "context"), "tensor"),
            P("tensor", ("shard", "context")),
            P("tensor", ("shard", "context")),
            P("tensor", ("shard", "context")),
            P(None, ("shard", "context"), "tensor"),
            P(None, ("shard", "context"), "tensor"),
            P(None, ("shard", "context"), "tensor"),
            P("tensor", ("shard", "context")),
            P("tensor", ("shard", "context")),
            P("tensor", ("shard", "context")),
        ),
        out_specs=(
            P("shard", ("context", "tensor"), None),
            P("shard", ("context", "tensor"), None),
            P(),
            P(),
            P(),
            P(),
            P(("shard", "context"), "tensor"),
            P(("shard", "context"), "tensor"),
            P(("shard", "context"), "tensor"),
            P("tensor", ("shard", "context")),
            P("tensor", ("shard", "context")),
            P("tensor", ("shard", "context")),
            P(None, ("shard", "context"), "tensor"),
            P(None, ("shard", "context"), "tensor"),
            P(None, ("shard", "context"), "tensor"),
            P("tensor", ("shard", "context")),
            P("tensor", ("shard", "context")),
            P("tensor", ("shard", "context")),
        ),
        check_vma=False,
    )
```

```python
import functools
import math

import jax
import jax.numpy as jnp
from jax import lax
from jax.experimental import pallas as pl
from jax.experimental.pallas import tpu as pltpu
from jax.sharding import PartitionSpec as P
import numpy as np

HD = 64
GROUP = 3
STEP = 10
HEADS = 2
BLOCKS = 7
VMEM_MOST = 60 * 2**20
MESH = pl.DeviceIdType.MESH


EPS = 1e-05
RESID = 1.4 / math.sqrt(52.0)
ROPE_BASE = 10000.0
MAX_NORM = 1.0
RATE = 0.1
GAIN_RATE = 1.0
BETA_ONE = 0.9
BETA_TWO = 0.95
ADAM_EPS = 1e-08
DECAY = 0.1
NEG = -1e30


def angles(places):
    frequency = (ROPE_BASE ** (-2.0 * np.arange(HD // 2) / HD)).astype(np.float32)
    phase_turn = places.astype(jnp.float32) * frequency[:, None]
    return (jnp.cos(phase_turn), jnp.sin(phase_turn))


def adamw(weight, gradient, momentum, variance, step_rate, decay_rate):
    momentum_new = BETA_ONE * momentum + (1.0 - BETA_ONE) * gradient
    variance_new = BETA_TWO * variance + (1.0 - BETA_TWO) * gradient * gradient
    momentum_hat = momentum_new / (1.0 - BETA_ONE**STEP)
    variance_hat = variance_new / (1.0 - BETA_TWO**STEP)
    updated = weight - step_rate * (
        momentum_hat / (jnp.sqrt(variance_hat) + ADAM_EPS) + decay_rate * weight
    )
    return (momentum_new, variance_new, updated)


def nn(a, b):
    return lax.dot_general(a, b, (((1,), (0,)), ((), ())), preferred_element_type=jnp.float32)


def nt(a, b):
    return lax.dot_general(a, b, (((1,), (1,)), ((), ())), preferred_element_type=jnp.float32)


def place():
    shard = lax.axis_index("shard")
    return (
        shard // 8,
        lax.rem(shard // 2, 4),
        lax.rem(shard, 2),
        lax.axis_index("context"),
        lax.axis_index("tensor"),
    )


def device(xh, y, core, xl, z):
    return {"shard": (xh * 4 + y) * 2 + core, "context": xl, "tensor": z}


def hail(peers):
    barrier = pltpu.get_barrier_semaphore()
    for peer in peers:
        pl.semaphore_signal(barrier, inc=1, device_id=peer, device_id_type=MESH)


def meet(peers):
    pl.semaphore_wait(pltpu.get_barrier_semaphore(), len(peers))


def remote(src, dst, send_sem, recv_sem, peer):
    return pltpu.make_async_remote_copy(
        src_ref=src,
        dst_ref=dst,
        send_sem=send_sem,
        recv_sem=recv_sem,
        device_id=peer,
        device_id_type=MESH,
    )


def turn(block, cos_part, sin_part):
    lower_half, upper_half = block[: HD // 2], block[HD // 2 :]
    return jnp.concatenate(
        [
            lower_half * cos_part - upper_half * sin_part,
            upper_half * cos_part + lower_half * sin_part,
        ],
        axis=0,
    )


def turn_back(block, cos_part, sin_part):
    return turn(block, cos_part, -sin_part)


def by_span(context, b, run):
    near = (context == 0) | (b <= 3)

    @pl.when(near)
    def _():
        run(1408)

    @pl.when(jnp.logical_not(near))
    def _():
        run(1792)


def limits(prefix, xl, b):
    lane = lax.broadcasted_iota(jnp.int32, (1, GROUP * 128), 1)
    row = xl * 896 + b * 128 + lax.rem(lane, 128)
    return jnp.maximum(row + 1, prefix[0])


def key_tables(cos_ref, sin_ref, key_cos, key_sin):
    cos_part, sin_part = jnp.transpose(cos_ref[...]), jnp.transpose(sin_ref[...])
    still = jnp.ones((896, HD), jnp.float32)
    key_cos[...] = jnp.concatenate([cos_part, cos_part, still], axis=1)
    key_sin[...] = jnp.concatenate([-sin_part, sin_part, 0.0 * still], axis=1)


def arrival(z, i):
    edge = (3 - z) // 3
    if isinstance(i, int) and i < 2:
        shift = i * (2 * edge - 1)
    elif isinstance(i, int) and i > 3:
        shift = i - 2 + edge
    else:
        shift = 3 * i - 8 + edge
    return lax.rem(2 * z + shift + 7, 7)


def arrival_far(z, i):
    return lax.rem(2 * z + i + 5 + (3 - z) // 3, 7)


def ring_peers():
    xh, y, core, xl, z = place()
    return (
        z,
        lax.rem(z + 1, 4),
        lax.rem(z + 2, 4),
        lax.rem(z + 3, 4),
        device(xh, y, core, xl, lax.rem(z + 1, 4)),
        device(xh, y, core, xl, lax.rem(z + 3, 4)),
    )


def halves(ref, index):
    rows = ref.shape[1] // 2
    return ref.at[index, pl.ds(0, rows)], ref.at[index, pl.ds(rows, rows)]


def ring_gather_begin(own, held, send_sem, recv_sem):
    z, zp, z2, zm, up, down = ring_peers()
    rows = own.shape[0] // 2
    first, second = own.at[pl.ds(0, rows)], own.at[pl.ds(rows, rows)]
    first_to, second_to = halves(held, z)
    copies = [
        remote(second, second_to, send_sem.at[0], recv_sem.at[0], up),
        remote(first, first_to, send_sem.at[1], recv_sem.at[1], down),
        remote(first, first_to, send_sem.at[2], recv_sem.at[2], up),
        remote(second, second_to, send_sem.at[3], recv_sem.at[3], down),
    ]
    for copy in copies:
        copy.start()
    return copies


def ring_gather_forward(held, copies, send_sem, recv_sem):
    z, zp, z2, zm, up, down = ring_peers()
    copies[0].wait_recv()
    below = halves(held, zm)[1]
    on_up = remote(below, below, send_sem.at[4], recv_sem.at[4], up)
    on_up.start()
    copies[1].wait_recv()
    above = halves(held, zp)[0]
    on_down = remote(above, above, send_sem.at[5], recv_sem.at[5], down)
    on_down.start()
    return copies + [on_up, on_down]


def ring_gather_end(copies):
    for copy in copies:
        copy.wait_send()
    for copy in copies[2:]:
        copy.wait_recv()


def in_rows(count, step, run):
    def body(i, carry):
        run(pl.ds(pl.multiple_of(i * step, step), step))
        return carry

    lax.fori_loop(0, count // step, body, 0)


def ring_scatter_near(parts, came, send_sem, recv_sem):
    z, zp, z2, zm, up, down = ring_peers()
    copies = [
        remote(halves(parts, zp)[0], came.at[2], send_sem.at[2], recv_sem.at[2], up),
        remote(halves(parts, zm)[1], came.at[3], send_sem.at[3], recv_sem.at[3], down),
    ]
    for copy in copies:
        copy.start()
    return copies


def ring_scatter_far(parts, came, send_sem, recv_sem):
    z, zp, z2, zm, up, down = ring_peers()
    copies = [
        remote(halves(parts, z2)[1], came.at[0], send_sem.at[0], recv_sem.at[0], up),
        remote(halves(parts, z2)[0], came.at[1], send_sem.at[1], recv_sem.at[1], down),
    ]
    for copy in copies:
        copy.start()
    return copies


def ring_scatter_begin(parts, came, send_sem, recv_sem):
    far = ring_scatter_far(parts, came, send_sem, recv_sem)
    return far + ring_scatter_near(parts, came, send_sem, recv_sem)


def ring_scatter_forward(parts, came, sums, copies, send_sem, recv_sem):
    z, zp, z2, zm, up, down = ring_peers()
    count = came.shape[1]
    copies[0].wait_recv()

    def add_up(rows):
        sums[0, rows] = (
            came[0, rows].astype(jnp.float32)
            + parts[zp, pl.ds(pl.multiple_of(rows.start + count, 16), 16)].astype(jnp.float32)
        ).astype(jnp.bfloat16)

    in_rows(count, 16, add_up)
    on_up = remote(sums.at[0], came.at[4], send_sem.at[4], recv_sem.at[4], up)
    on_up.start()
    copies[1].wait_recv()

    def add_down(rows):
        sums[1, rows] = (
            came[1, rows].astype(jnp.float32) + parts[zm, rows].astype(jnp.float32)
        ).astype(jnp.bfloat16)

    in_rows(count, 16, add_down)
    on_down = remote(sums.at[1], came.at[5], send_sem.at[5], recv_sem.at[5], down)
    on_down.start()
    return copies + [on_up, on_down]


def ring_scatter_end(parts, came, total, copies):
    z, zp, z2, zm, up, down = ring_peers()
    count = came.shape[1]
    for copy in copies[2:]:
        copy.wait_recv()
    for copy in copies:
        copy.wait_send()

    def add(rows):
        later = pl.ds(pl.multiple_of(rows.start + count, 16), 16)
        total[rows] = (
            parts[z, rows].astype(jnp.float32)
            + came[2, rows].astype(jnp.float32)
            + came[5, rows].astype(jnp.float32)
        )
        total[later] = (
            parts[z, later].astype(jnp.float32)
            + came[3, rows].astype(jnp.float32)
            + came[4, rows].astype(jnp.float32)
        )

    in_rows(count, 16, add)


def plane():
    xh, y, core, xl, z = place()
    ys = [lax.rem(y + d, 4) for d in (1, 3, 2)]
    step = xh * 2 + xl
    xs = [lax.rem(step + d, 4) for d in (1, 3, 2)]
    xs = [(x // 2, lax.rem(x, 2)) for x in xs]
    y_peers = [device(xh, other, core, xl, z) for other in ys]
    x_peers = [device(h, y, core, l, z) for h, l in xs]
    return ys, xs, y_peers, x_peers, device(xh, y, 1 - core, xl, z)


class PlaneGather:
    def __init__(self, own, held, y_first, shared, send_sem, recv_sem):
        self.own, self.held, self.y_first, self.shared = own, held, y_first, shared
        self.send_sem, self.recv_sem, self.used = send_sem, recv_sem, 0
        self.copies, self.first, self.second, self.third = [], [], [], []
        xh, y, core, xl, z = place()
        ys, xs, self.y_peers, self.x_peers, self.other = plane()
        self.core = core
        if y_first:
            self.mine, self.wheres, self.peers = (xh, xl), xs, self.x_peers
        else:
            self.mine, self.wheres, self.peers = y, ys, self.y_peers

    def send(self, src, dst, peer):
        copy = remote(src, dst, self.send_sem.at[self.used], self.recv_sem.at[self.used], peer)
        self.used += 1
        copy.start()
        self.copies.append(copy)
        return copy

    def begin(self):
        xh, y, core, xl, z = place()
        target = self.held.at[xh, y, core, xl]
        peers = self.y_peers if self.y_first else self.x_peers
        self.first = [self.send(self.own, target, peer) for peer in peers]

    def half(self, where, k):
        if self.y_first:
            return self.held.at[where[0], pl.ds(2 * k, 2), self.core, where[1]]
        return self.held.at[k, where, self.core]

    def line(self, where):
        if self.y_first:
            return self.held.at[where[0], :, self.core, where[1]]
        return self.held.at[:, where, self.core]

    def give(self, where):
        line = self.line(where)
        self.third.append(self.send(line, line, self.other))

    def spread(self):
        for copy in self.first:
            copy.wait_recv()
        low_half, high_half = self.half(self.mine, 0), self.half(self.mine, 1)
        ahead, behind = self.peers[:2]
        self.second = [
            self.send(high_half, high_half, ahead),
            self.send(low_half, low_half, behind),
            self.send(low_half, low_half, ahead),
            self.send(high_half, high_half, behind),
        ]
        if self.shared:
            self.give(self.mine)

    def relay(self):
        ahead, behind = self.peers[:2]
        self.second[0].wait_recv()
        part = self.half(self.wheres[1], 1)
        self.second.append(self.send(part, part, ahead))
        self.second[1].wait_recv()
        part = self.half(self.wheres[0], 0)
        self.second.append(self.send(part, part, behind))

    def share(self):
        self.second[2].wait_recv()
        self.give(self.wheres[1])
        self.second[3].wait_recv()
        self.give(self.wheres[0])
        self.second[4].wait_recv()
        self.second[5].wait_recv()
        self.give(self.wheres[2])

    def end(self):
        for copy in self.third if self.shared else self.second[2:]:
            copy.wait_recv()
        for copy in self.copies:
            copy.wait_send()


def swap_halves(block):
    lane = lax.broadcasted_iota(jnp.int32, block.shape, 1)
    return jnp.where(
        lane < HD // 2, pltpu.roll(block, 128 - HD // 2, 1), pltpu.roll(block, HD // 2, 1)
    )


def front_kernel(*refs):
    (hidden, cotangent, gain, m_in, m_expand, m_out, m_shrink) = refs[:7]
    (cos_ref, sin_ref, prefix) = refs[7:10]
    (first_to, shrunk_all, query_to, rest_to) = refs[10:14]
    (gate_all, up_all, out_all, shrink_all) = refs[14:18]
    (turned_to, rows_to, lines_to, attended, tokens, log_total, total) = refs[18:25]
    (first_all, shrunk, in_query, in_rest, w_gate, w_up, w_out, w_shrink) = refs[25:33]
    (turned, kv_rows, kv_lines, key_cos, key_sin) = refs[33:38]
    (packed, held_rows, own_tokens) = refs[38:41]
    (ring_send, ring_recv, plane_send, plane_recv, out_send, out_recv) = refs[41:47]
    (kv_send, kv_recv, token_send, token_recv, own_sem, out_sem) = refs[47:]
    xh, y, core, xl, z = place()
    z, zp, z2, zm, up, down = ring_peers()
    ys, xs, y_peers, x_peers, other = plane()
    beside = device(xh, y, core, 1 - xl, z)
    across = device(xh, y, core, xl, z2)
    peers = [up, down, across, other] + y_peers + x_peers
    hail(peers)
    low = jnp.bfloat16
    query_own, rest_own = in_query.at[xh, y, core, xl], in_rest.at[xh, y, core, xl]
    query_own[...] = m_in[:, :384].astype(low)
    rest_own[...] = m_in[:, 384:].astype(low)
    w_out[z] = m_out[...].astype(low)
    rows = hidden[...].astype(jnp.float32)
    scaling = lax.rsqrt(jnp.mean(rows * rows, axis=-1, keepdims=True) + EPS)
    first_all[z] = (rows * scaling * gain[0:1]).astype(low)
    meet(peers)
    out_copies = [
        remote(w_out.at[z], w_out.at[z], out_send.at[i], out_recv.at[i], peer)
        for i, peer in enumerate((up, down, across))
    ]
    for copy in out_copies:
        copy.start()
    owns = (query_own, rest_own, w_out, w_gate, w_up, w_shrink)
    helds = (in_query, in_rest, out_all, gate_all, up_all, shrink_all)
    gathers = [
        PlaneGather(own, held, y_first, i < 3, plane_send.at[i], plane_recv.at[i])
        for i, (own, held, y_first) in enumerate(zip(owns, helds, GATHER_TURNS))
    ]
    query_gather, rest_gather, out_gather, *feed_gathers = gathers
    query_gather.begin()
    rest_gather.begin()
    ring = ring_gather_begin(first_all.at[z], first_all, ring_send.at[0], ring_recv.at[0])
    w_gate[...] = m_expand[0].astype(low)
    w_up[...] = m_expand[1].astype(low)
    w_shrink[...] = m_shrink[...].astype(low)
    shrunk[...] = (RESID * cotangent[...].astype(jnp.float32)).astype(low)
    keeps = [
        pltpu.make_async_copy(own, held.at[xh, y, core, xl], own_sem.at[i])
        for i, (own, held) in enumerate(zip(owns[3:], helds[3:]))
    ]
    keeps.append(pltpu.make_async_copy(shrunk, shrunk_all.at[z], own_sem.at[3]))
    for keep in keeps:
        keep.start()
    for copy in out_copies:
        copy.wait_recv()
    out_gather.begin()
    keeps.append(pltpu.make_async_copy(w_out, out_all.at[xh, y, core, xl], own_sem.at[4]))
    keeps[-1].start()
    query_gather.spread()
    rest_gather.spread()
    for keep in keeps:
        keep.wait()
    for gather in feed_gathers:
        gather.begin()
    key_tables(cos_ref, sin_ref, key_cos, key_sin)
    query_gather.relay()
    rest_gather.relay()
    ring = ring_gather_forward(first_all, ring, ring_send.at[0], ring_recv.at[0])
    out_gather.spread()
    query_gather.share()
    rest_gather.share()
    query_gather.end()
    rest_gather.end()

    def project(c, rows):
        out = jnp.concatenate(
            [
                nn(first_all[c], in_query[...].reshape(1536, 384)),
                nn(first_all[c], in_rest[...].reshape(1536, 256)),
            ],
            axis=1,
        )
        packed[rows] = out
        for g in range(HEADS):
            block = out[:, g * 320 + 192 : g * 320 + 320]
            mine = pl.ds(pl.multiple_of(xl * 896 + c * 224, 16), 224)
            kv_rows[g, mine] = (
                block * key_cos[rows] + swap_halves(block) * key_sin[rows]
            ).astype(low)

    kv_copies = []
    for i, c in enumerate((z, zm, zp, z2)):
        if i == 1:
            ring[2].wait_recv()
        if i == 2:
            ring[3].wait_recv()
        if i == 3:
            ring[4].wait_recv()
            ring[5].wait_recv()
        project(c, pl.ds(pl.multiple_of(c * 224, 16), 224))
        mine = kv_rows.at[:, pl.ds(pl.multiple_of(xl * 896 + c * 224, 16), 224)]
        kv_copies.append(remote(mine, mine, kv_send.at[i], kv_recv.at[i], beside))
        kv_copies[-1].start()
    out_gather.relay()
    for gather in feed_gathers:
        gather.spread()
    later = ring_gather_begin(shrunk, shrunk_all, ring_send.at[1], ring_recv.at[1])
    saves = []

    def save(src, dst):
        saves.append(pltpu.make_async_copy(src, dst, own_sem.at[5 + len(saves)]))
        saves[-1].start()

    save(first_all, first_to)
    save(in_query, query_to)
    save(in_rest, rest_to)

    def turn_block(b, carry):
        columns = pl.ds(pl.multiple_of(b * 128, 128), 128)
        lines = jnp.transpose(packed[columns])
        cos_here, sin_here = cos_ref[:, columns], sin_ref[:, columns]
        for g in range(HEADS):
            for h in range(GROUP):
                at = (g * 5 + h) * HD
                turned[(g * GROUP + h) * HD : (g * GROUP + h + 1) * HD, columns] = (
                    turn(lines[at : at + HD], cos_here, sin_here) * HD ** (-0.5)
                ).astype(low)
        return carry

    lax.fori_loop(0, BLOCKS, turn_block, 0)
    save(turned, turned_to)
    for copy in kv_copies:
        copy.wait_recv()
    for g in range(HEADS):
        kv_lines[g] = jnp.transpose(kv_rows[g].astype(jnp.float32)).astype(low)
    save(kv_rows, rows_to)
    save(kv_lines, lines_to)

    def block(b, g):
        columns = pl.ds(pl.multiple_of(b * 128, 128), 128)

        def run(span):
            head_rows = [
                pl.ds(pl.multiple_of((g * GROUP + h) * HD, HD), HD) for h in range(GROUP)
            ]
            queries = jnp.concatenate([turned[r, columns] for r in head_rows], axis=1)
            queries = jnp.concatenate([queries, jnp.zeros_like(queries)], axis=0)
            scores = nn(kv_rows[g, :span], queries)
            key_index = lax.broadcasted_iota(jnp.int32, (span, 384), 0)
            scores = jnp.where(key_index < limits(prefix, xl, b), scores, NEG)
            row_max = jnp.max(scores, axis=0, keepdims=True)
            shifted = jnp.exp(scores - row_max)
            exp_total = jnp.sum(shifted, axis=0, keepdims=True)
            out = nn(kv_lines[g, HD:, :span], shifted.astype(low)) * (1.0 / exp_total)
            for h in range(GROUP):
                attended[head_rows[h], columns] = out[:, h * 128 : (h + 1) * 128].astype(low)
            log_total[b * HEADS + g] = row_max + jnp.log(exp_total)

        by_span(xl, b, run)

    def near_heads(t, carry):
        block(arrival(z, lax.div(t, 2)), lax.rem(t, 2))
        return carry

    def far_heads(t, carry):
        block(arrival_far(z, lax.div(t, 2)), lax.rem(t, 2))
        return carry

    def beside_block(g, carry):
        block(arrival(z, 1), g)
        return carry

    def own_block(g, carry):
        block(2 * z, g)
        return carry

    def lay(b):
        columns = pl.ds(pl.multiple_of(b * 128, 128), 128)
        tokens[columns] = jnp.transpose(attended[:, columns].astype(jnp.float32)).astype(low)

    def post(c, i, peer):
        mine = tokens.at[pl.ds(pl.multiple_of(c * 224, 16), 224)]
        copy = remote(mine, own_tokens.at[z], token_send.at[i], token_recv.at[i], peer)
        copy.start()
        return copy

    lax.fori_loop(8, 14, far_heads, 0)
    for gather in feed_gathers:
        gather.relay()
    later = ring_gather_forward(shrunk_all, later, ring_send.at[1], ring_recv.at[1])
    for i in range(4, 7):
        lay(arrival(z, i))
    token_copies = [post(z2, 0, across)]
    out_gather.share()
    lax.fori_loop(0, 2, beside_block, 0)
    lax.fori_loop(4, 8, near_heads, 0)
    for i in range(1, 4):
        lay(arrival(z, i))
    token_copies += [post(zp, 1, up), post(zm, 2, down)]
    out_gather.end()
    fetch = pltpu.make_async_copy(out_all, held_rows, out_sem)
    fetch.start()
    lax.fori_loop(0, 2, own_block, 0)
    lay(2 * z)
    own_tokens[z] = tokens[pl.ds(pl.multiple_of(z * 224, 16), 224)]
    fetch.wait()
    for copy in token_copies:
        copy.wait_recv()
    projected = jnp.zeros(total.shape, jnp.float32)
    for c in range(4):
        projected = projected + nt(own_tokens[c], held_rows[:, :, :, :, c].reshape(1536, 384))
    total[...] = projected
    for gather in feed_gathers:
        gather.end()
    ring_gather_end(later)
    for copy in kv_copies + ring + token_copies + out_copies:
        copy.wait_send()
    for copy in saves:
        copy.wait()


GATHER_TURNS = (True, False, False, True, True, False)


def front(hidden, cotangent, gain, weights, tables, prefix):
    any_place = pl.BlockSpec(memory_space=pl.ANY)
    whole = pl.BlockSpec(memory_space=pltpu.VMEM)
    rows, width = hidden.shape
    low, full = jnp.bfloat16, jnp.float32
    block = (2, 4, 2, 2, 48)
    first_shape, in_shapes = (4, rows, width), (block + (384,), block + (256,))
    out_shape = block[:4] + (4, 48, 384)
    turned_shape, rows_shape, lines_shape = (384, 896), (HEADS, 1792, 128), (HEADS, 128, 1792)
    kept = (first_shape, (4, rows, width)) + in_shapes + (block + (960,),) * 2
    kept += (out_shape, block + (960,), turned_shape, rows_shape, lines_shape)
    outs = pl.pallas_call(
        front_kernel,
        out_shape=(
            *(jax.ShapeDtypeStruct(shape, low) for shape in kept),
            jax.ShapeDtypeStruct((384, 896), low),
            jax.ShapeDtypeStruct((896, 384), low),
            jax.ShapeDtypeStruct((HEADS * BLOCKS, 1, 384), full),
            jax.ShapeDtypeStruct((rows, width), full),
        ),
        in_specs=[whole] * 9 + [pl.BlockSpec(memory_space=pltpu.SMEM)],
        out_specs=(any_place,) * 11 + (whole,) * 4,
        scratch_shapes=[
            pltpu.VMEM(first_shape, low),
            pltpu.VMEM((rows, width), low),
            pltpu.VMEM(in_shapes[0], low),
            pltpu.VMEM(in_shapes[1], low),
            pltpu.VMEM((48, 960), low),
            pltpu.VMEM((48, 960), low),
            pltpu.VMEM((4, 48, 384), low),
            pltpu.VMEM((48, 960), low),
            pltpu.VMEM(turned_shape, low),
            pltpu.VMEM(rows_shape, low),
            pltpu.VMEM(lines_shape, low),
            pltpu.VMEM((896, 128), full),
            pltpu.VMEM((896, 128), full),
            pltpu.VMEM((896, 640), full),
            pltpu.VMEM(out_shape, low),
            pltpu.VMEM((4, rows, 384), low),
            pltpu.SemaphoreType.DMA((2, 6)),
            pltpu.SemaphoreType.DMA((2, 6)),
            pltpu.SemaphoreType.DMA((6, 13)),
            pltpu.SemaphoreType.DMA((6, 13)),
            pltpu.SemaphoreType.DMA((3,)),
            pltpu.SemaphoreType.DMA((3,)),
            pltpu.SemaphoreType.DMA((4,)),
            pltpu.SemaphoreType.DMA((4,)),
            pltpu.SemaphoreType.DMA((3,)),
            pltpu.SemaphoreType.DMA((3,)),
            pltpu.SemaphoreType.DMA((11,)),
            pltpu.SemaphoreType.DMA,
        ],
        compiler_params=pltpu.CompilerParams(
            collective_id=0, has_side_effects=True, vmem_limit_bytes=VMEM_MOST
        ),
    )(hidden, cotangent, gain, *weights, *tables, prefix)
    return outs


def tn(a, b):
    return lax.dot_general(a, b, (((0,), (0,)), ((), ())), preferred_element_type=jnp.float32)


def middle_kernel(*refs):
    (hidden, cotangent, projected, gain) = refs[:4]
    (shrunk_from, gate_from, up_from, shrink_from) = refs[4:8]
    (residual, grad_residual, turned_back, gain_two) = refs[8:12]
    (gate_to, up_to, shrink_to, out_to) = refs[12:16]
    (shrunk_all, w_gate, w_up, w_shrink) = refs[16:20]
    (second_all, activated_back, gated, gate_back, up_back) = refs[20:25]
    (parts, came, sums, total) = refs[25:29]
    (grad_gate, grad_up, grad_shrink, out_parts) = refs[29:33]
    (ring_send, ring_recv, load_sem, share_send, share_recv) = refs[33:]
    z, zp, z2, zm, up, down = ring_peers()
    xh, y, core, xl, z = place()

    def flat(weight):
        return weight[...].reshape(1536, 960)

    other = device(xh, y, 1 - core, xl, z)
    hail([up, down, other])
    loads = [
        pltpu.make_async_copy(src, dst, load_sem.at[i])
        for i, (src, dst) in enumerate(
            (
                (shrink_from.at[:, :, core], w_shrink.at[:, :, core]),
                (shrunk_from, shrunk_all),
                (gate_from.at[:, :, core], w_gate.at[:, :, core]),
                (up_from.at[:, :, core], w_up.at[:, :, core]),
            )
        )
    ]
    for load in loads:
        load.start()
    rows = hidden[...].astype(jnp.float32) + RESID * projected[...]
    residual[...] = rows
    scaling = lax.rsqrt(jnp.mean(rows * rows, axis=-1, keepdims=True) + EPS)
    second_all[z] = (rows * scaling * gain[1:2]).astype(jnp.bfloat16)
    meet([up, down, other])
    ring = ring_gather_begin(second_all.at[z], second_all, ring_send.at[0], ring_recv.at[0])
    shares = [
        remote(
            src.at[:, :, core], dst.at[:, :, core], share_send.at[i], share_recv.at[i], other
        )
        for i, (src, dst) in enumerate(
            ((shrink_from, w_shrink), (gate_from, w_gate), (up_from, w_up))
        )
    ]
    for share in shares:
        share.start()
    loads[0].wait()
    loads[1].wait()
    shares[0].wait_recv()
    for c in range(4):
        activated_back[c] = nn(shrunk_all[c], flat(w_shrink))
    loads[2].wait()
    loads[3].wait()
    shares[1].wait_recv()
    shares[2].wait_recv()

    def feed(c):
        gate_value = nn(second_all[c], flat(w_gate))
        up_value = nn(second_all[c], flat(w_up))
        sigmoid_gate = 1.0 / (1.0 + jnp.exp(-gate_value))
        gate_active = gate_value * sigmoid_gate
        gated[c] = (gate_active * up_value).astype(jnp.bfloat16)
        gradient = activated_back[c]
        gate_back[c] = (
            gradient * up_value * sigmoid_gate * (1.0 + gate_value * (1.0 - sigmoid_gate))
        ).astype(jnp.bfloat16)
        up_back[c] = (gradient * gate_active).astype(jnp.bfloat16)
        parts[c] = (nt(gate_back[c], flat(w_gate)) + nt(up_back[c], flat(w_up))).astype(
            jnp.bfloat16
        )

    feed(z)
    ring = ring_gather_forward(second_all, ring, ring_send.at[0], ring_recv.at[0])
    ring[2].wait_recv()
    feed(zm)
    ring[3].wait_recv()
    feed(zp)
    near = ring_scatter_near(parts, came, ring_send.at[1], ring_recv.at[1])
    ring[4].wait_recv()
    ring[5].wait_recv()
    feed(z2)
    far = ring_scatter_far(parts, came, ring_send.at[1], ring_recv.at[1])
    second_rows = second_all[...].reshape(896, 1536)
    saves = []

    def save(src, dst):
        saves.append(pltpu.make_async_copy(src, dst, load_sem.at[4 + len(saves)]))
        saves[-1].start()

    grad_gate[...] = tn(second_rows, gate_back[...].reshape(896, 960)).astype(jnp.bfloat16)
    save(grad_gate, gate_to)
    scatter = ring_scatter_forward(
        parts, came, sums, far + near, ring_send.at[1], ring_recv.at[1]
    )
    grad_up[...] = tn(second_rows, up_back[...].reshape(896, 960)).astype(jnp.bfloat16)
    save(grad_up, up_to)
    grad_shrink[...] = tn(
        shrunk_all[...].reshape(896, 1536), gated[...].reshape(896, 960)
    ).astype(jnp.bfloat16)
    save(grad_shrink, shrink_to)
    for c in range(4):
        out_parts[c] = nt(gated[c], flat(w_shrink)).astype(jnp.bfloat16)
    save(out_parts, out_to)
    for copy in ring + shares:
        copy.wait_send()
    ring_scatter_end(parts, came, total, scatter)
    rows = residual[...]
    scaling = lax.rsqrt(jnp.mean(rows * rows, axis=-1, keepdims=True) + EPS)
    normed = rows * scaling
    gradient = total[...]
    gain_two[...] = jnp.sum(gradient * normed, axis=0, keepdims=True)
    gradient = gradient * gain[1:2]
    back = cotangent[...].astype(jnp.float32) + scaling * (
        gradient - normed * jnp.mean(gradient * normed, axis=-1, keepdims=True)
    )
    grad_residual[...] = back
    turned_back[...] = (RESID * back).astype(jnp.bfloat16)
    for copy in saves:
        copy.wait()


def middle(hidden, cotangent, projected, gain, shrunk_all, w_gate, w_up, w_shrink):
    any_place = pl.BlockSpec(memory_space=pl.ANY)
    whole = pl.BlockSpec(memory_space=pltpu.VMEM)
    rows, width = hidden.shape
    low, full = jnp.bfloat16, jnp.float32
    return pl.pallas_call(
        middle_kernel,
        out_shape=(
            jax.ShapeDtypeStruct((rows, width), full),
            jax.ShapeDtypeStruct((rows, width), full),
            jax.ShapeDtypeStruct((rows, width), low),
            jax.ShapeDtypeStruct((1, width), full),
            jax.ShapeDtypeStruct((1536, 960), low),
            jax.ShapeDtypeStruct((1536, 960), low),
            jax.ShapeDtypeStruct((1536, 960), low),
            jax.ShapeDtypeStruct((4, rows, width), low),
        ),
        in_specs=[whole] * 4 + [any_place] * 4,
        out_specs=(whole,) * 4 + (any_place,) * 4,
        scratch_shapes=[
            pltpu.VMEM((4, rows, width), low),
            pltpu.VMEM((2, 4, 2, 2, 48, 960), low),
            pltpu.VMEM((2, 4, 2, 2, 48, 960), low),
            pltpu.VMEM((2, 4, 2, 2, 48, 960), low),
            pltpu.VMEM((4, rows, width), low),
            pltpu.VMEM((4, rows, 960), full),
            pltpu.VMEM((4, rows, 960), low),
            pltpu.VMEM((4, rows, 960), low),
            pltpu.VMEM((4, rows, 960), low),
            pltpu.VMEM((4, rows, width), low),
            pltpu.VMEM((6, rows // 2, width), low),
            pltpu.VMEM((2, rows // 2, width), low),
            pltpu.VMEM((rows, width), full),
            pltpu.VMEM((1536, 960), low),
            pltpu.VMEM((1536, 960), low),
            pltpu.VMEM((1536, 960), low),
            pltpu.VMEM((4, rows, width), low),
            pltpu.SemaphoreType.DMA((2, 6)),
            pltpu.SemaphoreType.DMA((2, 6)),
            pltpu.SemaphoreType.DMA((8,)),
            pltpu.SemaphoreType.DMA((3,)),
            pltpu.SemaphoreType.DMA((3,)),
        ],
        compiler_params=pltpu.CompilerParams(
            collective_id=4, has_side_effects=True, vmem_limit_bytes=VMEM_MOST
        ),
    )(hidden, cotangent, projected, gain, shrunk_all, w_gate, w_up, w_shrink)


class Scatter:
    def __init__(self, parts, came, across, lined, last, x_first, send_sem, recv_sem):
        self.parts, self.came, self.across = parts, came, across
        self.lined, self.last, self.x_first = lined, last, x_first
        self.send_sem, self.recv_sem, self.used, self.copies = send_sem, recv_sem, 0, []
        xh, y, core, xl, z = place()
        ys, xs, y_peers, x_peers, self.other = plane()
        if x_first:
            self.lines, self.peers = xs[::-1] + [(xh, xl)], x_peers[::-1]
            self.mine, self.targets, self.target_peers = y, ys, y_peers
        else:
            self.lines, self.peers = ys[::-1] + [y], y_peers[::-1]
            self.mine, self.targets, self.target_peers = (xh, xl), xs, x_peers

    def send(self, src, dst, peer):
        copy = remote(src, dst, self.send_sem.at[self.used], self.recv_sem.at[self.used], peer)
        self.used += 1
        copy.start()
        self.copies.append(copy)
        return copy

    def in_line(self, line):
        return (line[0], slice(None), line[1]) if self.x_first else (slice(None), line)

    def begin(self):
        core = place()[2]
        self.first = []
        for line in self.lines:
            if self.x_first:
                src = self.parts.at[line[0], :, 1 - core, line[1]]
            else:
                src = self.parts.at[:, line, 1 - core]
            self.first.append(self.send(src, self.came.at[self.in_line(line)], self.other))

    def stage(self, held, sem):
        copy = pltpu.make_async_copy(self.parts.at[:, :, place()[2]], held, sem)
        copy.start()
        return copy

    def at(self, line, i):
        return (line[0], i, line[1]) if self.x_first else (i // 2, line, lax.rem(i, 2))

    def spot(self, i):
        if self.x_first:
            return (i,)
        return (i[0], i[1]) if isinstance(i, tuple) else (i // 2, lax.rem(i, 2))

    def fold(self, held=None):
        core = place()[2]
        self.second = []
        for k, (line, copy) in enumerate(zip(self.lines, self.first)):
            copy.wait_recv()

            def add(i, carry, line=line):
                at = self.at(line, i)
                if held is None:
                    own = self.parts[at[0], at[1], core, at[2]]
                else:
                    own = held[at]
                self.came[at] = (
                    own.astype(jnp.float32) + self.came[at].astype(jnp.float32)
                ).astype(jnp.bfloat16)
                return carry

            lax.fori_loop(0, 4, add, 0)
            if k < 3:
                self.second.append(
                    self.send(
                        self.came.at[self.in_line(line)], self.across.at[k], self.peers[k]
                    )
                )

    def line(self):
        for copy in self.second:
            copy.wait_recv()

        def add(i, carry):
            spot = self.spot(i)
            total = self.came[self.at(self.lines[3], i)].astype(jnp.float32)
            for k in range(3):
                total = total + self.across[(k,) + spot].astype(jnp.float32)
            self.lined[spot] = total.astype(jnp.bfloat16)
            return carry

        lax.fori_loop(0, 4, add, 0)
        self.third = [
            self.send(self.lined.at[self.spot(target)], self.last.at[k], peer)
            for k, (target, peer) in enumerate(zip(self.targets, self.target_peers))
        ]

    def end(self, total_ref):
        for copy in self.third:
            copy.wait_recv()
        total = self.lined[self.spot(self.mine)].astype(jnp.float32)
        for k in range(3):
            total = total + self.last[k].astype(jnp.float32)
        total_ref[...] = total
        for copy in self.copies:
            copy.wait_send()


def scatter_room(width, x_first):
    line = (4,) if x_first else (2, 2)
    return [
        pltpu.VMEM((2, 4, 2, 48, width), jnp.bfloat16),
        pltpu.VMEM((3,) + line + (48, width), jnp.bfloat16),
        pltpu.VMEM(line + (48, width), jnp.bfloat16),
        pltpu.VMEM((3, 48, width), jnp.bfloat16),
    ]


def back_kernel(*refs):
    (own, out_from, query_from, rest_from, first_from, out_terms) = refs[:6]
    gradients, refs = refs[6:9], refs[1:]
    (turned, kv_rows, kv_lines, attended, tokens, log_total) = refs[8:14]
    (cos_ref, sin_ref, hidden, gain_two, prefix) = refs[14:19]
    (shrunk_total, first_total) = refs[19:21]
    totals = refs[21:26]
    everywhere = refs[26]
    (proj_all, w_out, w_in, grad_tokens, grad_lines, grad_queries, grad_packed) = refs[27:34]
    (sums, outgoing, incoming, parts, came_one, came_two, ring_sums) = refs[34:41]
    stages, out_parts, in_parts = refs[41:43], refs[43], refs[44]
    rooms = refs[45:65]
    (key_cos, key_sin, gathered) = refs[65:68]
    (ring_send, ring_recv, plane_send, plane_recv, kv_send, kv_recv, load_sem) = refs[68:75]
    (sum_send, sum_recv) = refs[75:]
    xh, y, core, xl, z = place()
    z, zp, z2, zm, up, down = ring_peers()
    ys, xs, y_peers, x_peers, other = plane()
    beside = device(xh, y, core, 1 - xl, z)
    column = [
        device(xh, y, c, xl, lax.rem(z + d, 4))
        for d, c in ((1, core), (3, core), (0, 1 - core), (2, core))
        + ((1, 1 - core), (3, 1 - core), (2, 1 - core))
    ]
    peers = column + y_peers + x_peers
    hail(peers)
    sums[...] = jnp.zeros_like(sums)
    key_tables(cos_ref, sin_ref, key_cos, key_sin)
    meet(peers)
    ring = ring_gather_begin(own, proj_all, ring_send.at[0], ring_recv.at[0])
    every = [
        Scatter(
            terms,
            *rooms[4 * i : 4 * i + 4],
            SCATTER_TURNS[i],
            plane_send.at[i],
            plane_recv.at[i],
        )
        for i, terms in enumerate(tuple(gradients) + (out_parts, in_parts))
    ]
    feed, out_scatter, in_scatter = every[:3], every[3], every[4]
    for scatter in feed:
        scatter.begin()

    def load(src, dst, i):
        copy = pltpu.make_async_copy(src, dst, load_sem.at[i])
        copy.start()
        return copy

    load_out = load(out_from.at[:, :, :, :, z], w_out, 0)
    keep = load(own, proj_all.at[z], 1)
    staged = [feed[i].stage(stages[i], load_sem.at[2 + i]) for i in range(2)]
    load_terms = load(out_terms, parts, 5)
    load_query = load(query_from, w_in.at[:, pl.ds(0, 384)], 6)
    load_rest = load(rest_from, w_in.at[:, pl.ds(384, 256)], 8)

    def give(c, start=0, count=224):
        rows = pl.ds(pl.multiple_of(c * 224 + start, 16), count)
        grad_tokens[rows] = nn(
            proj_all[c, start : start + count], w_out[...].reshape(1536, 384)
        ).astype(jnp.bfloat16)

    def lay(b):
        columns = pl.ds(pl.multiple_of(b * 128, 128), 128)
        grad_lines[:, columns] = jnp.transpose(
            grad_tokens[columns].astype(jnp.float32)
        ).astype(jnp.bfloat16)

    def block(b, g):
        columns = pl.ds(pl.multiple_of(b * 128, 128), 128)

        def run(span):
            head_rows = [
                pl.ds(pl.multiple_of((g * GROUP + h) * HD, HD), HD) for h in range(GROUP)
            ]
            queries = jnp.concatenate([turned[r, columns] for r in head_rows], axis=1)
            gradient = jnp.concatenate([grad_lines[r, columns] for r in head_rows], axis=1)
            held = jnp.concatenate([attended[r, columns] for r in head_rows], axis=1)
            inner = jnp.sum(
                gradient.astype(jnp.float32) * held.astype(jnp.float32), axis=0, keepdims=True
            )
            nothing = jnp.zeros_like(queries)
            both = jnp.concatenate(
                [
                    jnp.concatenate([queries, nothing], axis=1),
                    jnp.concatenate([nothing, gradient], axis=1),
                ],
                axis=0,
            )
            products = nn(kv_rows[g, :span], both)
            key_index = lax.broadcasted_iota(jnp.int32, (span, 384), 0)
            probs = jnp.exp(
                jnp.where(key_index < limits(prefix, xl, b), products[:, :384], NEG)
                - log_total[b * HEADS + g]
            )
            grad_scores = (probs * (products[:, 384:] - inner)).astype(jnp.bfloat16)
            sums[g, :span] += nt(
                jnp.concatenate([grad_scores, probs.astype(jnp.bfloat16)], axis=1), both
            )
            total = nn(kv_lines[g, :HD, :span], grad_scores) * HD ** (-0.5)
            cos_here, sin_here = cos_ref[:, columns], sin_ref[:, columns]
            back = [
                turn_back(total[:, h * 128 : (h + 1) * 128], cos_here, sin_here)
                for h in range(GROUP)
            ]
            grad_queries[g, columns] = jnp.transpose(jnp.concatenate(back, axis=0)).astype(
                jnp.bfloat16
            )

        by_span(xl, b, run)

    def both_heads(t, carry):
        block(arrival(z, lax.div(t, 2)), lax.rem(t, 2))
        return carry

    keep.wait()
    load_out.wait()
    give(z)
    lay(2 * z)

    def own_block(g, carry):
        block(2 * z, g)
        return carry

    lax.fori_loop(0, 2, own_block, 0)
    ring = ring_gather_forward(proj_all, ring, ring_send.at[0], ring_recv.at[0])
    give(zm, 112, 112)
    give(zp, 0, 112)
    lay(arrival(z, 1))

    def beside_block(g, carry):
        block(arrival(z, 1), g)
        return carry

    staged[0].wait()
    feed[0].fold(stages[0])
    staged[0] = feed[2].stage(stages[0], load_sem.at[4])
    staged[1].wait()
    feed[1].fold(stages[1])
    staged[0].wait()
    feed[2].fold(stages[0])
    lax.fori_loop(0, 2, beside_block, 0)
    ring[2].wait_recv()
    give(zm, 0, 112)
    ring[3].wait_recv()
    give(zp, 112, 112)
    for i in range(2, 4):
        lay(arrival(z, i))
    lax.fori_loop(4, 8, both_heads, 0)
    ring[4].wait_recv()
    ring[5].wait_recv()
    give(z2)
    for i in range(4, 7):
        lay(arrival(z, i))
    for copy in ring:
        copy.wait_send()
    out_parts[...] = (
        tn(proj_all[...].reshape(896, 1536), tokens[...])
        .astype(jnp.bfloat16)
        .reshape(2, 4, 2, 2, 48, 384)
    )
    out_scatter.begin()
    load_first = load(first_from, proj_all, 7)
    load_terms.wait()
    shrunk = ring_scatter_begin(parts, came_one, ring_send.at[1], ring_recv.at[1])

    def exchange(g):
        theirs = sums[g, pl.ds(pl.multiple_of((1 - xl) * 896, 128), 896)]
        outgoing[g] = theirs.astype(jnp.bfloat16)
        copy = remote(outgoing.at[g], incoming.at[g], kv_send.at[g], kv_recv.at[g], beside)
        copy.start()
        return copy

    def far_block(g):
        def body(i, carry):
            block(arrival_far(z, i), g)
            return carry

        lax.fori_loop(4, 7, body, 0)

    far_block(0)
    kv_copies = [exchange(0)]
    shrunk = ring_scatter_forward(
        parts, came_one, ring_sums, shrunk, ring_send.at[1], ring_recv.at[1]
    )
    out_scatter.fold()
    far_block(1)
    kv_copies.append(exchange(1))
    for scatter in feed:
        scatter.line()
    out_scatter.line()
    load_query.wait()
    load_rest.wait()
    load_first.wait()
    ring_scatter_end(parts, came_one, shrunk_total, shrunk)
    for g in range(HEADS):
        kv_copies[g].wait()
        mine = sums[g, pl.ds(pl.multiple_of(xl * 896, 128), 896)] + incoming[g].astype(
            jnp.float32
        )
        mine = mine * key_cos[...] - swap_halves(mine) * key_sin[...]
        grad_packed[:, g * 320 : g * 320 + 192] = grad_queries[g]
        grad_packed[:, g * 320 + 192 : g * 320 + 320] = mine.astype(jnp.bfloat16)

    def spread(c):
        rows = pl.ds(pl.multiple_of(c * 224, 16), 224)
        parts[c] = nt(grad_packed[rows], w_in[...]).astype(jnp.bfloat16)

    spread(z2)
    far = ring_scatter_far(parts, came_two, ring_send.at[2], ring_recv.at[2])
    spread(zp)
    spread(zm)
    near = ring_scatter_near(parts, came_two, ring_send.at[2], ring_recv.at[2])
    in_parts[...] = (
        tn(proj_all[...].reshape(896, 1536), grad_packed[...])
        .astype(jnp.bfloat16)
        .reshape(2, 4, 2, 2, 48, 640)
    )
    in_scatter.begin()
    spread(z)
    in_scatter.fold()
    ring = ring_scatter_forward(
        parts, came_two, ring_sums, far + near, ring_send.at[2], ring_recv.at[2]
    )
    for i in range(4):
        every[i].end(totals[i])
    in_scatter.line()
    ring_scatter_end(parts, came_two, first_total, ring)
    rows = hidden[...].astype(jnp.float32)
    scaling = lax.rsqrt(jnp.mean(rows * rows, axis=-1, keepdims=True) + EPS)
    gain_one = jnp.sum(first_total[...] * rows * scaling, axis=0, keepdims=True)
    in_scatter.end(totals[4])
    squares = jnp.zeros((1, 1), jnp.float32)
    for total in totals:
        terms = total[...]
        squares = squares + jnp.sum(
            jnp.sum(terms * terms, axis=0, keepdims=True), axis=1, keepdims=True
        )
    for k in range(3):
        everywhere[k : k + 1] = gain_one[:, k * 512 : (k + 1) * 512]
        everywhere[3 + k : 4 + k] = gain_two[:, k * 512 : (k + 1) * 512]
    everywhere[6:8] = jnp.broadcast_to(squares, (2, 512))
    used = 0
    groups = ((column, z * 2 + core, 8), (x_peers, xh * 2 + xl, 4), (y_peers, y, 4))
    for axis, (group, here, count) in enumerate(groups):
        gathered[axis, here] = everywhere[...]
        spot = gathered.at[axis, here]
        copies = []
        for peer in group:
            copies.append(remote(spot, spot, sum_send.at[used], sum_recv.at[used], peer))
            copies[-1].start()
            used += 1
        for copy in copies:
            copy.wait()
        order = gathered[axis, 0]
        for k in range(1, count):
            order = order + gathered[axis, k]
        everywhere[...] = order


SCATTER_TURNS = (False, False, True, True, False)


def back(
    own, w_out, w_query, w_rest, first_all, out_terms, gradients, saved, tables, hidden, gain_two, prefix
):
    any_place = pl.BlockSpec(memory_space=pl.ANY)
    whole = pl.BlockSpec(memory_space=pltpu.VMEM)
    rows, width = own.shape
    low, full = jnp.bfloat16, jnp.float32
    widths = [g.shape[-1] for g in gradients] + [384, 640]
    rooms = []
    for w, turn_first in zip(widths, SCATTER_TURNS):
        rooms += scatter_room(w, turn_first)
    return pl.pallas_call(
        back_kernel,
        out_shape=(jax.ShapeDtypeStruct((rows, width), full),) * 2
        + tuple(jax.ShapeDtypeStruct((48, w), full) for w in widths)
        + (jax.ShapeDtypeStruct((8, 512), full),),
        in_specs=[whole]
        + [any_place] * 8
        + [whole] * 10
        + [pl.BlockSpec(memory_space=pltpu.SMEM)],
        out_specs=(whole,) * 8,
        scratch_shapes=[
            pltpu.VMEM((4, rows, width), low),
            pltpu.VMEM((2, 4, 2, 2, 48, 384), low),
            pltpu.VMEM((1536, 640), low),
            pltpu.VMEM((896, 384), low),
            pltpu.VMEM((384, 896), low),
            pltpu.VMEM((HEADS, 896, 192), low),
            pltpu.VMEM((896, 640), low),
            pltpu.VMEM((HEADS, 1792, 128), full),
            pltpu.VMEM((HEADS, 896, 128), low),
            pltpu.VMEM((HEADS, 896, 128), low),
            pltpu.VMEM((4, rows, width), low),
            pltpu.VMEM((6, rows // 2, width), low),
            pltpu.VMEM((6, rows // 2, width), low),
            pltpu.VMEM((2, rows // 2, width), low),
            pltpu.VMEM((2, 4, 2, 48, 960), low),
            pltpu.VMEM((2, 4, 2, 48, 960), low),
            pltpu.VMEM((2, 4, 2, 2, 48, 384), low),
            pltpu.VMEM((2, 4, 2, 2, 48, 640), low),
            *rooms,
            pltpu.VMEM((896, 128), full),
            pltpu.VMEM((896, 128), full),
            pltpu.VMEM((3, 8, 8, 512), full),
            pltpu.SemaphoreType.DMA((3, 6)),
            pltpu.SemaphoreType.DMA((3, 6)),
            pltpu.SemaphoreType.DMA((5, 10)),
            pltpu.SemaphoreType.DMA((5, 10)),
            pltpu.SemaphoreType.DMA((2,)),
            pltpu.SemaphoreType.DMA((2,)),
            pltpu.SemaphoreType.DMA((9,)),
            pltpu.SemaphoreType.DMA((13,)),
            pltpu.SemaphoreType.DMA((13,)),
        ],
        compiler_params=pltpu.CompilerParams(
            collective_id=2, has_side_effects=True, vmem_limit_bytes=BACK_VMEM
        ),
    )(
        own,
        w_out,
        w_query,
        w_rest,
        first_all,
        out_terms,
        *(g.reshape(2, 4, 2, 2, 48, g.shape[-1]) for g in gradients),
        *saved,
        *tables,
        hidden,
        gain_two,
        prefix,
    )


BACK_VMEM = 63 * 2**20


def finish_kernel(*refs):
    (sums, grad_first, hidden, grad_residual, residual, shrunk) = refs[:6]
    (gains, gains_first, gains_second) = refs[6:9]
    (grad_gate, grad_up, grad_shrink, grad_output, grad_input) = refs[9:14]
    masters = [refs[14 + 3 * i : 17 + 3 * i] for i in range(4)]
    (block_output, input_gradient, norm_ref) = refs[26:29]
    gains_new = refs[29:32]
    news = [refs[32 + 3 * i : 35 + 3 * i] for i in range(4)]
    block_output[...] = (residual[...] + RESID * shrunk[...]).astype(jnp.bfloat16)
    rows = hidden[...].astype(jnp.float32)
    scaling = lax.rsqrt(jnp.mean(rows * rows, axis=-1, keepdims=True) + EPS)
    normed = rows * scaling
    gradient = grad_first[...] * gains[0:1]
    input_gradient[...] = grad_residual[...] + scaling * (
        gradient - normed * jnp.mean(gradient * normed, axis=-1, keepdims=True)
    )
    grad_gains = jnp.concatenate(
        [
            jnp.concatenate([sums[3 * r + k : 3 * r + k + 1] for k in range(3)], axis=1)
            for r in range(2)
        ],
        axis=0,
    )
    gain_squares = jnp.sum(
        jnp.sum(grad_gains * grad_gains, axis=0, keepdims=True), axis=1, keepdims=True
    )
    gradient_norm = jnp.sqrt(sums[6:7, 0:1] + gain_squares)
    norm_ref[...] = gradient_norm
    factor = jnp.minimum(1.0, MAX_NORM / (gradient_norm + 1e-06))

    def put(targets, results):
        for target, result in zip(targets, results):
            target[...] = result

    put(
        gains_new,
        adamw(
            gains[...], factor * grad_gains, gains_first[...], gains_second[...], GAIN_RATE, 0.0
        ),
    )
    for i, terms in ((0, grad_input), (1, grad_output), (3, grad_shrink)):
        weight, first, second = masters[i]
        put(news[i], adamw(weight[...], factor * terms[...], first[...], second[...], RATE, DECAY))
    for k, terms in enumerate((grad_gate, grad_up)):
        weight, first, second = masters[2]
        results = adamw(weight[k], factor * terms[...], first[k], second[k], RATE, DECAY)
        for target, result in zip(news[2], results):
            target[k] = result


def finish(sums, rows_in, gains, gradients, masters):
    full = jnp.float32
    flat = [array for group in masters for array in group]

    def cut(array):
        shape = array.shape[:-2] + (array.shape[-2] // 2, array.shape[-1])
        lead = (0,) * (array.ndim - 2)
        return pl.BlockSpec(shape, lambda i: lead + (i, 0))

    def kept(shape):
        return pl.BlockSpec(shape, lambda i: (0, 0))

    width = rows_in[0].shape[1]
    rows = jax.ShapeDtypeStruct(rows_in[0].shape, full)
    return pl.pallas_call(
        finish_kernel,
        grid=(2,),
        out_shape=(
            jax.ShapeDtypeStruct(rows.shape, jnp.bfloat16),
            rows,
            jax.ShapeDtypeStruct((1, 1), full),
            *(jax.ShapeDtypeStruct((2, width), full) for _ in range(3)),
            *(jax.ShapeDtypeStruct(array.shape, full) for array in flat),
        ),
        in_specs=[kept(sums.shape)]
        + [cut(array) for array in rows_in]
        + [kept(array.shape) for array in gains]
        + [cut(array) for array in gradients]
        + [cut(array) for array in flat],
        out_specs=(cut(rows), cut(rows), kept((1, 1)))
        + (kept((2, width)),) * 3
        + tuple(cut(array) for array in flat),
        compiler_params=pltpu.CompilerParams(vmem_limit_bytes=VMEM_MOST),
    )(sums, *rows_in, *gains, *gradients, *flat)


def shards(
    hidden_in,
    cotangent,
    prefix,
    positions,
    norm_gains,
    gains_first,
    gains_second,
    input_weight,
    input_first,
    input_second,
    output_weight,
    output_first,
    output_second,
    expand_weight,
    expand_first,
    expand_second,
    shrink_weight,
    shrink_first,
    shrink_second,
):
    low = jnp.bfloat16
    hidden, upstream = hidden_in[0], cotangent[0]
    masters = (
        (input_weight, input_first, input_second),
        (output_weight.T, output_first.T, output_second.T),
        (expand_weight, expand_first, expand_second),
        (shrink_weight.T, shrink_first.T, shrink_second.T),
    )
    tables = angles(positions)
    (
        first_all,
        shrunk_all,
        w_query,
        w_rest,
        w_gate,
        w_up,
        w_out,
        w_shrink,
        turned,
        kv_rows,
        kv_lines,
        attended,
        tokens,
        log_total,
        projected,
    ) = front(
        hidden,
        upstream,
        norm_gains,
        (input_weight, expand_weight, output_weight.T, shrink_weight.T),
        tables,
        prefix,
    )
    (
        residual,
        grad_residual,
        projected_gradient,
        gain_two,
        grad_gate,
        grad_up,
        grad_shrink,
        out_parts,
    ) = middle(
        hidden, upstream, projected, norm_gains, shrunk_all, w_gate, w_up, w_shrink
    )
    shrunk, grad_first, *gradients, sums = back(
        projected_gradient,
        w_out,
        w_query.reshape(1536, 384),
        w_rest.reshape(1536, 256),
        first_all,
        out_parts,
        (grad_gate, grad_up, grad_shrink),
        (turned, kv_rows, kv_lines, attended, tokens, log_total),
        tables,
        hidden,
        gain_two,
        prefix,
    )
    outs = finish(
        sums,
        (grad_first, hidden, grad_residual, residual, shrunk),
        (norm_gains, gains_first, gains_second),
        gradients,
        masters,
    )
    block_output, input_gradient, gradient_norm = outs[0], outs[1], outs[2].reshape(())
    gains_new, input_new, output_new, expand_new, shrink_new = (
        outs[3 + 3 * i : 6 + 3 * i] for i in range(5)
    )
    return (
        block_output[None],
        input_gradient[None],
        gradient_norm,
        *gains_new,
        *input_new,
        *(array.T for array in output_new),
        *expand_new,
        *(array.T for array in shrink_new),
    )


def solution(mesh):
    return jax.shard_map(
        shards,
        mesh=mesh,
        in_specs=(
            P("shard", ("context", "tensor"), None),
            P("shard", ("context", "tensor"), None),
            P("shard"),
            P("shard", "context"),
            P(),
            P(),
            P(),
            P(("shard", "context"), "tensor"),
            P(("shard", "context"), "tensor"),
            P(("shard", "context"), "tensor"),
            P("tensor", ("shard", "context")),
            P("tensor", ("shard", "context")),
            P("tensor", ("shard", "context")),
            P(None, ("shard", "context"), "tensor"),
            P(None, ("shard", "context"), "tensor"),
            P(None, ("shard", "context"), "tensor"),
            P("tensor", ("shard", "context")),
            P("tensor", ("shard", "context")),
            P("tensor", ("shard", "context")),
        ),
        out_specs=(
            P("shard", ("context", "tensor"), None),
            P("shard", ("context", "tensor"), None),
            P(),
            P(),
            P(),
            P(),
            P(("shard", "context"), "tensor"),
            P(("shard", "context"), "tensor"),
            P(("shard", "context"), "tensor"),
            P("tensor", ("shard", "context")),
            P("tensor", ("shard", "context")),
            P("tensor", ("shard", "context")),
            P(None, ("shard", "context"), "tensor"),
            P(None, ("shard", "context"), "tensor"),
            P(None, ("shard", "context"), "tensor"),
            P("tensor", ("shard", "context")),
            P("tensor", ("shard", "context")),
            P("tensor", ("shard", "context")),
        ),
        check_vma=False,
    )
```
